32 devices in a mesh: stack: 2 (over y), gx: 4 (over z), gy: 2 (over x), gz: 2 (over core).
Axes of the slice: x: 2, y: 2, z: 4, core: 2. Of those that a mesh axis runs over, the one named last changes fastest.
Arguments:
- initial_solid_warmth: float32 [16, 256, 512], P(('stack', 'gz'), 'gy', 'gx'), parts along dimension 0, may hold values from 0 to 1
- dissipated_power: float32 [16, 256, 512], P(('stack', 'gz'), 'gy', 'gx'), parts along dimension 0, may hold values from 0.1 to 2
- thermal_storage: float32 [16, 256, 512], P(('stack', 'gz'), 'gy', 'gx'), parts along dimension 0, may hold values from 0.1 to 1
- thermal_conductance_pair: float32 [2, 16, 256, 512], P(None, ('stack', 'gz'), 'gy', 'gx'), parts along dimension 1, may hold values from 0.3 to 3
- fluid_warmth: float32 [8, 128, 128], P(('stack', 'gy', 'gz'), 'gx'), parts along dimension 0, may hold values from 0 to 1
- exchange_coefficient: float32 [8, 128, 128], P(('stack', 'gy', 'gz'), 'gx'), parts along dimension 0, may hold values from 0.5 to 4
- channel_block_holder: int32 [4, 128, 1], replicated, may hold values from 0 to 3; in each aligned block of 32 rows (0 to 31, 32 to 63, ..., all dimensions but the last counted through in order) at most 16 rows name the same one
- channel_stratum_slot: int32 [4, 128], replicated, may hold values from 0 to 3
- channel_transverse_slot: int32 [4, 128], replicated, may hold values from 0 to 127
Outputs:
- temperature_out: float32 [16, 256, 512], P(('stack', 'gz'), 'gy', 'gx'), parts along dimension 0
- coolant_out: float32 [8, 128, 128], P(('stack', 'gy', 'gz'), 'gx'), parts along dimension 0
The draws below stay inside these ranges and needn't reach their ends.
There are 2 independent parts, one for each index of `stack`. The reference program is written for one: setup_inputs(seed, part) draws one part's arguments, and reference() takes and returns one part's arrays. A program takes and returns all parts, laid end to end along the dimension named above; an argument that names none is the same for every part. Nothing has to cross between parts.
Inputs may be any that keep to these rules, and one draw needn't show every extreme that they name: `channel_block_holder`: within the 32 segments of one device (aligned blocks of 32 entries along the second dimension) no tile is named more than 16 times; some tile is named exactly 16 times.
All inputs are finite; a program needn't handle non-finite values.
Results may differ from the reference program's by a relative error of at most 0.00012.
Values sent between devices are 32-bit elements; how exact they have to be, the bound alone decides.
No kernel may reach another device: no remote copies, remote signals or barrier semaphores. Data moves between devices by JAX's collectives and lax.ppermute only.
A program may use at most 64 MiB of HBM per device.

```python
import math
import jax
import jax.numpy as jnp
import numpy as np

CZ = 4
CY = 128
LOCAL_STREAMWISE = 128
SEG = 32
STEPS = 2
ITERS = 4
SILICON_STRATA = 8
TRANSVERSE_COUNT = 256
STREAMWISE_COUNT = 512
NYZ = 4
NSEG = 128
SLOTS = 16
N_GX = 4
N_GZ = 2


def touch_ends(array, rng, smallest, high):
    spot = [jax.random.randint(jax.random.fold_in(rng, axis), (), 0, length) for axis, length in enumerate(array.shape)]
    longest = array.shape.index(max(array.shape))
    neighbour = spot[:longest] + [(spot[longest] + 1) % array.shape[longest]] + spot[longest + 1:]
    return array.at[tuple(spot)].set(smallest).at[tuple(neighbour)].set(high)


def shard_levels(rng, shape, cuts, low, top_value):
    factor_of, own = 1.0, jax.random.fold_in(rng, 6)
    for axis_at, shards_of in cuts:
        draws = jnp.exp(jax.random.uniform(jax.random.fold_in(own, axis_at), (shards_of,), jnp.float32, low / len(cuts), top_value / len(cuts)))
        factor_of = factor_of * jnp.repeat(draws, shape[axis_at] // shards_of).reshape([-1 if axis == axis_at else 1 for axis in range(len(shape))])
    return factor_of


def deal_out(key, own, number, rows, number_of, top, most, slope):
    ranking = jax.random.permutation(key, number_of)
    packed, ordinary = load_shares(number_of, rows * top, most, slope, True), load_shares(number_of, rows * top, most, slope, False)
    places = jnp.arange(number_of)

    def named(lengths, rotation):
        used = int((lengths > 0).sum())
        fixed = max(1, used // 4)
        passed = fixed + (places - fixed + rotation * (used - fixed)) % max(1, number_of - fixed)
        return jnp.zeros((number_of,), jnp.int32).at[ranking[jnp.where(places < fixed, places, passed)]].set(jnp.asarray(lengths, jnp.int32))

    lengths = jnp.where(number % 4 == 0, named(packed, number // 4), named(ordinary, number - number // 4 - 1))
    mixed = jax.random.permutation(jax.random.fold_in(own, 3), number_of)
    giver, taker = mixed[0:number_of // 2 * 2:2], mixed[1:number_of // 2 * 2:2]
    margin = jnp.minimum(lengths[giver] - 1, most - lengths[taker]) // 2
    margin = jnp.where((giver == ranking[0]) | (taker == ranking[0]) | (lengths[taker] == 0), 0, jnp.maximum(margin, 0))
    passed = jax.random.randint(jax.random.fold_in(own, 4), (number_of // 2,), 0, 1 << 20) % (margin + 1)
    lengths = lengths.at[giver].add(-passed).at[taker].add(passed)
    members = jnp.searchsorted(jnp.cumsum(lengths), jnp.arange(rows * top), side="right").astype(jnp.int32)
    table = members.reshape(top, rows).T
    table = table[jax.random.permutation(jax.random.fold_in(own, 1), rows)]
    rotation = jax.random.randint(jax.random.fold_in(own, 2), (rows, 1), 0, top)
    return jnp.take_along_axis(table, (jnp.arange(top)[None, :] + rotation) % top, axis=1)


def load_shares(number_of, total, limit, skew, full):
    loads = [(1 << 20) // math.isqrt(rank ** skew) + 1 for rank in range(1, number_of + 1)]
    largest = limit if full else min(limit, max(-(-total // number_of), total * loads[0] // sum(loads)))
    least = 1 if total - largest >= number_of - 1 else 0
    counts, spare = [largest] + [least] * (number_of - 1), total - largest - least * (number_of - 1)
    while spare > 0:
        free = [i for i in range(1, number_of) if counts[i] < largest] or [i for i in range(1, number_of) if counts[i] < limit]
        whole, left = sum([loads[i] for i in free]), spare
        for i in free:
            addition = min(limit - counts[i], max(1, left * loads[i] // whole), spare)
            counts[i] = counts[i] + addition
            spare = spare - addition
    return np.array(counts)


def setup_inputs(seed: int = 0, part: int = 0) -> dict:
    arg_keys = jax.random.split(jax.random.key(seed), 10)
    part_keys = jax.random.split(jax.random.fold_in(arg_keys[9], part), 10)
    initial_solid_warmth = jnp.clip(1.0 * jax.random.uniform(part_keys[0], (SILICON_STRATA, TRANSVERSE_COUNT, STREAMWISE_COUNT), jnp.float32) ** shard_levels(part_keys[0], (SILICON_STRATA, TRANSVERSE_COUNT, STREAMWISE_COUNT), ((0, 2), (1, 2), (2, 4)), -0.2, 0.2), 0.0, 1.0)
    dissipated_power = jnp.clip(jnp.exp(math.log(2.0) - 2.9957323 * jax.random.uniform(part_keys[1], (SILICON_STRATA, TRANSVERSE_COUNT, STREAMWISE_COUNT), jnp.float32) ** shard_levels(part_keys[1], (SILICON_STRATA, TRANSVERSE_COUNT, STREAMWISE_COUNT), ((0, 2), (1, 2), (2, 4)), -0.2, 0.2)), 0.1, 2.0)
    thermal_storage = jnp.clip(jnp.exp(math.log(1.0) - 2.3025851 * jax.random.uniform(part_keys[2], (SILICON_STRATA, TRANSVERSE_COUNT, STREAMWISE_COUNT), jnp.float32) ** shard_levels(part_keys[2], (SILICON_STRATA, TRANSVERSE_COUNT, STREAMWISE_COUNT), ((0, 2), (1, 2), (2, 4)), -0.2, 0.2)), 0.1, 1.0)
    thermal_conductance_pair = jnp.clip(jnp.exp(math.log(3.0) - 2.3025851 * jax.random.uniform(part_keys[3], (2, SILICON_STRATA, TRANSVERSE_COUNT, STREAMWISE_COUNT), jnp.float32) ** shard_levels(part_keys[3], (2, SILICON_STRATA, TRANSVERSE_COUNT, STREAMWISE_COUNT), ((1, 2), (2, 2), (3, 4)), -0.2, 0.2)), 0.3, 3.0)
    fluid_warmth = jnp.clip(1.0 * jax.random.uniform(part_keys[4], (NYZ, NSEG, LOCAL_STREAMWISE), jnp.float32) ** shard_levels(part_keys[4], (NYZ, NSEG, LOCAL_STREAMWISE), ((0, 4), (1, 4)), -0.2, 0.2), 0.0, 1.0)
    exchange_coefficient = jnp.clip(jnp.exp(math.log(4.0) - 2.0794415 * jax.random.uniform(part_keys[5], (NYZ, NSEG, LOCAL_STREAMWISE), jnp.float32) ** shard_levels(part_keys[5], (NYZ, NSEG, LOCAL_STREAMWISE), ((0, 4), (1, 4)), -0.2, 0.2)), 0.5, 4.0)
    channel_block_holder_keys = jax.random.split(jax.random.fold_in(arg_keys[6], 1), NYZ * NSEG // SEG)
    channel_block_holder_turns = jax.random.permutation(jax.random.fold_in(arg_keys[6], 3), NYZ * NSEG // SEG)
    channel_block_holder = jax.vmap(lambda own, number: deal_out(jax.random.fold_in(arg_keys[6], 2), own, number, SEG, N_GX, 1, SLOTS, 2))(channel_block_holder_keys, channel_block_holder_turns).reshape((NYZ, NSEG, 1))
    channel_stratum_slot = touch_ends(jax.random.randint(arg_keys[7], (NYZ, NSEG), 0, CZ), jax.random.fold_in(arg_keys[7], 1), 0, CZ - 1).astype(jnp.int32)
    channel_transverse_slot = touch_ends(jax.random.randint(arg_keys[8], (NYZ, NSEG), 0, CY), jax.random.fold_in(arg_keys[8], 1), 0, CY - 1).astype(jnp.int32)
    return {"initial_solid_warmth": initial_solid_warmth, "dissipated_power": dissipated_power, "thermal_storage": thermal_storage, "thermal_conductance_pair": thermal_conductance_pair, "fluid_warmth": fluid_warmth, "exchange_coefficient": exchange_coefficient, "channel_block_holder": channel_block_holder, "channel_stratum_slot": channel_stratum_slot, "channel_transverse_slot": channel_transverse_slot}


coolant_gain = 0.5

def face_terms(thermal_conductance_pair):
    lateral = jnp.pad(thermal_conductance_pair[0], 1)
    vertical = jnp.pad(thermal_conductance_pair[1], 1)
    lat_mid = lateral[1:-1, 1:-1, 1:-1]
    ver_mid = vertical[1:-1, 1:-1, 1:-1]
    return (jnp.sqrt(lat_mid * lateral[1:-1, 1:-1, 2:]), jnp.sqrt(lat_mid * lateral[1:-1, 1:-1, :-2]), jnp.sqrt(lat_mid * lateral[1:-1, 2:, 1:-1]), jnp.sqrt(lat_mid * lateral[1:-1, :-2, 1:-1]), jnp.sqrt(ver_mid * vertical[2:, 1:-1, 1:-1]), jnp.sqrt(ver_mid * vertical[:-2, 1:-1, 1:-1]))

def adjacent_volumes(boundary_planes, field):
    padded = jnp.pad(field, 1)
    total = boundary_planes[0] * padded[1:-1, 1:-1, 2:] + boundary_planes[1] * padded[1:-1, 1:-1, :-2]
    total = total + boundary_planes[2] * padded[1:-1, 2:, 1:-1] + boundary_planes[3] * padded[1:-1, :-2, 1:-1]
    total = total + boundary_planes[4] * padded[2:, 1:-1, 1:-1] + boundary_planes[5] * padded[:-2, 1:-1, 1:-1]
    return total

def reference(initial_solid_warmth, dissipated_power, thermal_storage, thermal_conductance_pair, fluid_warmth, exchange_coefficient, channel_block_holder, channel_stratum_slot, channel_transverse_slot):
    groups = jnp.arange(NYZ, dtype=jnp.int32)
    across = groups // N_GZ
    stacked = groups % N_GZ
    stratum_for_volume = (stacked[:, None] * CZ + channel_stratum_slot).astype(jnp.int32)
    transverse_for_volume = (across[:, None] * CY + channel_transverse_slot).astype(jnp.int32)
    block_for_volume = channel_block_holder[:, :, 0].astype(jnp.int32)
    boundary_planes = face_terms(thermal_conductance_pair)
    face_total = boundary_planes[0] + boundary_planes[1] + boundary_planes[2] + boundary_planes[3] + boundary_planes[4] + boundary_planes[5]
    for time_step in range(STEPS):
        empty = jnp.zeros((SILICON_STRATA, TRANSVERSE_COUNT, N_GX, LOCAL_STREAMWISE), jnp.float32)
        wall = empty.at[stratum_for_volume, transverse_for_volume, block_for_volume].add(exchange_coefficient).reshape(SILICON_STRATA, TRANSVERSE_COUNT, STREAMWISE_COUNT)
        inlet_fluid_warmth = empty.at[stratum_for_volume, transverse_for_volume, block_for_volume].add(exchange_coefficient * fluid_warmth).reshape(SILICON_STRATA, TRANSVERSE_COUNT, STREAMWISE_COUNT)
        linear_system_load = dissipated_power + thermal_storage * initial_solid_warmth + inlet_fluid_warmth
        main_diagonal_entry = thermal_storage + wall + face_total
        current_solid_warmth = initial_solid_warmth
        for sweep in range(ITERS):
            current_solid_warmth = (linear_system_load + adjacent_volumes(boundary_planes, current_solid_warmth)) / main_diagonal_entry
        initial_solid_warmth = current_solid_warmth
        beneath_adjacent = initial_solid_warmth.reshape(SILICON_STRATA, TRANSVERSE_COUNT, N_GX, LOCAL_STREAMWISE)[stratum_for_volume, transverse_for_volume, block_for_volume]
        heat = exchange_coefficient * (beneath_adjacent - fluid_warmth)
        fluid_warmth = fluid_warmth + coolant_gain * heat
    return (initial_solid_warmth, fluid_warmth)
```

```python
import functools

import jax
import jax.numpy as jnp
from jax import lax
from jax.experimental import pallas as pl
from jax.experimental.pallas import tpu as pltpu
from jax.sharding import PartitionSpec as P

STEPS = 2
ITERS = 4
HALO = STEPS * ITERS
GROUP = 2 * HALO
LANES = 128
RAW = 5
FIELDS = 7
coolant_gain = 0.5

VMEM = pl.BlockSpec(memory_space=pltpu.VMEM)
PARAMS = pltpu.CompilerParams(vmem_limit_bytes=40 * 1024 * 1024)


def lane_of(rows):
    return lax.broadcasted_iota(jnp.int32, (rows, LANES), 1)


def take(value, index):
    return jnp.take_along_axis(value, index, axis=1, mode="promise_in_bounds")


def near_edges(rows):
    k = lane_of(rows) % GROUP
    return jnp.where(k < HALO, HALO - 1 - k, LANES + HALO - 1 - k)


def far_edges(rows):
    k = lane_of(rows) % GROUP
    return jnp.where(k < HALO, LANES - 1 - k, GROUP - 1 - k)


def split(value):
    high = value.astype(jnp.bfloat16)
    low = (value - high.astype(jnp.float32)).astype(jnp.bfloat16)
    return high, low


def exact_dot(onehot, parts):
    high, low = parts
    total = jnp.dot(onehot, high, preferred_element_type=jnp.float32)
    return total + jnp.dot(onehot, low, preferred_element_type=jnp.float32)


def coupling(coef, warmth):
    flow = coef * warmth
    second = coolant_gain * coef * coef
    return jnp.concatenate([coef, flow, second, flow - second * warmth], axis=1)


def flip(z, layers, i):
    return jnp.where(z == 0, i, layers - 1 - i)


def pack_kernel(u_ref, p_ref, c_ref, k_ref, f_ref, x_ref, own_ref, left_ref, right_ref, seg_ref):
    layers, rows, _ = u_ref.shape
    seg = f_ref.shape[1]
    z = lax.axis_index("gz")
    plane = layers * rows
    for i in range(layers):
        src = flip(z, layers, i)
        at = i * rows
        own_ref[at : at + rows, :] = jnp.sqrt(k_ref[0, src])
        own_ref[plane + at : plane + at + rows, :] = jnp.sqrt(k_ref[1, src])
        own_ref[2 * plane + at : 2 * plane + at + rows, :] = u_ref[src]
        own_ref[3 * plane + at : 3 * plane + at + rows, :] = p_ref[src]
        own_ref[4 * plane + at : 4 * plane + at + rows, :] = c_ref[src]
    chunk = rows // 4
    lane = lane_of(chunk)
    first = lane % GROUP < HALO
    near, far = near_edges(chunk), far_edges(chunk)
    for part in range(RAW):
        even = jnp.zeros((chunk, LANES), jnp.float32)
        odd = even
        for h in range(2):
            for i in range(layers):
                here = lane // GROUP == h * layers + i
                for side in range(2):
                    g = 2 * h + side
                    if part < 4:
                        at = g * plane + i * rows + part * chunk
                    else:
                        at = 4 * plane + i * rows + g * chunk
                    block = own_ref[at : at + chunk, :]
                    if side == 0:
                        even = jnp.where(here, take(block, near), even)
                    else:
                        odd = jnp.where(here, take(block, far), odd)
        left_ref[part * chunk : (part + 1) * chunk, :] = jnp.where(first, even, odd)
        right_ref[part * chunk : (part + 1) * chunk, :] = jnp.where(first, odd, even)
    coef, warmth = x_ref[0], f_ref[0]
    at = RAW * chunk
    left_ref[at : at + seg, :] = coef
    left_ref[at + seg : at + 2 * seg, :] = warmth
    right_ref[at : at + seg, :] = coef
    right_ref[at + seg : at + 2 * seg, :] = warmth
    seg_ref[:seg, :] = coef
    seg_ref[seg:, :] = warmth
    at = RAW * plane
    own_ref[at : at + seg, :] = coef
    own_ref[at + seg : at + 2 * seg, :] = warmth


class Strips:
    def __init__(self, ref, right_at, left_at, rows, layers):
        self.ref, self.right_at, self.left_at = ref, right_at, left_at
        self.rows, self.layers = rows, layers

    def merged(self, field, start, n, x, gx):
        chunk = self.rows // 4
        if field < 4:
            g, at = field, start
        else:
            g, at = start // chunk, 4 * chunk + start % chunk
        ref_r, ref_l = self.ref
        a = ref_r[self.right_at + at : self.right_at + at + n, :]
        b = ref_l[self.left_at + at : self.left_at + at + n, :]
        a = jnp.where(x < gx - 1, a, 0.0)
        b = jnp.where(x > 0, b, 0.0)
        first = lane_of(n) % GROUP < HALO
        return g, (jnp.where(first, a, b) if g % 2 == 0 else jnp.where(first, b, a))

    def halo(self, field, start, n, x, gx, partner):
        g, both = self.merged(field, start, n, x, gx)
        lane = lane_of(n)
        half = self.layers * GROUP
        src = lane % half
        if partner:
            src = (self.layers - 1 - src // GROUP) * GROUP + src % GROUP
        if g % 2 == 1:
            src = jnp.where(src % GROUP < HALO, src + HALO, src - HALO)
        return take(both, src + half * (g // 2))


def place_segments(x, gx, seg, coef_ref, warmth_ref, first, rest):
    coef, warmth = first
    coef_ref[pl.ds(pl.multiple_of(x * seg, seg), seg), :] = coef
    warmth_ref[pl.ds(pl.multiple_of(x * seg, seg), seg), :] = warmth
    for k, (ref, at) in enumerate(rest, 1):
        holder = lax.rem(x + k, gx)
        place = pl.ds(pl.multiple_of(holder * seg, seg), seg)
        coef_ref[place, :] = ref[at : at + seg, :]
        warmth_ref[place, :] = ref[at + seg : at + 2 * seg, :]


def tables(z, group, layers, holder_ref, stratum_ref, transverse_ref):
    holder = holder_ref[pl.ds(group, 1), :]
    layer = stratum_ref[pl.ds(group, 1), :]
    layer = jnp.where(z == 0, layer, layers - 1 - layer)
    row = transverse_ref[pl.ds(group, 1), :]
    n = holder.shape[1]
    where = lax.broadcasted_iota(jnp.int32, (8, n), 0)
    stacked = jnp.where(where == 0, holder, jnp.where(where == 1, layer, row))
    eye = lax.broadcasted_iota(jnp.int32, (n, n), 0) == lax.broadcasted_iota(jnp.int32, (n, n), 1)
    column = lax.dot_general(
        eye.astype(jnp.float32).astype(jnp.bfloat16),
        stacked.astype(jnp.float32).astype(jnp.bfloat16),
        (((1,), (1,)), ((), ())),
        preferred_element_type=jnp.float32,
    ).astype(jnp.int32)
    return (holder, layer, row), (column[:, 0:1], column[:, 1:2], column[:, 2:3])


def as_onehot(mask):
    return jnp.where(mask, 1.0, 0.0).astype(jnp.bfloat16)


def halo_segments(coef, warmth, columns, base, x):
    n = coef.shape[0]
    lane = lane_of(n)
    holder, layer, _ = columns
    side = jnp.where(lane % GROUP < HALO, x + 1, x - 1)
    mine = jnp.logical_and(lane // GROUP == layer + base, holder == side)
    near = near_edges(n)
    return coupling(jnp.where(mine, take(coef, near), 0.0), take(warmth, near))


def combine(raw, added):
    s, t, u, power, storage = raw
    wall, flow, second, later = (added[:, i * LANES : (i + 1) * LANES] for i in range(4))
    return s, t, u, storage + wall, power + storage * u + flow, power + later, storage + second


def strip_kernel(gx, gy, shape, seg, *refs):
    layers, rows = shape
    own_ref, holder_ref, stratum_ref, transverse_ref = refs[:4]
    received = refs[4 : 4 + gx - 1]
    outs = refs[4 + gx - 1 : -2]
    coef_ref, warmth_ref = refs[-2:]
    x, y, z = (lax.axis_index(a) for a in ("gx", "gy", "gz"))
    plane, chunk = layers * rows, rows // 4
    at = RAW * plane
    rest = [(r, RAW * chunk if k in (1, gx - 1) else 0) for k, r in enumerate(received, 1)]
    own_segments = (own_ref[at : at + seg, :], own_ref[at + seg : at + 2 * seg, :])
    place_segments(x, gx, seg, coef_ref, warmth_ref, own_segments, rest)
    (holder, layer, row), columns = tables(z, y * 2 + z, layers, holder_ref, stratum_ref, transverse_ref)
    coef, warmth = coef_ref[...], warmth_ref[...]
    parts = split(coupling(coef, warmth))
    outer = split(halo_segments(coef, warmth, columns, 0, x))
    strips = Strips((received[0], received[-1]), 0, 0, rows, layers)
    n = holder.shape[1]

    def strip(out_ref, start):
        cell = lax.broadcasted_iota(jnp.int32, (layers * HALO, n), 0)
        match = jnp.logical_and(cell // HALO == layer, cell % HALO + start == row)
        added = exact_dot(as_onehot(jnp.logical_and(match, holder == x)), parts)
        for i in range(layers):
            raw = [own_ref[f * plane + i * rows + start : f * plane + i * rows + start + HALO, :] for f in range(RAW)]
            for f, value in enumerate(combine(raw, added[i * HALO : (i + 1) * HALO])):
                out_ref[(f * layers + i) * HALO : (f * layers + i + 1) * HALO, :] = value
        line = lax.broadcasted_iota(jnp.int32, (HALO, n), 0)
        beside = exact_dot(as_onehot(line + start == row), outer)
        raw = [strips.halo(f, start, HALO, x, gx, False) for f in range(RAW)]
        made = list(combine(raw, beside))
        made.append(jnp.zeros_like(made[0]))
        low = lane_of(HALO) < LANES // 2
        at = FIELDS * layers * HALO
        for j in range(4):
            packed = jnp.where(low, made[2 * j], pltpu.roll(made[2 * j + 1], LANES // 2, 1))
            out_ref[at + j * HALO : at + (j + 1) * HALO, :] = packed

    if gy == 2:
        pl.when(y == 0)(lambda: strip(outs[0], rows - HALO))
        pl.when(y == 1)(lambda: strip(outs[0], 0))
    else:
        strip(outs[0], 0)
        strip(outs[1], rows - HALO)


def lateral(buf, at, n, count):
    lane = lane_of(n)
    k, group = lane % GROUP, lane // GROUP
    top = buf.shape[0] - 1
    centre = [buf[i, pl.ds(at, n), :] for i in range(count)]
    halo = buf[top, pl.ds(at, n), :]
    border = jnp.zeros_like(halo)
    inner = jnp.logical_or(k == HALO - 1, k == HALO)
    sums = []
    for i in range(count):
        border = jnp.where(group == i, pltpu.roll(centre[i], i * GROUP + HALO, 1), border)
        beside = pltpu.roll(halo, LANES - (i * GROUP + HALO), 1)
        east = jnp.where(lane == LANES - 1, beside, pltpu.roll(centre[i], LANES - 1, 1))
        west = jnp.where(lane == 0, beside, pltpu.roll(centre[i], 1, 1))
        sums.append(east + west + buf[i, pl.ds(at - 1, n), :] + buf[i, pl.ds(at + 1, n), :])
    one = jnp.where(k == HALO, border, pltpu.roll(halo, 1, 1))
    other = jnp.where(k == HALO - 1, border, pltpu.roll(halo, LANES - 1, 1))
    sums.append(one + other + buf[top, pl.ds(at - 1, n), :] + buf[top, pl.ds(at + 1, n), :])
    return centre + [halo], sums


def vertical(values):
    planes, halo = values[:-1], values[-1]
    sums = []
    for i in range(len(planes)):
        near = [planes[j] for j in (i - 1, i + 1) if 0 <= j < len(planes)]
        sums.append(functools.reduce(jnp.add, near))
    lane = lane_of(halo.shape[0])
    up = jnp.where(lane >= GROUP, pltpu.roll(halo, GROUP, 1), 0.0)
    down = jnp.where(lane < LANES - GROUP, pltpu.roll(halo, LANES - GROUP, 1), 0.0)
    sums.append(up + down)
    return sums


def sweep_kernel(gx, gy, shape, seg, *refs):
    layers, rows = shape
    own_ref, partner_ref, holder_ref, stratum_ref, transverse_ref = refs[:5]
    received = refs[5 : 5 + gx - 1]
    refs = refs[5 + gx - 1 :]
    sides = 1 if gy == 2 else 2
    along = refs[:sides]
    late_ref, out_ref, keep_ref = refs[sides], refs[sides + 1], refs[sides + 2]
    refs = refs[sides + 3 :]
    sends, refs = refs[: gx - 1], refs[gx - 1 :]
    s_ref, t_ref, a_ref, r_ref, e_ref, g_ref, b_ref, q_ref, va_ref, vb_ref = refs[:10]
    seg_refs, ret_ref = refs[10:14], refs[14]
    x, y, z = (lax.axis_index(a) for a in ("gx", "gy", "gz"))
    plane, chunk = layers * rows, rows // 4
    top = 2 * layers
    pad = 8
    body = pad + HALO
    length = rows + 2 * HALO

    lengths = [RAW * chunk + 2 * seg if k in (1, gx - 1) else 2 * seg for k in range(1, gx)]
    starts = [sum(lengths[:k]) for k in range(gx)]
    at = RAW * plane
    groups = []
    for which, (ref, base) in enumerate(((own_ref, 0), (partner_ref, layers))):
        coef_ref, warmth_ref = seg_refs[2 * which : 2 * which + 2]
        offsets = [RAW * chunk if k in (1, gx - 1) else 0 for k in range(1, gx)]
        if which == 0:
            rest = list(zip(received, offsets))
        else:
            rest = [(late_ref, starts[k] + o) for k, o in enumerate(offsets)]
        first = (ref[at : at + seg, :], ref[at + seg : at + 2 * seg, :])
        place_segments(x, gx, seg, coef_ref, warmth_ref, first, rest)
        group = y * 2 + (z if which == 0 else 1 - z)
        along_lanes, columns = tables(z, group, layers, holder_ref, stratum_ref, transverse_ref)
        groups.append((ref, base, coef_ref[...], warmth_ref[...], along_lanes, columns))

    dests = (s_ref, t_ref, va_ref, a_ref, r_ref, e_ref, g_ref)
    zeros = jnp.zeros((pad, LANES), jnp.float32)
    for ref in (s_ref, va_ref, vb_ref):
        for i in range(top + 1):
            ref[i, 0:pad, :] = zeros
            ref[i, pad + length : pad + length + pad, :] = zeros

    def put(i, start, values):
        n = values[0].shape[0]
        for f, value in enumerate(values):
            if f == 2:
                value = value * values[0]
            dests[f][i, start : start + n, :] = value

    beside = 0.0
    for ref, base, coef, warmth, (holder, layer, row), columns in groups:
        n = holder.shape[1]
        parts = split(coupling(coef, warmth))
        line = lax.broadcasted_iota(jnp.int32, (rows, n), 0)
        for i in range(layers):
            match = jnp.logical_and(line == row, jnp.logical_and(layer == i, holder == x))
            added = exact_dot(as_onehot(match), parts)
            src = i if base == 0 else layers - 1 - i
            raw = [ref[f * plane + src * rows : f * plane + (src + 1) * rows, :] for f in range(RAW)]
            put(base + i, body, combine(raw, added))
        beside = beside + exact_dot(as_onehot(line == row), split(halo_segments(coef, warmth, columns, base, x)))
    mine = Strips((received[0], received[-1]), 0, 0, rows, layers)
    theirs = Strips((late_ref, late_ref), starts[0], starts[gx - 2], rows, layers)
    low = lane_of(chunk) < LANES // 2
    for part in range(4):
        raw = []
        for f in range(RAW):
            a = mine.halo(f, part * chunk, chunk, x, gx, False)
            b = theirs.halo(f, part * chunk, chunk, x, gx, True)
            raw.append(jnp.where(low, a, b))
        put(top, body + part * chunk, combine(raw, beside[part * chunk : (part + 1) * chunk]))

    for side in range(2):
        start = pad if side == 0 else body + rows
        if gy == 2:
            source, at, live = along[0], starts[gx - 1], y == 1 - side
        else:
            source, at, live = along[side], starts[gx - 1] + side * along[0].shape[0], True
        sources = ((source, 0), (late_ref, at))
        for i in range(top):
            ref, offset = sources[i // layers]
            src = i if i < layers else top - 1 - i
            values = []
            for f in range(FIELDS):
                place = offset + (f * layers + src) * HALO
                values.append(jnp.where(live, ref[place : place + HALO, :], 0.0))
            put(i, start, values)
        lane = lane_of(HALO)
        src = lane % (LANES // 2)
        turned = (layers - 1 - src // GROUP) * GROUP + src % GROUP
        values = []
        for f in range(FIELDS):
            place = FIELDS * layers * HALO + (f // 2) * HALO
            half = (LANES // 2) * (f % 2)
            a = take(source[place : place + HALO, :], src + half)
            b = take(late_ref[at + place : at + place + HALO, :], turned + half)
            values.append(jnp.where(live, jnp.where(lane < LANES // 2, a, b), 0.0))
        put(top, start, values)

    step_rows = 24
    for c in range(length // step_rows):
        at = pad + c * step_rows
        here = pl.ds(at, step_rows)
        centre, sums = lateral(s_ref, at, step_rows, top)
        t = [t_ref[i, here, :] for i in range(top + 1)]
        above = vertical(t)
        for i in range(top + 1):
            s = centre[i]
            diag = a_ref[i, here, :] + s * sums[i] + t[i] * above[i]
            inverse = 1.0 / jnp.where(diag > 0.0, diag, 1.0)
            scaled = s * inverse
            a_ref[i, here, :] = s * scaled
            b_ref[i, here, :] = t[i] * scaled
            r_ref[i, here, :] = r_ref[i, here, :] * scaled
            e_ref[i, here, :] = e_ref[i, here, :] * scaled
            g_ref[i, here, :] = g_ref[i, here, :] * inverse
            q_ref[i, here, :] = t[i] * jnp.where(s > 0.0, 1.0 / jnp.where(s > 0.0, s, 1.0), 0.0)

    def sweep(src_ref, dst_ref, count):
        for c in range(length // step_rows):
            at = pad + c * step_rows
            here = pl.ds(at, step_rows)
            centre, sums = lateral(src_ref, at, step_rows, top)
            above = vertical([q_ref[i, here, :] * centre[i] for i in range(top + 1)])
            for i in range(top + 1):
                value = r_ref[i, here, :] + a_ref[i, here, :] * sums[i] + b_ref[i, here, :] * above[i]
                dst_ref[i, here, :] = value

    own_body = pl.ds(body, rows)
    _, _, coef, warmth, _, (holder, layer, row) = groups[0]
    n = coef.shape[0]
    cell = lax.broadcasted_iota(jnp.int32, (n, rows), 1)
    picks = []
    for i in range(layers):
        match = jnp.logical_and(cell == row, jnp.logical_and(layer == i, holder == x))
        picks.append(as_onehot(match))

    for step in range(STEPS):
        def pair(_, carry):
            sweep(va_ref, vb_ref, top)
            sweep(vb_ref, va_ref, top)
            return carry

        lax.fori_loop(0, ITERS // 2, pair, 0)
        below = 0.0
        for i in range(layers):
            heat = va_ref[i, own_body, :] / s_ref[i, own_body, :]
            if step == STEPS - 1:
                out_ref[flip(z, layers, i)] = heat
            below = below + exact_dot(picks[i], split(heat))
        warmth = warmth + coolant_gain * coef * (below - warmth)
        if step < STEPS - 1:
            for i in range(top + 1):
                here = pl.ds(pad, length)
                r_ref[i, here, :] = e_ref[i, here, :] + g_ref[i, here, :] * va_ref[i, here, :]

    ret_ref[...] = jnp.where(holder == x, warmth, 0.0)
    for k, ref in enumerate((keep_ref,) + tuple(sends)):
        owner = lax.rem(x + k, gx)
        ref[...] = ret_ref[pl.ds(pl.multiple_of(owner * seg, seg), seg), :]


def local(gx, gy, gz, u, power, storage, conductance, warmth, coef, holder, stratum, transverse):
    layers, rows, columns = u.shape
    seg = warmth.shape[1]
    segments = stratum.shape[1]
    if gz != 2 or gx < 3 or columns != LANES or 2 * layers * GROUP != LANES or rows % 32:
        raise ValueError("unsupported shape")
    holder = holder[:, :, 0]
    shape = (layers, rows)
    f32 = jnp.float32
    chunk = rows // 4
    wide = RAW * chunk + 2 * seg

    def struct(*dims):
        return jax.ShapeDtypeStruct(dims, f32)

    own, to_left, to_right, only = pl.pallas_call(
        pack_kernel,
        out_shape=(
            struct(RAW * layers * rows + 2 * seg, LANES),
            struct(wide, LANES),
            struct(wide, LANES),
            struct(2 * seg, LANES),
        ),
        in_specs=[VMEM] * 6,
        out_specs=(VMEM,) * 4,
        compiler_params=PARAMS,
        name="pack",
    )(u, power, storage, conductance, warmth, coef)

    swap = [(0, 1), (1, 0)]
    partner = lax.ppermute(own, "gz", swap)
    received = []
    for k in range(1, gx):
        payload = to_left if k == 1 else to_right if k == gx - 1 else only
        received.append(lax.ppermute(payload, "gx", [(i, (i - k) % gx) for i in range(gx)]))

    strip_rows = FIELDS * layers * HALO + 4 * HALO
    sides = 1 if gy == 2 else 2
    strips = pl.pallas_call(
        functools.partial(strip_kernel, gx, gy, shape, seg),
        out_shape=(struct(strip_rows, LANES),) * sides,
        in_specs=[VMEM] * (4 + gx - 1),
        out_specs=(VMEM,) * sides,
        scratch_shapes=[pltpu.VMEM((segments, LANES), f32)] * 2,
        compiler_params=PARAMS,
        name="strips",
    )(own, holder, stratum, transverse, *received)
    if gy == 2:
        along = [lax.ppermute(strips[0], "gy", swap)]
    else:
        up = [(i, i + 1) for i in range(gy - 1)]
        down = [(j, i) for i, j in up]
        along = [lax.ppermute(strips[1], "gy", up), lax.ppermute(strips[0], "gy", down)]
    late = lax.ppermute(jnp.concatenate(received + along, axis=0), "gz", swap)

    field = pltpu.VMEM((2 * layers + 1, rows + 2 * HALO + 16, LANES), f32)
    results = pl.pallas_call(
        functools.partial(sweep_kernel, gx, gy, shape, seg),
        out_shape=(struct(layers, rows, LANES),) + (struct(seg, LANES),) * gx,
        in_specs=[VMEM] * (5 + gx - 1 + sides + 1),
        out_specs=(VMEM,) * (1 + gx),
        scratch_shapes=[field] * 10 + [pltpu.VMEM((segments, LANES), f32)] * 5,
        compiler_params=PARAMS,
        name="sweeps",
    )(own, partner, holder, stratum, transverse, *received, *along, late)
    temperature, total = results[0], results[1]
    for k in range(1, gx):
        total = total + lax.ppermute(results[1 + k], "gx", [(i, (i + k) % gx) for i in range(gx)])
    return temperature, total[None]


def solution(mesh):
    gx, gy, gz = (mesh.shape[a] for a in ("gx", "gy", "gz"))
    cells = P(("stack", "gz"), "gy", "gx")
    segments = P(("stack", "gy", "gz"), "gx", None)
    return jax.shard_map(
        functools.partial(local, gx, gy, gz),
        mesh=mesh,
        in_specs=(cells, cells, cells, P(None, ("stack", "gz"), "gy", "gx"), segments, segments, P(), P(), P()),
        out_specs=(cells, segments),
        check_vma=False,
    )
```

```python
import functools

import jax
import jax.numpy as jnp
from jax import lax
from jax.experimental import pallas as pl
from jax.experimental.pallas import tpu as pltpu
from jax.sharding import PartitionSpec as P

STEPS = 2
ITERS = 4
HALO = STEPS * ITERS
GROUP = 2 * HALO
LANES = 128
RAW = 5
FIELDS = 7
coolant_gain = 0.5

VMEM = pl.BlockSpec(memory_space=pltpu.VMEM)
PARAMS = pltpu.CompilerParams(vmem_limit_bytes=40 * 1024 * 1024)


def lane_of(rows):
    return lax.broadcasted_iota(jnp.int32, (rows, LANES), 1)


def take(value, index):
    return jnp.take_along_axis(value, index, axis=1, mode="promise_in_bounds")


def near_edges(rows):
    k = lane_of(rows) % GROUP
    return jnp.where(k < HALO, HALO - 1 - k, LANES + HALO - 1 - k)


def far_edges(rows):
    k = lane_of(rows) % GROUP
    return jnp.where(k < HALO, LANES - 1 - k, GROUP - 1 - k)


def split(value):
    high = value.astype(jnp.bfloat16)
    low = (value - high.astype(jnp.float32)).astype(jnp.bfloat16)
    return high, low


def exact_dot(onehot, parts):
    high, low = parts
    total = jnp.dot(onehot, high, preferred_element_type=jnp.float32)
    return total + jnp.dot(onehot, low, preferred_element_type=jnp.float32)


def coupling(coef, warmth):
    flow = coef * warmth
    second = coolant_gain * coef * coef
    return jnp.concatenate([coef, flow, second, flow - second * warmth], axis=1)


def flip(z, layers, i):
    return jnp.where(z == 0, i, layers - 1 - i)


def pack_kernel(u_ref, p_ref, c_ref, k_ref, f_ref, x_ref, own_ref, left_ref, right_ref, seg_ref, sems):
    layers, rows, _ = u_ref.shape
    seg = f_ref.shape[1]
    z = lax.axis_index("gz")
    plane = layers * rows
    copies = []

    def fetch(src, at, n):
        copies.append(pltpu.make_async_copy(src, own_ref.at[pl.ds(at, n), :], sems.at[len(copies)]))
        copies[-1].start()

    for field, ref in enumerate((k_ref.at[0], k_ref.at[1], u_ref, p_ref, c_ref)):
        for i in range(layers):
            fetch(ref.at[flip(z, layers, i)], field * plane + i * rows, rows)
    fetch(x_ref.at[0], RAW * plane, seg)
    fetch(f_ref.at[0], RAW * plane + seg, seg)
    for field in range(2):
        for i in range(layers):
            copies[field * layers + i].wait()
            here = pl.ds(field * plane + i * rows, rows)
            own_ref[here, :] = jnp.sqrt(own_ref[here, :])
    for copy in copies[2 * layers :]:
        copy.wait()
    chunk = rows // 4
    lane = lane_of(chunk)
    first = lane % GROUP < HALO
    near, far = near_edges(chunk), far_edges(chunk)
    for part in range(RAW):
        even = jnp.zeros((chunk, LANES), jnp.float32)
        odd = even
        for h in range(2):
            for i in range(layers):
                here = lane // GROUP == h * layers + i
                for side in range(2):
                    g = 2 * h + side
                    if part < 4:
                        at = g * plane + i * rows + part * chunk
                    else:
                        at = 4 * plane + i * rows + g * chunk
                    block = own_ref[at : at + chunk, :]
                    if side == 0:
                        even = jnp.where(here, take(block, near), even)
                    else:
                        odd = jnp.where(here, take(block, far), odd)
        left_ref[part * chunk : (part + 1) * chunk, :] = jnp.where(first, even, odd)
        right_ref[part * chunk : (part + 1) * chunk, :] = jnp.where(first, odd, even)
    segments = own_ref[RAW * plane : RAW * plane + 2 * seg, :]
    left_ref[RAW * chunk :, :] = segments
    right_ref[RAW * chunk :, :] = segments
    seg_ref[...] = segments


class Strips:
    def __init__(self, ref, right_at, left_at, rows, layers):
        self.ref, self.right_at, self.left_at = ref, right_at, left_at
        self.rows, self.layers = rows, layers

    def merged(self, field, start, n, x, gx):
        chunk = self.rows // 4
        if field < 4:
            g, at = field, start
        else:
            g, at = start // chunk, 4 * chunk + start % chunk
        ref_r, ref_l = self.ref
        a = ref_r[self.right_at + at : self.right_at + at + n, :]
        b = ref_l[self.left_at + at : self.left_at + at + n, :]
        a = jnp.where(x < gx - 1, a, 0.0)
        b = jnp.where(x > 0, b, 0.0)
        first = lane_of(n) % GROUP < HALO
        return g, (jnp.where(first, a, b) if g % 2 == 0 else jnp.where(first, b, a))

    def halo(self, field, start, n, x, gx, partner):
        g, both = self.merged(field, start, n, x, gx)
        lane = lane_of(n)
        half = self.layers * GROUP
        src = lane % half
        if partner:
            src = (self.layers - 1 - src // GROUP) * GROUP + src % GROUP
        if g % 2 == 1:
            src = jnp.where(src % GROUP < HALO, src + HALO, src - HALO)
        return take(both, src + half * (g // 2))


def place_segments(x, gx, seg, coef_ref, warmth_ref, first, rest):
    coef, warmth = first
    coef_ref[pl.ds(pl.multiple_of(x * seg, seg), seg), :] = coef
    warmth_ref[pl.ds(pl.multiple_of(x * seg, seg), seg), :] = warmth
    for k, (ref, at) in enumerate(rest, 1):
        holder = lax.rem(x + k, gx)
        place = pl.ds(pl.multiple_of(holder * seg, seg), seg)
        coef_ref[place, :] = ref[at : at + seg, :]
        warmth_ref[place, :] = ref[at + seg : at + 2 * seg, :]


def tables(z, group, layers, holder_ref, stratum_ref, transverse_ref):
    holder = holder_ref[pl.ds(group, 1), :]
    layer = stratum_ref[pl.ds(group, 1), :]
    layer = jnp.where(z == 0, layer, layers - 1 - layer)
    row = transverse_ref[pl.ds(group, 1), :]
    n = holder.shape[1]
    where = lax.broadcasted_iota(jnp.int32, (8, n), 0)
    stacked = jnp.where(where == 0, holder, jnp.where(where == 1, layer, row))
    eye = lax.broadcasted_iota(jnp.int32, (n, n), 0) == lax.broadcasted_iota(jnp.int32, (n, n), 1)
    column = lax.dot_general(
        eye.astype(jnp.float32).astype(jnp.bfloat16),
        stacked.astype(jnp.float32).astype(jnp.bfloat16),
        (((1,), (1,)), ((), ())),
        preferred_element_type=jnp.float32,
    ).astype(jnp.int32)
    return (holder, layer, row), (column[:, 0:1], column[:, 1:2], column[:, 2:3])


def as_onehot(mask):
    return jnp.where(mask, 1.0, 0.0).astype(jnp.bfloat16)


def halo_segments(coef, warmth, columns, base, x):
    n = coef.shape[0]
    lane = lane_of(n)
    holder, layer, _ = columns
    side = jnp.where(lane % GROUP < HALO, x + 1, x - 1)
    mine = jnp.logical_and(lane // GROUP == layer + base, holder == side)
    near = near_edges(n)
    return coupling(jnp.where(mine, take(coef, near), 0.0), take(warmth, near))


def combine(raw, added):
    s, t, u, power, storage = raw
    wall, flow, second, later = (added[:, i * LANES : (i + 1) * LANES] for i in range(4))
    return s, t, u, storage + wall, power + storage * u + flow, power + later, storage + second


def strip_kernel(gx, gy, shape, seg, *refs):
    layers, rows = shape
    own_ref, holder_ref, stratum_ref, transverse_ref = refs[:4]
    received = refs[4 : 4 + gx - 1]
    outs = refs[4 + gx - 1 : -2]
    coef_ref, warmth_ref = refs[-2:]
    x, y, z = (lax.axis_index(a) for a in ("gx", "gy", "gz"))
    plane, chunk = layers * rows, rows // 4
    at = RAW * plane
    rest = [(r, RAW * chunk if k in (1, gx - 1) else 0) for k, r in enumerate(received, 1)]
    own_segments = (own_ref[at : at + seg, :], own_ref[at + seg : at + 2 * seg, :])
    place_segments(x, gx, seg, coef_ref, warmth_ref, own_segments, rest)
    (holder, layer, row), columns = tables(z, y * 2 + z, layers, holder_ref, stratum_ref, transverse_ref)
    coef, warmth = coef_ref[...], warmth_ref[...]
    parts = split(coupling(coef, warmth))
    outer = split(halo_segments(coef, warmth, columns, 0, x))
    strips = Strips((received[0], received[-1]), 0, 0, rows, layers)
    n = holder.shape[1]

    def strip(out_ref, start):
        cell = lax.broadcasted_iota(jnp.int32, (layers * HALO, n), 0)
        match = jnp.logical_and(cell // HALO == layer, cell % HALO + start == row)
        added = exact_dot(as_onehot(jnp.logical_and(match, holder == x)), parts)
        for i in range(layers):
            raw = [own_ref[f * plane + i * rows + start : f * plane + i * rows + start + HALO, :] for f in range(RAW)]
            for f, value in enumerate(combine(raw, added[i * HALO : (i + 1) * HALO])):
                out_ref[(f * layers + i) * HALO : (f * layers + i + 1) * HALO, :] = value
        line = lax.broadcasted_iota(jnp.int32, (HALO, n), 0)
        beside = exact_dot(as_onehot(line + start == row), outer)
        raw = [strips.halo(f, start, HALO, x, gx, False) for f in range(RAW)]
        made = list(combine(raw, beside))
        made.append(jnp.zeros_like(made[0]))
        low = lane_of(HALO) < LANES // 2
        at = FIELDS * layers * HALO
        for j in range(4):
            packed = jnp.where(low, made[2 * j], pltpu.roll(made[2 * j + 1], LANES // 2, 1))
            out_ref[at + j * HALO : at + (j + 1) * HALO, :] = packed

    if gy == 2:
        pl.when(y == 0)(lambda: strip(outs[0], rows - HALO))
        pl.when(y == 1)(lambda: strip(outs[0], 0))
    else:
        strip(outs[0], 0)
        strip(outs[1], rows - HALO)


def lateral(buf, at, n, count):
    lane = lane_of(n)
    k, group = lane % GROUP, lane // GROUP
    top = buf.shape[0] - 1
    centre = [buf[i, pl.ds(at, n), :] for i in range(count)]
    halo = buf[top, pl.ds(at, n), :]
    border = jnp.zeros_like(halo)
    inner = jnp.logical_or(k == HALO - 1, k == HALO)
    sums = []
    for i in range(count):
        border = jnp.where(group == i, pltpu.roll(centre[i], i * GROUP + HALO, 1), border)
        beside = pltpu.roll(halo, LANES - (i * GROUP + HALO), 1)
        east = jnp.where(lane == LANES - 1, beside, pltpu.roll(centre[i], LANES - 1, 1))
        west = jnp.where(lane == 0, beside, pltpu.roll(centre[i], 1, 1))
        sums.append(east + west + buf[i, pl.ds(at - 1, n), :] + buf[i, pl.ds(at + 1, n), :])
    one = jnp.where(k == HALO, border, pltpu.roll(halo, 1, 1))
    other = jnp.where(k == HALO - 1, border, pltpu.roll(halo, LANES - 1, 1))
    sums.append(one + other + buf[top, pl.ds(at - 1, n), :] + buf[top, pl.ds(at + 1, n), :])
    return centre + [halo], sums


def vertical(values):
    planes, halo = values[:-1], values[-1]
    sums = []
    for i in range(len(planes)):
        near = [planes[j] for j in (i - 1, i + 1) if 0 <= j < len(planes)]
        sums.append(functools.reduce(jnp.add, near))
    lane = lane_of(halo.shape[0])
    up = jnp.where(lane >= GROUP, pltpu.roll(halo, GROUP, 1), 0.0)
    down = jnp.where(lane < LANES - GROUP, pltpu.roll(halo, LANES - GROUP, 1), 0.0)
    sums.append(up + down)
    return sums


def sweep_kernel(gx, gy, shape, seg, *refs):
    layers, rows = shape
    own_ref, partner_ref, holder_ref, stratum_ref, transverse_ref = refs[:5]
    received = refs[5 : 5 + gx - 1]
    refs = refs[5 + gx - 1 :]
    sides = 1 if gy == 2 else 2
    along = refs[:sides]
    late_ref, out_ref, keep_ref = refs[sides], refs[sides + 1], refs[sides + 2]
    refs = refs[sides + 3 :]
    sends, refs = refs[: gx - 1], refs[gx - 1 :]
    s_ref, t_ref, a_ref, r_ref, e_ref, g_ref, b_ref, q_ref, va_ref, vb_ref = refs[:10]
    seg_refs, ret_ref = refs[10:14], refs[14]
    x, y, z = (lax.axis_index(a) for a in ("gx", "gy", "gz"))
    plane, chunk = layers * rows, rows // 4
    top = 2 * layers
    pad = 8
    body = pad + HALO
    length = rows + 2 * HALO

    lengths = [RAW * chunk + 2 * seg if k in (1, gx - 1) else 2 * seg for k in range(1, gx)]
    starts = [sum(lengths[:k]) for k in range(gx)]
    at = RAW * plane
    groups = []
    for which, (ref, base) in enumerate(((own_ref, 0), (partner_ref, layers))):
        coef_ref, warmth_ref = seg_refs[2 * which : 2 * which + 2]
        offsets = [RAW * chunk if k in (1, gx - 1) else 0 for k in range(1, gx)]
        if which == 0:
            rest = list(zip(received, offsets))
        else:
            rest = [(late_ref, starts[k] + o) for k, o in enumerate(offsets)]
        first = (ref[at : at + seg, :], ref[at + seg : at + 2 * seg, :])
        place_segments(x, gx, seg, coef_ref, warmth_ref, first, rest)
        group = y * 2 + (z if which == 0 else 1 - z)
        along_lanes, columns = tables(z, group, layers, holder_ref, stratum_ref, transverse_ref)
        groups.append((ref, base, coef_ref[...], warmth_ref[...], along_lanes, columns))

    dests = (s_ref, t_ref, va_ref, a_ref, r_ref, e_ref, g_ref)
    zeros = jnp.zeros((pad, LANES), jnp.float32)
    for ref in (s_ref, va_ref, vb_ref):
        for i in range(top + 1):
            ref[i, 0:pad, :] = zeros
            ref[i, pad + length : pad + length + pad, :] = zeros

    def put(i, start, values):
        n = values[0].shape[0]
        for f, value in enumerate(values):
            if f == 2:
                value = value * values[0]
            dests[f][i, start : start + n, :] = value

    beside = 0.0
    for ref, base, coef, warmth, (holder, layer, row), columns in groups:
        n = holder.shape[1]
        parts = split(coupling(coef, warmth))
        line = lax.broadcasted_iota(jnp.int32, (rows, n), 0)
        for i in range(layers):
            match = jnp.logical_and(line == row, jnp.logical_and(layer == i, holder == x))
            added = exact_dot(as_onehot(match), parts)
            src = i if base == 0 else layers - 1 - i
            raw = [ref[f * plane + src * rows : f * plane + (src + 1) * rows, :] for f in range(RAW)]
            put(base + i, body, combine(raw, added))
        beside = beside + exact_dot(as_onehot(line == row), split(halo_segments(coef, warmth, columns, base, x)))
    mine = Strips((received[0], received[-1]), 0, 0, rows, layers)
    theirs = Strips((late_ref, late_ref), starts[0], starts[gx - 2], rows, layers)
    low = lane_of(chunk) < LANES // 2
    for part in range(4):
        raw = []
        for f in range(RAW):
            a = mine.halo(f, part * chunk, chunk, x, gx, False)
            b = theirs.halo(f, part * chunk, chunk, x, gx, True)
            raw.append(jnp.where(low, a, b))
        put(top, body + part * chunk, combine(raw, beside[part * chunk : (part + 1) * chunk]))

    for side in range(2):
        start = pad if side == 0 else body + rows
        if gy == 2:
            source, at, live = along[0], starts[gx - 1], y == 1 - side
        else:
            source, at, live = along[side], starts[gx - 1] + side * along[0].shape[0], True
        sources = ((source, 0), (late_ref, at))
        for i in range(top):
            ref, offset = sources[i // layers]
            src = i if i < layers else top - 1 - i
            values = []
            for f in range(FIELDS):
                place = offset + (f * layers + src) * HALO
                values.append(jnp.where(live, ref[place : place + HALO, :], 0.0))
            put(i, start, values)
        lane = lane_of(HALO)
        src = lane % (LANES // 2)
        turned = (layers - 1 - src // GROUP) * GROUP + src % GROUP
        values = []
        for f in range(FIELDS):
            place = FIELDS * layers * HALO + (f // 2) * HALO
            half = (LANES // 2) * (f % 2)
            a = take(source[place : place + HALO, :], src + half)
            b = take(late_ref[at + place : at + place + HALO, :], turned + half)
            values.append(jnp.where(live, jnp.where(lane < LANES // 2, a, b), 0.0))
        put(top, start, values)

    step_rows = 24
    for c in range(length // step_rows):
        at = pad + c * step_rows
        here = pl.ds(at, step_rows)
        centre, sums = lateral(s_ref, at, step_rows, top)
        t = [t_ref[i, here, :] for i in range(top + 1)]
        above = vertical(t)
        for i in range(top + 1):
            s = centre[i]
            diag = a_ref[i, here, :] + s * sums[i] + t[i] * above[i]
            inverse = 1.0 / jnp.where(diag > 0.0, diag, 1.0)
            scaled = s * inverse
            a_ref[i, here, :] = s * scaled
            b_ref[i, here, :] = t[i] * scaled
            r_ref[i, here, :] = r_ref[i, here, :] * scaled
            e_ref[i, here, :] = e_ref[i, here, :] * scaled
            g_ref[i, here, :] = g_ref[i, here, :] * inverse
            q_ref[i, here, :] = t[i] * jnp.where(s > 0.0, 1.0 / jnp.where(s > 0.0, s, 1.0), 0.0)

    def sweep(src_ref, dst_ref, count):
        for c in range(length // step_rows):
            at = pad + c * step_rows
            here = pl.ds(at, step_rows)
            centre, sums = lateral(src_ref, at, step_rows, top)
            above = vertical([q_ref[i, here, :] * centre[i] for i in range(top + 1)])
            for i in range(top + 1):
                value = r_ref[i, here, :] + a_ref[i, here, :] * sums[i] + b_ref[i, here, :] * above[i]
                dst_ref[i, here, :] = value

    own_body = pl.ds(body, rows)
    _, _, coef, warmth, _, (holder, layer, row) = groups[0]
    n = coef.shape[0]
    cell = lax.broadcasted_iota(jnp.int32, (n, rows), 1)
    picks = []
    for i in range(layers):
        match = jnp.logical_and(cell == row, jnp.logical_and(layer == i, holder == x))
        picks.append(as_onehot(match))

    for step in range(STEPS):
        def pair(_, carry):
            sweep(va_ref, vb_ref, top)
            sweep(vb_ref, va_ref, top)
            return carry

        lax.fori_loop(0, ITERS // 2, pair, 0)
        below = 0.0
        for i in range(layers):
            heat = va_ref[i, own_body, :] / s_ref[i, own_body, :]
            if step == STEPS - 1:
                out_ref[flip(z, layers, i)] = heat
            below = below + exact_dot(picks[i], split(heat))
        warmth = warmth + coolant_gain * coef * (below - warmth)
        if step < STEPS - 1:
            for i in range(top + 1):
                here = pl.ds(pad, length)
                r_ref[i, here, :] = e_ref[i, here, :] + g_ref[i, here, :] * va_ref[i, here, :]

    ret_ref[...] = jnp.where(holder == x, warmth, 0.0)
    for k, ref in enumerate((keep_ref,) + tuple(sends)):
        owner = lax.rem(x + k, gx)
        ref[...] = ret_ref[pl.ds(pl.multiple_of(owner * seg, seg), seg), :]


def local(gx, gy, gz, u, power, storage, conductance, warmth, coef, holder, stratum, transverse):
    layers, rows, columns = u.shape
    seg = warmth.shape[1]
    segments = stratum.shape[1]
    if gz != 2 or gx < 3 or columns != LANES or 2 * layers * GROUP != LANES or rows % 32:
        raise ValueError("unsupported shape")
    holder = holder[:, :, 0]
    shape = (layers, rows)
    f32 = jnp.float32
    chunk = rows // 4
    wide = RAW * chunk + 2 * seg

    def struct(*dims):
        return jax.ShapeDtypeStruct(dims, f32)

    own, to_left, to_right, only = pl.pallas_call(
        pack_kernel,
        out_shape=(
            struct(RAW * layers * rows + 2 * seg, LANES),
            struct(wide, LANES),
            struct(wide, LANES),
            struct(2 * seg, LANES),
        ),
        in_specs=[pl.BlockSpec(memory_space=pltpu.HBM)] * 6,
        out_specs=(VMEM,) * 4,
        scratch_shapes=[pltpu.SemaphoreType.DMA((RAW * layers + 2,))],
        compiler_params=PARAMS,
        name="pack",
    )(u, power, storage, conductance, warmth, coef)

    swap = [(0, 1), (1, 0)]
    partner = lax.ppermute(own, "gz", swap)
    received = []
    for k in range(1, gx):
        payload = to_left if k == 1 else to_right if k == gx - 1 else only
        received.append(lax.ppermute(payload, "gx", [(i, (i - k) % gx) for i in range(gx)]))

    strip_rows = FIELDS * layers * HALO + 4 * HALO
    sides = 1 if gy == 2 else 2
    strips = pl.pallas_call(
        functools.partial(strip_kernel, gx, gy, shape, seg),
        out_shape=(struct(strip_rows, LANES),) * sides,
        in_specs=[VMEM] * (4 + gx - 1),
        out_specs=(VMEM,) * sides,
        scratch_shapes=[pltpu.VMEM((segments, LANES), f32)] * 2,
        compiler_params=PARAMS,
        name="strips",
    )(own, holder, stratum, transverse, *received)
    if gy == 2:
        along = [lax.ppermute(strips[0], "gy", swap)]
    else:
        up = [(i, i + 1) for i in range(gy - 1)]
        down = [(j, i) for i, j in up]
        along = [lax.ppermute(strips[1], "gy", up), lax.ppermute(strips[0], "gy", down)]
    late = lax.ppermute(jnp.concatenate(received + along, axis=0), "gz", swap)

    field = pltpu.VMEM((2 * layers + 1, rows + 2 * HALO + 16, LANES), f32)
    results = pl.pallas_call(
        functools.partial(sweep_kernel, gx, gy, shape, seg),
        out_shape=(struct(layers, rows, LANES),) + (struct(seg, LANES),) * gx,
        in_specs=[VMEM] * (5 + gx - 1 + sides + 1),
        out_specs=(VMEM,) * (1 + gx),
        scratch_shapes=[field] * 10 + [pltpu.VMEM((segments, LANES), f32)] * 5,
        compiler_params=PARAMS,
        name="sweeps",
    )(own, partner, holder, stratum, transverse, *received, *along, late)
    temperature, total = results[0], results[1]
    for k in range(1, gx):
        total = total + lax.ppermute(results[1 + k], "gx", [(i, (i + k) % gx) for i in range(gx)])
    return temperature, total[None]


def solution(mesh):
    gx, gy, gz = (mesh.shape[a] for a in ("gx", "gy", "gz"))
    cells = P(("stack", "gz"), "gy", "gx")
    segments = P(("stack", "gy", "gz"), "gx", None)
    return jax.shard_map(
        functools.partial(local, gx, gy, gz),
        mesh=mesh,
        in_specs=(cells, cells, cells, P(None, ("stack", "gz"), "gy", "gx"), segments, segments, P(), P(), P()),
        out_specs=(cells, segments),
        check_vma=False,
    )
```

```python
import functools

import jax
import jax.numpy as jnp
from jax import lax
from jax.experimental import pallas as pl
from jax.experimental.pallas import tpu as pltpu
from jax.sharding import PartitionSpec as P

STEPS = 2
ITERS = 4
HALO = STEPS * ITERS
GROUP = 2 * HALO
LANES = 128
RAW = 5
FIELDS = 7
coolant_gain = 0.5

VMEM = pl.BlockSpec(memory_space=pltpu.VMEM)
FETCH = pltpu.CompilerParams(vmem_limit_bytes=56 * 1024 * 1024)
PARAMS = pltpu.CompilerParams(vmem_limit_bytes=40 * 1024 * 1024)


def lane_of(rows):
    return lax.broadcasted_iota(jnp.int32, (rows, LANES), 1)


def take(value, index):
    return jnp.take_along_axis(value, index, axis=1, mode="promise_in_bounds")


def near_edges(rows):
    k = lane_of(rows) % GROUP
    return jnp.where(k < HALO, HALO - 1 - k, LANES + HALO - 1 - k)


def far_edges(rows):
    k = lane_of(rows) % GROUP
    return jnp.where(k < HALO, LANES - 1 - k, GROUP - 1 - k)


def split(value):
    high = value.astype(jnp.bfloat16)
    low = (value - high.astype(jnp.float32)).astype(jnp.bfloat16)
    return high, low


def exact_dot(onehot, parts):
    high, low = parts
    total = jnp.dot(onehot, high, preferred_element_type=jnp.float32)
    return total + jnp.dot(onehot, low, preferred_element_type=jnp.float32)


def coupling(coef, warmth):
    flow = coef * warmth
    second = coolant_gain * coef * coef
    return jnp.concatenate([coef, flow, second, flow - second * warmth], axis=1)


def flip(z, layers, i):
    return jnp.where(z == 0, i, layers - 1 - i)


def fetch_cells(refs, layers, rows, z, dest_ref, sems):
    u_ref, p_ref, c_ref, k_ref = refs
    copies = []
    for field, ref in enumerate((k_ref.at[0], k_ref.at[1], u_ref, p_ref, c_ref)):
        for i in range(layers):
            place = pl.ds((field * layers + i) * rows, rows)
            copies.append(pltpu.make_async_copy(ref.at[flip(z, layers, i)], dest_ref.at[place, :], sems.at[len(copies)]))
            copies[-1].start()
    return copies


def edges_kernel(u_ref, p_ref, c_ref, k_ref, f_ref, x_ref, left_ref, right_ref, seg_ref, cells_ref, sems):
    layers, rows, _ = u_ref.shape
    seg = f_ref.shape[1]
    plane = layers * rows
    copies = fetch_cells((u_ref, p_ref, c_ref, k_ref), layers, rows, lax.axis_index("gz"), cells_ref, sems)
    for j, ref in enumerate((x_ref, f_ref)):
        place = pl.ds(j * seg, seg)
        copies.append(pltpu.make_async_copy(ref.at[0], seg_ref.at[place, :], sems.at[len(copies)]))
        copies[-1].start()
    for copy in copies:
        copy.wait()
    for holder in range(1, seg_ref.shape[0] // (2 * seg)):
        seg_ref[2 * seg * holder : 2 * seg * (holder + 1), :] = seg_ref[: 2 * seg, :]
    chunk = rows // 4
    lane = lane_of(chunk)
    first = lane % GROUP < HALO
    near, far = near_edges(chunk), far_edges(chunk)
    for part in range(RAW):
        even = jnp.zeros((chunk, LANES), jnp.float32)
        odd = even
        for h in range(2):
            for i in range(layers):
                here = lane // GROUP == h * layers + i
                for side in range(2):
                    g = 2 * h + side
                    if part < 4:
                        at = g * plane + i * rows + part * chunk
                    else:
                        at = 4 * plane + i * rows + g * chunk
                    block = cells_ref[at : at + chunk, :]
                    if side == 0:
                        even = jnp.where(here, take(block, near), even)
                    else:
                        odd = jnp.where(here, take(block, far), odd)
        left_ref[part * chunk : (part + 1) * chunk, :] = jnp.where(first, even, odd)
        right_ref[part * chunk : (part + 1) * chunk, :] = jnp.where(first, odd, even)


def own_kernel(u_ref, p_ref, c_ref, k_ref, own_ref, sems):
    layers, rows, _ = u_ref.shape
    copies = fetch_cells((u_ref, p_ref, c_ref, k_ref), layers, rows, lax.axis_index("gz"), own_ref, sems)
    for copy in copies:
        copy.wait()
    roots = pl.ds(0, 2 * layers * rows)
    own_ref[roots, :] = jnp.sqrt(own_ref[roots, :])


class Strips:
    def __init__(self, ref, right_at, left_at, rows, layers):
        self.ref, self.right_at, self.left_at = ref, right_at, left_at
        self.rows, self.layers = rows, layers

    def merged(self, field, start, n, x, gx):
        chunk = self.rows // 4
        if field < 4:
            g, at = field, start
        else:
            g, at = start // chunk, 4 * chunk + start % chunk
        ref_r, ref_l = self.ref
        a = ref_r[self.right_at + at : self.right_at + at + n, :]
        b = ref_l[self.left_at + at : self.left_at + at + n, :]
        a = jnp.where(x < gx - 1, a, 0.0)
        b = jnp.where(x > 0, b, 0.0)
        first = lane_of(n) % GROUP < HALO
        return g, (jnp.where(first, a, b) if g % 2 == 0 else jnp.where(first, b, a))

    def halo(self, field, start, n, x, gx, partner):
        g, both = self.merged(field, start, n, x, gx)
        if field < 2:
            both = jnp.sqrt(both)
        lane = lane_of(n)
        half = self.layers * GROUP
        src = lane % half
        if partner:
            src = (self.layers - 1 - src // GROUP) * GROUP + src % GROUP
        if g % 2 == 1:
            src = jnp.where(src % GROUP < HALO, src + HALO, src - HALO)
        return take(both, src + half * (g // 2))


def segments_of(ref, start, gx, seg):
    at = [start + 2 * seg * holder for holder in range(gx)]
    coef = jnp.concatenate([ref[i : i + seg, :] for i in at], axis=0)
    warmth = jnp.concatenate([ref[i + seg : i + 2 * seg, :] for i in at], axis=0)
    return coef, warmth


def tables(z, group, layers, holder_ref, stratum_ref, transverse_ref):
    holder = holder_ref[pl.ds(group, 1), :]
    layer = stratum_ref[pl.ds(group, 1), :]
    layer = jnp.where(z == 0, layer, layers - 1 - layer)
    row = transverse_ref[pl.ds(group, 1), :]
    n = holder.shape[1]
    where = lax.broadcasted_iota(jnp.int32, (8, n), 0)
    stacked = jnp.where(where == 0, holder, jnp.where(where == 1, layer, row))
    eye = lax.broadcasted_iota(jnp.int32, (n, n), 0) == lax.broadcasted_iota(jnp.int32, (n, n), 1)
    column = lax.dot_general(
        eye.astype(jnp.float32).astype(jnp.bfloat16),
        stacked.astype(jnp.float32).astype(jnp.bfloat16),
        (((1,), (1,)), ((), ())),
        preferred_element_type=jnp.float32,
    ).astype(jnp.int32)
    return (holder, layer, row), (column[:, 0:1], column[:, 1:2], column[:, 2:3])


def as_onehot(mask):
    return jnp.where(mask, 1.0, 0.0).astype(jnp.bfloat16)


def halo_segments(coef, warmth, columns, base, x):
    n = coef.shape[0]
    lane = lane_of(n)
    holder, layer, _ = columns
    side = jnp.where(lane % GROUP < HALO, x + 1, x - 1)
    mine = jnp.logical_and(lane // GROUP == layer + base, holder == side)
    near = near_edges(n)
    return coupling(jnp.where(mine, take(coef, near), 0.0), take(warmth, near))


def combine(raw, added):
    s, t, u, power, storage = raw
    wall, flow, second, later = (added[:, i * LANES : (i + 1) * LANES] for i in range(4))
    return s, t, u, storage + wall, power + storage * u + flow, power + later, storage + second


def strip_kernel(gx, gy, shape, seg, *refs):
    layers, rows = shape
    own_ref, holder_ref, stratum_ref, transverse_ref, right_ref, left_ref, seg_ref = refs[:7]
    outs = refs[7:]
    x, y, z = (lax.axis_index(a) for a in ("gx", "gy", "gz"))
    plane = layers * rows
    (holder, layer, row), columns = tables(z, y * 2 + z, layers, holder_ref, stratum_ref, transverse_ref)
    coef, warmth = segments_of(seg_ref, 0, gx, seg)
    parts = split(coupling(coef, warmth))
    outer = split(halo_segments(coef, warmth, columns, 0, x))
    strips = Strips((right_ref, left_ref), 0, 0, rows, layers)
    n = holder.shape[1]

    def strip(out_ref, start):
        cell = lax.broadcasted_iota(jnp.int32, (layers * HALO, n), 0)
        match = jnp.logical_and(cell // HALO == layer, cell % HALO + start == row)
        added = exact_dot(as_onehot(jnp.logical_and(match, holder == x)), parts)
        for i in range(layers):
            raw = [own_ref[f * plane + i * rows + start : f * plane + i * rows + start + HALO, :] for f in range(RAW)]
            for f, value in enumerate(combine(raw, added[i * HALO : (i + 1) * HALO])):
                out_ref[(f * layers + i) * HALO : (f * layers + i + 1) * HALO, :] = value
        line = lax.broadcasted_iota(jnp.int32, (HALO, n), 0)
        beside = exact_dot(as_onehot(line + start == row), outer)
        raw = [strips.halo(f, start, HALO, x, gx, False) for f in range(RAW)]
        made = list(combine(raw, beside))
        made.append(jnp.zeros_like(made[0]))
        low = lane_of(HALO) < LANES // 2
        at = FIELDS * layers * HALO
        for j in range(4):
            packed = jnp.where(low, made[2 * j], pltpu.roll(made[2 * j + 1], LANES // 2, 1))
            out_ref[at + j * HALO : at + (j + 1) * HALO, :] = packed

    if gy == 2:
        pl.when(y == 0)(lambda: strip(outs[0], rows - HALO))
        pl.when(y == 1)(lambda: strip(outs[0], 0))
    else:
        strip(outs[0], 0)
        strip(outs[1], rows - HALO)


def lateral(buf, at, n, count):
    lane = lane_of(n)
    k, group = lane % GROUP, lane // GROUP
    top = buf.shape[0] - 1
    centre = [buf[i, pl.ds(at, n), :] for i in range(count)]
    halo = buf[top, pl.ds(at, n), :]
    border = jnp.zeros_like(halo)
    inner = jnp.logical_or(k == HALO - 1, k == HALO)
    sums = []
    for i in range(count):
        border = jnp.where(group == i, pltpu.roll(centre[i], i * GROUP + HALO, 1), border)
        beside = pltpu.roll(halo, LANES - (i * GROUP + HALO), 1)
        east = jnp.where(lane == LANES - 1, beside, pltpu.roll(centre[i], LANES - 1, 1))
        west = jnp.where(lane == 0, beside, pltpu.roll(centre[i], 1, 1))
        sums.append(east + west + buf[i, pl.ds(at - 1, n), :] + buf[i, pl.ds(at + 1, n), :])
    one = jnp.where(k == HALO, border, pltpu.roll(halo, 1, 1))
    other = jnp.where(k == HALO - 1, border, pltpu.roll(halo, LANES - 1, 1))
    sums.append(one + other + buf[top, pl.ds(at - 1, n), :] + buf[top, pl.ds(at + 1, n), :])
    return centre + [halo], sums


def vertical(values):
    planes, halo = values[:-1], values[-1]
    sums = []
    for i in range(len(planes)):
        near = [planes[j] for j in (i - 1, i + 1) if 0 <= j < len(planes)]
        sums.append(functools.reduce(jnp.add, near))
    lane = lane_of(halo.shape[0])
    up = jnp.where(lane >= GROUP, pltpu.roll(halo, GROUP, 1), 0.0)
    down = jnp.where(lane < LANES - GROUP, pltpu.roll(halo, LANES - GROUP, 1), 0.0)
    sums.append(up + down)
    return sums


def sweep_kernel(gx, gy, shape, seg, *refs):
    layers, rows = shape
    own_ref, partner_ref, holder_ref, stratum_ref, transverse_ref, right_ref, left_ref, seg_ref = refs[:8]
    refs = refs[8:]
    sides = 1 if gy == 2 else 2
    along = refs[:sides]
    late_ref, out_ref, ret_ref = refs[sides : sides + 3]
    s_ref, t_ref, a_ref, r_ref, e_ref, g_ref, b_ref, q_ref, va_ref, vb_ref = refs[sides + 3 :]
    x, y, z = (lax.axis_index(a) for a in ("gx", "gy", "gz"))
    plane, chunk = layers * rows, rows // 4
    top = 2 * layers
    pad = 8
    body = pad + HALO
    length = rows + 2 * HALO

    lengths = (right_ref.shape[0], left_ref.shape[0], seg_ref.shape[0])
    starts = [sum(lengths[:k]) for k in range(4)]
    groups = []
    for ref, base, sources, start in ((own_ref, 0, seg_ref, 0), (partner_ref, layers, late_ref, starts[2])):
        coef, warmth = segments_of(sources, start, gx, seg)
        group = y * 2 + (z if base == 0 else 1 - z)
        along_lanes, columns = tables(z, group, layers, holder_ref, stratum_ref, transverse_ref)
        groups.append((ref, base, coef, warmth, along_lanes, columns))

    dests = (s_ref, t_ref, va_ref, a_ref, r_ref, e_ref, g_ref)
    zeros = jnp.zeros((pad, LANES), jnp.float32)
    for ref in (s_ref, va_ref, vb_ref):
        for i in range(top + 1):
            ref[i, 0:pad, :] = zeros
            ref[i, pad + length : pad + length + pad, :] = zeros

    def put(i, start, values):
        n = values[0].shape[0]
        for f, value in enumerate(values):
            if f == 2:
                value = value * values[0]
            dests[f][i, start : start + n, :] = value

    beside = 0.0
    for ref, base, coef, warmth, (holder, layer, row), columns in groups:
        n = holder.shape[1]
        parts = split(coupling(coef, warmth))
        line = lax.broadcasted_iota(jnp.int32, (rows, n), 0)
        for i in range(layers):
            match = jnp.logical_and(line == row, jnp.logical_and(layer == i, holder == x))
            added = exact_dot(as_onehot(match), parts)
            src = i if base == 0 else layers - 1 - i
            raw = [ref[f * plane + src * rows : f * plane + (src + 1) * rows, :] for f in range(RAW)]
            put(base + i, body, combine(raw, added))
        beside = beside + exact_dot(as_onehot(line == row), split(halo_segments(coef, warmth, columns, base, x)))
    mine = Strips((right_ref, left_ref), 0, 0, rows, layers)
    theirs = Strips((late_ref, late_ref), starts[0], starts[1], rows, layers)
    low = lane_of(chunk) < LANES // 2
    for part in range(4):
        raw = []
        for f in range(RAW):
            a = mine.halo(f, part * chunk, chunk, x, gx, False)
            b = theirs.halo(f, part * chunk, chunk, x, gx, True)
            raw.append(jnp.where(low, a, b))
        put(top, body + part * chunk, combine(raw, beside[part * chunk : (part + 1) * chunk]))

    for side in range(2):
        start = pad if side == 0 else body + rows
        if gy == 2:
            source, at, live = along[0], starts[3], y == 1 - side
        else:
            source, at, live = along[side], starts[3] + side * along[0].shape[0], True
        sources = ((source, 0), (late_ref, at))
        for i in range(top):
            ref, offset = sources[i // layers]
            src = i if i < layers else top - 1 - i
            values = []
            for f in range(FIELDS):
                place = offset + (f * layers + src) * HALO
                values.append(jnp.where(live, ref[place : place + HALO, :], 0.0))
            put(i, start, values)
        lane = lane_of(HALO)
        src = lane % (LANES // 2)
        turned = (layers - 1 - src // GROUP) * GROUP + src % GROUP
        values = []
        for f in range(FIELDS):
            place = FIELDS * layers * HALO + (f // 2) * HALO
            half = (LANES // 2) * (f % 2)
            a = take(source[place : place + HALO, :], src + half)
            b = take(late_ref[at + place : at + place + HALO, :], turned + half)
            values.append(jnp.where(live, jnp.where(lane < LANES // 2, a, b), 0.0))
        put(top, start, values)

    step_rows = 24
    for c in range(length // step_rows):
        at = pad + c * step_rows
        here = pl.ds(at, step_rows)
        centre, sums = lateral(s_ref, at, step_rows, top)
        t = [t_ref[i, here, :] for i in range(top + 1)]
        above = vertical(t)
        for i in range(top + 1):
            s = centre[i]
            diag = a_ref[i, here, :] + s * sums[i] + t[i] * above[i]
            inverse = 1.0 / jnp.where(diag > 0.0, diag, 1.0)
            scaled = s * inverse
            a_ref[i, here, :] = s * scaled
            b_ref[i, here, :] = t[i] * scaled
            r_ref[i, here, :] = r_ref[i, here, :] * scaled
            e_ref[i, here, :] = e_ref[i, here, :] * scaled
            g_ref[i, here, :] = g_ref[i, here, :] * inverse
            q_ref[i, here, :] = t[i] * jnp.where(s > 0.0, 1.0 / jnp.where(s > 0.0, s, 1.0), 0.0)

    def sweep(src_ref, dst_ref, count):
        for c in range(length // step_rows):
            at = pad + c * step_rows
            here = pl.ds(at, step_rows)
            centre, sums = lateral(src_ref, at, step_rows, top)
            above = vertical([q_ref[i, here, :] * centre[i] for i in range(top + 1)])
            for i in range(top + 1):
                value = r_ref[i, here, :] + a_ref[i, here, :] * sums[i] + b_ref[i, here, :] * above[i]
                dst_ref[i, here, :] = value

    own_body = pl.ds(body, rows)
    _, _, coef, warmth, _, (holder, layer, row) = groups[0]
    n = coef.shape[0]
    cell = lax.broadcasted_iota(jnp.int32, (n, rows), 1)
    picks = []
    for i in range(layers):
        match = jnp.logical_and(cell == row, jnp.logical_and(layer == i, holder == x))
        picks.append(as_onehot(match))

    for step in range(STEPS):
        def pair(_, carry):
            sweep(va_ref, vb_ref, top)
            sweep(vb_ref, va_ref, top)
            return carry

        lax.fori_loop(0, ITERS // 2, pair, 0)
        below = 0.0
        for i in range(layers):
            heat = va_ref[i, own_body, :] / s_ref[i, own_body, :]
            if step == STEPS - 1:
                out_ref[flip(z, layers, i)] = heat
            below = below + exact_dot(picks[i], split(heat))
        warmth = warmth + coolant_gain * coef * (below - warmth)
        if step < STEPS - 1:
            for i in range(top + 1):
                here = pl.ds(pad, length)
                r_ref[i, here, :] = e_ref[i, here, :] + g_ref[i, here, :] * va_ref[i, here, :]

    ret_ref[...] = jnp.where(holder == x, warmth, 0.0)


def local(gx, gy, gz, u, power, storage, conductance, warmth, coef, holder, stratum, transverse):
    layers, rows, columns = u.shape
    seg = warmth.shape[1]
    segments = stratum.shape[1]
    if gz != 2 or gx < 3 or columns != LANES or 2 * layers * GROUP != LANES or rows % 32:
        raise ValueError("unsupported shape")
    holder = holder[:, :, 0]
    shape = (layers, rows)
    f32 = jnp.float32
    chunk = rows // 4

    def struct(*dims):
        return jax.ShapeDtypeStruct(dims, f32)

    hbm = pl.BlockSpec(memory_space=pltpu.HBM)
    to_left, to_right, to_all = pl.pallas_call(
        edges_kernel,
        out_shape=(struct(RAW * chunk, LANES), struct(RAW * chunk, LANES), struct(gx * 2 * seg, LANES)),
        in_specs=[hbm] * 6,
        out_specs=(VMEM,) * 3,
        scratch_shapes=[pltpu.VMEM((RAW * layers * rows, LANES), f32), pltpu.SemaphoreType.DMA((RAW * layers + 2,))],
        compiler_params=FETCH,
        name="edges",
    )(u, power, storage, conductance, warmth, coef)
    up = [(i, i + 1) for i in range(gx - 1)]
    down = [(j, i) for i, j in up]
    from_right = lax.ppermute(to_left, "gx", down)
    from_left = lax.ppermute(to_right, "gx", up)
    gathered = lax.all_to_all(to_all, "gx", 0, 0, tiled=True)

    own = pl.pallas_call(
        own_kernel,
        out_shape=struct(RAW * layers * rows, LANES),
        in_specs=[hbm] * 4,
        out_specs=VMEM,
        scratch_shapes=[pltpu.SemaphoreType.DMA((RAW * layers,))],
        compiler_params=FETCH,
        name="own",
    )(u, power, storage, conductance)
    swap = [(0, 1), (1, 0)]
    partner = lax.ppermute(own, "gz", swap)

    received = [from_right, from_left, gathered]
    strip_rows = FIELDS * layers * HALO + 4 * HALO
    sides = 1 if gy == 2 else 2
    strips = pl.pallas_call(
        functools.partial(strip_kernel, gx, gy, shape, seg),
        out_shape=(struct(strip_rows, LANES),) * sides,
        in_specs=[VMEM] * 7,
        out_specs=(VMEM,) * sides,
        compiler_params=PARAMS,
        name="strips",
    )(own, holder, stratum, transverse, *received)
    if gy == 2:
        along = [lax.ppermute(strips[0], "gy", swap)]
    else:
        up = [(i, i + 1) for i in range(gy - 1)]
        down = [(j, i) for i, j in up]
        along = [lax.ppermute(strips[1], "gy", up), lax.ppermute(strips[0], "gy", down)]
    late = lax.ppermute(jnp.concatenate(received + along, axis=0), "gz", swap)

    field = pltpu.VMEM((2 * layers + 1, rows + 2 * HALO + 16, LANES), f32)
    temperature, back = pl.pallas_call(
        functools.partial(sweep_kernel, gx, gy, shape, seg),
        out_shape=(struct(layers, rows, LANES), struct(segments, LANES)),
        in_specs=[VMEM] * (8 + sides + 1),
        out_specs=(VMEM,) * 2,
        scratch_shapes=[field] * 10,
        compiler_params=PARAMS,
        name="sweeps",
    )(own, partner, holder, stratum, transverse, *received, *along, late)
    shares = lax.all_to_all(back, "gx", 0, 0, tiled=True).reshape(gx, seg, LANES)
    total = shares[0]
    for k in range(1, gx):
        total = total + shares[k]
    return temperature, total[None]


def solution(mesh):
    gx, gy, gz = (mesh.shape[a] for a in ("gx", "gy", "gz"))
    cells = P(("stack", "gz"), "gy", "gx")
    segments = P(("stack", "gy", "gz"), "gx", None)
    return jax.shard_map(
        functools.partial(local, gx, gy, gz),
        mesh=mesh,
        in_specs=(cells, cells, cells, P(None, ("stack", "gz"), "gy", "gx"), segments, segments, P(), P(), P()),
        out_specs=(cells, segments),
        check_vma=False,
    )
```

```python
import functools

import jax
import jax.numpy as jnp
from jax import lax
from jax.experimental import pallas as pl
from jax.experimental.pallas import tpu as pltpu
from jax.sharding import PartitionSpec as P

STEPS = 2
ITERS = 4
HALO = STEPS * ITERS
GROUP = 2 * HALO
LANES = 128
RAW = 5
FIELDS = 7
coolant_gain = 0.5

VMEM = pl.BlockSpec(memory_space=pltpu.VMEM)
PARAMS = pltpu.CompilerParams(vmem_limit_bytes=40 * 1024 * 1024)


def cost(microseconds):
    return pl.CostEstimate(flops=0, bytes_accessed=int(microseconds * 3e6), transcendentals=0)


def lane_of(rows):
    return lax.broadcasted_iota(jnp.int32, (rows, LANES), 1)


def take(value, index):
    return jnp.take_along_axis(value, index, axis=1, mode="promise_in_bounds")


def near_edges(rows):
    k = lane_of(rows) % GROUP
    return jnp.where(k < HALO, HALO - 1 - k, LANES + HALO - 1 - k)


def far_edges(rows):
    k = lane_of(rows) % GROUP
    return jnp.where(k < HALO, LANES - 1 - k, GROUP - 1 - k)


def split(value):
    high = value.astype(jnp.bfloat16)
    low = (value - high.astype(jnp.float32)).astype(jnp.bfloat16)
    return high, low


def exact_dot(onehot, value):
    high, low = split(value)
    both = jnp.concatenate([high, low], axis=0)
    return jnp.dot(jnp.concatenate([onehot, onehot], axis=1), both, preferred_element_type=jnp.float32)


def coupling(coef, warmth):
    flow = coef * warmth
    second = coolant_gain * coef * coef
    return jnp.concatenate([coef, flow, second, flow - second * warmth], axis=1)


def flip(z, layers, i):
    return jnp.where(z == 0, i, layers - 1 - i)


def pack_kernel(u_ref, p_ref, c_ref, k_ref, f_ref, x_ref, own_ref, left_ref, right_ref, seg_ref):
    layers, rows, _ = u_ref.shape
    seg = f_ref.shape[1]
    z = lax.axis_index("gz")
    plane = layers * rows
    for i in range(layers):
        src = flip(z, layers, i)
        at = i * rows
        own_ref[at : at + rows, :] = k_ref[0, src]
        own_ref[plane + at : plane + at + rows, :] = k_ref[1, src]
        own_ref[2 * plane + at : 2 * plane + at + rows, :] = u_ref[src]
        own_ref[3 * plane + at : 3 * plane + at + rows, :] = p_ref[src]
        own_ref[4 * plane + at : 4 * plane + at + rows, :] = c_ref[src]
    chunk = rows // 4
    lane = lane_of(chunk)
    first = lane % GROUP < HALO
    near, far = near_edges(chunk), far_edges(chunk)
    for part in range(RAW):
        even = jnp.zeros((chunk, LANES), jnp.float32)
        odd = even
        for h in range(2):
            for i in range(layers):
                here = lane // GROUP == h * layers + i
                for side in range(2):
                    g = 2 * h + side
                    if part < 4:
                        at = g * plane + i * rows + part * chunk
                    else:
                        at = 4 * plane + i * rows + g * chunk
                    block = own_ref[at : at + chunk, :]
                    if side == 0:
                        even = jnp.where(here, take(block, near), even)
                    else:
                        odd = jnp.where(here, take(block, far), odd)
        left_ref[part * chunk : (part + 1) * chunk, :] = jnp.where(first, even, odd)
        right_ref[part * chunk : (part + 1) * chunk, :] = jnp.where(first, odd, even)
    coef, warmth = x_ref[0], f_ref[0]
    at = RAW * chunk
    left_ref[at : at + seg, :] = coef
    left_ref[at + seg : at + 2 * seg, :] = warmth
    right_ref[at : at + seg, :] = coef
    right_ref[at + seg : at + 2 * seg, :] = warmth
    seg_ref[:seg, :] = coef
    seg_ref[seg:, :] = warmth
    at = RAW * plane
    own_ref[at : at + seg, :] = coef
    own_ref[at + seg : at + 2 * seg, :] = warmth


class Strips:
    def __init__(self, ref, right_at, left_at, rows, layers):
        self.ref, self.right_at, self.left_at = ref, right_at, left_at
        self.rows, self.layers = rows, layers

    def merged(self, field, start, n, x, gx):
        chunk = self.rows // 4
        if field < 4:
            g, at = field, start
        else:
            g, at = start // chunk, 4 * chunk + start % chunk
        ref_r, ref_l = self.ref
        a = ref_r[self.right_at + at : self.right_at + at + n, :]
        b = ref_l[self.left_at + at : self.left_at + at + n, :]
        a = jnp.where(x < gx - 1, a, 0.0)
        b = jnp.where(x > 0, b, 0.0)
        first = lane_of(n) % GROUP < HALO
        return g, (jnp.where(first, a, b) if g % 2 == 0 else jnp.where(first, b, a))

    def halo(self, field, start, n, x, gx, partner):
        g, both = self.merged(field, start, n, x, gx)
        lane = lane_of(n)
        half = self.layers * GROUP
        src = lane % half
        if partner:
            src = (self.layers - 1 - src // GROUP) * GROUP + src % GROUP
        if g % 2 == 1:
            src = jnp.where(src % GROUP < HALO, src + HALO, src - HALO)
        return take(both, src + half * (g // 2))


def place_segments(x, gx, seg, coef_ref, warmth_ref, first, rest):
    coef, warmth = first
    coef_ref[pl.ds(pl.multiple_of(x * seg, seg), seg), :] = coef
    warmth_ref[pl.ds(pl.multiple_of(x * seg, seg), seg), :] = warmth
    for k, (ref, at) in enumerate(rest, 1):
        holder = lax.rem(x + k, gx)
        place = pl.ds(pl.multiple_of(holder * seg, seg), seg)
        coef_ref[place, :] = ref[at : at + seg, :]
        warmth_ref[place, :] = ref[at + seg : at + 2 * seg, :]


def tables(z, group, layers, holder_ref, stratum_ref, transverse_ref):
    holder = holder_ref[pl.ds(group, 1), :]
    layer = stratum_ref[pl.ds(group, 1), :]
    layer = jnp.where(z == 0, layer, layers - 1 - layer)
    row = transverse_ref[pl.ds(group, 1), :]
    n = holder.shape[1]
    which = lax.broadcasted_iota(jnp.int32, (8, n), 0)
    stacked = jnp.where(which == 0, holder, jnp.where(which == 1, layer, row))
    eye = lax.broadcasted_iota(jnp.int32, (n, n), 0) == lax.broadcasted_iota(jnp.int32, (n, n), 1)
    columns = lax.dot_general(
        eye.astype(jnp.float32).astype(jnp.bfloat16),
        stacked.astype(jnp.float32).astype(jnp.bfloat16),
        (((1,), (1,)), ((), ())),
        preferred_element_type=jnp.float32,
    )
    return (holder, layer, row), columns


def as_onehot(mask):
    return jnp.where(mask, 1.0, 0.0).astype(jnp.bfloat16)


def halo_segments(coef, warmth, columns, base, x):
    n = coef.shape[0]
    lane = lane_of(n)
    holder, layer = columns[:, 0:1].astype(jnp.int32), columns[:, 1:2].astype(jnp.int32)
    side = jnp.where(lane % GROUP < HALO, x + 1, x - 1)
    mine = jnp.logical_and(lane // GROUP == layer + base, holder == side)
    near = near_edges(n)
    return coupling(jnp.where(mine, take(coef, near), 0.0), take(warmth, near))


def combine(raw, added):
    s, t, u, power, storage = raw
    wall, flow, second, later = (added[:, i * LANES : (i + 1) * LANES] for i in range(4))
    return s, t, s * u, storage + wall, power + storage * u + flow, power + later, storage + second


def starts_of(gx, chunk, seg):
    lengths = [RAW * chunk + 2 * seg if k in (1, gx - 1) else 2 * seg for k in range(1, gx)]
    return [sum(lengths[:k]) for k in range(gx)]


def edge_at(top, rows):
    return 0 if top is True else rows - HALO if top is False else pl.multiple_of(jnp.where(top, 0, rows - HALO), HALO)


def inner_at(top, rows):
    return HALO if top is True else rows - 2 * HALO if top is False else pl.multiple_of(jnp.where(top, HALO, rows - 2 * HALO), HALO)


def sides_of(gy, y):
    return [(y == 1, True)] if gy == 2 else [(True, y > 0), (False, y < gy - 1)]


def fill_kernel(partner, gx, gy, shape, seg, *refs):
    layers, rows = shape
    cells_ref, holder_ref, stratum_ref, transverse_ref = refs[:4]
    plane, chunk = layers * rows, rows // 4
    starts = starts_of(gx, chunk, seg)
    if partner:
        received = [refs[4]] * (gx - 1)
        refs = refs[5:]
    else:
        received = refs[4 : 4 + gx - 1]
        refs = refs[4 + gx - 1 :]
        starts = [0] * gx
    sides = 1 if gy == 2 else 2
    out_ref = refs[0]
    if partner:
        coef_ref, warmth_ref = refs[1:3]
    else:
        strip_refs, info_ref, segments_ref = refs[1 : 1 + sides], refs[1 + sides], refs[2 + sides]
        n = segments_ref.shape[0] // 2
        coef_ref, warmth_ref = segments_ref.at[pl.ds(0, n), :], segments_ref.at[pl.ds(n, n), :]
    x, y, z = (lax.axis_index(a) for a in ("gx", "gy", "gz"))
    base = layers if partner else 0
    rest = [(r, starts[k] + (RAW * chunk if k in (0, gx - 2) else 0)) for k, r in enumerate(received)]
    at = RAW * plane
    first = (cells_ref[at : at + seg, :], cells_ref[at + seg : at + 2 * seg, :])
    place_segments(x, gx, seg, coef_ref, warmth_ref, first, rest)
    group = y * 2 + ((1 - z) if partner else z)
    (holder, layer, row), columns = tables(z, group, layers, holder_ref, stratum_ref, transverse_ref)
    coef, warmth = coef_ref[...], warmth_ref[...]
    n = coef.shape[0]
    if not partner:
        info_ref[...] = columns

    cell = jnp.where(holder == x, layer * rows + row, -1)
    line = lax.broadcasted_iota(jnp.int32, (plane, n), 0)
    added = exact_dot(as_onehot(line == cell), coupling(coef, warmth))
    line = lax.broadcasted_iota(jnp.int32, (rows, n), 0)
    beside = exact_dot(as_onehot(line == row), halo_segments(coef, warmth, columns, base, x))
    for i in range(layers):
        src = layers - 1 - i if partner else i
        raw = [cells_ref[f * plane + src * rows : f * plane + (src + 1) * rows, :] for f in range(RAW)]
        for f, value in enumerate(combine(raw, added[i * rows : (i + 1) * rows])):
            out_ref[f * (layers + 1) + i] = value
    strips = Strips((received[0], received[-1]), starts[0], starts[gx - 2], rows, layers)
    half = lane_of(chunk) // (LANES // 2) == (1 if partner else 0)
    for part in range(4):
        here = slice(part * chunk, (part + 1) * chunk)
        raw = [jnp.where(half, strips.halo(f, part * chunk, chunk, x, gx, partner), 0.0) for f in range(RAW)]
        for f, value in enumerate(combine(raw, beside[here])):
            out_ref[f * (layers + 1) + layers, here, :] = value
    if partner:
        return
    low = lane_of(HALO) < LANES // 2
    for strip_ref, (top, _) in zip(strip_refs, sides_of(gy, y)):
        edge = pl.ds(edge_at(top, rows), HALO)
        for f in range(FIELDS):
            for i in range(layers):
                strip_ref[(f * layers + i) * HALO : (f * layers + i + 1) * HALO, :] = out_ref[f * (layers + 1) + i, edge, :]
        at = FIELDS * layers * HALO
        made = [out_ref[f * (layers + 1) + layers, edge, :] for f in range(FIELDS)]
        made.append(jnp.zeros_like(made[0]))
        for j in range(4):
            packed = jnp.where(low, made[2 * j], pltpu.roll(made[2 * j + 1], LANES // 2, 1))
            strip_ref[at + j * HALO : at + (j + 1) * HALO, :] = packed


def lateral(buf, at, n, count):
    lane = lane_of(n)
    k, group = lane % GROUP, lane // GROUP
    top = buf.shape[0] - 1
    centre = [buf[i, pl.ds(at, n), :] for i in range(min(count + 1, top))]
    halo = buf[top, pl.ds(at, n), :]
    border = jnp.zeros_like(halo)
    sums = []
    for i in range(count):
        border = jnp.where(group == i, pltpu.roll(centre[i], i * GROUP + HALO, 1), border)
        beside = pltpu.roll(halo, LANES - (i * GROUP + HALO), 1)
        east = jnp.where(lane == LANES - 1, beside, pltpu.roll(centre[i], LANES - 1, 1))
        west = jnp.where(lane == 0, beside, pltpu.roll(centre[i], 1, 1))
        sums.append(east + west + buf[i, pl.ds(at - 1, n), :] + buf[i, pl.ds(at + 1, n), :])
    one = jnp.where(k == HALO, border, pltpu.roll(halo, 1, 1))
    other = jnp.where(k == HALO - 1, border, pltpu.roll(halo, LANES - 1, 1))
    sums.append(one + other + buf[top, pl.ds(at - 1, n), :] + buf[top, pl.ds(at + 1, n), :])
    return centre + [halo], sums


def vertical(values, count):
    planes, halo = values[:-1], values[-1]
    sums = []
    for i in range(count):
        near = [planes[j] for j in (i - 1, i + 1) if 0 <= j < len(planes)]
        sums.append(functools.reduce(jnp.add, near))
    lane = lane_of(halo.shape[0])
    up = jnp.where(lane >= GROUP, pltpu.roll(halo, GROUP, 1), 0.0)
    down = jnp.where(lane < LANES - GROUP, pltpu.roll(halo, LANES - GROUP, 1), 0.0)
    sums.append(up + down)
    return sums


def coefficients(s_ref, at, n, raw, dests, to):
    a_ref, b_ref, q_ref, r_ref, e_ref, g_ref = dests
    top = s_ref.shape[0] - 1
    centre, sums = lateral(s_ref, at, n, top)
    t = [raw(1, i) for i in range(top + 1)]
    above = vertical(t, top)
    here = pl.ds(to, n)
    for i in range(top + 1):
        s = centre[i]
        diag = raw(3, i) + s * sums[i] + t[i] * above[i]
        inverse = 1.0 / jnp.where(diag > 0.0, diag, 1.0)
        scaled = s * inverse
        a_ref[i, here, :] = s * scaled
        b_ref[i, here, :] = t[i] * scaled
        r_ref[i, here, :] = raw(4, i) * scaled
        e_ref[i, here, :] = raw(5, i) * scaled
        g_ref[i, here, :] = raw(6, i) * inverse
        q_ref[i, here, :] = t[i] * jnp.where(s > 0.0, 1.0 / jnp.where(s > 0.0, s, 1.0), 0.0)


def sweep(src_ref, dst_ref, at, n, count, coefs, base):
    a_ref, b_ref, q_ref, r_ref = coefs[:4]
    top = src_ref.shape[0] - 1
    here = pl.ds(base, n)
    centre, sums = lateral(src_ref, at, n, count)
    layers = list(range(len(centre) - 1)) + [top]
    above = vertical([q_ref[i, here, :] * c for i, c in zip(layers, centre)], count)
    for j, i in enumerate(list(range(count)) + [top]):
        value = r_ref[i, here, :] + a_ref[i, here, :] * sums[j] + b_ref[i, here, :] * above[j]
        dst_ref[i, pl.ds(at, n), :] = value


def next_rhs(coefs, v_ref, at, n, base):
    r_ref, e_ref, g_ref = coefs[3:]
    here = pl.ds(base, n)
    for i in range(v_ref.shape[0]):
        r_ref[i, here, :] = e_ref[i, here, :] + g_ref[i, here, :] * v_ref[i, pl.ds(at, n), :]


def needed(layers, n):
    return min(2 * layers, layers + STEPS * ITERS - 1 - n)


def two_steps(layers, sweep_all, between, after):
    for step in range(STEPS):
        whole = [n for n in range(step * ITERS, (step + 1) * ITERS) if needed(layers, n) == 2 * layers]
        pairs = len(whole) // 2

        def pair(k, carry):
            n = step * ITERS + 2 * k
            sweep_all(n, 0, 2 * layers)
            sweep_all(n + 1, 1, 2 * layers)
            return carry

        if pairs:
            lax.fori_loop(0, pairs, pair, 0)
        for n in range(step * ITERS + 2 * pairs, (step + 1) * ITERS):
            sweep_all(n, n % 2, needed(layers, n))
        after(step)
        if step < STEPS - 1:
            between()


PAD = 8


def tile_kernel(gx, gy, shape, *refs):
    layers, rows = shape
    own_ref, partner_ref, info_ref, out_ref, below_ref, level_ref = refs[:6]
    s_ref, va_ref, vb_ref = refs[6:9]
    coefs = refs[9:]
    x, y, z = (lax.axis_index(a) for a in ("gx", "gy", "gz"))
    top = 2 * layers
    zeros = jnp.zeros((PAD, LANES), jnp.float32)
    for ref in (s_ref, va_ref, vb_ref):
        for i in range(top + 1):
            ref[i, 0:PAD, :] = zeros
            ref[i, PAD + rows : PAD + rows + PAD, :] = zeros

    def field(f, i, here):
        j = f * (layers + 1)
        if i == top:
            return own_ref[j + layers, here, :] + partner_ref[j + layers, here, :]
        return own_ref[j + i, here, :] if i < layers else partner_ref[j + i - layers, here, :]

    for i in range(top + 1):
        s_ref[i, PAD : PAD + rows, :] = field(0, i, slice(None))
        va_ref[i, PAD : PAD + rows, :] = field(2, i, slice(None))
    n = 16
    for at in range(0, rows, n):
        coefficients(s_ref, PAD + at, n, lambda f, i: field(f, i, slice(at, at + n)), coefs, at)

    bufs = (va_ref, vb_ref)
    sides = sides_of(gy, y)

    def sweep_all(number, which, count):
        src_ref, dst_ref = bufs[which], bufs[1 - which]
        for side, (above, _) in enumerate(sides):
            inner = pl.ds(PAD + inner_at(above, rows), HALO)
            for i in range(top + 1):
                level_ref[(side * STEPS * ITERS + number) * (top + 1) + i] = src_ref[i, inner, :]
        for at in range(0, rows, n):
            sweep(src_ref, dst_ref, PAD + at, n, count, coefs, at)

    holder, layer, row = (info_ref[:, j : j + 1].astype(jnp.int32) for j in range(3))
    spoilt = None
    for above, live in sides:
        part = jnp.logical_and(row // HALO == edge_at(above, rows) // HALO, live)
        spoilt = part if spoilt is None else jnp.logical_or(spoilt, part)
    cell = jnp.where(jnp.logical_and(holder == x, jnp.logical_not(spoilt)), layer * rows + row, -1)
    picks = as_onehot(lax.broadcasted_iota(jnp.int32, (cell.shape[0], layers * rows), 1) == cell)

    def after(step):
        heat = []
        for i in range(layers):
            here = pl.ds(PAD, rows)
            heat.append(va_ref[i, here, :] / s_ref[i, here, :])
            if step == STEPS - 1:
                out_ref[flip(z, layers, i)] = heat[-1]
        below_ref[step] = exact_dot(picks, jnp.concatenate(heat, axis=0))

    def between():
        for at in range(0, rows, n):
            next_rhs(coefs, va_ref, PAD + at, n, at)

    two_steps(layers, sweep_all, between, after)


def edge_kernel(gx, gy, shape, seg, *refs):
    layers, rows = shape
    own_ref, partner_ref, info_ref, segments_ref, below_ref, level_ref = refs[:6]
    sides_n = 1 if gy == 2 else 2
    along, across = refs[6 : 6 + sides_n], refs[6 + sides_n : 6 + 2 * sides_n]
    refs = refs[6 + 2 * sides_n :]
    heat_ref, returns = refs[0], refs[1 : 1 + gx]
    ret_ref, s_ref, va_ref, vb_ref = refs[1 + gx : 5 + gx]
    coefs = refs[5 + gx :]
    x, y, z = (lax.axis_index(a) for a in ("gx", "gy", "gz"))
    top = 2 * layers
    count = info_ref.shape[0]
    holder, layer, row = (info_ref[:, j : j + 1].astype(jnp.int32) for j in range(3))
    below = [below_ref[step] for step in range(STEPS)]
    lane = lane_of(HALO)
    low = lane < LANES // 2
    bufs = (va_ref, vb_ref)

    def tile(j):
        return pl.ds(j if isinstance(j, int) else pl.multiple_of(j, HALO), HALO)

    for side, (above, live) in enumerate(sides_of(gy, y)):
        def place(when_top, otherwise):
            if above is True or above is False:
                return when_top * HALO if above else otherwise * HALO
            return jnp.where(above, when_top * HALO, otherwise * HALO)

        outer, strip, edge, inner = place(0, 3), place(1, 2), place(2, 1), place(3, 0)
        edge_rows = tile(edge_at(above, rows))
        inner_rows = tile(inner_at(above, rows))

        def field(f, i, here):
            j = f * (layers + 1)
            if i == top:
                return own_ref[j + layers, here, :] + partner_ref[j + layers, here, :]
            return own_ref[j + i, here, :] if i < layers else partner_ref[j + i - layers, here, :]

        t_ref, d_ref, q_ref, e_ref, g_ref = coefs[1], coefs[0], coefs[3], coefs[4], coefs[5]
        keep = {0: s_ref, 1: t_ref, 2: va_ref, 3: d_ref, 4: q_ref, 5: e_ref, 6: g_ref}
        zeros = jnp.zeros((HALO, LANES), jnp.float32)
        src = lane % (LANES // 2)
        turned = (layers - 1 - src // GROUP) * GROUP + src % GROUP
        for f in range(FIELDS):
            for i in range(top + 1):
                if i < top:
                    ref, j = (along[side], i) if i < layers else (across[side], top - 1 - i)
                    at = (f * layers + j) * HALO
                    value = ref[at : at + HALO, :]
                else:
                    at = FIELDS * layers * HALO + (f // 2) * HALO
                    half = (LANES // 2) * (f % 2)
                    a = take(along[side][at : at + HALO, :], src + half)
                    b = take(across[side][at : at + HALO, :], turned + half)
                    value = jnp.where(low, a, b)
                ref, shift = keep[f], 0 if f in (0, 2) else HALO
                ref[i, tile(strip - shift), :] = value
                ref[i, tile(edge - shift), :] = field(f, i, edge_rows)
        for i in range(top + 1):
            s_ref[i, tile(outer), :] = zeros
            va_ref[i, tile(outer), :] = zeros
            vb_ref[i, tile(outer), :] = zeros
            s_ref[i, tile(inner), :] = field(0, i, inner_rows)
        n = 2 * HALO
        held = [[keep[f][i, pl.ds(0, n), :] for i in range(top + 1)] if f in (1, 3, 4, 5, 6) else None for f in range(FIELDS)]
        coefficients(s_ref, HALO, n, lambda f, i: held[f][i], coefs, 0)

        def sweep_all(number, which, needed_layers):
            src_ref, dst_ref = bufs[which], bufs[1 - which]
            for i in range(top + 1):
                src_ref[i, tile(inner), :] = level_ref[(side * STEPS * ITERS + number) * (top + 1) + i]
            sweep(src_ref, dst_ref, HALO, n, needed_layers, coefs, 0)

        first = edge_at(above, rows)
        hit = jnp.logical_and(jnp.logical_and(holder == x, row // HALO == first // HALO), live)
        cell = jnp.where(hit, layer * HALO + row - first, -1)
        picks = as_onehot(lax.broadcasted_iota(jnp.int32, (count, LANES), 1) == cell)

        def after(step):
            heat = []
            for i in range(layers):
                heat.append(va_ref[i, tile(edge), :] / s_ref[i, tile(edge), :])
                if step == STEPS - 1:
                    heat_ref[side * layers + flip(z, layers, i)] = heat[-1]
            heat.append(jnp.zeros((LANES - layers * HALO, LANES), jnp.float32))
            below[step] = below[step] + exact_dot(picks, jnp.concatenate(heat, axis=0))

        two_steps(layers, sweep_all, lambda: next_rhs(coefs, va_ref, HALO, n, 0), after)

    coef, warmth = segments_ref[:count, :], segments_ref[count:, :]
    for step in range(STEPS):
        warmth = warmth + coolant_gain * coef * (below[step] - warmth)
    ret_ref[...] = jnp.where(holder == x, warmth, 0.0)
    for k, ref in enumerate(returns):
        owner = lax.rem(x + k, gx)
        ref[...] = ret_ref[pl.ds(pl.multiple_of(owner * seg, seg), seg), :]


def merge_kernel(gy, whole_ref, heat_ref, out_ref):
    layers, rows, _ = whole_ref.shape
    out_ref[...] = whole_ref[...]
    for side, (above, live) in enumerate(sides_of(gy, lax.axis_index("gy"))):
        def put(side=side, above=above):
            out_ref[:, pl.ds(edge_at(above, rows), HALO), :] = heat_ref[side * layers : (side + 1) * layers]

        if live is True:
            put()
        else:
            pl.when(live)(put)


def local(gx, gy, gz, u, power, storage, conductance, warmth, coef, holder, stratum, transverse):
    layers, rows, columns = u.shape
    seg = warmth.shape[1]
    segments = stratum.shape[1]
    if gz != 2 or gx < 3 or columns != LANES or 2 * layers * GROUP != LANES or rows % 32:
        raise ValueError("unsupported shape")
    holder = holder[:, :, 0]
    shape = (layers, rows)
    f32 = jnp.float32
    chunk = rows // 4
    wide = RAW * chunk + 2 * seg

    def struct(*dims):
        return jax.ShapeDtypeStruct(dims, f32)

    def vmem(*dims):
        return pltpu.VMEM(dims, f32)

    own, to_left, to_right, only = pl.pallas_call(
        pack_kernel,
        out_shape=(
            struct(RAW * layers * rows + 2 * seg, LANES),
            struct(wide, LANES),
            struct(wide, LANES),
            struct(2 * seg, LANES),
        ),
        in_specs=[VMEM] * 6,
        out_specs=(VMEM,) * 4,
        compiler_params=PARAMS,
        name="pack",
    )(u, power, storage, jnp.sqrt(conductance), warmth, coef)

    swap = [(0, 1), (1, 0)]
    partner = lax.ppermute(own, "gz", swap)
    received = []
    for k in range(1, gx):
        payload = to_left if k == 1 else to_right if k == gx - 1 else only
        received.append(lax.ppermute(payload, "gx", [(i, (i - k) % gx) for i in range(gx)]))
    late = lax.ppermute(jnp.concatenate(received, axis=0), "gz", swap)

    sides = 1 if gy == 2 else 2
    fields = struct(FIELDS * (layers + 1), rows, LANES)
    strip_rows = FIELDS * layers * HALO + 4 * HALO
    filled = pl.pallas_call(
        functools.partial(fill_kernel, False, gx, gy, shape, seg),
        out_shape=(fields,) + (struct(strip_rows, LANES),) * sides + (struct(segments, 8), struct(2 * segments, LANES)),
        in_specs=[VMEM] * (4 + gx - 1),
        out_specs=(VMEM,) * (3 + sides),
        compiler_params=PARAMS,
        cost_estimate=cost(1.5),
        name="fill_own",
    )(own, holder, stratum, transverse, *received)
    own_fields, strips, (info, held) = filled[0], filled[1 : 1 + sides], filled[1 + sides :]
    if gy == 2:
        routes = [(strips[0], swap)]
    else:
        up = [(i, i + 1) for i in range(gy - 1)]
        routes = [(strips[1], up), (strips[0], [(j, i) for i, j in up])]
    along = [lax.ppermute(value, "gy", pairs) for value, pairs in routes]
    across = []
    for value, pairs in routes:
        both = [(2 * i + z, 2 * j + 1 - z) for i, j in pairs for z in range(2)]
        across.append(lax.ppermute(value, ("gy", "gz"), both))

    partner_fields = pl.pallas_call(
        functools.partial(fill_kernel, True, gx, gy, shape, seg),
        out_shape=fields,
        in_specs=[VMEM] * 5,
        out_specs=VMEM,
        scratch_shapes=[vmem(segments, LANES)] * 2,
        compiler_params=PARAMS,
        cost_estimate=cost(1.5),
        name="fill_partner",
    )(partner, holder, stratum, transverse, late)

    top = 2 * layers
    padded = vmem(top + 1, rows + 2 * PAD, LANES)
    inside, below, levels = pl.pallas_call(
        functools.partial(tile_kernel, gx, gy, shape),
        out_shape=(
            struct(layers, rows, LANES),
            struct(STEPS, segments, LANES),
            struct(sides * STEPS * ITERS * (top + 1), HALO, LANES),
        ),
        in_specs=[VMEM] * 3,
        out_specs=(VMEM,) * 3,
        scratch_shapes=[padded] * 3 + [vmem(top + 1, rows, LANES)] * 6,
        compiler_params=PARAMS,
        cost_estimate=cost(7),
        name="tile_sweeps",
    )(own_fields, partner_fields, info)

    results = pl.pallas_call(
        functools.partial(edge_kernel, gx, gy, shape, seg),
        out_shape=(struct(sides * layers, HALO, LANES),) + (struct(seg, LANES),) * gx,
        in_specs=[VMEM] * (6 + 2 * sides),
        out_specs=(VMEM,) * (1 + gx),
        scratch_shapes=[vmem(segments, LANES)]
        + [vmem(top + 1, 4 * HALO, LANES)] * 3
        + [vmem(top + 1, 2 * HALO, LANES)] * 6,
        compiler_params=PARAMS,
        cost_estimate=cost(1.5),
        name="edge_sweeps",
    )(own_fields, partner_fields, info, held, below, levels, *along, *across)
    heat, total = results[0], results[1]
    returned = [lax.ppermute(results[1 + k], "gx", [(i, (i + k) % gx) for i in range(gx)]) for k in range(1, gx)]
    temperature = pl.pallas_call(
        functools.partial(merge_kernel, gy),
        out_shape=struct(layers, rows, LANES),
        in_specs=[VMEM] * 2,
        out_specs=VMEM,
        compiler_params=PARAMS,
        cost_estimate=cost(1),
        name="merge",
    )(inside, heat)
    for value in returned:
        total = total + value
    return temperature, total[None]


def solution(mesh):
    gx, gy, gz = (mesh.shape[a] for a in ("gx", "gy", "gz"))
    cells = P(("stack", "gz"), "gy", "gx")
    segments = P(("stack", "gy", "gz"), "gx", None)
    return jax.shard_map(
        functools.partial(local, gx, gy, gz),
        mesh=mesh,
        in_specs=(cells, cells, cells, P(None, ("stack", "gz"), "gy", "gx"), segments, segments, P(), P(), P()),
        out_specs=(cells, segments),
        check_vma=False,
    )
```

```python
import functools

import jax
import jax.numpy as jnp
from jax import lax
from jax.experimental import pallas as pl
from jax.experimental.pallas import tpu as pltpu
from jax.sharding import PartitionSpec as P

STEPS = 2
ITERS = 4
HALO = STEPS * ITERS
GROUP = 2 * HALO
LANES = 128
RAW = 5
FIELDS = 7
coolant_gain = 0.5

VMEM = pl.BlockSpec(memory_space=pltpu.VMEM)
PARAMS = pltpu.CompilerParams(vmem_limit_bytes=40 * 1024 * 1024)


def cost(microseconds):
    return pl.CostEstimate(flops=0, bytes_accessed=int(microseconds * 3e6), transcendentals=0)


def lane_of(rows):
    return lax.broadcasted_iota(jnp.int32, (rows, LANES), 1)


def take(value, index):
    return jnp.take_along_axis(value, index, axis=1, mode="promise_in_bounds")


def near_edges(rows):
    k = lane_of(rows) % GROUP
    return jnp.where(k < HALO, HALO - 1 - k, LANES + HALO - 1 - k)


def far_edges(rows):
    k = lane_of(rows) % GROUP
    return jnp.where(k < HALO, LANES - 1 - k, GROUP - 1 - k)


def split(value):
    high = value.astype(jnp.bfloat16)
    low = (value - high.astype(jnp.float32)).astype(jnp.bfloat16)
    return high, low


def exact_dot(onehot, value):
    high, low = split(value)
    both = jnp.concatenate([high, low], axis=0)
    return jnp.dot(jnp.concatenate([onehot, onehot], axis=1), both, preferred_element_type=jnp.float32)


def coupling(coef, warmth):
    flow = coef * warmth
    second = coolant_gain * coef * coef
    return jnp.concatenate([coef, flow, second, flow - second * warmth], axis=1)


def flip(z, layers, i):
    return jnp.where(z == 0, i, layers - 1 - i)


def pack_kernel(u_ref, p_ref, c_ref, k_ref, f_ref, x_ref, *refs):
    own_ref, left_ref, right_ref, seg_ref = refs[3:7]
    sems = refs[-1]
    layers, rows, _ = u_ref.shape
    seg = f_ref.shape[1]
    z = lax.axis_index("gz")
    plane = layers * rows
    copies = []

    def fetch(src, at, n):
        copies.append(pltpu.make_async_copy(src, own_ref.at[pl.ds(at, n), :], sems.at[len(copies)]))
        copies[-1].start()

    for field, ref in enumerate((k_ref.at[0], k_ref.at[1], u_ref, p_ref, c_ref)):
        for i in range(layers):
            fetch(ref.at[flip(z, layers, i)], field * plane + i * rows, rows)
    fetch(x_ref.at[0], RAW * plane, seg)
    fetch(f_ref.at[0], RAW * plane + seg, seg)
    for table, place in zip(refs[:3], refs[7:10]):
        copies.append(pltpu.make_async_copy(table, place, sems.at[len(copies)]))
        copies[-1].start()
    for field in range(2):
        for i in range(layers):
            copies[field * layers + i].wait()
            here = pl.ds(field * plane + i * rows, rows)
            own_ref[here, :] = jnp.sqrt(own_ref[here, :])
    for copy in copies[2 * layers :]:
        copy.wait()
    chunk = rows // 4
    lane = lane_of(chunk)
    first = lane % GROUP < HALO
    near, far = near_edges(chunk), far_edges(chunk)
    for part in range(RAW):
        even = jnp.zeros((chunk, LANES), jnp.float32)
        odd = even
        for h in range(2):
            for i in range(layers):
                here = lane // GROUP == h * layers + i
                for side in range(2):
                    g = 2 * h + side
                    if part < 4:
                        at = g * plane + i * rows + part * chunk
                    else:
                        at = 4 * plane + i * rows + g * chunk
                    block = own_ref[at : at + chunk, :]
                    if side == 0:
                        even = jnp.where(here, take(block, near), even)
                    else:
                        odd = jnp.where(here, take(block, far), odd)
        left_ref[part * chunk : (part + 1) * chunk, :] = jnp.where(first, even, odd)
        right_ref[part * chunk : (part + 1) * chunk, :] = jnp.where(first, odd, even)
    segments = own_ref[RAW * plane : RAW * plane + 2 * seg, :]
    left_ref[RAW * chunk :, :] = segments
    right_ref[RAW * chunk :, :] = segments
    seg_ref[...] = segments


class Strips:
    def __init__(self, ref, right_at, left_at, rows, layers):
        self.ref, self.right_at, self.left_at = ref, right_at, left_at
        self.rows, self.layers = rows, layers

    def merged(self, field, start, n, x, gx):
        chunk = self.rows // 4
        if field < 4:
            g, at = field, start
        else:
            g, at = start // chunk, 4 * chunk + start % chunk
        ref_r, ref_l = self.ref
        a = ref_r[self.right_at + at : self.right_at + at + n, :]
        b = ref_l[self.left_at + at : self.left_at + at + n, :]
        a = jnp.where(x < gx - 1, a, 0.0)
        b = jnp.where(x > 0, b, 0.0)
        first = lane_of(n) % GROUP < HALO
        return g, (jnp.where(first, a, b) if g % 2 == 0 else jnp.where(first, b, a))

    def halo(self, field, start, n, x, gx, partner):
        g, both = self.merged(field, start, n, x, gx)
        lane = lane_of(n)
        half = self.layers * GROUP
        src = lane % half
        if partner:
            src = (self.layers - 1 - src // GROUP) * GROUP + src % GROUP
        if g % 2 == 1:
            src = jnp.where(src % GROUP < HALO, src + HALO, src - HALO)
        return take(both, src + half * (g // 2))


def place_segments(x, gx, seg, coef_ref, warmth_ref, first, rest):
    coef, warmth = first
    coef_ref[pl.ds(pl.multiple_of(x * seg, seg), seg), :] = coef
    warmth_ref[pl.ds(pl.multiple_of(x * seg, seg), seg), :] = warmth
    for k, (ref, at) in enumerate(rest, 1):
        holder = lax.rem(x + k, gx)
        place = pl.ds(pl.multiple_of(holder * seg, seg), seg)
        coef_ref[place, :] = ref[at : at + seg, :]
        warmth_ref[place, :] = ref[at + seg : at + 2 * seg, :]


def tables(z, group, layers, holder_ref, stratum_ref, transverse_ref):
    holder = holder_ref[pl.ds(group, 1), :]
    layer = stratum_ref[pl.ds(group, 1), :]
    layer = jnp.where(z == 0, layer, layers - 1 - layer)
    row = transverse_ref[pl.ds(group, 1), :]
    n = holder.shape[1]
    which = lax.broadcasted_iota(jnp.int32, (8, n), 0)
    stacked = jnp.where(which == 0, holder, jnp.where(which == 1, layer, row))
    eye = lax.broadcasted_iota(jnp.int32, (n, n), 0) == lax.broadcasted_iota(jnp.int32, (n, n), 1)
    columns = lax.dot_general(
        eye.astype(jnp.float32).astype(jnp.bfloat16),
        stacked.astype(jnp.float32).astype(jnp.bfloat16),
        (((1,), (1,)), ((), ())),
        preferred_element_type=jnp.float32,
    )
    return (holder, layer, row), columns


def as_onehot(mask):
    return jnp.where(mask, 1.0, 0.0).astype(jnp.bfloat16)


def halo_segments(coef, warmth, columns, base, x):
    n = coef.shape[0]
    lane = lane_of(n)
    holder, layer = columns[:, 0:1].astype(jnp.int32), columns[:, 1:2].astype(jnp.int32)
    side = jnp.where(lane % GROUP < HALO, x + 1, x - 1)
    mine = jnp.logical_and(lane // GROUP == layer + base, holder == side)
    near = near_edges(n)
    return coupling(jnp.where(mine, take(coef, near), 0.0), take(warmth, near))


def combine(raw, added):
    s, t, u, power, storage = raw
    wall, flow, second, later = (added[:, i * LANES : (i + 1) * LANES] for i in range(4))
    return s, t, s * u, storage + wall, power + storage * u + flow, power + later, storage + second


def starts_of(gx, chunk, seg):
    lengths = [RAW * chunk + 2 * seg if k in (1, gx - 1) else 2 * seg for k in range(1, gx)]
    return [sum(lengths[:k]) for k in range(gx)]


def edge_at(top, rows):
    return 0 if top is True else rows - HALO if top is False else pl.multiple_of(jnp.where(top, 0, rows - HALO), HALO)


def inner_at(top, rows):
    return HALO if top is True else rows - 2 * HALO if top is False else pl.multiple_of(jnp.where(top, HALO, rows - 2 * HALO), HALO)


def sides_of(gy, y):
    return [(y == 1, True)] if gy == 2 else [(True, y > 0), (False, y < gy - 1)]


def fill_kernel(partner, gx, gy, shape, seg, *refs):
    layers, rows = shape
    cells_ref, holder_ref, stratum_ref, transverse_ref = refs[:4]
    plane, chunk = layers * rows, rows // 4
    starts = starts_of(gx, chunk, seg)
    if partner:
        received = [refs[4]] * (gx - 1)
        refs = refs[5:]
    else:
        received = refs[4 : 4 + gx - 1]
        refs = refs[4 + gx - 1 :]
        starts = [0] * gx
    sides = 1 if gy == 2 else 2
    out_ref = refs[0]
    if partner:
        coef_ref, warmth_ref = refs[1:3]
    else:
        strip_refs, info_ref, segments_ref = refs[1 : 1 + sides], refs[1 + sides], refs[2 + sides]
        n = segments_ref.shape[0] // 2
        coef_ref, warmth_ref = segments_ref.at[pl.ds(0, n), :], segments_ref.at[pl.ds(n, n), :]
    x, y, z = (lax.axis_index(a) for a in ("gx", "gy", "gz"))
    base = layers if partner else 0
    rest = [(r, starts[k] + (RAW * chunk if k in (0, gx - 2) else 0)) for k, r in enumerate(received)]
    at = RAW * plane
    first = (cells_ref[at : at + seg, :], cells_ref[at + seg : at + 2 * seg, :])
    place_segments(x, gx, seg, coef_ref, warmth_ref, first, rest)
    group = y * 2 + ((1 - z) if partner else z)
    (holder, layer, row), columns = tables(z, group, layers, holder_ref, stratum_ref, transverse_ref)
    coef, warmth = coef_ref[...], warmth_ref[...]
    n = coef.shape[0]
    if not partner:
        info_ref[...] = columns

    cell = jnp.where(holder == x, layer * rows + row, -1)
    line = lax.broadcasted_iota(jnp.int32, (plane, n), 0)
    added = exact_dot(as_onehot(line == cell), coupling(coef, warmth))
    line = lax.broadcasted_iota(jnp.int32, (rows, n), 0)
    beside = exact_dot(as_onehot(line == row), halo_segments(coef, warmth, columns, base, x))
    for i in range(layers):
        src = layers - 1 - i if partner else i
        raw = [cells_ref[f * plane + src * rows : f * plane + (src + 1) * rows, :] for f in range(RAW)]
        for f, value in enumerate(combine(raw, added[i * rows : (i + 1) * rows])):
            out_ref[f * (layers + 1) + i] = value
    strips = Strips((received[0], received[-1]), starts[0], starts[gx - 2], rows, layers)
    half = lane_of(chunk) // (LANES // 2) == (1 if partner else 0)
    for part in range(4):
        here = slice(part * chunk, (part + 1) * chunk)
        raw = [jnp.where(half, strips.halo(f, part * chunk, chunk, x, gx, partner), 0.0) for f in range(RAW)]
        for f, value in enumerate(combine(raw, beside[here])):
            out_ref[f * (layers + 1) + layers, here, :] = value
    if partner:
        return
    low = lane_of(HALO) < LANES // 2
    for strip_ref, (top, _) in zip(strip_refs, sides_of(gy, y)):
        edge = pl.ds(edge_at(top, rows), HALO)
        for f in range(FIELDS):
            for i in range(layers):
                strip_ref[(f * layers + i) * HALO : (f * layers + i + 1) * HALO, :] = out_ref[f * (layers + 1) + i, edge, :]
        at = FIELDS * layers * HALO
        made = [out_ref[f * (layers + 1) + layers, edge, :] for f in range(FIELDS)]
        made.append(jnp.zeros_like(made[0]))
        for j in range(4):
            packed = jnp.where(low, made[2 * j], pltpu.roll(made[2 * j + 1], LANES // 2, 1))
            strip_ref[at + j * HALO : at + (j + 1) * HALO, :] = packed


def lateral(buf, at, n, count):
    lane = lane_of(n)
    k, group = lane % GROUP, lane // GROUP
    top = buf.shape[0] - 1
    centre = [buf[i, pl.ds(at, n), :] for i in range(min(count + 1, top))]
    halo = buf[top, pl.ds(at, n), :]
    border = jnp.zeros_like(halo)
    sums = []
    for i in range(count):
        border = jnp.where(group == i, pltpu.roll(centre[i], i * GROUP + HALO, 1), border)
        beside = pltpu.roll(halo, LANES - (i * GROUP + HALO), 1)
        east = jnp.where(lane == LANES - 1, beside, pltpu.roll(centre[i], LANES - 1, 1))
        west = jnp.where(lane == 0, beside, pltpu.roll(centre[i], 1, 1))
        sums.append(east + west + buf[i, pl.ds(at - 1, n), :] + buf[i, pl.ds(at + 1, n), :])
    one = jnp.where(k == HALO, border, pltpu.roll(halo, 1, 1))
    other = jnp.where(k == HALO - 1, border, pltpu.roll(halo, LANES - 1, 1))
    sums.append(one + other + buf[top, pl.ds(at - 1, n), :] + buf[top, pl.ds(at + 1, n), :])
    return centre + [halo], sums


def vertical(values, count):
    planes, halo = values[:-1], values[-1]
    sums = []
    for i in range(count):
        near = [planes[j] for j in (i - 1, i + 1) if 0 <= j < len(planes)]
        sums.append(functools.reduce(jnp.add, near))
    lane = lane_of(halo.shape[0])
    up = jnp.where(lane >= GROUP, pltpu.roll(halo, GROUP, 1), 0.0)
    down = jnp.where(lane < LANES - GROUP, pltpu.roll(halo, LANES - GROUP, 1), 0.0)
    sums.append(up + down)
    return sums


def coefficients(s_ref, at, n, raw, dests, to):
    a_ref, b_ref, q_ref, r_ref, e_ref, g_ref = dests
    top = s_ref.shape[0] - 1
    centre, sums = lateral(s_ref, at, n, top)
    t = [raw(1, i) for i in range(top + 1)]
    above = vertical(t, top)
    here = pl.ds(to, n)
    for i in range(top + 1):
        s = centre[i]
        diag = raw(3, i) + s * sums[i] + t[i] * above[i]
        inverse = 1.0 / jnp.where(diag > 0.0, diag, 1.0)
        scaled = s * inverse
        a_ref[i, here, :] = s * scaled
        b_ref[i, here, :] = t[i] * scaled
        r_ref[i, here, :] = raw(4, i) * scaled
        e_ref[i, here, :] = raw(5, i) * scaled
        g_ref[i, here, :] = raw(6, i) * inverse
        q_ref[i, here, :] = t[i] * jnp.where(s > 0.0, 1.0 / jnp.where(s > 0.0, s, 1.0), 0.0)


def sweep(src_ref, dst_ref, at, n, count, coefs, base):
    a_ref, b_ref, q_ref, r_ref = coefs[:4]
    top = src_ref.shape[0] - 1
    here = pl.ds(base, n)
    centre, sums = lateral(src_ref, at, n, count)
    layers = list(range(len(centre) - 1)) + [top]
    above = vertical([q_ref[i, here, :] * c for i, c in zip(layers, centre)], count)
    for j, i in enumerate(list(range(count)) + [top]):
        value = r_ref[i, here, :] + a_ref[i, here, :] * sums[j] + b_ref[i, here, :] * above[j]
        dst_ref[i, pl.ds(at, n), :] = value


def next_rhs(coefs, v_ref, at, n, base):
    r_ref, e_ref, g_ref = coefs[3:]
    here = pl.ds(base, n)
    for i in range(v_ref.shape[0]):
        r_ref[i, here, :] = e_ref[i, here, :] + g_ref[i, here, :] * v_ref[i, pl.ds(at, n), :]


def needed(layers, n):
    return min(2 * layers, layers + STEPS * ITERS - 1 - n)


def two_steps(layers, sweep_all, between, after):
    for step in range(STEPS):
        whole = [n for n in range(step * ITERS, (step + 1) * ITERS) if needed(layers, n) == 2 * layers]
        pairs = len(whole) // 2

        def pair(k, carry):
            n = step * ITERS + 2 * k
            sweep_all(n, 0, 2 * layers)
            sweep_all(n + 1, 1, 2 * layers)
            return carry

        if pairs:
            lax.fori_loop(0, pairs, pair, 0)
        for n in range(step * ITERS + 2 * pairs, (step + 1) * ITERS):
            sweep_all(n, n % 2, needed(layers, n))
        after(step)
        if step < STEPS - 1:
            between()


PAD = 8


def tile_kernel(gx, gy, shape, *refs):
    layers, rows = shape
    own_ref, partner_ref, info_ref, out_ref, below_ref, level_ref = refs[:6]
    s_ref, va_ref, vb_ref = refs[6:9]
    coefs = refs[9:]
    x, y, z = (lax.axis_index(a) for a in ("gx", "gy", "gz"))
    top = 2 * layers
    zeros = jnp.zeros((PAD, LANES), jnp.float32)
    for ref in (s_ref, va_ref, vb_ref):
        for i in range(top + 1):
            ref[i, 0:PAD, :] = zeros
            ref[i, PAD + rows : PAD + rows + PAD, :] = zeros

    def field(f, i, here):
        j = f * (layers + 1)
        if i == top:
            return own_ref[j + layers, here, :] + partner_ref[j + layers, here, :]
        return own_ref[j + i, here, :] if i < layers else partner_ref[j + i - layers, here, :]

    for i in range(top + 1):
        s_ref[i, PAD : PAD + rows, :] = field(0, i, slice(None))
        va_ref[i, PAD : PAD + rows, :] = field(2, i, slice(None))
    n = 16
    for at in range(0, rows, n):
        coefficients(s_ref, PAD + at, n, lambda f, i: field(f, i, slice(at, at + n)), coefs, at)

    bufs = (va_ref, vb_ref)
    sides = sides_of(gy, y)

    def sweep_all(number, which, count):
        src_ref, dst_ref = bufs[which], bufs[1 - which]
        for side, (above, _) in enumerate(sides):
            inner = pl.ds(PAD + inner_at(above, rows), HALO)
            for i in range(top + 1):
                level_ref[(side * STEPS * ITERS + number) * (top + 1) + i] = src_ref[i, inner, :]
        for at in range(0, rows, n):
            sweep(src_ref, dst_ref, PAD + at, n, count, coefs, at)

    holder, layer, row = (info_ref[:, j : j + 1].astype(jnp.int32) for j in range(3))
    spoilt = None
    for above, live in sides:
        part = jnp.logical_and(row // HALO == edge_at(above, rows) // HALO, live)
        spoilt = part if spoilt is None else jnp.logical_or(spoilt, part)
    cell = jnp.where(jnp.logical_and(holder == x, jnp.logical_not(spoilt)), layer * rows + row, -1)
    picks = as_onehot(lax.broadcasted_iota(jnp.int32, (cell.shape[0], layers * rows), 1) == cell)

    def after(step):
        heat = []
        for i in range(layers):
            here = pl.ds(PAD, rows)
            heat.append(va_ref[i, here, :] / s_ref[i, here, :])
            if step == STEPS - 1:
                out_ref[flip(z, layers, i)] = heat[-1]
        below_ref[step] = exact_dot(picks, jnp.concatenate(heat, axis=0))

    def between():
        for at in range(0, rows, n):
            next_rhs(coefs, va_ref, PAD + at, n, at)

    two_steps(layers, sweep_all, between, after)


def edge_kernel(gx, gy, shape, seg, *refs):
    layers, rows = shape
    own_ref, partner_ref, info_ref, segments_ref, below_ref, level_ref = refs[:6]
    sides_n = 1 if gy == 2 else 2
    along, across = refs[6 : 6 + sides_n], refs[6 + sides_n : 6 + 2 * sides_n]
    refs = refs[6 + 2 * sides_n :]
    heat_ref, returns = refs[0], refs[1 : 1 + gx]
    ret_ref, s_ref, va_ref, vb_ref = refs[1 + gx : 5 + gx]
    coefs = refs[5 + gx :]
    x, y, z = (lax.axis_index(a) for a in ("gx", "gy", "gz"))
    top = 2 * layers
    count = info_ref.shape[0]
    holder, layer, row = (info_ref[:, j : j + 1].astype(jnp.int32) for j in range(3))
    below = [below_ref[step] for step in range(STEPS)]
    lane = lane_of(HALO)
    low = lane < LANES // 2
    bufs = (va_ref, vb_ref)

    def tile(j):
        return pl.ds(j if isinstance(j, int) else pl.multiple_of(j, HALO), HALO)

    for side, (above, live) in enumerate(sides_of(gy, y)):
        def place(when_top, otherwise):
            if above is True or above is False:
                return when_top * HALO if above else otherwise * HALO
            return jnp.where(above, when_top * HALO, otherwise * HALO)

        outer, strip, edge, inner = place(0, 3), place(1, 2), place(2, 1), place(3, 0)
        edge_rows = tile(edge_at(above, rows))
        inner_rows = tile(inner_at(above, rows))

        def field(f, i, here):
            j = f * (layers + 1)
            if i == top:
                return own_ref[j + layers, here, :] + partner_ref[j + layers, here, :]
            return own_ref[j + i, here, :] if i < layers else partner_ref[j + i - layers, here, :]

        t_ref, d_ref, q_ref, e_ref, g_ref = coefs[1], coefs[0], coefs[3], coefs[4], coefs[5]
        keep = {0: s_ref, 1: t_ref, 2: va_ref, 3: d_ref, 4: q_ref, 5: e_ref, 6: g_ref}
        zeros = jnp.zeros((HALO, LANES), jnp.float32)
        src = lane % (LANES // 2)
        turned = (layers - 1 - src // GROUP) * GROUP + src % GROUP
        for f in range(FIELDS):
            for i in range(top + 1):
                if i < top:
                    ref, j = (along[side], i) if i < layers else (across[side], top - 1 - i)
                    at = (f * layers + j) * HALO
                    value = ref[at : at + HALO, :]
                else:
                    at = FIELDS * layers * HALO + (f // 2) * HALO
                    half = (LANES // 2) * (f % 2)
                    a = take(along[side][at : at + HALO, :], src + half)
                    b = take(across[side][at : at + HALO, :], turned + half)
                    value = jnp.where(low, a, b)
                ref, shift = keep[f], 0 if f in (0, 2) else HALO
                ref[i, tile(strip - shift), :] = value
                ref[i, tile(edge - shift), :] = field(f, i, edge_rows)
        for i in range(top + 1):
            s_ref[i, tile(outer), :] = zeros
            va_ref[i, tile(outer), :] = zeros
            vb_ref[i, tile(outer), :] = zeros
            s_ref[i, tile(inner), :] = field(0, i, inner_rows)
        n = 2 * HALO
        held = [[keep[f][i, pl.ds(0, n), :] for i in range(top + 1)] if f in (1, 3, 4, 5, 6) else None for f in range(FIELDS)]
        coefficients(s_ref, HALO, n, lambda f, i: held[f][i], coefs, 0)

        def sweep_all(number, which, needed_layers):
            src_ref, dst_ref = bufs[which], bufs[1 - which]
            for i in range(top + 1):
                src_ref[i, tile(inner), :] = level_ref[(side * STEPS * ITERS + number) * (top + 1) + i]
            sweep(src_ref, dst_ref, HALO, n, needed_layers, coefs, 0)

        first = edge_at(above, rows)
        hit = jnp.logical_and(jnp.logical_and(holder == x, row // HALO == first // HALO), live)
        cell = jnp.where(hit, layer * HALO + row - first, -1)
        picks = as_onehot(lax.broadcasted_iota(jnp.int32, (count, LANES), 1) == cell)

        def after(step):
            heat = []
            for i in range(layers):
                heat.append(va_ref[i, tile(edge), :] / s_ref[i, tile(edge), :])
                if step == STEPS - 1:
                    heat_ref[side * layers + flip(z, layers, i)] = heat[-1]
            heat.append(jnp.zeros((LANES - layers * HALO, LANES), jnp.float32))
            below[step] = below[step] + exact_dot(picks, jnp.concatenate(heat, axis=0))

        two_steps(layers, sweep_all, lambda: next_rhs(coefs, va_ref, HALO, n, 0), after)

    coef, warmth = segments_ref[:count, :], segments_ref[count:, :]
    for step in range(STEPS):
        warmth = warmth + coolant_gain * coef * (below[step] - warmth)
    ret_ref[...] = jnp.where(holder == x, warmth, 0.0)
    for k, ref in enumerate(returns):
        owner = lax.rem(x + k, gx)
        ref[...] = ret_ref[pl.ds(pl.multiple_of(owner * seg, seg), seg), :]


def merge_kernel(gy, whole_ref, heat_ref, out_ref):
    layers, rows, _ = whole_ref.shape
    out_ref[...] = whole_ref[...]
    for side, (above, live) in enumerate(sides_of(gy, lax.axis_index("gy"))):
        def put(side=side, above=above):
            out_ref[:, pl.ds(edge_at(above, rows), HALO), :] = heat_ref[side * layers : (side + 1) * layers]

        if live is True:
            put()
        else:
            pl.when(live)(put)


def local(gx, gy, gz, u, power, storage, conductance, warmth, coef, holder, stratum, transverse):
    layers, rows, columns = u.shape
    seg = warmth.shape[1]
    segments = stratum.shape[1]
    if gz != 2 or gx < 3 or columns != LANES or 2 * layers * GROUP != LANES or rows % 32:
        raise ValueError("unsupported shape")
    holder = holder[:, :, 0]
    shape = (layers, rows)
    f32 = jnp.float32
    chunk = rows // 4
    wide = RAW * chunk + 2 * seg

    def struct(*dims):
        return jax.ShapeDtypeStruct(dims, f32)

    def vmem(*dims):
        return pltpu.VMEM(dims, f32)

    indices = (holder, stratum, transverse)
    own, to_left, to_right, only, *indices = pl.pallas_call(
        pack_kernel,
        out_shape=(
            struct(RAW * layers * rows + 2 * seg, LANES),
            struct(wide, LANES),
            struct(wide, LANES),
            struct(2 * seg, LANES),
            *(jax.ShapeDtypeStruct(a.shape, a.dtype) for a in indices),
        ),
        in_specs=[pl.BlockSpec(memory_space=pltpu.HBM)] * 9,
        out_specs=(VMEM,) * 7,
        scratch_shapes=[pltpu.SemaphoreType.DMA((RAW * layers + 5,))],
        compiler_params=PARAMS,
        name="pack",
    )(*(pltpu.with_memory_space_constraint(a, pltpu.HBM) for a in (u, power, storage, conductance, warmth, coef, *indices)))

    swap = [(0, 1), (1, 0)]
    partner = lax.ppermute(own, "gz", swap)
    received = []
    for k in range(1, gx):
        payload = to_left if k == 1 else to_right if k == gx - 1 else only
        received.append(lax.ppermute(payload, "gx", [(i, (i - k) % gx) for i in range(gx)]))
    late = lax.ppermute(jnp.concatenate(received, axis=0), "gz", swap)

    sides = 1 if gy == 2 else 2
    fields = struct(FIELDS * (layers + 1), rows, LANES)
    strip_rows = FIELDS * layers * HALO + 4 * HALO
    filled = pl.pallas_call(
        functools.partial(fill_kernel, False, gx, gy, shape, seg),
        out_shape=(fields,) + (struct(strip_rows, LANES),) * sides + (struct(segments, 8), struct(2 * segments, LANES)),
        in_specs=[VMEM] * (4 + gx - 1),
        out_specs=(VMEM,) * (3 + sides),
        compiler_params=PARAMS,
        cost_estimate=cost(1.5),
        name="fill_own",
    )(own, *indices, *received)
    own_fields, strips, (info, held) = filled[0], filled[1 : 1 + sides], filled[1 + sides :]
    if gy == 2:
        routes = [(strips[0], swap)]
    else:
        up = [(i, i + 1) for i in range(gy - 1)]
        routes = [(strips[1], up), (strips[0], [(j, i) for i, j in up])]
    along = [lax.ppermute(value, "gy", pairs) for value, pairs in routes]
    across = []
    for value, pairs in routes:
        both = [(2 * i + z, 2 * j + 1 - z) for i, j in pairs for z in range(2)]
        across.append(lax.ppermute(value, ("gy", "gz"), both))

    partner_fields = pl.pallas_call(
        functools.partial(fill_kernel, True, gx, gy, shape, seg),
        out_shape=fields,
        in_specs=[VMEM] * 5,
        out_specs=VMEM,
        scratch_shapes=[vmem(segments, LANES)] * 2,
        compiler_params=PARAMS,
        cost_estimate=cost(1.5),
        name="fill_partner",
    )(partner, *indices, late)

    top = 2 * layers
    padded = vmem(top + 1, rows + 2 * PAD, LANES)
    inside, below, levels = pl.pallas_call(
        functools.partial(tile_kernel, gx, gy, shape),
        out_shape=(
            struct(layers, rows, LANES),
            struct(STEPS, segments, LANES),
            struct(sides * STEPS * ITERS * (top + 1), HALO, LANES),
        ),
        in_specs=[VMEM] * 3,
        out_specs=(VMEM,) * 3,
        scratch_shapes=[padded] * 3 + [vmem(top + 1, rows, LANES)] * 6,
        compiler_params=PARAMS,
        cost_estimate=cost(7),
        name="tile_sweeps",
    )(own_fields, partner_fields, info)

    results = pl.pallas_call(
        functools.partial(edge_kernel, gx, gy, shape, seg),
        out_shape=(struct(sides * layers, HALO, LANES),) + (struct(seg, LANES),) * gx,
        in_specs=[VMEM] * (6 + 2 * sides),
        out_specs=(VMEM,) * (1 + gx),
        scratch_shapes=[vmem(segments, LANES)]
        + [vmem(top + 1, 4 * HALO, LANES)] * 3
        + [vmem(top + 1, 2 * HALO, LANES)] * 6,
        compiler_params=PARAMS,
        cost_estimate=cost(1.5),
        name="edge_sweeps",
    )(own_fields, partner_fields, info, held, below, levels, *along, *across)
    heat, total = results[0], results[1]
    returned = [lax.ppermute(results[1 + k], "gx", [(i, (i + k) % gx) for i in range(gx)]) for k in range(1, gx)]
    temperature = pl.pallas_call(
        functools.partial(merge_kernel, gy),
        out_shape=struct(layers, rows, LANES),
        in_specs=[VMEM] * 2,
        out_specs=VMEM,
        compiler_params=PARAMS,
        cost_estimate=cost(1),
        name="merge",
    )(inside, heat)
    for value in returned:
        total = total + value
    return temperature, total[None]


def solution(mesh):
    gx, gy, gz = (mesh.shape[a] for a in ("gx", "gy", "gz"))
    cells = P(("stack", "gz"), "gy", "gx")
    segments = P(("stack", "gy", "gz"), "gx", None)
    return jax.shard_map(
        functools.partial(local, gx, gy, gz),
        mesh=mesh,
        in_specs=(cells, cells, cells, P(None, ("stack", "gz"), "gy", "gx"), segments, segments, P(), P(), P()),
        out_specs=(cells, segments),
        check_vma=False,
    )
```

```python
import functools

import jax
import jax.numpy as jnp
from jax import lax
from jax.experimental import pallas as pl
from jax.experimental.pallas import tpu as pltpu
from jax.sharding import PartitionSpec as P

STEPS = 2
ITERS = 4
HALO = STEPS * ITERS
GROUP = 2 * HALO
LANES = 128
RAW = 5
FIELDS = 7
coolant_gain = 0.5

VMEM = pl.BlockSpec(memory_space=pltpu.VMEM)
PARAMS = pltpu.CompilerParams(vmem_limit_bytes=40 * 1024 * 1024)


def cost(microseconds):
    return pl.CostEstimate(flops=0, bytes_accessed=int(microseconds * 3e6), transcendentals=0)


def lane_of(rows):
    return lax.broadcasted_iota(jnp.int32, (rows, LANES), 1)


def take(value, index):
    return jnp.take_along_axis(value, index, axis=1, mode="promise_in_bounds")


def near_edges(rows):
    k = lane_of(rows) % GROUP
    return jnp.where(k < HALO, HALO - 1 - k, LANES + HALO - 1 - k)


def far_edges(rows):
    k = lane_of(rows) % GROUP
    return jnp.where(k < HALO, LANES - 1 - k, GROUP - 1 - k)


def split(value):
    high = value.astype(jnp.bfloat16)
    low = (value - high.astype(jnp.float32)).astype(jnp.bfloat16)
    return high, low


def exact_dot(onehot, value):
    high, low = split(value)
    both = jnp.concatenate([high, low], axis=0)
    return jnp.dot(jnp.concatenate([onehot, onehot], axis=1), both, preferred_element_type=jnp.float32)


def coupling(coef, warmth):
    flow = coef * warmth
    second = coolant_gain * coef * coef
    return jnp.concatenate([coef, flow, second, flow - second * warmth], axis=1)


def flip(z, layers, i):
    return jnp.where(z == 0, i, layers - 1 - i)


def pack_kernel(shape, u_ref, p_ref, c_ref, k_ref, f_ref, x_ref, *refs):
    own_ref, even_ref, odd_ref, seg_ref = refs[3:7]
    sems = refs[-1]
    layers, rows = shape
    seg = f_ref.shape[0]
    x, z = lax.axis_index("gx"), lax.axis_index("gz")
    plane = layers * rows
    copies = []

    def fetch(src, dst):
        copies.append(pltpu.make_async_copy(src, dst, sems.at[len(copies)]))
        copies[-1].start()

    fetch(k_ref, own_ref.at[pl.ds(0, 2 * plane), :])
    for field, ref in enumerate((u_ref, p_ref, c_ref), 2):
        fetch(ref, own_ref.at[pl.ds(field * plane, plane), :])
    for j, ref in enumerate((x_ref, f_ref)):
        fetch(ref, own_ref.at[pl.ds(RAW * plane + j * seg, seg), :])
    for table, place in zip(refs[:3], refs[7:10]):
        fetch(table, place)
    copies[0].wait()
    roots = pl.ds(0, 2 * plane)
    own_ref[roots, :] = jnp.sqrt(own_ref[roots, :])
    for copy in copies[1:]:
        copy.wait()
    chunk = rows // 4
    lane = lane_of(chunk)
    same = (lane % GROUP < HALO) == (x % 2 == 1)
    near, far = near_edges(chunk), far_edges(chunk)
    for part in range(RAW):
        even = jnp.zeros((chunk, LANES), jnp.float32)
        odd = even
        for h in range(2):
            for i in range(layers):
                here = lane // GROUP == h * layers + i
                src = flip(z, layers, i)
                for side in range(2):
                    g = 2 * h + side
                    field, at = (g, part * chunk) if part < 4 else (4, g * chunk)
                    block = own_ref[pl.ds(pl.multiple_of((field * layers + src) * rows + at, chunk), chunk), :]
                    if side == 0:
                        even = jnp.where(here, take(block, near), even)
                    else:
                        odd = jnp.where(here, take(block, far), odd)
        even_ref[part * chunk : (part + 1) * chunk, :] = jnp.where(same, even, odd)
        odd_ref[part * chunk : (part + 1) * chunk, :] = jnp.where(same, odd, even)
    segments = own_ref[RAW * plane : RAW * plane + 2 * seg, :]
    seg_ref[...] = segments
    even_ref[RAW * chunk :, :] = segments
    odd_ref[RAW * chunk :, :] = segments


class Strips:
    def __init__(self, refs, starts, rows, layers):
        self.refs, self.starts = refs, starts
        self.rows, self.layers = rows, layers

    def merged(self, field, start, n, x):
        chunk = self.rows // 4
        if field < 4:
            g, at = field, start
        else:
            g, at = start // chunk, 4 * chunk + start % chunk
        a, b = (ref[at + begin : at + begin + n, :] for ref, begin in zip(self.refs, self.starts))
        right_half = (lane_of(n) % GROUP < HALO) if g % 2 == 0 else (lane_of(n) % GROUP >= HALO)
        return g, jnp.where(right_half == (x % 2 == 0), a, b)

    def halo(self, field, start, n, x, partner):
        g, both = self.merged(field, start, n, x)
        lane = lane_of(n)
        half = self.layers * GROUP
        src = lane % half
        if partner:
            src = (self.layers - 1 - src // GROUP) * GROUP + src % GROUP
        if g % 2 == 1:
            src = jnp.where(src % GROUP < HALO, src + HALO, src - HALO)
        return take(both, src + half * (g // 2))


def place_segments(x, gx, seg, coef_ref, warmth_ref, own, even, odd, far):
    def put(holder, source):
        ref, at = source
        place = pl.ds(pl.multiple_of(holder * seg, seg), seg)
        coef_ref[place, :] = ref[at : at + seg, :]
        warmth_ref[place, :] = ref[at + seg : at + 2 * seg, :]

    for k, source in far:
        put(x ^ k, source)
    put(x, own)
    put(x ^ 1, even)
    beside = jnp.where(x % 2 == 0, x - 1, x + 1)
    pl.when(jnp.logical_and(beside >= 0, beside < gx))(lambda: put(beside, odd))


def tables(z, group, layers, holder_ref, stratum_ref, transverse_ref):
    holder = holder_ref[pl.ds(group, 1), :]
    layer = stratum_ref[pl.ds(group, 1), :]
    layer = jnp.where(z == 0, layer, layers - 1 - layer)
    row = transverse_ref[pl.ds(group, 1), :]
    n = holder.shape[1]
    which = lax.broadcasted_iota(jnp.int32, (8, n), 0)
    stacked = jnp.where(which == 0, holder, jnp.where(which == 1, layer, row))
    eye = lax.broadcasted_iota(jnp.int32, (n, n), 0) == lax.broadcasted_iota(jnp.int32, (n, n), 1)
    columns = lax.dot_general(
        eye.astype(jnp.float32).astype(jnp.bfloat16),
        stacked.astype(jnp.float32).astype(jnp.bfloat16),
        (((1,), (1,)), ((), ())),
        preferred_element_type=jnp.float32,
    )
    return (holder, layer, row), columns


def as_onehot(mask):
    return jnp.where(mask, 1.0, 0.0).astype(jnp.bfloat16)


def halo_segments(coef, warmth, columns, base, x):
    n = coef.shape[0]
    lane = lane_of(n)
    holder, layer = columns[:, 0:1].astype(jnp.int32), columns[:, 1:2].astype(jnp.int32)
    side = jnp.where(lane % GROUP < HALO, x + 1, x - 1)
    mine = jnp.logical_and(lane // GROUP == layer + base, holder == side)
    near = near_edges(n)
    return coupling(jnp.where(mine, take(coef, near), 0.0), take(warmth, near))


def combine(raw, added):
    s, t, u, power, storage = raw
    wall, flow, second, later = (added[:, i * LANES : (i + 1) * LANES] for i in range(4))
    return s, t, s * u, storage + wall, power + storage * u + flow, power + later, storage + second


def lengths_of(gx, chunk, seg):
    return [RAW * chunk + 2 * seg] * 2 + [2 * seg] * (gx - 2)


def edge_at(top, rows):
    return 0 if top is True else rows - HALO if top is False else pl.multiple_of(jnp.where(top, 0, rows - HALO), HALO)


def inner_at(top, rows):
    return HALO if top is True else rows - 2 * HALO if top is False else pl.multiple_of(jnp.where(top, HALO, rows - 2 * HALO), HALO)


def sides_of(gy, y):
    return [(y == 1, True)] if gy == 2 else [(True, y > 0), (False, y < gy - 1)]


def fill_kernel(partner, gx, gy, shape, seg, *refs):
    layers, rows = shape
    cells_ref, holder_ref, stratum_ref, transverse_ref = refs[:4]
    plane, chunk = layers * rows, rows // 4
    lengths = lengths_of(gx, chunk, seg)
    if partner:
        sources = [(refs[4], sum(lengths[:k])) for k in range(gx)]
        refs = refs[5:]
    else:
        sources = [(ref, 0) for ref in refs[4 : 4 + gx]]
        refs = refs[4 + gx :]
    sides = 1 if gy == 2 else 2
    out_ref = refs[0]
    if partner:
        coef_ref, warmth_ref = refs[1:3]
    else:
        strip_refs, info_ref, segments_ref = refs[1 : 1 + sides], refs[1 + sides], refs[2 + sides]
        n = segments_ref.shape[0] // 2
        coef_ref, warmth_ref = segments_ref.at[pl.ds(0, n), :], segments_ref.at[pl.ds(n, n), :]
    x, y, z = (lax.axis_index(a) for a in ("gx", "gy", "gz"))
    base = layers if partner else 0
    even, odd = ((ref, at + RAW * chunk) for ref, at in sources[:2])
    place_segments(x, gx, seg, coef_ref, warmth_ref, (cells_ref, RAW * plane), even, odd, list(enumerate(sources[2:gx], 2)))
    group = y * 2 + ((1 - z) if partner else z)
    (holder, layer, row), columns = tables(z, group, layers, holder_ref, stratum_ref, transverse_ref)
    coef, warmth = coef_ref[...], warmth_ref[...]
    n = coef.shape[0]
    if not partner:
        info_ref[...] = columns

    cell = jnp.where(holder == x, layer * rows + row, -1)
    line = lax.broadcasted_iota(jnp.int32, (plane, n), 0)
    added = exact_dot(as_onehot(line == cell), coupling(coef, warmth))
    line = lax.broadcasted_iota(jnp.int32, (rows, n), 0)
    beside = exact_dot(as_onehot(line == row), halo_segments(coef, warmth, columns, base, x))
    for i in range(layers):
        src = flip(z, layers, i)
        raw = [cells_ref[pl.ds(pl.multiple_of((f * layers + src) * rows, rows), rows), :] for f in range(RAW)]
        for f, value in enumerate(combine(raw, added[i * rows : (i + 1) * rows])):
            out_ref[f * (layers + 1) + i] = value
    strips = Strips([ref for ref, _ in sources[:2]], [at for _, at in sources[:2]], rows, layers)
    half = lane_of(chunk) // (LANES // 2) == (1 if partner else 0)
    for part in range(4):
        here = slice(part * chunk, (part + 1) * chunk)
        raw = [jnp.where(half, strips.halo(f, part * chunk, chunk, x, partner), 0.0) for f in range(RAW)]
        for f, value in enumerate(combine(raw, beside[here])):
            out_ref[f * (layers + 1) + layers, here, :] = value
    if partner:
        return
    low = lane_of(HALO) < LANES // 2
    for strip_ref, (top, _) in zip(strip_refs, sides_of(gy, y)):
        edge = pl.ds(edge_at(top, rows), HALO)
        for f in range(FIELDS):
            for i in range(layers):
                strip_ref[(f * layers + i) * HALO : (f * layers + i + 1) * HALO, :] = out_ref[f * (layers + 1) + i, edge, :]
        at = FIELDS * layers * HALO
        made = [out_ref[f * (layers + 1) + layers, edge, :] for f in range(FIELDS)]
        made.append(jnp.zeros_like(made[0]))
        for j in range(4):
            packed = jnp.where(low, made[2 * j], pltpu.roll(made[2 * j + 1], LANES // 2, 1))
            strip_ref[at + j * HALO : at + (j + 1) * HALO, :] = packed


def lateral(buf, at, n, count):
    lane = lane_of(n)
    k, group = lane % GROUP, lane // GROUP
    top = buf.shape[0] - 1
    centre = [buf[i, pl.ds(at, n), :] for i in range(min(count + 1, top))]
    halo = buf[top, pl.ds(at, n), :]
    border = jnp.zeros_like(halo)
    sums = []
    for i in range(count):
        border = jnp.where(group == i, pltpu.roll(centre[i], i * GROUP + HALO, 1), border)
        beside = pltpu.roll(halo, LANES - (i * GROUP + HALO), 1)
        east = jnp.where(lane == LANES - 1, beside, pltpu.roll(centre[i], LANES - 1, 1))
        west = jnp.where(lane == 0, beside, pltpu.roll(centre[i], 1, 1))
        sums.append(east + west + buf[i, pl.ds(at - 1, n), :] + buf[i, pl.ds(at + 1, n), :])
    one = jnp.where(k == HALO, border, pltpu.roll(halo, 1, 1))
    other = jnp.where(k == HALO - 1, border, pltpu.roll(halo, LANES - 1, 1))
    sums.append(one + other + buf[top, pl.ds(at - 1, n), :] + buf[top, pl.ds(at + 1, n), :])
    return centre + [halo], sums


def vertical(values, count):
    planes, halo = values[:-1], values[-1]
    sums = []
    for i in range(count):
        near = [planes[j] for j in (i - 1, i + 1) if 0 <= j < len(planes)]
        sums.append(functools.reduce(jnp.add, near))
    lane = lane_of(halo.shape[0])
    up = jnp.where(lane >= GROUP, pltpu.roll(halo, GROUP, 1), 0.0)
    down = jnp.where(lane < LANES - GROUP, pltpu.roll(halo, LANES - GROUP, 1), 0.0)
    sums.append(up + down)
    return sums


def coefficients(s_ref, at, n, raw, dests, to):
    a_ref, q_ref, r_ref, e_ref, g_ref = dests
    top = s_ref.shape[0] - 1
    centre, sums = lateral(s_ref, at, n, top)
    t = [raw(1, i) for i in range(top + 1)]
    above = vertical(t, top)
    here = pl.ds(to, n)
    for i in range(top + 1):
        s = centre[i]
        diag = raw(3, i) + s * sums[i] + t[i] * above[i]
        inverse = 1.0 / jnp.where(diag > 0.0, diag, 1.0)
        scaled = s * inverse
        a_ref[i, here, :] = s * scaled
        r_ref[i, here, :] = raw(4, i) * scaled
        e_ref[i, here, :] = raw(5, i) * scaled
        g_ref[i, here, :] = raw(6, i) * inverse
        q_ref[i, here, :] = t[i] * jnp.where(s > 0.0, 1.0 / jnp.where(s > 0.0, s, 1.0), 0.0)


def sweep(src_ref, dst_ref, at, n, count, coefs, base):
    a_ref, q_ref, r_ref = coefs[:3]
    top = src_ref.shape[0] - 1
    here = pl.ds(base, n)
    centre, sums = lateral(src_ref, at, n, count)
    layers = list(range(len(centre) - 1)) + [top]
    ratio = [q_ref[i, here, :] for i in layers]
    above = vertical([q * c for q, c in zip(ratio, centre)], count)
    ratio = ratio[:count] + ratio[-1:]
    for j, i in enumerate(list(range(count)) + [top]):
        value = r_ref[i, here, :] + a_ref[i, here, :] * (sums[j] + ratio[j] * above[j])
        dst_ref[i, pl.ds(at, n), :] = value


def next_rhs(coefs, v_ref, at, n, base):
    r_ref, e_ref, g_ref = coefs[2:]
    here = pl.ds(base, n)
    for i in range(v_ref.shape[0]):
        r_ref[i, here, :] = e_ref[i, here, :] + g_ref[i, here, :] * v_ref[i, pl.ds(at, n), :]


def needed(layers, n):
    return min(2 * layers, layers + STEPS * ITERS - 1 - n)


def two_steps(layers, sweep_all, between, after):
    for step in range(STEPS):
        whole = [n for n in range(step * ITERS, (step + 1) * ITERS) if needed(layers, n) == 2 * layers]
        pairs = len(whole) // 2

        def pair(k, carry):
            n = step * ITERS + 2 * k
            sweep_all(n, 0, 2 * layers)
            sweep_all(n + 1, 1, 2 * layers)
            return carry

        if pairs:
            lax.fori_loop(0, pairs, pair, 0)
        for n in range(step * ITERS + 2 * pairs, (step + 1) * ITERS):
            sweep_all(n, n % 2, needed(layers, n))
        after(step)
        if step < STEPS - 1:
            between()


PAD = 8


def tile_kernel(gx, gy, shape, *refs):
    layers, rows = shape
    own_ref, partner_ref, info_ref, out_ref, below_ref, level_ref = refs[:6]
    s_ref, va_ref, vb_ref = refs[6:9]
    coefs = refs[9:]
    x, y, z = (lax.axis_index(a) for a in ("gx", "gy", "gz"))
    top = 2 * layers
    zeros = jnp.zeros((PAD, LANES), jnp.float32)
    for ref in (s_ref, va_ref, vb_ref):
        for i in range(top + 1):
            ref[i, 0:PAD, :] = zeros
            ref[i, PAD + rows : PAD + rows + PAD, :] = zeros

    def field(f, i, here):
        j = f * (layers + 1)
        if i == top:
            return own_ref[j + layers, here, :] + partner_ref[j + layers, here, :]
        return own_ref[j + i, here, :] if i < layers else partner_ref[j + i - layers, here, :]

    for i in range(top + 1):
        s_ref[i, PAD : PAD + rows, :] = field(0, i, slice(None))
        va_ref[i, PAD : PAD + rows, :] = field(2, i, slice(None))
    n = 8
    for at in range(0, rows, n):
        coefficients(s_ref, PAD + at, n, lambda f, i: field(f, i, slice(at, at + n)), coefs, at)

    bufs = (va_ref, vb_ref)
    sides = sides_of(gy, y)

    def sweep_all(number, which, count):
        src_ref, dst_ref = bufs[which], bufs[1 - which]
        for side, (above, _) in enumerate(sides):
            inner = pl.ds(PAD + inner_at(above, rows), HALO)
            for i in range(top + 1):
                level_ref[(side * STEPS * ITERS + number) * (top + 1) + i] = src_ref[i, inner, :]
        for at in range(0, rows, n):
            sweep(src_ref, dst_ref, PAD + at, n, count, coefs, at)

    holder, layer, row = (info_ref[:, j : j + 1].astype(jnp.int32) for j in range(3))
    spoilt = None
    for above, live in sides:
        part = jnp.logical_and(row // HALO == edge_at(above, rows) // HALO, live)
        spoilt = part if spoilt is None else jnp.logical_or(spoilt, part)
    cell = jnp.where(jnp.logical_and(holder == x, jnp.logical_not(spoilt)), layer * rows + row, -1)
    picks = as_onehot(lax.broadcasted_iota(jnp.int32, (cell.shape[0], layers * rows), 1) == cell)

    def after(step):
        heat = []
        for i in range(layers):
            here = pl.ds(PAD, rows)
            heat.append(va_ref[i, here, :] / s_ref[i, here, :])
            if step == STEPS - 1:
                out_ref[flip(z, layers, i)] = heat[-1]
        below_ref[step] = exact_dot(picks, jnp.concatenate(heat, axis=0))

    def between():
        for at in range(0, rows, n):
            next_rhs(coefs, va_ref, PAD + at, n, at)

    two_steps(layers, sweep_all, between, after)


def edge_kernel(gx, gy, shape, seg, *refs):
    layers, rows = shape
    own_ref, partner_ref, info_ref, segments_ref, below_ref, level_ref = refs[:6]
    sides_n = 1 if gy == 2 else 2
    along, across = refs[6 : 6 + sides_n], refs[6 + sides_n : 6 + 2 * sides_n]
    refs = refs[6 + 2 * sides_n :]
    heat_ref, returns = refs[0], refs[1 : 1 + gx]
    ret_ref, s_ref, va_ref, vb_ref = refs[1 + gx : 5 + gx]
    coefs = refs[5 + gx :]
    x, y, z = (lax.axis_index(a) for a in ("gx", "gy", "gz"))
    top = 2 * layers
    count = info_ref.shape[0]
    holder, layer, row = (info_ref[:, j : j + 1].astype(jnp.int32) for j in range(3))
    below = [below_ref[step] for step in range(STEPS)]
    lane = lane_of(HALO)
    low = lane < LANES // 2
    bufs = (va_ref, vb_ref)

    def tile(j):
        return pl.ds(j if isinstance(j, int) else pl.multiple_of(j, HALO), HALO)

    for side, (above, live) in enumerate(sides_of(gy, y)):
        def place(when_top, otherwise):
            if above is True or above is False:
                return when_top * HALO if above else otherwise * HALO
            return jnp.where(above, when_top * HALO, otherwise * HALO)

        outer, strip, edge, inner = place(0, 3), place(1, 2), place(2, 1), place(3, 0)
        edge_rows = tile(edge_at(above, rows))
        inner_rows = tile(inner_at(above, rows))

        def field(f, i, here):
            j = f * (layers + 1)
            if i == top:
                return own_ref[j + layers, here, :] + partner_ref[j + layers, here, :]
            return own_ref[j + i, here, :] if i < layers else partner_ref[j + i - layers, here, :]

        t_ref, d_ref, q_ref, e_ref, g_ref = coefs[1], coefs[0], coefs[2], coefs[3], coefs[4]
        keep = {0: s_ref, 1: t_ref, 2: va_ref, 3: d_ref, 4: q_ref, 5: e_ref, 6: g_ref}
        zeros = jnp.zeros((HALO, LANES), jnp.float32)
        src = lane % (LANES // 2)
        turned = (layers - 1 - src // GROUP) * GROUP + src % GROUP
        for f in range(FIELDS):
            for i in range(top + 1):
                if i < top:
                    ref, j = (along[side], i) if i < layers else (across[side], top - 1 - i)
                    at = (f * layers + j) * HALO
                    value = ref[at : at + HALO, :]
                else:
                    at = FIELDS * layers * HALO + (f // 2) * HALO
                    half = (LANES // 2) * (f % 2)
                    a = take(along[side][at : at + HALO, :], src + half)
                    b = take(across[side][at : at + HALO, :], turned + half)
                    value = jnp.where(low, a, b)
                ref, shift = keep[f], 0 if f in (0, 2) else HALO
                ref[i, tile(strip - shift), :] = value
                ref[i, tile(edge - shift), :] = field(f, i, edge_rows)
        for i in range(top + 1):
            s_ref[i, tile(outer), :] = zeros
            va_ref[i, tile(outer), :] = zeros
            vb_ref[i, tile(outer), :] = zeros
            s_ref[i, tile(inner), :] = field(0, i, inner_rows)
        n = 2 * HALO
        held = [[keep[f][i, pl.ds(0, n), :] for i in range(top + 1)] if f in (1, 3, 4, 5, 6) else None for f in range(FIELDS)]
        coefficients(s_ref, HALO, n, lambda f, i: held[f][i], coefs, 0)

        def sweep_all(number, which, needed_layers):
            src_ref, dst_ref = bufs[which], bufs[1 - which]
            for i in range(top + 1):
                src_ref[i, tile(inner), :] = level_ref[(side * STEPS * ITERS + number) * (top + 1) + i]
            sweep(src_ref, dst_ref, HALO, n, needed_layers, coefs, 0)

        first = edge_at(above, rows)
        hit = jnp.logical_and(jnp.logical_and(holder == x, row // HALO == first // HALO), live)
        cell = jnp.where(hit, layer * HALO + row - first, -1)
        picks = as_onehot(lax.broadcasted_iota(jnp.int32, (count, LANES), 1) == cell)

        def after(step):
            heat = []
            for i in range(layers):
                heat.append(va_ref[i, tile(edge), :] / s_ref[i, tile(edge), :])
                if step == STEPS - 1:
                    heat_ref[side * layers + flip(z, layers, i)] = heat[-1]
            heat.append(jnp.zeros((LANES - layers * HALO, LANES), jnp.float32))
            below[step] = below[step] + exact_dot(picks, jnp.concatenate(heat, axis=0))

        two_steps(layers, sweep_all, lambda: next_rhs(coefs, va_ref, HALO, n, 0), after)

    coef, warmth = segments_ref[:count, :], segments_ref[count:, :]
    for step in range(STEPS):
        warmth = warmth + coolant_gain * coef * (below[step] - warmth)
    ret_ref[...] = jnp.where(holder == x, warmth, 0.0)
    for k, ref in enumerate(returns):
        ref[...] = ret_ref[pl.ds(pl.multiple_of((x ^ k) * seg, seg), seg), :]


def merge_kernel(gy, whole_ref, heat_ref, out_ref):
    layers, rows, _ = whole_ref.shape
    out_ref[...] = whole_ref[...]
    for side, (above, live) in enumerate(sides_of(gy, lax.axis_index("gy"))):
        def put(side=side, above=above):
            out_ref[:, pl.ds(edge_at(above, rows), HALO), :] = heat_ref[side * layers : (side + 1) * layers]

        if live is True:
            put()
        else:
            pl.when(live)(put)


def local(gx, gy, gz, u, power, storage, conductance, warmth, coef, holder, stratum, transverse):
    layers, rows, columns = u.shape
    seg = warmth.shape[1]
    segments = stratum.shape[1]
    if gz != 2 or gx < 4 or gx & (gx - 1) or columns != LANES or 2 * layers * GROUP != LANES or rows % 32:
        raise ValueError("unsupported shape")
    holder = holder[:, :, 0]
    shape = (layers, rows)
    f32 = jnp.float32
    chunk = rows // 4
    wide = RAW * chunk + 2 * seg

    def struct(*dims):
        return jax.ShapeDtypeStruct(dims, f32)

    def vmem(*dims):
        return pltpu.VMEM(dims, f32)

    indices = (holder, stratum, transverse)
    flat = [a.reshape(-1, LANES) for a in (u, power, storage, conductance, warmth, coef)]
    own, to_even, to_odd, only, *indices = pl.pallas_call(
        functools.partial(pack_kernel, shape),
        out_shape=(
            struct(RAW * layers * rows + 2 * seg, LANES),
            struct(wide, LANES),
            struct(wide, LANES),
            struct(2 * seg, LANES),
            *(jax.ShapeDtypeStruct(a.shape, a.dtype) for a in indices),
        ),
        in_specs=[pl.BlockSpec(memory_space=pltpu.HBM)] * 9,
        out_specs=(VMEM,) * 7,
        scratch_shapes=[pltpu.SemaphoreType.DMA((9,))],
        compiler_params=PARAMS,
        name="pack",
    )(*(pltpu.with_memory_space_constraint(a, pltpu.HBM) for a in (*flat, *indices)))

    swap = [(0, 1), (1, 0)]
    partner = lax.ppermute(own, "gz", swap)
    even = [(i, i ^ 1) for i in range(gx)]
    odd = [pair for i in range(1, gx - 1, 2) for pair in ((i, i + 1), (i + 1, i))]
    received = [lax.ppermute(to_even, "gx", even), lax.ppermute(to_odd, "gx", odd)]
    far = {}
    for k in range(2, gx):
        far[k] = lax.ppermute(only, "gx", [(i, i ^ k) for i in range(gx) if abs(i - (i ^ k)) > 1])
    received += [far[k] for k in range(2, gx)]
    late = lax.ppermute(jnp.concatenate(received, axis=0), "gz", swap)

    sides = 1 if gy == 2 else 2
    fields = struct(FIELDS * (layers + 1), rows, LANES)
    strip_rows = FIELDS * layers * HALO + 4 * HALO
    filled = pl.pallas_call(
        functools.partial(fill_kernel, False, gx, gy, shape, seg),
        out_shape=(fields,) + (struct(strip_rows, LANES),) * sides + (struct(segments, 8), struct(2 * segments, LANES)),
        in_specs=[VMEM] * (4 + gx),
        out_specs=(VMEM,) * (3 + sides),
        compiler_params=PARAMS,
        cost_estimate=cost(1.5),
        name="fill_own",
    )(own, *indices, *received)
    own_fields, strips, (info, held) = filled[0], filled[1 : 1 + sides], filled[1 + sides :]
    if gy == 2:
        routes = [(strips[0], swap)]
    else:
        up = [(i, i + 1) for i in range(gy - 1)]
        routes = [(strips[1], up), (strips[0], [(j, i) for i, j in up])]
    along = [lax.ppermute(value, "gy", pairs) for value, pairs in routes]
    across = []
    for value, pairs in routes:
        both = [(2 * i + z, 2 * j + 1 - z) for i, j in pairs for z in range(2)]
        across.append(lax.ppermute(value, ("gy", "gz"), both))

    partner_fields = pl.pallas_call(
        functools.partial(fill_kernel, True, gx, gy, shape, seg),
        out_shape=fields,
        in_specs=[VMEM] * 5,
        out_specs=VMEM,
        scratch_shapes=[vmem(segments, LANES)] * 2,
        compiler_params=PARAMS,
        cost_estimate=cost(1.5),
        name="fill_partner",
    )(partner, *indices, late)

    top = 2 * layers
    padded = vmem(top + 1, rows + 2 * PAD, LANES)
    inside, below, levels = pl.pallas_call(
        functools.partial(tile_kernel, gx, gy, shape),
        out_shape=(
            struct(layers, rows, LANES),
            struct(STEPS, segments, LANES),
            struct(sides * STEPS * ITERS * (top + 1), HALO, LANES),
        ),
        in_specs=[VMEM] * 3,
        out_specs=(VMEM,) * 3,
        scratch_shapes=[padded] * 3 + [vmem(top + 1, rows, LANES)] * 5,
        compiler_params=PARAMS,
        cost_estimate=cost(7),
        name="tile_sweeps",
    )(own_fields, partner_fields, info)

    results = pl.pallas_call(
        functools.partial(edge_kernel, gx, gy, shape, seg),
        out_shape=(struct(sides * layers, HALO, LANES),) + (struct(seg, LANES),) * gx,
        in_specs=[VMEM] * (6 + 2 * sides),
        out_specs=(VMEM,) * (1 + gx),
        scratch_shapes=[vmem(segments, LANES)]
        + [vmem(top + 1, 4 * HALO, LANES)] * 3
        + [vmem(top + 1, 2 * HALO, LANES)] * 5,
        compiler_params=PARAMS,
        cost_estimate=cost(1.5),
        name="edge_sweeps",
    )(own_fields, partner_fields, info, held, below, levels, *along, *across)
    heat, total = results[0], results[1]
    returned = [lax.ppermute(results[1 + k], "gx", [(i, i ^ k) for i in range(gx)]) for k in range(gx - 1, 0, -1)]
    temperature = pl.pallas_call(
        functools.partial(merge_kernel, gy),
        out_shape=struct(layers, rows, LANES),
        in_specs=[VMEM] * 2,
        out_specs=VMEM,
        compiler_params=PARAMS,
        cost_estimate=cost(1),
        name="merge",
    )(inside, heat)
    for value in returned:
        total = total + value
    return temperature, total[None]


def solution(mesh):
    gx, gy, gz = (mesh.shape[a] for a in ("gx", "gy", "gz"))
    cells = P(("stack", "gz"), "gy", "gx")
    segments = P(("stack", "gy", "gz"), "gx", None)
    return jax.shard_map(
        functools.partial(local, gx, gy, gz),
        mesh=mesh,
        in_specs=(cells, cells, cells, P(None, ("stack", "gz"), "gy", "gx"), segments, segments, P(), P(), P()),
        out_specs=(cells, segments),
        check_vma=False,
    )
```

```python
import functools

import jax
import jax.numpy as jnp
from jax import lax
from jax.experimental import pallas as pl
from jax.experimental.pallas import tpu as pltpu
from jax.sharding import PartitionSpec as P

STEPS = 2
ITERS = 4
HALO = STEPS * ITERS
GROUP = 2 * HALO
LANES = 128
RAW = 5
FIELDS = 7
coolant_gain = 0.5

VMEM = pl.BlockSpec(memory_space=pltpu.VMEM)
PARAMS = pltpu.CompilerParams(vmem_limit_bytes=40 * 1024 * 1024)


def cost(microseconds):
    return pl.CostEstimate(flops=0, bytes_accessed=int(microseconds * 3e6), transcendentals=0)


def lane_of(rows):
    return lax.broadcasted_iota(jnp.int32, (rows, LANES), 1)


def take(value, index):
    return jnp.take_along_axis(value, index, axis=1, mode="promise_in_bounds")


def near_edges(rows):
    k = lane_of(rows) % GROUP
    return jnp.where(k < HALO, HALO - 1 - k, LANES + HALO - 1 - k)


def far_edges(rows):
    k = lane_of(rows) % GROUP
    return jnp.where(k < HALO, LANES - 1 - k, GROUP - 1 - k)


def split(value):
    high = value.astype(jnp.bfloat16)
    low = (value - high.astype(jnp.float32)).astype(jnp.bfloat16)
    return high, low


def exact_dot(onehot, value):
    high, low = split(value)
    both = jnp.concatenate([high, low], axis=0)
    return jnp.dot(jnp.concatenate([onehot, onehot], axis=1), both, preferred_element_type=jnp.float32)


def coupling(coef, warmth):
    flow = coef * warmth
    second = coolant_gain * coef * coef
    return jnp.concatenate([coef, flow, second, flow - second * warmth], axis=1)


def flip(z, layers, i):
    return jnp.where(z == 0, i, layers - 1 - i)


def pack_kernel(shape, u_ref, p_ref, c_ref, k_ref, f_ref, x_ref, *refs):
    own_ref, even_ref, odd_ref, seg_ref = refs[3:7]
    sems = refs[-1]
    layers, rows = shape
    seg = f_ref.shape[0]
    x, z = lax.axis_index("gx"), lax.axis_index("gz")
    plane = layers * rows
    copies = []

    def fetch(src, dst):
        copies.append(pltpu.make_async_copy(src, dst, sems.at[len(copies)]))
        copies[-1].start()

    fetch(k_ref, own_ref.at[pl.ds(0, 2 * plane), :])
    for field, ref in enumerate((u_ref, p_ref, c_ref), 2):
        fetch(ref, own_ref.at[pl.ds(field * plane, plane), :])
    for j, ref in enumerate((x_ref, f_ref)):
        fetch(ref, own_ref.at[pl.ds(RAW * plane + j * seg, seg), :])
    for table, place in zip(refs[:3], refs[7:10]):
        fetch(table, place)
    copies[0].wait()
    roots = pl.ds(0, 2 * plane)
    own_ref[roots, :] = jnp.sqrt(own_ref[roots, :])
    for copy in copies[1:]:
        copy.wait()
    chunk = rows // 4
    lane = lane_of(chunk)
    same = (lane % GROUP < HALO) == (x % 2 == 1)
    near, far = near_edges(chunk), far_edges(chunk)
    for part in range(RAW):
        even = jnp.zeros((chunk, LANES), jnp.float32)
        odd = even
        for h in range(2):
            for i in range(layers):
                here = lane // GROUP == h * layers + i
                src = flip(z, layers, i)
                for side in range(2):
                    g = 2 * h + side
                    field, at = (g, part * chunk) if part < 4 else (4, g * chunk)
                    block = own_ref[pl.ds(pl.multiple_of((field * layers + src) * rows + at, chunk), chunk), :]
                    if side == 0:
                        even = jnp.where(here, take(block, near), even)
                    else:
                        odd = jnp.where(here, take(block, far), odd)
        even_ref[part * chunk : (part + 1) * chunk, :] = jnp.where(same, even, odd)
        odd_ref[part * chunk : (part + 1) * chunk, :] = jnp.where(same, odd, even)
    segments = own_ref[RAW * plane : RAW * plane + 2 * seg, :]
    seg_ref[...] = segments
    even_ref[RAW * chunk :, :] = segments
    odd_ref[RAW * chunk :, :] = segments


class Strips:
    def __init__(self, refs, starts, rows, layers):
        self.refs, self.starts = refs, starts
        self.rows, self.layers = rows, layers

    def merged(self, field, start, n, x):
        chunk = self.rows // 4
        if field < 4:
            g, at = field, start
        else:
            g, at = start // chunk, 4 * chunk + start % chunk
        a, b = (ref[at + begin : at + begin + n, :] for ref, begin in zip(self.refs, self.starts))
        right_half = (lane_of(n) % GROUP < HALO) if g % 2 == 0 else (lane_of(n) % GROUP >= HALO)
        return g, jnp.where(right_half == (x % 2 == 0), a, b)

    def halo(self, field, start, n, x, partner):
        g, both = self.merged(field, start, n, x)
        lane = lane_of(n)
        half = self.layers * GROUP
        src = lane % half
        if partner:
            src = (self.layers - 1 - src // GROUP) * GROUP + src % GROUP
        if g % 2 == 1:
            src = jnp.where(src % GROUP < HALO, src + HALO, src - HALO)
        return take(both, src + half * (g // 2))


def place_segments(x, gx, seg, coef_ref, warmth_ref, own, even, odd, far):
    def put(holder, source):
        ref, at = source
        place = pl.ds(pl.multiple_of(holder * seg, seg), seg)
        coef_ref[place, :] = ref[at : at + seg, :]
        warmth_ref[place, :] = ref[at + seg : at + 2 * seg, :]

    for k, source in far:
        put(x ^ k, source)
    put(x, own)
    put(x ^ 1, even)
    beside = jnp.where(x % 2 == 0, x - 1, x + 1)
    pl.when(jnp.logical_and(beside >= 0, beside < gx))(lambda: put(beside, odd))


def tables(z, group, layers, holder_ref, stratum_ref, transverse_ref):
    holder = holder_ref[pl.ds(group, 1), :]
    layer = stratum_ref[pl.ds(group, 1), :]
    layer = jnp.where(z == 0, layer, layers - 1 - layer)
    row = transverse_ref[pl.ds(group, 1), :]
    n = holder.shape[1]
    which = lax.broadcasted_iota(jnp.int32, (8, n), 0)
    stacked = jnp.where(which == 0, holder, jnp.where(which == 1, layer, row))
    eye = lax.broadcasted_iota(jnp.int32, (n, n), 0) == lax.broadcasted_iota(jnp.int32, (n, n), 1)
    columns = lax.dot_general(
        eye.astype(jnp.float32).astype(jnp.bfloat16),
        stacked.astype(jnp.float32).astype(jnp.bfloat16),
        (((1,), (1,)), ((), ())),
        preferred_element_type=jnp.float32,
    )
    return (holder, layer, row), columns


def as_onehot(mask):
    return jnp.where(mask, 1.0, 0.0).astype(jnp.bfloat16)


def halo_segments(coef, warmth, columns, base, x):
    n = coef.shape[0]
    lane = lane_of(n)
    holder, layer = columns[:, 0:1].astype(jnp.int32), columns[:, 1:2].astype(jnp.int32)
    side = jnp.where(lane % GROUP < HALO, x + 1, x - 1)
    mine = jnp.logical_and(lane // GROUP == layer + base, holder == side)
    near = near_edges(n)
    return coupling(jnp.where(mine, take(coef, near), 0.0), take(warmth, near))


def combine(raw, added):
    s, t, u, power, storage = raw
    wall, flow, second, later = (added[:, i * LANES : (i + 1) * LANES] for i in range(4))
    return s, t, s * u, storage + wall, power + storage * u + flow, power + later, storage + second


def lengths_of(gx, chunk, seg):
    return [RAW * chunk + 2 * seg] * 2 + [2 * seg] * (gx - 2)


def edge_at(top, rows):
    return 0 if top is True else rows - HALO if top is False else pl.multiple_of(jnp.where(top, 0, rows - HALO), HALO)


def inner_at(top, rows):
    return HALO if top is True else rows - 2 * HALO if top is False else pl.multiple_of(jnp.where(top, HALO, rows - 2 * HALO), HALO)


def sides_of(gy, y):
    return [(y == 1, True)] if gy == 2 else [(True, y > 0), (False, y < gy - 1)]


def fill_kernel(partner, gx, gy, shape, seg, *refs):
    layers, rows = shape
    cells_ref, holder_ref, stratum_ref, transverse_ref = refs[:4]
    plane, chunk = layers * rows, rows // 4
    lengths = lengths_of(gx, chunk, seg)
    if partner:
        sources = [(refs[4], sum(lengths[:k])) for k in range(gx)]
        refs = refs[5:]
    else:
        sources = [(ref, 0) for ref in refs[4 : 4 + gx]]
        refs = refs[4 + gx :]
    sides = 1 if gy == 2 else 2
    out_ref = refs[0]
    if partner:
        coef_ref, warmth_ref = refs[1:3]
    else:
        strip_refs, info_ref, segments_ref = refs[1 : 1 + sides], refs[1 + sides], refs[2 + sides]
        n = segments_ref.shape[0] // 2
        coef_ref, warmth_ref = segments_ref.at[pl.ds(0, n), :], segments_ref.at[pl.ds(n, n), :]
    x, y, z = (lax.axis_index(a) for a in ("gx", "gy", "gz"))
    base = layers if partner else 0
    even, odd = ((ref, at + RAW * chunk) for ref, at in sources[:2])
    place_segments(x, gx, seg, coef_ref, warmth_ref, (cells_ref, RAW * plane), even, odd, list(enumerate(sources[2:gx], 2)))
    group = y * 2 + ((1 - z) if partner else z)
    (holder, layer, row), columns = tables(z, group, layers, holder_ref, stratum_ref, transverse_ref)
    coef, warmth = coef_ref[...], warmth_ref[...]
    n = coef.shape[0]
    if not partner:
        info_ref[...] = columns

    cell = jnp.where(holder == x, layer * rows + row, -1)
    line = lax.broadcasted_iota(jnp.int32, (plane, n), 0)
    added = exact_dot(as_onehot(line == cell), coupling(coef, warmth))
    line = lax.broadcasted_iota(jnp.int32, (rows, n), 0)
    beside = exact_dot(as_onehot(line == row), halo_segments(coef, warmth, columns, base, x))
    for i in range(layers):
        src = flip(z, layers, i)
        raw = [cells_ref[pl.ds(pl.multiple_of((f * layers + src) * rows, rows), rows), :] for f in range(RAW)]
        for f, value in enumerate(combine(raw, added[i * rows : (i + 1) * rows])):
            out_ref[f * (layers + 1) + i] = value
    strips = Strips([ref for ref, _ in sources[:2]], [at for _, at in sources[:2]], rows, layers)
    half = lane_of(chunk) // (LANES // 2) == (1 if partner else 0)
    for part in range(4):
        here = slice(part * chunk, (part + 1) * chunk)
        raw = [jnp.where(half, strips.halo(f, part * chunk, chunk, x, partner), 0.0) for f in range(RAW)]
        for f, value in enumerate(combine(raw, beside[here])):
            out_ref[f * (layers + 1) + layers, here, :] = value
    if partner:
        return
    low = lane_of(HALO) < LANES // 2
    for strip_ref, (top, _) in zip(strip_refs, sides_of(gy, y)):
        edge = pl.ds(edge_at(top, rows), HALO)
        for f in range(FIELDS):
            for i in range(layers):
                strip_ref[(f * layers + i) * HALO : (f * layers + i + 1) * HALO, :] = out_ref[f * (layers + 1) + i, edge, :]
        at = FIELDS * layers * HALO
        made = [out_ref[f * (layers + 1) + layers, edge, :] for f in range(FIELDS)]
        made.append(jnp.zeros_like(made[0]))
        for j in range(4):
            packed = jnp.where(low, made[2 * j], pltpu.roll(made[2 * j + 1], LANES // 2, 1))
            strip_ref[at + j * HALO : at + (j + 1) * HALO, :] = packed


def lateral(buf, at, n, count):
    lane = lane_of(n)
    k, group = lane % GROUP, lane // GROUP
    top = buf.shape[0] - 1
    centre = [buf[i, pl.ds(at, n), :] for i in range(min(count + 1, top))]
    halo = buf[top, pl.ds(at, n), :]
    border = jnp.zeros_like(halo)
    sums = []
    for i in range(count):
        border = jnp.where(group == i, pltpu.roll(centre[i], i * GROUP + HALO, 1), border)
        beside = pltpu.roll(halo, LANES - (i * GROUP + HALO), 1)
        east = jnp.where(lane == LANES - 1, beside, pltpu.roll(centre[i], LANES - 1, 1))
        west = jnp.where(lane == 0, beside, pltpu.roll(centre[i], 1, 1))
        sums.append(east + west + buf[i, pl.ds(at - 1, n), :] + buf[i, pl.ds(at + 1, n), :])
    one = jnp.where(k == HALO, border, pltpu.roll(halo, 1, 1))
    other = jnp.where(k == HALO - 1, border, pltpu.roll(halo, LANES - 1, 1))
    sums.append(one + other + buf[top, pl.ds(at - 1, n), :] + buf[top, pl.ds(at + 1, n), :])
    return centre + [halo], sums


def vertical(values, count):
    planes, halo = values[:-1], values[-1]
    sums = []
    for i in range(count):
        near = [planes[j] for j in (i - 1, i + 1) if 0 <= j < len(planes)]
        sums.append(functools.reduce(jnp.add, near))
    lane = lane_of(halo.shape[0])
    up = jnp.where(lane >= GROUP, pltpu.roll(halo, GROUP, 1), 0.0)
    down = jnp.where(lane < LANES - GROUP, pltpu.roll(halo, LANES - GROUP, 1), 0.0)
    sums.append(up + down)
    return sums


def coefficients(s_ref, at, n, raw, dests, to):
    a_ref, q_ref, r_ref, e_ref, g_ref = dests
    top = s_ref.shape[0] - 1
    centre, sums = lateral(s_ref, at, n, top)
    t = [raw(1, i) for i in range(top + 1)]
    above = vertical(t, top)
    here = pl.ds(to, n)
    for i in range(top + 1):
        s = centre[i]
        diag = raw(3, i) + s * sums[i] + t[i] * above[i]
        inverse = 1.0 / jnp.where(diag > 0.0, diag, 1.0)
        scaled = s * inverse
        a_ref[i, here, :] = s * scaled
        r_ref[i, here, :] = raw(4, i) * scaled
        e_ref[i, here, :] = raw(5, i) * scaled
        g_ref[i, here, :] = raw(6, i) * inverse
        q_ref[i, here, :] = t[i] * jnp.where(s > 0.0, 1.0 / jnp.where(s > 0.0, s, 1.0), 0.0)


def sweep(src_ref, dst_ref, at, n, count, coefs, base):
    a_ref, q_ref, r_ref = coefs[:3]
    top = src_ref.shape[0] - 1
    here = pl.ds(base, n)
    centre, sums = lateral(src_ref, at, n, count)
    layers = list(range(len(centre) - 1)) + [top]
    ratio = [q_ref[i, here, :] for i in layers]
    above = vertical([q * c for q, c in zip(ratio, centre)], count)
    ratio = ratio[:count] + ratio[-1:]
    for j, i in enumerate(list(range(count)) + [top]):
        value = r_ref[i, here, :] + a_ref[i, here, :] * (sums[j] + ratio[j] * above[j])
        dst_ref[i, pl.ds(at, n), :] = value


def next_rhs(coefs, v_ref, at, n, base):
    r_ref, e_ref, g_ref = coefs[2:]
    here = pl.ds(base, n)
    for i in range(v_ref.shape[0]):
        r_ref[i, here, :] = e_ref[i, here, :] + g_ref[i, here, :] * v_ref[i, pl.ds(at, n), :]


def needed(layers, n):
    return min(2 * layers, layers + STEPS * ITERS - 1 - n)


def two_steps(layers, sweep_all, between, after):
    for step in range(STEPS):
        whole = [n for n in range(step * ITERS, (step + 1) * ITERS) if needed(layers, n) == 2 * layers]
        pairs = len(whole) // 2

        def pair(k, carry):
            n = step * ITERS + 2 * k
            sweep_all(n, 0, 2 * layers)
            sweep_all(n + 1, 1, 2 * layers)
            return carry

        if pairs:
            lax.fori_loop(0, pairs, pair, 0)
        for n in range(step * ITERS + 2 * pairs, (step + 1) * ITERS):
            sweep_all(n, n % 2, needed(layers, n))
        after(step)
        if step < STEPS - 1:
            between()


PAD = 8


def tile_kernel(gx, gy, shape, *refs):
    layers, rows = shape
    own_ref, partner_ref, info_ref, out_ref, below_ref, level_ref = refs[:6]
    s_ref, va_ref, vb_ref = refs[6:9]
    coefs = refs[9:]
    x, y, z = (lax.axis_index(a) for a in ("gx", "gy", "gz"))
    top = 2 * layers
    zeros = jnp.zeros((PAD, LANES), jnp.float32)
    for ref in (s_ref, va_ref, vb_ref):
        for i in range(top + 1):
            ref[i, 0:PAD, :] = zeros
            ref[i, PAD + rows : PAD + rows + PAD, :] = zeros

    def field(f, i, here):
        j = f * (layers + 1)
        if i == top:
            return own_ref[j + layers, here, :] + partner_ref[j + layers, here, :]
        return own_ref[j + i, here, :] if i < layers else partner_ref[j + i - layers, here, :]

    for i in range(top + 1):
        s_ref[i, PAD : PAD + rows, :] = field(0, i, slice(None))
        va_ref[i, PAD : PAD + rows, :] = field(2, i, slice(None))
    n = 8
    for at in range(0, rows, n):
        coefficients(s_ref, PAD + at, n, lambda f, i: field(f, i, slice(at, at + n)), coefs, at)

    bufs = (va_ref, vb_ref)
    sides = sides_of(gy, y)

    def sweep_all(number, which, count):
        src_ref, dst_ref = bufs[which], bufs[1 - which]
        for side, (above, _) in enumerate(sides):
            inner = pl.ds(PAD + inner_at(above, rows), HALO)
            for i in range(top + 1):
                level_ref[(side * STEPS * ITERS + number) * (top + 1) + i] = src_ref[i, inner, :]
        for at in range(0, rows, n):
            sweep(src_ref, dst_ref, PAD + at, n, count, coefs, at)

    holder, layer, row = (info_ref[:, j : j + 1].astype(jnp.int32) for j in range(3))
    spoilt = None
    for above, live in sides:
        part = jnp.logical_and(row // HALO == edge_at(above, rows) // HALO, live)
        spoilt = part if spoilt is None else jnp.logical_or(spoilt, part)
    cell = jnp.where(jnp.logical_and(holder == x, jnp.logical_not(spoilt)), layer * rows + row, -1)
    picks = as_onehot(lax.broadcasted_iota(jnp.int32, (cell.shape[0], layers * rows), 1) == cell)

    def after(step):
        heat = []
        for i in range(layers):
            here = pl.ds(PAD, rows)
            heat.append(va_ref[i, here, :] / s_ref[i, here, :])
            if step == STEPS - 1:
                out_ref[flip(z, layers, i)] = heat[-1]
        below_ref[step] = exact_dot(picks, jnp.concatenate(heat, axis=0))

    def between():
        for at in range(0, rows, n):
            next_rhs(coefs, va_ref, PAD + at, n, at)

    two_steps(layers, sweep_all, between, after)


def edge_kernel(gx, gy, shape, seg, *refs):
    layers, rows = shape
    own_ref, partner_ref, info_ref, segments_ref, below_ref, level_ref = refs[:6]
    sides_n = 1 if gy == 2 else 2
    along, across = refs[6 : 6 + sides_n], refs[6 + sides_n : 6 + 2 * sides_n]
    refs = refs[6 + 2 * sides_n :]
    heat_ref, returns = refs[0], refs[1 : 1 + gx]
    ret_ref, s_ref, va_ref, vb_ref = refs[1 + gx : 5 + gx]
    coefs = refs[5 + gx :]
    x, y, z = (lax.axis_index(a) for a in ("gx", "gy", "gz"))
    top = 2 * layers
    count = info_ref.shape[0]
    holder, layer, row = (info_ref[:, j : j + 1].astype(jnp.int32) for j in range(3))
    below = [below_ref[step] for step in range(STEPS)]
    lane = lane_of(HALO)
    low = lane < LANES // 2
    bufs = (va_ref, vb_ref)

    def tile(j):
        return pl.ds(j if isinstance(j, int) else pl.multiple_of(j, HALO), HALO)

    for side, (above, live) in enumerate(sides_of(gy, y)):
        def place(when_top, otherwise):
            if above is True or above is False:
                return when_top * HALO if above else otherwise * HALO
            return jnp.where(above, when_top * HALO, otherwise * HALO)

        outer, strip, edge, inner = place(0, 3), place(1, 2), place(2, 1), place(3, 0)
        edge_rows = tile(edge_at(above, rows))
        inner_rows = tile(inner_at(above, rows))

        def field(f, i, here):
            j = f * (layers + 1)
            if i == top:
                return own_ref[j + layers, here, :] + partner_ref[j + layers, here, :]
            return own_ref[j + i, here, :] if i < layers else partner_ref[j + i - layers, here, :]

        t_ref, d_ref, q_ref, e_ref, g_ref = coefs[1], coefs[0], coefs[2], coefs[3], coefs[4]
        keep = {0: s_ref, 1: t_ref, 2: va_ref, 3: d_ref, 4: q_ref, 5: e_ref, 6: g_ref}
        zeros = jnp.zeros((HALO, LANES), jnp.float32)
        src = lane % (LANES // 2)
        turned = (layers - 1 - src // GROUP) * GROUP + src % GROUP
        for f in range(FIELDS):
            for i in range(top + 1):
                if i < top:
                    ref, j = (along[side], i) if i < layers else (across[side], top - 1 - i)
                    at = (f * layers + j) * HALO
                    value = ref[at : at + HALO, :]
                else:
                    at = FIELDS * layers * HALO + (f // 2) * HALO
                    half = (LANES // 2) * (f % 2)
                    a = take(along[side][at : at + HALO, :], src + half)
                    b = take(across[side][at : at + HALO, :], turned + half)
                    value = jnp.where(low, a, b)
                ref, shift = keep[f], 0 if f in (0, 2) else HALO
                ref[i, tile(strip - shift), :] = value
                ref[i, tile(edge - shift), :] = field(f, i, edge_rows)
        for i in range(top + 1):
            s_ref[i, tile(outer), :] = zeros
            va_ref[i, tile(outer), :] = zeros
            vb_ref[i, tile(outer), :] = zeros
            s_ref[i, tile(inner), :] = field(0, i, inner_rows)
        n = 2 * HALO
        held = [[keep[f][i, pl.ds(0, n), :] for i in range(top + 1)] if f in (1, 3, 4, 5, 6) else None for f in range(FIELDS)]
        coefficients(s_ref, HALO, n, lambda f, i: held[f][i], coefs, 0)

        def sweep_all(number, which, needed_layers):
            src_ref, dst_ref = bufs[which], bufs[1 - which]
            for i in range(top + 1):
                src_ref[i, tile(inner), :] = level_ref[(side * STEPS * ITERS + number) * (top + 1) + i]
            sweep(src_ref, dst_ref, HALO, n, needed_layers, coefs, 0)

        first = edge_at(above, rows)
        hit = jnp.logical_and(jnp.logical_and(holder == x, row // HALO == first // HALO), live)
        cell = jnp.where(hit, layer * HALO + row - first, -1)
        picks = as_onehot(lax.broadcasted_iota(jnp.int32, (count, LANES), 1) == cell)

        def after(step):
            heat = []
            for i in range(layers):
                heat.append(va_ref[i, tile(edge), :] / s_ref[i, tile(edge), :])
                if step == STEPS - 1:
                    heat_ref[side * layers + flip(z, layers, i)] = heat[-1]
            heat.append(jnp.zeros((LANES - layers * HALO, LANES), jnp.float32))
            below[step] = below[step] + exact_dot(picks, jnp.concatenate(heat, axis=0))

        two_steps(layers, sweep_all, lambda: next_rhs(coefs, va_ref, HALO, n, 0), after)

    coef, warmth = segments_ref[:count, :], segments_ref[count:, :]
    for step in range(STEPS):
        warmth = warmth + coolant_gain * coef * (below[step] - warmth)
    ret_ref[...] = jnp.where(holder == x, warmth, 0.0)
    for k, ref in enumerate(returns):
        ref[...] = ret_ref[pl.ds(pl.multiple_of((x ^ k) * seg, seg), seg), :]


def merge_kernel(gy, whole_ref, heat_ref, out_ref):
    layers, rows, _ = whole_ref.shape
    out_ref[...] = whole_ref[...]
    for side, (above, live) in enumerate(sides_of(gy, lax.axis_index("gy"))):
        def put(side=side, above=above):
            out_ref[:, pl.ds(edge_at(above, rows), HALO), :] = heat_ref[side * layers : (side + 1) * layers]

        if live is True:
            put()
        else:
            pl.when(live)(put)


def after_kernel(*refs):
    pass


def local(gx, gy, gz, u, power, storage, conductance, warmth, coef, holder, stratum, transverse):
    layers, rows, columns = u.shape
    seg = warmth.shape[1]
    segments = stratum.shape[1]
    if gz != 2 or gx < 4 or gx & (gx - 1) or columns != LANES or 2 * layers * GROUP != LANES or rows % 32:
        raise ValueError("unsupported shape")
    holder = holder[:, :, 0]
    shape = (layers, rows)
    f32 = jnp.float32
    chunk = rows // 4
    wide = RAW * chunk + 2 * seg

    def struct(*dims):
        return jax.ShapeDtypeStruct(dims, f32)

    def vmem(*dims):
        return pltpu.VMEM(dims, f32)

    indices = (holder, stratum, transverse)
    flat = [a.reshape(-1, LANES) for a in (u, power, storage, conductance, warmth, coef)]
    own, to_even, to_odd, only, *indices = pl.pallas_call(
        functools.partial(pack_kernel, shape),
        out_shape=(
            struct(RAW * layers * rows + 2 * seg, LANES),
            struct(wide, LANES),
            struct(wide, LANES),
            struct(2 * seg, LANES),
            *(jax.ShapeDtypeStruct(a.shape, a.dtype) for a in indices),
        ),
        in_specs=[pl.BlockSpec(memory_space=pltpu.HBM)] * 9,
        out_specs=(VMEM,) * 7,
        scratch_shapes=[pltpu.SemaphoreType.DMA((9,))],
        compiler_params=PARAMS,
        name="pack",
    )(*(pltpu.with_memory_space_constraint(a, pltpu.HBM) for a in (*flat, *indices)))

    swap = [(0, 1), (1, 0)]
    even = [(i, i ^ 1) for i in range(gx)]
    odd = [pair for i in range(1, gx - 1, 2) for pair in ((i, i + 1), (i + 1, i))]
    received = [lax.ppermute(to_even, "gx", even), lax.ppermute(to_odd, "gx", odd)]
    far = {}
    for k in range(2, gx):
        far[k] = lax.ppermute(only, "gx", [(i, i ^ k) for i in range(gx) if abs(i - (i ^ k)) > 1])
    received += [far[k] for k in range(2, gx)]
    anywhere = pl.BlockSpec(memory_space=pl.ANY)
    own = pl.pallas_call(
        after_kernel,
        out_shape=struct(*own.shape),
        in_specs=[anywhere] * (1 + gx),
        out_specs=anywhere,
        input_output_aliases={0: 0},
        compiler_params=PARAMS,
        name="after_swap",
    )(own, *received)
    partner = lax.ppermute(own, "gz", swap)
    late = lax.ppermute(jnp.concatenate(received, axis=0), "gz", swap)

    sides = 1 if gy == 2 else 2
    fields = struct(FIELDS * (layers + 1), rows, LANES)
    strip_rows = FIELDS * layers * HALO + 4 * HALO
    filled = pl.pallas_call(
        functools.partial(fill_kernel, False, gx, gy, shape, seg),
        out_shape=(fields,) + (struct(strip_rows, LANES),) * sides + (struct(segments, 8), struct(2 * segments, LANES)),
        in_specs=[VMEM] * (4 + gx),
        out_specs=(VMEM,) * (3 + sides),
        compiler_params=PARAMS,
        cost_estimate=cost(1.5),
        name="fill_own",
    )(own, *indices, *received)
    own_fields, strips, (info, held) = filled[0], filled[1 : 1 + sides], filled[1 + sides :]
    if gy == 2:
        routes = [(strips[0], swap)]
    else:
        up = [(i, i + 1) for i in range(gy - 1)]
        routes = [(strips[1], up), (strips[0], [(j, i) for i, j in up])]
    along = [lax.ppermute(value, "gy", pairs) for value, pairs in routes]
    across = []
    for value, pairs in routes:
        both = [(2 * i + z, 2 * j + 1 - z) for i, j in pairs for z in range(2)]
        across.append(lax.ppermute(value, ("gy", "gz"), both))

    partner_fields = pl.pallas_call(
        functools.partial(fill_kernel, True, gx, gy, shape, seg),
        out_shape=fields,
        in_specs=[VMEM] * 5,
        out_specs=VMEM,
        scratch_shapes=[vmem(segments, LANES)] * 2,
        compiler_params=PARAMS,
        cost_estimate=cost(1.5),
        name="fill_partner",
    )(partner, *indices, late)

    top = 2 * layers
    padded = vmem(top + 1, rows + 2 * PAD, LANES)
    inside, below, levels = pl.pallas_call(
        functools.partial(tile_kernel, gx, gy, shape),
        out_shape=(
            struct(layers, rows, LANES),
            struct(STEPS, segments, LANES),
            struct(sides * STEPS * ITERS * (top + 1), HALO, LANES),
        ),
        in_specs=[VMEM] * 3,
        out_specs=(VMEM,) * 3,
        scratch_shapes=[padded] * 3 + [vmem(top + 1, rows, LANES)] * 5,
        compiler_params=PARAMS,
        cost_estimate=cost(7),
        name="tile_sweeps",
    )(own_fields, partner_fields, info)

    results = pl.pallas_call(
        functools.partial(edge_kernel, gx, gy, shape, seg),
        out_shape=(struct(sides * layers, HALO, LANES),) + (struct(seg, LANES),) * gx,
        in_specs=[VMEM] * (6 + 2 * sides),
        out_specs=(VMEM,) * (1 + gx),
        scratch_shapes=[vmem(segments, LANES)]
        + [vmem(top + 1, 4 * HALO, LANES)] * 3
        + [vmem(top + 1, 2 * HALO, LANES)] * 5,
        compiler_params=PARAMS,
        cost_estimate=cost(1.5),
        name="edge_sweeps",
    )(own_fields, partner_fields, info, held, below, levels, *along, *across)
    heat, total = results[0], results[1]
    returned = [lax.ppermute(results[1 + k], "gx", [(i, i ^ k) for i in range(gx)]) for k in range(gx - 1, 0, -1)]
    temperature = pl.pallas_call(
        functools.partial(merge_kernel, gy),
        out_shape=struct(layers, rows, LANES),
        in_specs=[VMEM] * 2,
        out_specs=VMEM,
        compiler_params=PARAMS,
        cost_estimate=cost(1),
        name="merge",
    )(inside, heat)
    for value in returned:
        total = total + value
    return temperature, total[None]


def solution(mesh):
    gx, gy, gz = (mesh.shape[a] for a in ("gx", "gy", "gz"))
    cells = P(("stack", "gz"), "gy", "gx")
    segments = P(("stack", "gy", "gz"), "gx", None)
    return jax.shard_map(
        functools.partial(local, gx, gy, gz),
        mesh=mesh,
        in_specs=(cells, cells, cells, P(None, ("stack", "gz"), "gy", "gx"), segments, segments, P(), P(), P()),
        out_specs=(cells, segments),
        check_vma=False,
    )
```

```python
import functools

import jax
import jax.numpy as jnp
from jax import lax
from jax.experimental import pallas as pl
from jax.experimental.pallas import tpu as pltpu
from jax.sharding import PartitionSpec as P

STEPS = 2
ITERS = 4
HALO = STEPS * ITERS
GROUP = 2 * HALO
LANES = 128
RAW = 5
FIELDS = 7
coolant_gain = 0.5

VMEM = pl.BlockSpec(memory_space=pltpu.VMEM)
PARAMS = pltpu.CompilerParams(vmem_limit_bytes=40 * 1024 * 1024)


def cost(microseconds):
    return pl.CostEstimate(flops=0, bytes_accessed=int(microseconds * 3e6), transcendentals=0)


def lane_of(rows):
    return lax.broadcasted_iota(jnp.int32, (rows, LANES), 1)


def take(value, index):
    return jnp.take_along_axis(value, index, axis=1, mode="promise_in_bounds")


def edge_columns(rows, turned):
    j = lane_of(rows) % GROUP
    first = j < HALO
    return jnp.where(first, LANES - HALO + j, j - HALO) if not turned else jnp.where(first, j, LANES - GROUP + j)


def split(value):
    high = value.astype(jnp.bfloat16)
    low = (value - high.astype(jnp.float32)).astype(jnp.bfloat16)
    return high, low


def exact_dot(onehot, value):
    high, low = split(value)
    both = jnp.concatenate([high, low], axis=0)
    return jnp.dot(jnp.concatenate([onehot, onehot], axis=1), both, preferred_element_type=jnp.float32)


def coupling(coef, warmth):
    flow = coef * warmth
    second = coolant_gain * coef * coef
    return jnp.concatenate([coef, flow, second, flow - second * warmth], axis=1)


def flip(z, layers, i):
    return jnp.where(z == 0, i, layers - 1 - i)


def pack_kernel(shape, u_ref, p_ref, c_ref, k_ref, f_ref, x_ref, *refs):
    own_ref, even_ref, odd_ref, seg_ref = refs[3:7]
    sems = refs[-1]
    layers, rows = shape
    seg = f_ref.shape[0]
    x, z = lax.axis_index("gx"), lax.axis_index("gz")
    plane = layers * rows
    copies = []

    def fetch(src, dst):
        copies.append(pltpu.make_async_copy(src, dst, sems.at[len(copies)]))
        copies[-1].start()

    fetch(k_ref, own_ref.at[pl.ds(0, 2 * plane), :])
    for field, ref in enumerate((u_ref, p_ref, c_ref), 2):
        fetch(ref, own_ref.at[pl.ds(field * plane, plane), :])
    for j, ref in enumerate((x_ref, f_ref)):
        fetch(ref, own_ref.at[pl.ds(RAW * plane + j * seg, seg), :])
    for table, place in zip(refs[:3], refs[7:10]):
        fetch(table, place)
    copies[0].wait()
    roots = pl.ds(0, 2 * plane)
    own_ref[roots, :] = jnp.sqrt(own_ref[roots, :])
    for copy in copies[1:]:
        copy.wait()
    chunk = rows // 4
    lane = lane_of(chunk)
    same = (lane % GROUP < HALO) == (x % 2 == 0)
    near, far = edge_columns(chunk, False), edge_columns(chunk, True)
    for part in range(RAW):
        even = jnp.zeros((chunk, LANES), jnp.float32)
        odd = even
        for h in range(2):
            for i in range(layers):
                here = lane // GROUP == h * layers + i
                src = flip(z, layers, i)
                for side in range(2):
                    g = 2 * h + side
                    field, at = (g, part * chunk) if part < 4 else (4, g * chunk)
                    block = own_ref[pl.ds(pl.multiple_of((field * layers + src) * rows + at, chunk), chunk), :]
                    if side == 0:
                        even = jnp.where(here, take(block, near), even)
                    else:
                        odd = jnp.where(here, take(block, far), odd)
        even_ref[part * chunk : (part + 1) * chunk, :] = jnp.where(same, even, odd)
        odd_ref[part * chunk : (part + 1) * chunk, :] = jnp.where(same, odd, even)
        at = RAW * plane + 2 * seg + part * chunk
        own_ref[at : at + chunk, :] = even
        own_ref[at + RAW * chunk : at + (RAW + 1) * chunk, :] = odd
    segments = own_ref[RAW * plane : RAW * plane + 2 * seg, :]
    seg_ref[...] = segments
    even_ref[RAW * chunk :, :] = segments
    odd_ref[RAW * chunk :, :] = segments


class Strips:
    def __init__(self, refs, starts, cells_ref, start, rows, layers):
        self.refs, self.starts = refs, starts
        self.cells_ref, self.start = cells_ref, start
        self.rows, self.layers = rows, layers

    def both(self, field, start, n, x, partner):
        chunk = self.rows // 4
        if field < 4:
            g, at = field, start
        else:
            g, at = start // chunk, 4 * chunk + start % chunk
        a, b = (ref[at + begin : at + begin + n, :] for ref, begin in zip(self.refs, self.starts))
        at = self.start + (g % 2) * RAW * chunk + at
        inside = self.cells_ref[at : at + n, :]
        from_left, from_right = jnp.where(x % 2 == 0, b, a), jnp.where(x % 2 == 0, a, b)
        lane = lane_of(n)
        first = (lane % GROUP < HALO) if g % 2 == 0 else (lane % GROUP >= HALO)
        half = self.layers * GROUP
        src = lane % half
        if partner:
            src = (self.layers - 1 - src // GROUP) * GROUP + src % GROUP
        if g % 2 == 1:
            src = jnp.where(src % GROUP < HALO, src + HALO, src - HALO)
        src = src + half * (g // 2)
        return take(jnp.where(first, from_left, inside), src), take(jnp.where(first, inside, from_right), src)


def place_segments(x, gx, seg, coef_ref, warmth_ref, own, even, odd, far):
    def put(holder, source):
        ref, at = source
        place = pl.ds(pl.multiple_of(holder * seg, seg), seg)
        coef_ref[place, :] = ref[at : at + seg, :]
        warmth_ref[place, :] = ref[at + seg : at + 2 * seg, :]

    for k, source in far:
        put(x ^ k, source)
    put(x, own)
    put(x ^ 1, even)
    beside = jnp.where(x % 2 == 0, x - 1, x + 1)
    pl.when(jnp.logical_and(beside >= 0, beside < gx))(lambda: put(beside, odd))


def tables(z, group, layers, holder_ref, stratum_ref, transverse_ref):
    holder = holder_ref[pl.ds(group, 1), :]
    layer = stratum_ref[pl.ds(group, 1), :]
    layer = jnp.where(z == 0, layer, layers - 1 - layer)
    row = transverse_ref[pl.ds(group, 1), :]
    n = holder.shape[1]
    which = lax.broadcasted_iota(jnp.int32, (8, n), 0)
    stacked = jnp.where(which == 0, holder, jnp.where(which == 1, layer, row))
    eye = lax.broadcasted_iota(jnp.int32, (n, n), 0) == lax.broadcasted_iota(jnp.int32, (n, n), 1)
    columns = lax.dot_general(
        eye.astype(jnp.float32).astype(jnp.bfloat16),
        stacked.astype(jnp.float32).astype(jnp.bfloat16),
        (((1,), (1,)), ((), ())),
        preferred_element_type=jnp.float32,
    )
    return (holder, layer, row), columns


def as_onehot(mask):
    return jnp.where(mask, 1.0, 0.0).astype(jnp.bfloat16)


def edge_segments(coef, warmth, columns, base, x):
    n = coef.shape[0]
    lane = lane_of(n)
    first = lane % GROUP < HALO
    holder, layer = columns[:, 0:1].astype(jnp.int32), columns[:, 1:2].astype(jnp.int32)
    here = lane // GROUP == layer + base
    near = edge_columns(n, False)
    coef, warmth = take(coef, near), take(warmth, near)
    sides = []
    for begin in (x - 1, x):
        mine = jnp.logical_and(here, holder == jnp.where(first, begin, begin + 1))
        sides.append(coupling(jnp.where(mine, coef, 0.0), warmth))
    return sides


def combine(raw, added):
    s, t, u, power, storage = raw
    wall, flow, second, later = (added[:, i * LANES : (i + 1) * LANES] for i in range(4))
    return s, t, s * u, storage + wall, power + storage * u + flow, power + later, storage + second


def lengths_of(gx, chunk, seg):
    return [RAW * chunk + 2 * seg] * 2 + [2 * seg] * (gx - 2)


def edge_at(top, rows):
    return 0 if top is True else rows - HALO if top is False else pl.multiple_of(jnp.where(top, 0, rows - HALO), HALO)


def inner_at(top, rows):
    return HALO if top is True else rows - 2 * HALO if top is False else pl.multiple_of(jnp.where(top, HALO, rows - 2 * HALO), HALO)


def sides_of(gy, y):
    return [(y == 1, True)] if gy == 2 else [(True, y > 0), (False, y < gy - 1)]


def fill_kernel(partner, gx, gy, shape, seg, *refs):
    layers, rows = shape
    cells_ref, holder_ref, stratum_ref, transverse_ref = refs[:4]
    plane, chunk = layers * rows, rows // 4
    lengths = lengths_of(gx, chunk, seg)
    if partner:
        sources = [(refs[4], sum(lengths[:k])) for k in range(gx)]
        refs = refs[5:]
    else:
        sources = [(ref, 0) for ref in refs[4 : 4 + gx]]
        refs = refs[4 + gx :]
    sides = 1 if gy == 2 else 2
    out_ref = refs[0]
    if partner:
        coef_ref, warmth_ref = refs[1:3]
    else:
        strip_refs, info_ref, segments_ref = refs[1 : 1 + sides], refs[1 + sides], refs[2 + sides]
        n = segments_ref.shape[0] // 2
        coef_ref, warmth_ref = segments_ref.at[pl.ds(0, n), :], segments_ref.at[pl.ds(n, n), :]
    x, y, z = (lax.axis_index(a) for a in ("gx", "gy", "gz"))
    base = layers if partner else 0
    even, odd = ((ref, at + RAW * chunk) for ref, at in sources[:2])
    place_segments(x, gx, seg, coef_ref, warmth_ref, (cells_ref, RAW * plane), even, odd, list(enumerate(sources[2:gx], 2)))
    group = y * 2 + ((1 - z) if partner else z)
    (holder, layer, row), columns = tables(z, group, layers, holder_ref, stratum_ref, transverse_ref)
    coef, warmth = coef_ref[...], warmth_ref[...]
    n = coef.shape[0]
    if not partner:
        info_ref[...] = columns

    cell = jnp.where(holder == x, layer * rows + row, -1)
    line = lax.broadcasted_iota(jnp.int32, (plane, n), 0)
    added = exact_dot(as_onehot(line == cell), coupling(coef, warmth))
    line = as_onehot(lax.broadcasted_iota(jnp.int32, (rows, n), 0) == row)
    beside = [exact_dot(line, side) for side in edge_segments(coef, warmth, columns, base, x)]
    planes = layers + 2
    for i in range(layers):
        src = flip(z, layers, i)
        raw = [cells_ref[pl.ds(pl.multiple_of((f * layers + src) * rows, rows), rows), :] for f in range(RAW)]
        for f, value in enumerate(combine(raw, added[i * rows : (i + 1) * rows])):
            out_ref[f * planes + i] = value
    strips = Strips(
        [ref for ref, _ in sources[:2]], [at for _, at in sources[:2]], cells_ref, RAW * plane + 2 * seg, rows, layers
    )
    half = lane_of(chunk) // (LANES // 2) == (1 if partner else 0)
    for part in range(4):
        here = slice(part * chunk, (part + 1) * chunk)
        raw = [strips.both(f, part * chunk, chunk, x, partner) for f in range(RAW)]
        for side in range(2):
            cells = [jnp.where(half, value[side], 0.0) for value in raw]
            for f, value in enumerate(combine(cells, beside[side][here])):
                out_ref[f * planes + layers + side, here, :] = value
    if partner:
        return
    low = lane_of(HALO) < LANES // 2
    for strip_ref, (top, _) in zip(strip_refs, sides_of(gy, y)):
        edge = pl.ds(edge_at(top, rows), HALO)
        for f in range(FIELDS):
            for i in range(layers):
                strip_ref[(f * layers + i) * HALO : (f * layers + i + 1) * HALO, :] = out_ref[f * planes + i, edge, :]
        at = FIELDS * layers * HALO
        for f in range(FIELDS):
            left, right = (out_ref[f * planes + layers + side, edge, :] for side in range(2))
            packed = jnp.where(low, left, pltpu.roll(right, LANES // 2, 1))
            strip_ref[at + f * HALO : at + (f + 1) * HALO, :] = packed


def planes_of(count, total):
    return list(range(count)) + [total - 2, total - 1]


def lateral(buf, at, n, which):
    sums = []
    for i in which:
        centre = buf[i, pl.ds(at, n), :]
        beside = pltpu.roll(centre, 1, 1) + pltpu.roll(centre, LANES - 1, 1)
        sums.append(beside + (buf[i, pl.ds(at - 1, n), :] + buf[i, pl.ds(at + 1, n), :]))
    return sums


def vertical(planes, edges, count):
    sums = []
    for i in range(count):
        near = [planes[j] for j in (i - 1, i + 1) if 0 <= j < len(planes)]
        sums.append(functools.reduce(jnp.add, near))
    for edge in edges:
        lane = lane_of(edge.shape[0])
        up = jnp.where(lane >= GROUP, pltpu.roll(edge, GROUP, 1), 0.0)
        down = jnp.where(lane < LANES - GROUP, pltpu.roll(edge, LANES - GROUP, 1), 0.0)
        sums.append(up + down)
    return sums


def coefficients(s_ref, at, n, raw, dests, to):
    a_ref, q_ref, r_ref, e_ref, g_ref = dests
    total = s_ref.shape[0]
    sums = lateral(s_ref, at, n, range(total))
    t = [raw(1, i) for i in range(total)]
    above = vertical(t[:-2], t[-2:], total - 2)
    here = pl.ds(to, n)
    for i in range(total):
        s = s_ref[i, pl.ds(at, n), :]
        diag = raw(3, i) + s * sums[i] + t[i] * above[i]
        inverse = 1.0 / jnp.where(diag > 0.0, diag, 1.0)
        scaled = s * inverse
        a_ref[i, here, :] = s * scaled
        r_ref[i, here, :] = raw(4, i) * scaled
        e_ref[i, here, :] = raw(5, i) * scaled
        g_ref[i, here, :] = raw(6, i) * inverse
        q_ref[i, here, :] = t[i] * jnp.where(s > 0.0, 1.0 / jnp.where(s > 0.0, s, 1.0), 0.0)


def sweep(src_ref, dst_ref, at, n, count, coefs, base):
    a_ref, q_ref, r_ref = coefs[:3]
    total = src_ref.shape[0]
    here, there = pl.ds(base, n), pl.ds(at, n)
    which = planes_of(count, total)
    sums = lateral(src_ref, at, n, which)
    scaled = [q_ref[i, here, :] * src_ref[i, there, :] for i in planes_of(min(count + 1, total - 2), total)]
    above = vertical(scaled[:-2], scaled[-2:], count)
    for j, i in enumerate(which):
        dst_ref[i, there, :] = r_ref[i, here, :] + a_ref[i, here, :] * (sums[j] + q_ref[i, here, :] * above[j])


def next_rhs(coefs, v_ref, at, n, base):
    r_ref, e_ref, g_ref = coefs[2:]
    here = pl.ds(base, n)
    for i in range(v_ref.shape[0]):
        r_ref[i, here, :] = e_ref[i, here, :] + g_ref[i, here, :] * v_ref[i, pl.ds(at, n), :]


def meet(v_ref, at, n, count, back):
    total = v_ref.shape[0]
    here = pl.ds(at, n)
    lane = lane_of(n)
    j, group = lane % GROUP, lane // GROUP
    outer = jnp.logical_or(lane < ITERS, lane >= LANES - ITERS)
    left, right = v_ref[total - 2, here, :], v_ref[total - 1, here, :]
    middle = jnp.where(j < HALO, right, left)
    for i in range(count):
        value = v_ref[i, here, :]
        if back:
            moved = pltpu.roll(value, (i * GROUP + HALO) % LANES, 1)
            left = jnp.where(jnp.logical_and(group == i, j >= GROUP - ITERS), moved, left)
            right = jnp.where(jnp.logical_and(group == i, j < ITERS), moved, right)
        v_ref[i, here, :] = jnp.where(outer, pltpu.roll(middle, LANES - (i * GROUP + HALO), 1), value)
    if back:
        v_ref[total - 2, here, :] = left
        v_ref[total - 1, here, :] = right


def needed(layers, n):
    return min(2 * layers, layers + STEPS * ITERS - 1 - n)


def two_steps(layers, sweep_all, between, after):
    for step in range(STEPS):
        whole = [n for n in range(step * ITERS, (step + 1) * ITERS) if needed(layers, n) == 2 * layers]
        pairs = len(whole) // 2

        def pair(k, carry):
            n = step * ITERS + 2 * k
            sweep_all(n, 0, 2 * layers)
            sweep_all(n + 1, 1, 2 * layers)
            return carry

        if pairs:
            lax.fori_loop(0, pairs, pair, 0)
        for n in range(step * ITERS + 2 * pairs, (step + 1) * ITERS):
            sweep_all(n, n % 2, needed(layers, n))
        after(step)
        if step < STEPS - 1:
            between()


PAD = 8


def tile_kernel(gx, gy, shape, *refs):
    layers, rows = shape
    own_ref, partner_ref, info_ref, out_ref, below_ref, level_ref = refs[:6]
    s_ref, va_ref, vb_ref = refs[6:9]
    coefs = refs[9:]
    x, y, z = (lax.axis_index(a) for a in ("gx", "gy", "gz"))
    total = 2 * layers + 2
    zeros = jnp.zeros((PAD, LANES), jnp.float32)
    for ref in (s_ref, va_ref, vb_ref):
        for i in range(total):
            ref[i, 0:PAD, :] = zeros
            ref[i, PAD + rows : PAD + rows + PAD, :] = zeros

    def field(f, i, here):
        j = f * (layers + 2)
        if i >= 2 * layers:
            j = j + i - layers
            return own_ref[j, here, :] + partner_ref[j, here, :]
        return own_ref[j + i, here, :] if i < layers else partner_ref[j + i - layers, here, :]

    for i in range(total):
        s_ref[i, PAD : PAD + rows, :] = field(0, i, slice(None))
        va_ref[i, PAD : PAD + rows, :] = field(2, i, slice(None))
    n = 8
    for at in range(0, rows, n):
        coefficients(s_ref, PAD + at, n, lambda f, i: field(f, i, slice(at, at + n)), coefs, at)

    bufs = (va_ref, vb_ref)
    sides = sides_of(gy, y)

    def sweep_all(number, which, count):
        src_ref, dst_ref = bufs[which], bufs[1 - which]
        for side, (above, _) in enumerate(sides):
            inner = pl.ds(PAD + inner_at(above, rows), HALO)
            for i in range(total):
                level_ref[(side * STEPS * ITERS + number) * total + i] = src_ref[i, inner, :]
        for at in range(0, rows, n):
            sweep(src_ref, dst_ref, PAD + at, n, count, coefs, at)

    holder, layer, row = (info_ref[:, j : j + 1].astype(jnp.int32) for j in range(3))
    spoilt = None
    for above, live in sides:
        part = jnp.logical_and(row // HALO == edge_at(above, rows) // HALO, live)
        spoilt = part if spoilt is None else jnp.logical_or(spoilt, part)
    cell = jnp.where(jnp.logical_and(holder == x, jnp.logical_not(spoilt)), layer * rows + row, -1)
    picks = as_onehot(lax.broadcasted_iota(jnp.int32, (cell.shape[0], layers * rows), 1) == cell)

    def after(step):
        last = step == STEPS - 1
        for at in range(0, rows, n):
            meet(va_ref, PAD + at, n, layers if last else 2 * layers, not last)
        heat = []
        for i in range(layers):
            here = pl.ds(PAD, rows)
            heat.append(va_ref[i, here, :] / s_ref[i, here, :])
            if step == STEPS - 1:
                out_ref[flip(z, layers, i)] = heat[-1]
        below_ref[step] = exact_dot(picks, jnp.concatenate(heat, axis=0))

    def between():
        for at in range(0, rows, n):
            next_rhs(coefs, va_ref, PAD + at, n, at)

    two_steps(layers, sweep_all, between, after)


def edge_kernel(gx, gy, shape, seg, *refs):
    layers, rows = shape
    own_ref, partner_ref, info_ref, segments_ref, below_ref, level_ref = refs[:6]
    sides_n = 1 if gy == 2 else 2
    along, across = refs[6 : 6 + sides_n], refs[6 + sides_n : 6 + 2 * sides_n]
    refs = refs[6 + 2 * sides_n :]
    heat_ref, returns = refs[0], refs[1 : 1 + gx]
    ret_ref, s_ref, va_ref, vb_ref = refs[1 + gx : 5 + gx]
    coefs = refs[5 + gx :]
    x, y, z = (lax.axis_index(a) for a in ("gx", "gy", "gz"))
    total = 2 * layers + 2
    count = info_ref.shape[0]
    holder, layer, row = (info_ref[:, j : j + 1].astype(jnp.int32) for j in range(3))
    below = [below_ref[step] for step in range(STEPS)]
    lane = lane_of(HALO)
    low = lane < LANES // 2
    bufs = (va_ref, vb_ref)

    def tile(j):
        return pl.ds(j if isinstance(j, int) else pl.multiple_of(j, HALO), HALO)

    for side, (above, live) in enumerate(sides_of(gy, y)):
        def place(when_top, otherwise):
            if above is True or above is False:
                return when_top * HALO if above else otherwise * HALO
            return jnp.where(above, when_top * HALO, otherwise * HALO)

        outer, strip, edge, inner = place(0, 3), place(1, 2), place(2, 1), place(3, 0)
        edge_rows = tile(edge_at(above, rows))
        inner_rows = tile(inner_at(above, rows))

        def field(f, i, here):
            j = f * (layers + 2)
            if i >= 2 * layers:
                j = j + i - layers
                return own_ref[j, here, :] + partner_ref[j, here, :]
            return own_ref[j + i, here, :] if i < layers else partner_ref[j + i - layers, here, :]

        t_ref, d_ref, q_ref, e_ref, g_ref = coefs[1], coefs[0], coefs[2], coefs[3], coefs[4]
        keep = {0: s_ref, 1: t_ref, 2: va_ref, 3: d_ref, 4: q_ref, 5: e_ref, 6: g_ref}
        zeros = jnp.zeros((HALO, LANES), jnp.float32)
        src = lane % (LANES // 2)
        turned = (layers - 1 - src // GROUP) * GROUP + src % GROUP
        for f in range(FIELDS):
            for i in range(total):
                if i < 2 * layers:
                    ref, j = (along[side], i) if i < layers else (across[side], 2 * layers - 1 - i)
                    at = (f * layers + j) * HALO
                    value = ref[at : at + HALO, :]
                else:
                    at = FIELDS * layers * HALO + f * HALO
                    half = (LANES // 2) * (i - 2 * layers)
                    a = take(along[side][at : at + HALO, :], src + half)
                    b = take(across[side][at : at + HALO, :], turned + half)
                    value = jnp.where(low, a, b)
                ref, shift = keep[f], 0 if f in (0, 2) else HALO
                ref[i, tile(strip - shift), :] = value
                ref[i, tile(edge - shift), :] = field(f, i, edge_rows)
        for i in range(total):
            s_ref[i, tile(outer), :] = zeros
            va_ref[i, tile(outer), :] = zeros
            vb_ref[i, tile(outer), :] = zeros
            s_ref[i, tile(inner), :] = field(0, i, inner_rows)
        n = 2 * HALO
        held = [[keep[f][i, pl.ds(0, n), :] for i in range(total)] if f in (1, 3, 4, 5, 6) else None for f in range(FIELDS)]
        coefficients(s_ref, HALO, n, lambda f, i: held[f][i], coefs, 0)

        def sweep_all(number, which, needed_layers):
            src_ref, dst_ref = bufs[which], bufs[1 - which]
            for i in range(total):
                src_ref[i, tile(inner), :] = level_ref[(side * STEPS * ITERS + number) * total + i]
            sweep(src_ref, dst_ref, HALO, n, needed_layers, coefs, 0)

        first = edge_at(above, rows)
        hit = jnp.logical_and(jnp.logical_and(holder == x, row // HALO == first // HALO), live)
        cell = jnp.where(hit, layer * HALO + row - first, -1)
        picks = as_onehot(lax.broadcasted_iota(jnp.int32, (count, LANES), 1) == cell)

        def after(step):
            last = step == STEPS - 1
            meet(va_ref, HALO, n, layers if last else 2 * layers, not last)
            heat = []
            for i in range(layers):
                heat.append(va_ref[i, tile(edge), :] / s_ref[i, tile(edge), :])
                if step == STEPS - 1:
                    heat_ref[side * layers + flip(z, layers, i)] = heat[-1]
            heat.append(jnp.zeros((LANES - layers * HALO, LANES), jnp.float32))
            below[step] = below[step] + exact_dot(picks, jnp.concatenate(heat, axis=0))

        two_steps(layers, sweep_all, lambda: next_rhs(coefs, va_ref, HALO, n, 0), after)

    coef, warmth = segments_ref[:count, :], segments_ref[count:, :]
    for step in range(STEPS):
        warmth = warmth + coolant_gain * coef * (below[step] - warmth)
    ret_ref[...] = jnp.where(holder == x, warmth, 0.0)
    for k, ref in enumerate(returns):
        ref[...] = ret_ref[pl.ds(pl.multiple_of(lax.rem(x + k, gx) * seg, seg), seg), :]


def merge_kernel(gy, whole_ref, heat_ref, out_ref):
    layers, rows, _ = whole_ref.shape
    out_ref[...] = whole_ref[...]
    for side, (above, live) in enumerate(sides_of(gy, lax.axis_index("gy"))):
        def put(side=side, above=above):
            out_ref[:, pl.ds(edge_at(above, rows), HALO), :] = heat_ref[side * layers : (side + 1) * layers]

        if live is True:
            put()
        else:
            pl.when(live)(put)


def local(gx, gy, gz, u, power, storage, conductance, warmth, coef, holder, stratum, transverse):
    layers, rows, columns = u.shape
    seg = warmth.shape[1]
    segments = stratum.shape[1]
    if gz != 2 or gx < 4 or gx & (gx - 1) or columns != LANES or 2 * layers * GROUP != LANES or rows % 32:
        raise ValueError("unsupported shape")
    holder = holder[:, :, 0]
    shape = (layers, rows)
    f32 = jnp.float32
    chunk = rows // 4
    wide = RAW * chunk + 2 * seg

    def struct(*dims):
        return jax.ShapeDtypeStruct(dims, f32)

    def vmem(*dims):
        return pltpu.VMEM(dims, f32)

    indices = (holder, stratum, transverse)
    flat = [a.reshape(-1, LANES) for a in (u, power, storage, conductance, warmth, coef)]
    own, to_even, to_odd, only, *indices = pl.pallas_call(
        functools.partial(pack_kernel, shape),
        out_shape=(
            struct(RAW * layers * rows + 2 * seg + 2 * RAW * chunk, LANES),
            struct(wide, LANES),
            struct(wide, LANES),
            struct(2 * seg, LANES),
            *(jax.ShapeDtypeStruct(a.shape, a.dtype) for a in indices),
        ),
        in_specs=[pl.BlockSpec(memory_space=pltpu.HBM)] * 9,
        out_specs=(VMEM,) * 7,
        scratch_shapes=[pltpu.SemaphoreType.DMA((9,))],
        compiler_params=PARAMS,
        name="pack",
    )(*(pltpu.with_memory_space_constraint(a, pltpu.HBM) for a in (*flat, *indices)))

    swap = [(0, 1), (1, 0)]
    partner = lax.ppermute(own, "gz", swap)
    even = [(i, i ^ 1) for i in range(gx)]
    odd = [pair for i in range(1, gx - 1, 2) for pair in ((i, i + 1), (i + 1, i))]
    received = [lax.ppermute(to_even, "gx", even), lax.ppermute(to_odd, "gx", odd)]
    far = {}
    for k in range(2, gx):
        far[k] = lax.ppermute(only, "gx", [(i, i ^ k) for i in range(gx) if abs(i - (i ^ k)) > 1])
    received += [far[k] for k in range(2, gx)]
    late = lax.ppermute(jnp.concatenate(received, axis=0), "gz", swap)

    sides = 1 if gy == 2 else 2
    fields = struct(FIELDS * (layers + 2), rows, LANES)
    strip_rows = FIELDS * (layers + 1) * HALO
    filled = pl.pallas_call(
        functools.partial(fill_kernel, False, gx, gy, shape, seg),
        out_shape=(fields,) + (struct(strip_rows, LANES),) * sides + (struct(segments, 8), struct(2 * segments, LANES)),
        in_specs=[VMEM] * (4 + gx),
        out_specs=(VMEM,) * (3 + sides),
        compiler_params=PARAMS,
        cost_estimate=cost(1.5),
        name="fill_own",
    )(own, *indices, *received)
    own_fields, strips, (info, held) = filled[0], filled[1 : 1 + sides], filled[1 + sides :]
    if gy == 2:
        routes = [(strips[0], swap)]
    else:
        up = [(i, i + 1) for i in range(gy - 1)]
        routes = [(strips[1], up), (strips[0], [(j, i) for i, j in up])]
    along = [lax.ppermute(value, "gy", pairs) for value, pairs in routes]
    across = []
    for value, pairs in routes:
        both = [(2 * i + z, 2 * j + 1 - z) for i, j in pairs for z in range(2)]
        across.append(lax.ppermute(value, ("gy", "gz"), both))

    partner_fields = pl.pallas_call(
        functools.partial(fill_kernel, True, gx, gy, shape, seg),
        out_shape=fields,
        in_specs=[VMEM] * 5,
        out_specs=VMEM,
        scratch_shapes=[vmem(segments, LANES)] * 2,
        compiler_params=PARAMS,
        cost_estimate=cost(1.5),
        name="fill_partner",
    )(partner, *indices, late)

    total = 2 * layers + 2
    padded = vmem(total, rows + 2 * PAD, LANES)
    inside, below, levels = pl.pallas_call(
        functools.partial(tile_kernel, gx, gy, shape),
        out_shape=(
            struct(layers, rows, LANES),
            struct(STEPS, segments, LANES),
            struct(sides * STEPS * ITERS * total, HALO, LANES),
        ),
        in_specs=[VMEM] * 3,
        out_specs=(VMEM,) * 3,
        scratch_shapes=[padded] * 3 + [vmem(total, rows, LANES)] * 5,
        compiler_params=PARAMS,
        cost_estimate=cost(7),
        name="tile_sweeps",
    )(own_fields, partner_fields, info)

    results = pl.pallas_call(
        functools.partial(edge_kernel, gx, gy, shape, seg),
        out_shape=(struct(sides * layers, HALO, LANES),) + (struct(seg, LANES),) * gx,
        in_specs=[VMEM] * (6 + 2 * sides),
        out_specs=(VMEM,) * (1 + gx),
        scratch_shapes=[vmem(segments, LANES)]
        + [vmem(total, 4 * HALO, LANES)] * 3
        + [vmem(total, 2 * HALO, LANES)] * 5,
        compiler_params=PARAMS,
        cost_estimate=cost(1.5),
        name="edge_sweeps",
    )(own_fields, partner_fields, info, held, below, levels, *along, *across)
    heat, coolant = results[0], results[1]
    returned = [lax.ppermute(results[1 + k], "gx", [(i, (i + k) % gx) for i in range(gx)]) for k in range(1, gx)]
    temperature = pl.pallas_call(
        functools.partial(merge_kernel, gy),
        out_shape=struct(layers, rows, LANES),
        in_specs=[VMEM] * 2,
        out_specs=VMEM,
        compiler_params=PARAMS,
        cost_estimate=cost(1),
        name="merge",
    )(inside, heat)
    for value in returned:
        coolant = coolant + value
    return temperature, coolant[None]


def solution(mesh):
    gx, gy, gz = (mesh.shape[a] for a in ("gx", "gy", "gz"))
    cells = P(("stack", "gz"), "gy", "gx")
    segments = P(("stack", "gy", "gz"), "gx", None)
    return jax.shard_map(
        functools.partial(local, gx, gy, gz),
        mesh=mesh,
        in_specs=(cells, cells, cells, P(None, ("stack", "gz"), "gy", "gx"), segments, segments, P(), P(), P()),
        out_specs=(cells, segments),
        check_vma=False,
    )
```

```python
import functools

import jax
import jax.numpy as jnp
from jax import lax
from jax.experimental import pallas as pl
from jax.experimental.pallas import tpu as pltpu
from jax.sharding import PartitionSpec as P

STEPS = 2
ITERS = 4
HALO = STEPS * ITERS
GROUP = 2 * HALO
LANES = 128
RAW = 5
FIELDS = 7
coolant_gain = 0.5

VMEM = pl.BlockSpec(memory_space=pltpu.VMEM)
PARAMS = pltpu.CompilerParams(vmem_limit_bytes=40 * 1024 * 1024)


def cost(microseconds):
    return pl.CostEstimate(flops=0, bytes_accessed=int(microseconds * 3e6), transcendentals=0)


def lane_of(rows):
    return lax.broadcasted_iota(jnp.int32, (rows, LANES), 1)


def take(value, index):
    return jnp.take_along_axis(value, index, axis=1, mode="promise_in_bounds")


def edge_columns(rows, turned):
    j = lane_of(rows) % GROUP
    first = j < HALO
    return jnp.where(first, LANES - HALO + j, j - HALO) if not turned else jnp.where(first, j, LANES - GROUP + j)


def split(value):
    high = value.astype(jnp.bfloat16)
    low = (value - high.astype(jnp.float32)).astype(jnp.bfloat16)
    return high, low


def exact_dot(onehot, value):
    high, low = split(value)
    both = jnp.concatenate([high, low], axis=0)
    return jnp.dot(jnp.concatenate([onehot, onehot], axis=1), both, preferred_element_type=jnp.float32)


def coupling(coef, warmth):
    flow = coef * warmth
    second = coolant_gain * coef * coef
    return jnp.concatenate([coef, flow, second, flow - second * warmth], axis=1)


def flip(z, layers, i):
    return jnp.where(z == 0, i, layers - 1 - i)


def pack_kernel(shape, u_ref, p_ref, c_ref, k_ref, f_ref, x_ref, *refs):
    own_ref, left_ref, right_ref, seg_ref = refs[3:7]
    sems = refs[-1]
    layers, rows = shape
    seg = f_ref.shape[0]
    z = lax.axis_index("gz")
    plane = layers * rows
    copies = []

    def fetch(src, dst):
        copies.append(pltpu.make_async_copy(src, dst, sems.at[len(copies)]))
        copies[-1].start()

    fetch(k_ref, own_ref.at[pl.ds(0, 2 * plane), :])
    for field, ref in enumerate((u_ref, p_ref, c_ref), 2):
        fetch(ref, own_ref.at[pl.ds(field * plane, plane), :])
    for j, ref in enumerate((x_ref, f_ref)):
        fetch(ref, own_ref.at[pl.ds(RAW * plane + j * seg, seg), :])
    for table, place in zip(refs[:3], refs[7:10]):
        fetch(table, place)
    copies[0].wait()
    roots = pl.ds(0, 2 * plane)
    own_ref[roots, :] = jnp.sqrt(own_ref[roots, :])
    for copy in copies[1:]:
        copy.wait()
    chunk = rows // 4
    lane = lane_of(chunk)
    first = lane % GROUP < HALO
    near, far = edge_columns(chunk, False), edge_columns(chunk, True)
    for part in range(RAW):
        even = jnp.zeros((chunk, LANES), jnp.float32)
        odd = even
        for h in range(2):
            for i in range(layers):
                here = lane // GROUP == h * layers + i
                src = flip(z, layers, i)
                for side in range(2):
                    g = 2 * h + side
                    field, at = (g, part * chunk) if part < 4 else (4, g * chunk)
                    block = own_ref[pl.ds(pl.multiple_of((field * layers + src) * rows + at, chunk), chunk), :]
                    if side == 0:
                        even = jnp.where(here, take(block, near), even)
                    else:
                        odd = jnp.where(here, take(block, far), odd)
        left_ref[part * chunk : (part + 1) * chunk, :] = jnp.where(first, odd, even)
        right_ref[part * chunk : (part + 1) * chunk, :] = jnp.where(first, even, odd)
        at = RAW * plane + 2 * seg + part * chunk
        own_ref[at : at + chunk, :] = even
        own_ref[at + RAW * chunk : at + (RAW + 1) * chunk, :] = odd
    segments = own_ref[RAW * plane : RAW * plane + 2 * seg, :]
    seg_ref[...] = segments
    left_ref[RAW * chunk :, :] = segments
    right_ref[RAW * chunk :, :] = segments


class Strips:
    def __init__(self, refs, starts, cells_ref, start, rows, layers):
        self.refs, self.starts = refs, starts
        self.cells_ref, self.start = cells_ref, start
        self.rows, self.layers = rows, layers

    def both(self, field, start, n, x, gx, partner):
        chunk = self.rows // 4
        if field < 4:
            g, at = field, start
        else:
            g, at = start // chunk, 4 * chunk + start % chunk
        a, b = (ref[at + begin : at + begin + n, :] for ref, begin in zip(self.refs, self.starts))
        at = self.start + (g % 2) * RAW * chunk + at
        inside = self.cells_ref[at : at + n, :]
        from_left, from_right = jnp.where(x > 0, b, 0.0), jnp.where(x < gx - 1, a, 0.0)
        lane = lane_of(n)
        first = (lane % GROUP < HALO) if g % 2 == 0 else (lane % GROUP >= HALO)
        half = self.layers * GROUP
        src = lane % half
        if partner:
            src = (self.layers - 1 - src // GROUP) * GROUP + src % GROUP
        if g % 2 == 1:
            src = jnp.where(src % GROUP < HALO, src + HALO, src - HALO)
        src = src + half * (g // 2)
        return take(jnp.where(first, from_left, inside), src), take(jnp.where(first, inside, from_right), src)


def place_segments(x, gx, seg, coef_ref, warmth_ref, sources):
    for k, ref, at in sources:
        place = pl.ds(pl.multiple_of(lax.rem(x + k, gx) * seg, seg), seg)
        coef_ref[place, :] = ref[at : at + seg, :]
        warmth_ref[place, :] = ref[at + seg : at + 2 * seg, :]


def tables(z, group, layers, holder_ref, stratum_ref, transverse_ref):
    holder = holder_ref[pl.ds(group, 1), :]
    layer = stratum_ref[pl.ds(group, 1), :]
    layer = jnp.where(z == 0, layer, layers - 1 - layer)
    row = transverse_ref[pl.ds(group, 1), :]
    n = holder.shape[1]
    which = lax.broadcasted_iota(jnp.int32, (8, n), 0)
    stacked = jnp.where(which == 0, holder, jnp.where(which == 1, layer, row))
    eye = lax.broadcasted_iota(jnp.int32, (n, n), 0) == lax.broadcasted_iota(jnp.int32, (n, n), 1)
    columns = lax.dot_general(
        eye.astype(jnp.float32).astype(jnp.bfloat16),
        stacked.astype(jnp.float32).astype(jnp.bfloat16),
        (((1,), (1,)), ((), ())),
        preferred_element_type=jnp.float32,
    )
    return (holder, layer, row), columns


def as_onehot(mask):
    return jnp.where(mask, 1.0, 0.0).astype(jnp.bfloat16)


def edge_segments(coef, warmth, columns, base, x):
    n = coef.shape[0]
    lane = lane_of(n)
    first = lane % GROUP < HALO
    holder, layer = columns[:, 0:1].astype(jnp.int32), columns[:, 1:2].astype(jnp.int32)
    here = lane // GROUP == layer + base
    near = edge_columns(n, False)
    coef, warmth = take(coef, near), take(warmth, near)
    sides = []
    for begin in (x - 1, x):
        mine = jnp.logical_and(here, holder == jnp.where(first, begin, begin + 1))
        sides.append(coupling(jnp.where(mine, coef, 0.0), warmth))
    return sides


def combine(raw, added):
    s, t, u, power, storage = raw
    wall, flow, second, later = (added[:, i * LANES : (i + 1) * LANES] for i in range(4))
    return s, t, s * u, storage + wall, power + storage * u + flow, power + later, storage + second


def lengths_of(gx, chunk, seg):
    return [RAW * chunk + 2 * seg] * 2 + [2 * seg] * (gx - 3)


def edge_at(top, rows):
    return 0 if top is True else rows - HALO if top is False else pl.multiple_of(jnp.where(top, 0, rows - HALO), HALO)


def inner_at(top, rows):
    return HALO if top is True else rows - 2 * HALO if top is False else pl.multiple_of(jnp.where(top, HALO, rows - 2 * HALO), HALO)


def sides_of(gy, y):
    return [(y == 1, True)] if gy == 2 else [(True, y > 0), (False, y < gy - 1)]


def fill_kernel(partner, gx, gy, shape, seg, *refs):
    layers, rows = shape
    cells_ref, holder_ref, stratum_ref, transverse_ref = refs[:4]
    plane, chunk = layers * rows, rows // 4
    lengths = lengths_of(gx, chunk, seg)
    if partner:
        sources = [(refs[4], sum(lengths[:k])) for k in range(gx - 1)]
        refs = refs[5:]
    else:
        sources = [(ref, 0) for ref in refs[4 : 4 + gx - 1]]
        refs = refs[4 + gx - 1 :]
    sides = 1 if gy == 2 else 2
    out_ref = refs[0]
    if partner:
        coef_ref, warmth_ref = refs[1:3]
    else:
        strip_refs, info_ref, segments_ref = refs[1 : 1 + sides], refs[1 + sides], refs[2 + sides]
        n = segments_ref.shape[0] // 2
        coef_ref, warmth_ref = segments_ref.at[pl.ds(0, n), :], segments_ref.at[pl.ds(n, n), :]
    x, y, z = (lax.axis_index(a) for a in ("gx", "gy", "gz"))
    base = layers if partner else 0
    distances = [1, gx - 1] + list(range(2, gx - 1))
    held = [(k, ref, at + (RAW * chunk if j < 2 else 0)) for j, (k, (ref, at)) in enumerate(zip(distances, sources))]
    place_segments(x, gx, seg, coef_ref, warmth_ref, [(0, cells_ref, RAW * plane)] + held)
    group = y * 2 + ((1 - z) if partner else z)
    (holder, layer, row), columns = tables(z, group, layers, holder_ref, stratum_ref, transverse_ref)
    coef, warmth = coef_ref[...], warmth_ref[...]
    n = coef.shape[0]
    if not partner:
        info_ref[...] = columns

    cell = jnp.where(holder == x, layer * rows + row, -1)
    line = lax.broadcasted_iota(jnp.int32, (plane, n), 0)
    added = exact_dot(as_onehot(line == cell), coupling(coef, warmth))
    line = as_onehot(lax.broadcasted_iota(jnp.int32, (rows, n), 0) == row)
    beside = [exact_dot(line, side) for side in edge_segments(coef, warmth, columns, base, x)]
    planes = layers + 2
    for i in range(layers):
        src = flip(z, layers, i)
        raw = [cells_ref[pl.ds(pl.multiple_of((f * layers + src) * rows, rows), rows), :] for f in range(RAW)]
        for f, value in enumerate(combine(raw, added[i * rows : (i + 1) * rows])):
            out_ref[f * planes + i] = value
    strips = Strips(
        [ref for ref, _ in sources[:2]], [at for _, at in sources[:2]], cells_ref, RAW * plane + 2 * seg, rows, layers
    )
    half = lane_of(chunk) // (LANES // 2) == (1 if partner else 0)
    for part in range(4):
        here = slice(part * chunk, (part + 1) * chunk)
        raw = [strips.both(f, part * chunk, chunk, x, gx, partner) for f in range(RAW)]
        for side in range(2):
            cells = [jnp.where(half, value[side], 0.0) for value in raw]
            for f, value in enumerate(combine(cells, beside[side][here])):
                out_ref[f * planes + layers + side, here, :] = value
    if partner:
        return
    low = lane_of(HALO) < LANES // 2
    upper = lax.broadcasted_iota(jnp.int32, (HALO, LANES), 0) < HALO // 2
    sent = FIELDS - 1
    for strip_ref, (top, _) in zip(strip_refs, sides_of(gy, y)):
        edge = pl.ds(edge_at(top, rows), HALO)

        def give(j, values):
            *whole, e, g = values
            e = jnp.where(top, e, pltpu.roll(e, HALO // 2, 0))
            g = jnp.where(top, pltpu.roll(g, HALO // 2, 0), g)
            for f, value in enumerate(whole + [jnp.where(upper, e, g)]):
                at = (j * sent + f) * HALO
                strip_ref[at : at + HALO, :] = value

        for i in range(layers):
            give(i, [out_ref[f * planes + i, edge, :] for f in range(FIELDS)])
        values = []
        for f in range(FIELDS):
            left, right = (out_ref[f * planes + layers + side, edge, :] for side in range(2))
            values.append(jnp.where(low, left, pltpu.roll(right, LANES // 2, 1)))
        give(layers, values)


def planes_of(count, total):
    return list(range(count)) + [total - 2, total - 1]


def lateral(buf, at, n, which):
    sums = []
    for i in which:
        centre = buf[i, pl.ds(at, n), :]
        beside = pltpu.roll(centre, 1, 1) + pltpu.roll(centre, LANES - 1, 1)
        sums.append(beside + (buf[i, pl.ds(at - 1, n), :] + buf[i, pl.ds(at + 1, n), :]))
    return sums


def vertical(planes, edges, count):
    sums = []
    for i in range(count):
        near = [planes[j] for j in (i - 1, i + 1) if 0 <= j < len(planes)]
        sums.append(functools.reduce(jnp.add, near))
    for edge in edges:
        lane = lane_of(edge.shape[0])
        up = jnp.where(lane >= GROUP, pltpu.roll(edge, GROUP, 1), 0.0)
        down = jnp.where(lane < LANES - GROUP, pltpu.roll(edge, LANES - GROUP, 1), 0.0)
        sums.append(up + down)
    return sums


def coefficients(s_ref, at, n, raw, dests, to):
    a_ref, q_ref, r_ref, e_ref, g_ref = dests
    total = s_ref.shape[0]
    sums = lateral(s_ref, at, n, range(total))
    t = [raw(1, i) for i in range(total)]
    above = vertical(t[:-2], t[-2:], total - 2)
    here = pl.ds(to, n)
    for i in range(total):
        s = s_ref[i, pl.ds(at, n), :]
        diag = raw(3, i) + s * sums[i] + t[i] * above[i]
        inverse = 1.0 / jnp.where(diag > 0.0, diag, 1.0)
        scaled = s * inverse
        a_ref[i, here, :] = s * scaled
        r_ref[i, here, :] = raw(4, i) * scaled
        e_ref[i, here, :] = raw(5, i) * scaled
        g_ref[i, here, :] = raw(6, i) * inverse
        q_ref[i, here, :] = t[i] * jnp.where(s > 0.0, 1.0 / jnp.where(s > 0.0, s, 1.0), 0.0)


def sweep(src_ref, dst_ref, at, n, count, coefs, base):
    a_ref, q_ref, r_ref = coefs[:3]
    total = src_ref.shape[0]
    here, there = pl.ds(base, n), pl.ds(at, n)
    which = planes_of(count, total)
    sums = lateral(src_ref, at, n, which)
    scaled = [q_ref[i, here, :] * src_ref[i, there, :] for i in planes_of(min(count + 1, total - 2), total)]
    above = vertical(scaled[:-2], scaled[-2:], count)
    for j, i in enumerate(which):
        dst_ref[i, there, :] = r_ref[i, here, :] + a_ref[i, here, :] * (sums[j] + q_ref[i, here, :] * above[j])


def next_rhs(coefs, v_ref, at, n, base):
    r_ref, e_ref, g_ref = coefs[2:]
    here = pl.ds(base, n)
    for i in range(v_ref.shape[0]):
        r_ref[i, here, :] = e_ref[i, here, :] + g_ref[i, here, :] * v_ref[i, pl.ds(at, n), :]


def meet(v_ref, at, n, count, back):
    total = v_ref.shape[0]
    here = pl.ds(at, n)
    lane = lane_of(n)
    j, group = lane % GROUP, lane // GROUP
    outer = jnp.logical_or(lane < ITERS, lane >= LANES - ITERS)
    left, right = v_ref[total - 2, here, :], v_ref[total - 1, here, :]
    middle = jnp.where(j < HALO, right, left)
    for i in range(count):
        value = v_ref[i, here, :]
        if back:
            moved = pltpu.roll(value, (i * GROUP + HALO) % LANES, 1)
            left = jnp.where(jnp.logical_and(group == i, j >= GROUP - ITERS), moved, left)
            right = jnp.where(jnp.logical_and(group == i, j < ITERS), moved, right)
        v_ref[i, here, :] = jnp.where(outer, pltpu.roll(middle, LANES - (i * GROUP + HALO), 1), value)
    if back:
        v_ref[total - 2, here, :] = left
        v_ref[total - 1, here, :] = right


def needed(layers, n):
    return min(2 * layers, layers + STEPS * ITERS - 1 - n)


def two_steps(layers, sweep_all, between, after, every=False):
    for step in range(STEPS):
        whole = [n for n in range(step * ITERS, (step + 1) * ITERS) if every or needed(layers, n) == 2 * layers]
        pairs = len(whole) // 2

        def pair(k, carry):
            n = step * ITERS + 2 * k
            sweep_all(n, 0, 2 * layers)
            sweep_all(n + 1, 1, 2 * layers)
            return carry

        if pairs:
            lax.fori_loop(0, pairs, pair, 0)
        for n in range(step * ITERS + 2 * pairs, (step + 1) * ITERS):
            sweep_all(n, n % 2, needed(layers, n))
        after(step)
        if step < STEPS - 1:
            between()


PAD = 8


def tile_kernel(gx, gy, shape, *refs):
    layers, rows = shape
    own_ref, partner_ref, info_ref, out_ref, below_ref, level_ref = refs[:6]
    s_ref, va_ref, vb_ref = refs[6:9]
    coefs = refs[9:]
    x, y, z = (lax.axis_index(a) for a in ("gx", "gy", "gz"))
    total = 2 * layers + 2
    zeros = jnp.zeros((PAD, LANES), jnp.float32)
    for ref in (s_ref, va_ref, vb_ref):
        for i in range(total):
            ref[i, 0:PAD, :] = zeros
            ref[i, PAD + rows : PAD + rows + PAD, :] = zeros

    def field(f, i, here):
        j = f * (layers + 2)
        if i >= 2 * layers:
            j = j + i - layers
            return own_ref[j, here, :] + partner_ref[j, here, :]
        return own_ref[j + i, here, :] if i < layers else partner_ref[j + i - layers, here, :]

    for i in range(total):
        s_ref[i, PAD : PAD + rows, :] = field(0, i, slice(None))
        va_ref[i, PAD : PAD + rows, :] = field(2, i, slice(None))
    n, block = 8, 32

    def each(body):
        def many(c, carry):
            for sub in range(0, block, n):
                body(pl.multiple_of(c * block, block) + sub)
            return carry

        lax.fori_loop(0, rows // block, many, 0)

    each(lambda at: coefficients(s_ref, PAD + at, n, lambda f, i: field(f, i, pl.ds(at, n)), coefs, at))

    bufs = (va_ref, vb_ref)
    sides = sides_of(gy, y)

    def sweep_all(number, which, count):
        src_ref, dst_ref = bufs[which], bufs[1 - which]
        for side, (above, _) in enumerate(sides):
            inner = pl.ds(PAD + inner_at(above, rows), HALO)
            for i in range(total):
                level_ref[(side * STEPS * ITERS + number) * total + i] = src_ref[i, inner, :]
        each(lambda at: sweep(src_ref, dst_ref, PAD + at, n, count, coefs, at))

    holder, layer, row = (info_ref[:, j : j + 1].astype(jnp.int32) for j in range(3))
    spoilt = None
    for above, live in sides:
        part = jnp.logical_and(row // HALO == edge_at(above, rows) // HALO, live)
        spoilt = part if spoilt is None else jnp.logical_or(spoilt, part)
    cell = jnp.where(jnp.logical_and(holder == x, jnp.logical_not(spoilt)), layer * rows + row, -1)
    picks = as_onehot(lax.broadcasted_iota(jnp.int32, (cell.shape[0], layers * rows), 1) == cell)

    def after(step):
        last = step == STEPS - 1
        each(lambda at: meet(va_ref, PAD + at, n, layers if last else 2 * layers, not last))
        heat = []
        for i in range(layers):
            here = pl.ds(PAD, rows)
            heat.append(va_ref[i, here, :] / s_ref[i, here, :])
            if step == STEPS - 1:
                out_ref[flip(z, layers, i)] = heat[-1]
        below_ref[step] = exact_dot(picks, jnp.concatenate(heat, axis=0))

    def between():
        each(lambda at: next_rhs(coefs, va_ref, PAD + at, n, at))

    two_steps(layers, sweep_all, between, after)


def edge_kernel(gx, gy, shape, seg, *refs):
    layers, rows = shape
    own_ref, partner_ref, info_ref, segments_ref, below_ref, level_ref = refs[:6]
    sides_n = 1 if gy == 2 else 2
    along, across = refs[6 : 6 + sides_n], refs[6 + sides_n : 6 + 2 * sides_n]
    refs = refs[6 + 2 * sides_n :]
    heat_ref, returns = refs[0], refs[1 : 1 + gx]
    ret_ref, s_ref, va_ref, vb_ref = refs[1 + gx : 5 + gx]
    coefs = refs[5 + gx :]
    x, y, z = (lax.axis_index(a) for a in ("gx", "gy", "gz"))
    total = 2 * layers + 2
    count = info_ref.shape[0]
    holder, layer, row = (info_ref[:, j : j + 1].astype(jnp.int32) for j in range(3))
    below = [below_ref[step] for step in range(STEPS)]
    lane = lane_of(HALO)
    low = lane < LANES // 2
    bufs = (va_ref, vb_ref)

    def tile(j):
        return pl.ds(j if isinstance(j, int) else pl.multiple_of(j, HALO), HALO)

    for side, (above, live) in enumerate(sides_of(gy, y)):
        def place(when_top, otherwise):
            if above is True or above is False:
                return when_top * HALO if above else otherwise * HALO
            return jnp.where(above, when_top * HALO, otherwise * HALO)

        outer, strip, edge, inner = place(0, 3), place(1, 2), place(2, 1), place(3, 0)
        edge_rows = tile(edge_at(above, rows))
        inner_rows = tile(inner_at(above, rows))

        def field(f, i, here):
            j = f * (layers + 2)
            if i >= 2 * layers:
                j = j + i - layers
                return own_ref[j, here, :] + partner_ref[j, here, :]
            return own_ref[j + i, here, :] if i < layers else partner_ref[j + i - layers, here, :]

        t_ref, d_ref, q_ref, e_ref, g_ref = coefs[1], coefs[0], coefs[2], coefs[3], coefs[4]
        keep = {0: s_ref, 1: t_ref, 2: va_ref, 3: d_ref, 4: q_ref, 5: e_ref, 6: g_ref}
        zeros = jnp.zeros((HALO, LANES), jnp.float32)
        src = lane % (LANES // 2)
        turned = (layers - 1 - src // GROUP) * GROUP + src % GROUP
        half_tile = lax.broadcasted_iota(jnp.int32, (HALO, LANES), 0) < HALO // 2

        def unpack(value, f):
            if f < FIELDS - 2:
                return value
            turned_value = pltpu.roll(value, HALO // 2, 0)
            if f == FIELDS - 2:
                at_top, at_bottom = jnp.where(half_tile, 0.0, turned_value), jnp.where(half_tile, value, 0.0)
            else:
                at_top, at_bottom = jnp.where(half_tile, 0.0, value), jnp.where(half_tile, turned_value, 0.0)
            return jnp.where(above, at_top, at_bottom)

        for f in range(FIELDS):
            g = min(f, FIELDS - 2)
            for i in range(total):
                if i < 2 * layers:
                    ref, j = (along[side], i) if i < layers else (across[side], 2 * layers - 1 - i)
                    at = (j * (FIELDS - 1) + g) * HALO
                    value = ref[at : at + HALO, :]
                else:
                    at = (layers * (FIELDS - 1) + g) * HALO
                    half = (LANES // 2) * (i - 2 * layers)
                    a = take(along[side][at : at + HALO, :], src + half)
                    b = take(across[side][at : at + HALO, :], turned + half)
                    value = jnp.where(low, a, b)
                ref, shift = keep[f], 0 if f in (0, 2) else HALO
                ref[i, tile(strip - shift), :] = unpack(value, f)
                ref[i, tile(edge - shift), :] = field(f, i, edge_rows)
        for i in range(total):
            s_ref[i, tile(outer), :] = zeros
            va_ref[i, tile(outer), :] = zeros
            vb_ref[i, tile(outer), :] = zeros
            s_ref[i, tile(inner), :] = field(0, i, inner_rows)
        n = 2 * HALO
        held = [[keep[f][i, pl.ds(0, n), :] for i in range(total)] if f in (1, 3, 4, 5, 6) else None for f in range(FIELDS)]
        coefficients(s_ref, HALO, n, lambda f, i: held[f][i], coefs, 0)

        def sweep_all(number, which, needed_layers):
            src_ref, dst_ref = bufs[which], bufs[1 - which]
            for i in range(total):
                src_ref[i, tile(inner), :] = level_ref[(side * STEPS * ITERS + number) * total + i]
            sweep(src_ref, dst_ref, HALO, n, needed_layers, coefs, 0)

        first = edge_at(above, rows)
        hit = jnp.logical_and(jnp.logical_and(holder == x, row // HALO == first // HALO), live)
        cell = jnp.where(hit, layer * HALO + row - first, -1)
        picks = as_onehot(lax.broadcasted_iota(jnp.int32, (count, LANES), 1) == cell)

        def after(step):
            last = step == STEPS - 1
            meet(va_ref, HALO, n, layers if last else 2 * layers, not last)
            heat = []
            for i in range(layers):
                heat.append(va_ref[i, tile(edge), :] / s_ref[i, tile(edge), :])
                if step == STEPS - 1:
                    heat_ref[side * layers + flip(z, layers, i)] = heat[-1]
            heat.append(jnp.zeros((LANES - layers * HALO, LANES), jnp.float32))
            below[step] = below[step] + exact_dot(picks, jnp.concatenate(heat, axis=0))

        two_steps(layers, sweep_all, lambda: next_rhs(coefs, va_ref, HALO, n, 0), after, every=True)

    coef, warmth = segments_ref[:count, :], segments_ref[count:, :]
    for step in range(STEPS):
        warmth = warmth + coolant_gain * coef * (below[step] - warmth)
    ret_ref[...] = jnp.where(holder == x, warmth, 0.0)
    for k, ref in enumerate(returns):
        ref[...] = ret_ref[pl.ds(pl.multiple_of(lax.rem(x + k, gx) * seg, seg), seg), :]


def merge_kernel(gy, whole_ref, heat_ref, out_ref):
    layers, rows, _ = whole_ref.shape
    out_ref[...] = whole_ref[...]
    for side, (above, live) in enumerate(sides_of(gy, lax.axis_index("gy"))):
        def put(side=side, above=above):
            out_ref[:, pl.ds(edge_at(above, rows), HALO), :] = heat_ref[side * layers : (side + 1) * layers]

        if live is True:
            put()
        else:
            pl.when(live)(put)


def local(gx, gy, gz, u, power, storage, conductance, warmth, coef, holder, stratum, transverse):
    layers, rows, columns = u.shape
    seg = warmth.shape[1]
    segments = stratum.shape[1]
    if gz != 2 or gx < 3 or columns != LANES or 2 * layers * GROUP != LANES or rows % 32:
        raise ValueError("unsupported shape")
    holder = holder[:, :, 0]
    shape = (layers, rows)
    f32 = jnp.float32
    chunk = rows // 4
    wide = RAW * chunk + 2 * seg

    def struct(*dims):
        return jax.ShapeDtypeStruct(dims, f32)

    def vmem(*dims):
        return pltpu.VMEM(dims, f32)

    indices = (holder, stratum, transverse)
    flat = [a.reshape(-1, LANES) for a in (u, power, storage, conductance, warmth, coef)]
    own, to_left, to_right, only, *indices = pl.pallas_call(
        functools.partial(pack_kernel, shape),
        out_shape=(
            struct(RAW * layers * rows + 2 * seg + 2 * RAW * chunk, LANES),
            struct(wide, LANES),
            struct(wide, LANES),
            struct(2 * seg, LANES),
            *(jax.ShapeDtypeStruct(a.shape, a.dtype) for a in indices),
        ),
        in_specs=[pl.BlockSpec(memory_space=pltpu.HBM)] * 9,
        out_specs=(VMEM,) * 7,
        scratch_shapes=[pltpu.SemaphoreType.DMA((9,))],
        compiler_params=PARAMS,
        name="pack",
    )(*(pltpu.with_memory_space_constraint(a, pltpu.HBM) for a in (*flat, *indices)))

    swap = [(0, 1), (1, 0)]
    partner = lax.ppermute(own, "gz", swap)
    def from_distance(value, k):
        return lax.ppermute(value, "gx", [(i, (i - k) % gx) for i in range(gx)])

    received = [from_distance(to_left, 1), from_distance(to_right, gx - 1)]
    received += [from_distance(only, k) for k in range(2, gx - 1)]
    late = lax.ppermute(jnp.concatenate(received, axis=0), "gz", swap)

    sides = 1 if gy == 2 else 2
    fields = struct(FIELDS * (layers + 2), rows, LANES)
    strip_rows = (FIELDS - 1) * (layers + 1) * HALO
    filled = pl.pallas_call(
        functools.partial(fill_kernel, False, gx, gy, shape, seg),
        out_shape=(fields,) + (struct(strip_rows, LANES),) * sides + (struct(segments, 8), struct(2 * segments, LANES)),
        in_specs=[VMEM] * (4 + gx - 1),
        out_specs=(VMEM,) * (3 + sides),
        compiler_params=PARAMS,
        cost_estimate=cost(1.5),
        name="fill_own",
    )(own, *indices, *received)
    own_fields, strips, (info, held) = filled[0], filled[1 : 1 + sides], filled[1 + sides :]
    if gy == 2:
        routes = [(strips[0], swap)]
    else:
        up = [(i, i + 1) for i in range(gy - 1)]
        routes = [(strips[1], up), (strips[0], [(j, i) for i, j in up])]
    along = [lax.ppermute(value, "gy", pairs) for value, pairs in routes]
    across = []
    for value, pairs in routes:
        both = [(2 * i + z, 2 * j + 1 - z) for i, j in pairs for z in range(2)]
        across.append(lax.ppermute(value, ("gy", "gz"), both))

    partner_fields = pl.pallas_call(
        functools.partial(fill_kernel, True, gx, gy, shape, seg),
        out_shape=fields,
        in_specs=[VMEM] * 5,
        out_specs=VMEM,
        scratch_shapes=[vmem(segments, LANES)] * 2,
        compiler_params=PARAMS,
        cost_estimate=cost(1.5),
        name="fill_partner",
    )(partner, *indices, late)

    total = 2 * layers + 2
    padded = vmem(total, rows + 2 * PAD, LANES)
    inside, below, levels = pl.pallas_call(
        functools.partial(tile_kernel, gx, gy, shape),
        out_shape=(
            struct(layers, rows, LANES),
            struct(STEPS, segments, LANES),
            struct(sides * STEPS * ITERS * total, HALO, LANES),
        ),
        in_specs=[VMEM] * 3,
        out_specs=(VMEM,) * 3,
        scratch_shapes=[padded] * 3 + [vmem(total, rows, LANES)] * 5,
        compiler_params=PARAMS,
        cost_estimate=cost(7),
        name="tile_sweeps",
    )(own_fields, partner_fields, info)

    results = pl.pallas_call(
        functools.partial(edge_kernel, gx, gy, shape, seg),
        out_shape=(struct(sides * layers, HALO, LANES),) + (struct(seg, LANES),) * gx,
        in_specs=[VMEM] * (6 + 2 * sides),
        out_specs=(VMEM,) * (1 + gx),
        scratch_shapes=[vmem(segments, LANES)]
        + [vmem(total, 4 * HALO, LANES)] * 3
        + [vmem(total, 2 * HALO, LANES)] * 5,
        compiler_params=PARAMS,
        cost_estimate=cost(1.5),
        name="edge_sweeps",
    )(own_fields, partner_fields, info, held, below, levels, *along, *across)
    heat, coolant = results[0], results[1]
    returned = [lax.ppermute(results[1 + k], "gx", [(i, (i + k) % gx) for i in range(gx)]) for k in range(1, gx)]
    temperature = pl.pallas_call(
        functools.partial(merge_kernel, gy),
        out_shape=struct(layers, rows, LANES),
        in_specs=[VMEM] * 2,
        out_specs=VMEM,
        compiler_params=PARAMS,
        cost_estimate=cost(1),
        name="merge",
    )(inside, heat)
    for value in returned:
        coolant = coolant + value
    return temperature, coolant[None]


def solution(mesh):
    gx, gy, gz = (mesh.shape[a] for a in ("gx", "gy", "gz"))
    cells = P(("stack", "gz"), "gy", "gx")
    segments = P(("stack", "gy", "gz"), "gx", None)
    return jax.shard_map(
        functools.partial(local, gx, gy, gz),
        mesh=mesh,
        in_specs=(cells, cells, cells, P(None, ("stack", "gz"), "gy", "gx"), segments, segments, P(), P(), P()),
        out_specs=(cells, segments),
        check_vma=False,
    )
```

```python
import functools

import jax
import jax.numpy as jnp
from jax import lax
from jax.experimental import pallas as pl
from jax.experimental.pallas import tpu as pltpu
from jax.sharding import PartitionSpec as P

STEPS = 2
ITERS = 4
HALO = STEPS * ITERS
GROUP = 2 * HALO
LANES = 128
RAW = 5
FIELDS = 7
coolant_gain = 0.5

VMEM = pl.BlockSpec(memory_space=pltpu.VMEM)
PARAMS = pltpu.CompilerParams(vmem_limit_bytes=40 * 1024 * 1024)


def cost(microseconds):
    return pl.CostEstimate(flops=0, bytes_accessed=int(microseconds * 3e6), transcendentals=0)


def lane_of(rows):
    return lax.broadcasted_iota(jnp.int32, (rows, LANES), 1)


def take(value, index):
    return jnp.take_along_axis(value, index, axis=1, mode="promise_in_bounds")


def edge_columns(rows, turned):
    j = lane_of(rows) % GROUP
    first = j < HALO
    return jnp.where(first, LANES - HALO + j, j - HALO) if not turned else jnp.where(first, j, LANES - GROUP + j)


def split(value):
    high = value.astype(jnp.bfloat16)
    low = (value - high.astype(jnp.float32)).astype(jnp.bfloat16)
    return high, low


def exact_dot(onehot, value):
    high, low = split(value)
    both = jnp.concatenate([high, low], axis=0)
    return jnp.dot(jnp.concatenate([onehot, onehot], axis=1), both, preferred_element_type=jnp.float32)


def coupling(coef, warmth):
    flow = coef * warmth
    second = coolant_gain * coef * coef
    return jnp.concatenate([coef, flow, second, flow - second * warmth], axis=1)


def flip(z, layers, i):
    return jnp.where(z == 0, i, layers - 1 - i)


def pack_kernel(shape, u_ref, p_ref, c_ref, k_ref, f_ref, x_ref, *refs):
    own_ref, left_ref, right_ref, seg_ref = refs[3:7]
    sems = refs[-1]
    layers, rows = shape
    seg = f_ref.shape[0]
    z = lax.axis_index("gz")
    plane = layers * rows
    copies = []

    def fetch(src, dst):
        copies.append(pltpu.make_async_copy(src, dst, sems.at[len(copies)]))
        copies[-1].start()

    fetch(k_ref, own_ref.at[pl.ds(0, 2 * plane), :])
    for field, ref in enumerate((u_ref, p_ref, c_ref), 2):
        fetch(ref, own_ref.at[pl.ds(field * plane, plane), :])
    for j, ref in enumerate((x_ref, f_ref)):
        fetch(ref, own_ref.at[pl.ds(RAW * plane + j * seg, seg), :])
    for table, place in zip(refs[:3], refs[7:10]):
        fetch(table, place)
    chunk = rows // 4
    lane = lane_of(chunk)
    first = lane % GROUP < HALO
    columns = edge_columns(chunk, False), edge_columns(chunk, True)
    edges = RAW * plane + 2 * seg

    def gather(field, at, g):
        value = None
        for i in range(layers):
            start = pl.multiple_of((field * layers + flip(z, layers, i)) * rows + at, chunk)
            taken = take(own_ref[pl.ds(start, chunk), :], columns[g % 2])
            value = taken if value is None else jnp.where(lane // GROUP == (g // 2) * layers + i, taken, value)
        return value

    def place(g, part):
        return pl.ds(edges + ((g % 2) * RAW + part) * chunk, chunk)

    copies[0].wait()
    roots = pl.ds(0, 2 * plane)
    own_ref[roots, :] = jnp.sqrt(own_ref[roots, :])
    for field in range(4):
        if field >= 2:
            copies[field - 1].wait()
        for part in range(4):
            value = gather(field, part * chunk, field)
            if field >= 2:
                value = jnp.where(lane < LANES // 2, own_ref[place(field, part), :], value)
            own_ref[place(field, part), :] = value
    copies[3].wait()
    for g in range(4):
        value = gather(4, g * chunk, g)
        if g >= 2:
            value = jnp.where(lane < LANES // 2, own_ref[place(g, 4), :], value)
        own_ref[place(g, 4), :] = value
    for part in range(RAW):
        even, odd = own_ref[place(0, part), :], own_ref[place(1, part), :]
        left_ref[part * chunk : (part + 1) * chunk, :] = jnp.where(first, odd, even)
        right_ref[part * chunk : (part + 1) * chunk, :] = jnp.where(first, even, odd)
    for copy in copies[4:]:
        copy.wait()
    segments = own_ref[RAW * plane : RAW * plane + 2 * seg, :]
    seg_ref[...] = segments
    left_ref[RAW * chunk :, :] = segments
    right_ref[RAW * chunk :, :] = segments


class Strips:
    def __init__(self, refs, starts, cells_ref, start, rows, layers):
        self.refs, self.starts = refs, starts
        self.cells_ref, self.start = cells_ref, start
        self.rows, self.layers = rows, layers

    def both(self, field, start, n, x, gx, partner):
        chunk = self.rows // 4
        if field < 4:
            g, at = field, start
        else:
            g, at = start // chunk, 4 * chunk + start % chunk
        a, b = (ref[at + begin : at + begin + n, :] for ref, begin in zip(self.refs, self.starts))
        at = self.start + (g % 2) * RAW * chunk + at
        inside = self.cells_ref[at : at + n, :]
        from_left, from_right = jnp.where(x > 0, b, 0.0), jnp.where(x < gx - 1, a, 0.0)
        lane = lane_of(n)
        first = (lane % GROUP < HALO) if g % 2 == 0 else (lane % GROUP >= HALO)
        half = self.layers * GROUP
        src = lane % half
        if partner:
            src = (self.layers - 1 - src // GROUP) * GROUP + src % GROUP
        if g % 2 == 1:
            src = jnp.where(src % GROUP < HALO, src + HALO, src - HALO)
        src = src + half * (g // 2)
        return take(jnp.where(first, from_left, inside), src), take(jnp.where(first, inside, from_right), src)


def place_segments(x, gx, seg, coef_ref, warmth_ref, sources):
    for k, ref, at in sources:
        place = pl.ds(pl.multiple_of(lax.rem(x + k, gx) * seg, seg), seg)
        coef_ref[place, :] = ref[at : at + seg, :]
        warmth_ref[place, :] = ref[at + seg : at + 2 * seg, :]


def tables(z, group, layers, holder_ref, stratum_ref, transverse_ref):
    holder = holder_ref[pl.ds(group, 1), :]
    layer = stratum_ref[pl.ds(group, 1), :]
    layer = jnp.where(z == 0, layer, layers - 1 - layer)
    row = transverse_ref[pl.ds(group, 1), :]
    n = holder.shape[1]
    which = lax.broadcasted_iota(jnp.int32, (8, n), 0)
    stacked = jnp.where(which == 0, holder, jnp.where(which == 1, layer, row))
    eye = lax.broadcasted_iota(jnp.int32, (n, n), 0) == lax.broadcasted_iota(jnp.int32, (n, n), 1)
    columns = lax.dot_general(
        eye.astype(jnp.float32).astype(jnp.bfloat16),
        stacked.astype(jnp.float32).astype(jnp.bfloat16),
        (((1,), (1,)), ((), ())),
        preferred_element_type=jnp.float32,
    )
    return (holder, layer, row), columns


def as_onehot(mask):
    return jnp.where(mask, 1.0, 0.0).astype(jnp.bfloat16)


def edge_segments(coef, warmth, columns, base, x):
    n = coef.shape[0]
    lane = lane_of(n)
    first = lane % GROUP < HALO
    holder, layer = columns[:, 0:1].astype(jnp.int32), columns[:, 1:2].astype(jnp.int32)
    here = lane // GROUP == layer + base
    near = edge_columns(n, False)
    coef, warmth = take(coef, near), take(warmth, near)
    sides = []
    for begin in (x - 1, x):
        mine = jnp.logical_and(here, holder == jnp.where(first, begin, begin + 1))
        sides.append(coupling(jnp.where(mine, coef, 0.0), warmth))
    return sides


def combine(raw, added):
    s, t, u, power, storage = raw
    wall, flow, second, later = (added[:, i * LANES : (i + 1) * LANES] for i in range(4))
    return s, t, s * u, storage + wall, power + storage * u + flow, power + later, storage + second


def lengths_of(gx, chunk, seg):
    return [RAW * chunk + 2 * seg] * 2 + [2 * seg] * (gx - 3)


def edge_at(top, rows):
    return 0 if top is True else rows - HALO if top is False else pl.multiple_of(jnp.where(top, 0, rows - HALO), HALO)


def inner_at(top, rows):
    return HALO if top is True else rows - 2 * HALO if top is False else pl.multiple_of(jnp.where(top, HALO, rows - 2 * HALO), HALO)


def sides_of(gy, y):
    return [(y == 1, True)] if gy == 2 else [(True, y > 0), (False, y < gy - 1)]


def fill_kernel(partner, gx, gy, shape, seg, *refs):
    layers, rows = shape
    cells_ref, holder_ref, stratum_ref, transverse_ref = refs[:4]
    plane, chunk = layers * rows, rows // 4
    lengths = lengths_of(gx, chunk, seg)
    if partner:
        sources = [(refs[4], sum(lengths[:k])) for k in range(gx - 1)]
        refs = refs[5:]
    else:
        sources = [(ref, 0) for ref in refs[4 : 4 + gx - 1]]
        refs = refs[4 + gx - 1 :]
    sides = 1 if gy == 2 else 2
    out_ref = refs[0]
    if partner:
        coef_ref, warmth_ref = refs[1:3]
    else:
        strip_refs, info_ref, segments_ref = refs[1 : 1 + sides], refs[1 + sides], refs[2 + sides]
        n = segments_ref.shape[0] // 2
        coef_ref, warmth_ref = segments_ref.at[pl.ds(0, n), :], segments_ref.at[pl.ds(n, n), :]
    x, y, z = (lax.axis_index(a) for a in ("gx", "gy", "gz"))
    base = layers if partner else 0
    distances = [1, gx - 1] + list(range(2, gx - 1))
    held = [(k, ref, at + (RAW * chunk if j < 2 else 0)) for j, (k, (ref, at)) in enumerate(zip(distances, sources))]
    place_segments(x, gx, seg, coef_ref, warmth_ref, [(0, cells_ref, RAW * plane)] + held)
    group = y * 2 + ((1 - z) if partner else z)
    (holder, layer, row), columns = tables(z, group, layers, holder_ref, stratum_ref, transverse_ref)
    coef, warmth = coef_ref[...], warmth_ref[...]
    n = coef.shape[0]
    if not partner:
        info_ref[...] = columns

    cell = jnp.where(holder == x, layer * rows + row, -1)
    line = lax.broadcasted_iota(jnp.int32, (plane, n), 0)
    added = exact_dot(as_onehot(line == cell), coupling(coef, warmth))
    line = as_onehot(lax.broadcasted_iota(jnp.int32, (rows, n), 0) == row)
    beside = [exact_dot(line, side) for side in edge_segments(coef, warmth, columns, base, x)]
    planes = layers + 2
    for i in range(layers):
        src = flip(z, layers, i)
        raw = [cells_ref[pl.ds(pl.multiple_of((f * layers + src) * rows, rows), rows), :] for f in range(RAW)]
        for f, value in enumerate(combine(raw, added[i * rows : (i + 1) * rows])):
            out_ref[f * planes + i] = value
    strips = Strips(
        [ref for ref, _ in sources[:2]], [at for _, at in sources[:2]], cells_ref, RAW * plane + 2 * seg, rows, layers
    )
    half = lane_of(chunk) // (LANES // 2) == (1 if partner else 0)
    for part in range(4):
        here = slice(part * chunk, (part + 1) * chunk)
        raw = [strips.both(f, part * chunk, chunk, x, gx, partner) for f in range(RAW)]
        for side in range(2):
            cells = [jnp.where(half, value[side], 0.0) for value in raw]
            for f, value in enumerate(combine(cells, beside[side][here])):
                out_ref[f * planes + layers + side, here, :] = value
    if partner:
        return
    low = lane_of(HALO) < LANES // 2
    upper = lax.broadcasted_iota(jnp.int32, (HALO, LANES), 0) < HALO // 2
    sent = FIELDS - 1
    for strip_ref, (top, _) in zip(strip_refs, sides_of(gy, y)):
        edge = pl.ds(edge_at(top, rows), HALO)

        def give(j, values):
            *whole, e, g = values
            e = jnp.where(top, e, pltpu.roll(e, HALO // 2, 0))
            g = jnp.where(top, pltpu.roll(g, HALO // 2, 0), g)
            for f, value in enumerate(whole + [jnp.where(upper, e, g)]):
                at = (j * sent + f) * HALO
                strip_ref[at : at + HALO, :] = value

        for i in range(layers):
            give(i, [out_ref[f * planes + i, edge, :] for f in range(FIELDS)])
        values = []
        for f in range(FIELDS):
            left, right = (out_ref[f * planes + layers + side, edge, :] for side in range(2))
            values.append(jnp.where(low, left, pltpu.roll(right, LANES // 2, 1)))
        give(layers, values)


def planes_of(count, total):
    return list(range(count)) + [total - 2, total - 1]


def lateral(buf, at, n, which):
    sums = []
    for i in which:
        centre = buf[i, pl.ds(at, n), :]
        beside = pltpu.roll(centre, 1, 1) + pltpu.roll(centre, LANES - 1, 1)
        sums.append(beside + (buf[i, pl.ds(at - 1, n), :] + buf[i, pl.ds(at + 1, n), :]))
    return sums


def vertical(planes, edges, count):
    sums = []
    for i in range(count):
        near = [planes[j] for j in (i - 1, i + 1) if 0 <= j < len(planes)]
        sums.append(functools.reduce(jnp.add, near))
    for edge in edges:
        lane = lane_of(edge.shape[0])
        up = jnp.where(lane >= GROUP, pltpu.roll(edge, GROUP, 1), 0.0)
        down = jnp.where(lane < LANES - GROUP, pltpu.roll(edge, LANES - GROUP, 1), 0.0)
        sums.append(up + down)
    return sums


def coefficients(s_ref, at, n, raw, dests, to):
    a_ref, q_ref, r_ref, e_ref, g_ref = dests
    total = s_ref.shape[0]
    sums = lateral(s_ref, at, n, range(total))
    t = [raw(1, i) for i in range(total)]
    above = vertical(t[:-2], t[-2:], total - 2)
    here = pl.ds(to, n)
    for i in range(total):
        s = s_ref[i, pl.ds(at, n), :]
        diag = raw(3, i) + s * sums[i] + t[i] * above[i]
        inverse = 1.0 / jnp.where(diag > 0.0, diag, 1.0)
        scaled = s * inverse
        a_ref[i, here, :] = s * scaled
        r_ref[i, here, :] = raw(4, i) * scaled
        e_ref[i, here, :] = raw(5, i) * scaled
        g_ref[i, here, :] = raw(6, i) * inverse
        q_ref[i, here, :] = t[i] * jnp.where(s > 0.0, 1.0 / jnp.where(s > 0.0, s, 1.0), 0.0)


def sweep(src_ref, dst_ref, at, n, count, coefs, base):
    a_ref, q_ref, r_ref = coefs[:3]
    total = src_ref.shape[0]
    here, there = pl.ds(base, n), pl.ds(at, n)
    which = planes_of(count, total)
    sums = lateral(src_ref, at, n, which)
    scaled = [q_ref[i, here, :] * src_ref[i, there, :] for i in planes_of(min(count + 1, total - 2), total)]
    above = vertical(scaled[:-2], scaled[-2:], count)
    for j, i in enumerate(which):
        dst_ref[i, there, :] = r_ref[i, here, :] + a_ref[i, here, :] * (sums[j] + q_ref[i, here, :] * above[j])


def next_rhs(coefs, v_ref, at, n, base):
    r_ref, e_ref, g_ref = coefs[2:]
    here = pl.ds(base, n)
    for i in range(v_ref.shape[0]):
        r_ref[i, here, :] = e_ref[i, here, :] + g_ref[i, here, :] * v_ref[i, pl.ds(at, n), :]


def meet(v_ref, at, n, count, back):
    total = v_ref.shape[0]
    here = pl.ds(at, n)
    lane = lane_of(n)
    j, group = lane % GROUP, lane // GROUP
    outer = jnp.logical_or(lane < ITERS, lane >= LANES - ITERS)
    left, right = v_ref[total - 2, here, :], v_ref[total - 1, here, :]
    middle = jnp.where(j < HALO, right, left)
    for i in range(count):
        value = v_ref[i, here, :]
        if back:
            moved = pltpu.roll(value, (i * GROUP + HALO) % LANES, 1)
            left = jnp.where(jnp.logical_and(group == i, j >= GROUP - ITERS), moved, left)
            right = jnp.where(jnp.logical_and(group == i, j < ITERS), moved, right)
        v_ref[i, here, :] = jnp.where(outer, pltpu.roll(middle, LANES - (i * GROUP + HALO), 1), value)
    if back:
        v_ref[total - 2, here, :] = left
        v_ref[total - 1, here, :] = right


def needed(layers, n):
    return min(2 * layers, layers + STEPS * ITERS - 1 - n)


def two_steps(layers, sweep_all, between, after):
    for step in range(STEPS):
        whole = [n for n in range(step * ITERS, (step + 1) * ITERS) if needed(layers, n) == 2 * layers]
        pairs = len(whole) // 2

        def pair(k, carry):
            n = step * ITERS + 2 * k
            sweep_all(n, 0, 2 * layers)
            sweep_all(n + 1, 1, 2 * layers)
            return carry

        if pairs:
            lax.fori_loop(0, pairs, pair, 0)
        for n in range(step * ITERS + 2 * pairs, (step + 1) * ITERS):
            sweep_all(n, n % 2, needed(layers, n))
        after(step)
        if step < STEPS - 1:
            between()


PAD = 8


def tile_kernel(gx, gy, shape, *refs):
    layers, rows = shape
    own_ref, partner_ref, info_ref, out_ref, below_ref, level_ref = refs[:6]
    s_ref, va_ref, vb_ref = refs[6:9]
    coefs = refs[9:]
    x, y, z = (lax.axis_index(a) for a in ("gx", "gy", "gz"))
    total = 2 * layers + 2
    zeros = jnp.zeros((PAD, LANES), jnp.float32)
    for ref in (s_ref, va_ref, vb_ref):
        for i in range(total):
            ref[i, 0:PAD, :] = zeros
            ref[i, PAD + rows : PAD + rows + PAD, :] = zeros

    def field(f, i, here):
        j = f * (layers + 2)
        if i >= 2 * layers:
            j = j + i - layers
            return own_ref[j, here, :] + partner_ref[j, here, :]
        return own_ref[j + i, here, :] if i < layers else partner_ref[j + i - layers, here, :]

    for i in range(total):
        s_ref[i, PAD : PAD + rows, :] = field(0, i, slice(None))
        va_ref[i, PAD : PAD + rows, :] = field(2, i, slice(None))
    n = 8
    for at in range(0, rows, n):
        coefficients(s_ref, PAD + at, n, lambda f, i: field(f, i, slice(at, at + n)), coefs, at)

    bufs = (va_ref, vb_ref)
    sides = sides_of(gy, y)

    def sweep_all(number, which, count):
        src_ref, dst_ref = bufs[which], bufs[1 - which]
        for side, (above, _) in enumerate(sides):
            inner = pl.ds(PAD + inner_at(above, rows), HALO)
            for i in range(total):
                level_ref[(side * STEPS * ITERS + number) * total + i] = src_ref[i, inner, :]
        for at in range(0, rows, n):
            sweep(src_ref, dst_ref, PAD + at, n, count, coefs, at)

    holder, layer, row = (info_ref[:, j : j + 1].astype(jnp.int32) for j in range(3))
    spoilt = None
    for above, live in sides:
        part = jnp.logical_and(row // HALO == edge_at(above, rows) // HALO, live)
        spoilt = part if spoilt is None else jnp.logical_or(spoilt, part)
    cell = jnp.where(jnp.logical_and(holder == x, jnp.logical_not(spoilt)), layer * rows + row, -1)
    picks = as_onehot(lax.broadcasted_iota(jnp.int32, (cell.shape[0], layers * rows), 1) == cell)

    def after(step):
        last = step == STEPS - 1
        for at in range(0, rows, n):
            meet(va_ref, PAD + at, n, layers if last else 2 * layers, not last)
        heat = []
        for i in range(layers):
            here = pl.ds(PAD, rows)
            heat.append(va_ref[i, here, :] / s_ref[i, here, :])
            if step == STEPS - 1:
                out_ref[flip(z, layers, i)] = heat[-1]
        below_ref[step] = exact_dot(picks, jnp.concatenate(heat, axis=0))

    def between():
        for at in range(0, rows, n):
            next_rhs(coefs, va_ref, PAD + at, n, at)

    two_steps(layers, sweep_all, between, after)


def edge_kernel(gx, gy, shape, seg, *refs):
    layers, rows = shape
    own_ref, partner_ref, info_ref, segments_ref, below_ref, level_ref = refs[:6]
    sides_n = 1 if gy == 2 else 2
    along, across = refs[6 : 6 + sides_n], refs[6 + sides_n : 6 + 2 * sides_n]
    refs = refs[6 + 2 * sides_n :]
    heat_ref, returns = refs[0], refs[1 : 1 + gx]
    ret_ref, s_ref, va_ref, vb_ref = refs[1 + gx : 5 + gx]
    coefs = refs[5 + gx :]
    x, y, z = (lax.axis_index(a) for a in ("gx", "gy", "gz"))
    total = 2 * layers + 2
    count = info_ref.shape[0]
    holder, layer, row = (info_ref[:, j : j + 1].astype(jnp.int32) for j in range(3))
    below = [below_ref[step] for step in range(STEPS)]
    lane = lane_of(HALO)
    low = lane < LANES // 2
    bufs = (va_ref, vb_ref)

    def tile(j):
        return pl.ds(j if isinstance(j, int) else pl.multiple_of(j, HALO), HALO)

    for side, (above, live) in enumerate(sides_of(gy, y)):
        def place(when_top, otherwise):
            if above is True or above is False:
                return when_top * HALO if above else otherwise * HALO
            return jnp.where(above, when_top * HALO, otherwise * HALO)

        outer, strip, edge, inner = place(0, 3), place(1, 2), place(2, 1), place(3, 0)
        edge_rows = tile(edge_at(above, rows))
        inner_rows = tile(inner_at(above, rows))

        def field(f, i, here):
            j = f * (layers + 2)
            if i >= 2 * layers:
                j = j + i - layers
                return own_ref[j, here, :] + partner_ref[j, here, :]
            return own_ref[j + i, here, :] if i < layers else partner_ref[j + i - layers, here, :]

        t_ref, d_ref, q_ref, e_ref, g_ref = coefs[1], coefs[0], coefs[2], coefs[3], coefs[4]
        keep = {0: s_ref, 1: t_ref, 2: va_ref, 3: d_ref, 4: q_ref, 5: e_ref, 6: g_ref}
        zeros = jnp.zeros((HALO, LANES), jnp.float32)
        src = lane % (LANES // 2)
        turned = (layers - 1 - src // GROUP) * GROUP + src % GROUP
        half_tile = lax.broadcasted_iota(jnp.int32, (HALO, LANES), 0) < HALO // 2

        def unpack(value, f):
            if f < FIELDS - 2:
                return value
            turned_value = pltpu.roll(value, HALO // 2, 0)
            if f == FIELDS - 2:
                at_top, at_bottom = jnp.where(half_tile, 0.0, turned_value), jnp.where(half_tile, value, 0.0)
            else:
                at_top, at_bottom = jnp.where(half_tile, 0.0, value), jnp.where(half_tile, turned_value, 0.0)
            return jnp.where(above, at_top, at_bottom)

        for f in range(FIELDS):
            g = min(f, FIELDS - 2)
            for i in range(total):
                if i < 2 * layers:
                    ref, j = (along[side], i) if i < layers else (across[side], 2 * layers - 1 - i)
                    at = (j * (FIELDS - 1) + g) * HALO
                    value = ref[at : at + HALO, :]
                else:
                    at = (layers * (FIELDS - 1) + g) * HALO
                    half = (LANES // 2) * (i - 2 * layers)
                    a = take(along[side][at : at + HALO, :], src + half)
                    b = take(across[side][at : at + HALO, :], turned + half)
                    value = jnp.where(low, a, b)
                ref, shift = keep[f], 0 if f in (0, 2) else HALO
                ref[i, tile(strip - shift), :] = unpack(value, f)
                ref[i, tile(edge - shift), :] = field(f, i, edge_rows)
        for i in range(total):
            s_ref[i, tile(outer), :] = zeros
            va_ref[i, tile(outer), :] = zeros
            vb_ref[i, tile(outer), :] = zeros
            s_ref[i, tile(inner), :] = field(0, i, inner_rows)
        n = 2 * HALO
        held = [[keep[f][i, pl.ds(0, n), :] for i in range(total)] if f in (1, 3, 4, 5, 6) else None for f in range(FIELDS)]
        coefficients(s_ref, HALO, n, lambda f, i: held[f][i], coefs, 0)

        def sweep_all(number, which, needed_layers):
            src_ref, dst_ref = bufs[which], bufs[1 - which]
            for i in range(total):
                src_ref[i, tile(inner), :] = level_ref[(side * STEPS * ITERS + number) * total + i]
            sweep(src_ref, dst_ref, HALO, n, needed_layers, coefs, 0)

        first = edge_at(above, rows)
        hit = jnp.logical_and(jnp.logical_and(holder == x, row // HALO == first // HALO), live)
        cell = jnp.where(hit, layer * HALO + row - first, -1)
        picks = as_onehot(lax.broadcasted_iota(jnp.int32, (count, LANES), 1) == cell)

        def after(step):
            last = step == STEPS - 1
            meet(va_ref, HALO, n, layers if last else 2 * layers, not last)
            heat = []
            for i in range(layers):
                heat.append(va_ref[i, tile(edge), :] / s_ref[i, tile(edge), :])
                if step == STEPS - 1:
                    heat_ref[side * layers + flip(z, layers, i)] = heat[-1]
            heat.append(jnp.zeros((LANES - layers * HALO, LANES), jnp.float32))
            below[step] = below[step] + exact_dot(picks, jnp.concatenate(heat, axis=0))

        two_steps(layers, sweep_all, lambda: next_rhs(coefs, va_ref, HALO, n, 0), after)

    coef, warmth = segments_ref[:count, :], segments_ref[count:, :]
    for step in range(STEPS):
        warmth = warmth + coolant_gain * coef * (below[step] - warmth)
    ret_ref[...] = jnp.where(holder == x, warmth, 0.0)
    for k, ref in enumerate(returns):
        ref[...] = ret_ref[pl.ds(pl.multiple_of(lax.rem(x + k, gx) * seg, seg), seg), :]


def merge_kernel(gy, whole_ref, heat_ref, out_ref):
    layers, rows, _ = whole_ref.shape
    out_ref[...] = whole_ref[...]
    for side, (above, live) in enumerate(sides_of(gy, lax.axis_index("gy"))):
        def put(side=side, above=above):
            out_ref[:, pl.ds(edge_at(above, rows), HALO), :] = heat_ref[side * layers : (side + 1) * layers]

        if live is True:
            put()
        else:
            pl.when(live)(put)


def local(gx, gy, gz, u, power, storage, conductance, warmth, coef, holder, stratum, transverse):
    layers, rows, columns = u.shape
    seg = warmth.shape[1]
    segments = stratum.shape[1]
    if gz != 2 or gx < 3 or columns != LANES or 2 * layers * GROUP != LANES or rows % 32:
        raise ValueError("unsupported shape")
    holder = holder[:, :, 0]
    shape = (layers, rows)
    f32 = jnp.float32
    chunk = rows // 4
    wide = RAW * chunk + 2 * seg

    def struct(*dims):
        return jax.ShapeDtypeStruct(dims, f32)

    def vmem(*dims):
        return pltpu.VMEM(dims, f32)

    indices = (holder, stratum, transverse)
    flat = [a.reshape(-1, LANES) for a in (u, power, storage, conductance, warmth, coef)]
    own, to_left, to_right, only, *indices = pl.pallas_call(
        functools.partial(pack_kernel, shape),
        out_shape=(
            struct(RAW * layers * rows + 2 * seg + 2 * RAW * chunk, LANES),
            struct(wide, LANES),
            struct(wide, LANES),
            struct(2 * seg, LANES),
            *(jax.ShapeDtypeStruct(a.shape, a.dtype) for a in indices),
        ),
        in_specs=[pl.BlockSpec(memory_space=pltpu.HBM)] * 9,
        out_specs=(VMEM,) * 7,
        scratch_shapes=[pltpu.SemaphoreType.DMA((9,))],
        compiler_params=PARAMS,
        name="pack",
    )(*(pltpu.with_memory_space_constraint(a, pltpu.HBM) for a in (*flat, *indices)))

    swap = [(0, 1), (1, 0)]
    partner = lax.ppermute(own, "gz", swap)
    def from_distance(value, k):
        return lax.ppermute(value, "gx", [(i, (i - k) % gx) for i in range(gx)])

    received = [from_distance(to_left, 1), from_distance(to_right, gx - 1)]
    received += [from_distance(only, k) for k in range(2, gx - 1)]
    late = lax.ppermute(jnp.concatenate(received, axis=0), "gz", swap)

    sides = 1 if gy == 2 else 2
    fields = struct(FIELDS * (layers + 2), rows, LANES)
    strip_rows = (FIELDS - 1) * (layers + 1) * HALO
    filled = pl.pallas_call(
        functools.partial(fill_kernel, False, gx, gy, shape, seg),
        out_shape=(fields,) + (struct(strip_rows, LANES),) * sides + (struct(segments, 8), struct(2 * segments, LANES)),
        in_specs=[VMEM] * (4 + gx - 1),
        out_specs=(VMEM,) * (3 + sides),
        compiler_params=PARAMS,
        cost_estimate=cost(1.5),
        name="fill_own",
    )(own, *indices, *received)
    own_fields, strips, (info, held) = filled[0], filled[1 : 1 + sides], filled[1 + sides :]
    if gy == 2:
        routes = [(strips[0], swap)]
    else:
        up = [(i, i + 1) for i in range(gy - 1)]
        routes = [(strips[1], up), (strips[0], [(j, i) for i, j in up])]
    along = [lax.ppermute(value, "gy", pairs) for value, pairs in routes]
    across = []
    for value, pairs in routes:
        both = [(2 * i + z, 2 * j + 1 - z) for i, j in pairs for z in range(2)]
        across.append(lax.ppermute(value, ("gy", "gz"), both))

    partner_fields = pl.pallas_call(
        functools.partial(fill_kernel, True, gx, gy, shape, seg),
        out_shape=fields,
        in_specs=[VMEM] * 5,
        out_specs=VMEM,
        scratch_shapes=[vmem(segments, LANES)] * 2,
        compiler_params=PARAMS,
        cost_estimate=cost(1.5),
        name="fill_partner",
    )(partner, *indices, late)

    total = 2 * layers + 2
    padded = vmem(total, rows + 2 * PAD, LANES)
    inside, below, levels = pl.pallas_call(
        functools.partial(tile_kernel, gx, gy, shape),
        out_shape=(
            struct(layers, rows, LANES),
            struct(STEPS, segments, LANES),
            struct(sides * STEPS * ITERS * total, HALO, LANES),
        ),
        in_specs=[VMEM] * 3,
        out_specs=(VMEM,) * 3,
        scratch_shapes=[padded] * 3 + [vmem(total, rows, LANES)] * 5,
        compiler_params=PARAMS,
        cost_estimate=cost(7),
        name="tile_sweeps",
    )(own_fields, partner_fields, info)

    results = pl.pallas_call(
        functools.partial(edge_kernel, gx, gy, shape, seg),
        out_shape=(struct(sides * layers, HALO, LANES),) + (struct(seg, LANES),) * gx,
        in_specs=[VMEM] * (6 + 2 * sides),
        out_specs=(VMEM,) * (1 + gx),
        scratch_shapes=[vmem(segments, LANES)]
        + [vmem(total, 4 * HALO, LANES)] * 3
        + [vmem(total, 2 * HALO, LANES)] * 5,
        compiler_params=PARAMS,
        cost_estimate=cost(1.5),
        name="edge_sweeps",
    )(own_fields, partner_fields, info, held, below, levels, *along, *across)
    heat, coolant = results[0], results[1]
    returned = [lax.ppermute(results[1 + k], "gx", [(i, (i + k) % gx) for i in range(gx)]) for k in range(1, gx)]
    temperature = pl.pallas_call(
        functools.partial(merge_kernel, gy),
        out_shape=struct(layers, rows, LANES),
        in_specs=[VMEM] * 2,
        out_specs=VMEM,
        compiler_params=PARAMS,
        cost_estimate=cost(1),
        name="merge",
    )(inside, heat)
    for value in returned:
        coolant = coolant + value
    return temperature, coolant[None]


def solution(mesh):
    gx, gy, gz = (mesh.shape[a] for a in ("gx", "gy", "gz"))
    cells = P(("stack", "gz"), "gy", "gx")
    segments = P(("stack", "gy", "gz"), "gx", None)
    return jax.shard_map(
        functools.partial(local, gx, gy, gz),
        mesh=mesh,
        in_specs=(cells, cells, cells, P(None, ("stack", "gz"), "gy", "gx"), segments, segments, P(), P(), P()),
        out_specs=(cells, segments),
        check_vma=False,
    )
```

```python
import functools

import jax
import jax.numpy as jnp
from jax import lax
from jax.experimental import pallas as pl
from jax.experimental.pallas import tpu as pltpu
from jax.sharding import PartitionSpec as P

STEPS = 2
ITERS = 4
HALO = STEPS * ITERS
GROUP = 2 * HALO
LANES = 128
RAW = 5
FIELDS = 7
coolant_gain = 0.5

VMEM = pl.BlockSpec(memory_space=pltpu.VMEM)
PARAMS = pltpu.CompilerParams(vmem_limit_bytes=40 * 1024 * 1024)


def cost(microseconds):
    return pl.CostEstimate(flops=0, bytes_accessed=int(microseconds * 3e6), transcendentals=0)


def lane_of(rows):
    return lax.broadcasted_iota(jnp.int32, (rows, LANES), 1)


def take(value, index):
    return jnp.take_along_axis(value, index, axis=1, mode="promise_in_bounds")


def edge_columns(rows, turned):
    j = lane_of(rows) % GROUP
    first = j < HALO
    return jnp.where(first, LANES - HALO + j, j - HALO) if not turned else jnp.where(first, j, LANES - GROUP + j)


def split(value):
    high = value.astype(jnp.bfloat16)
    low = (value - high.astype(jnp.float32)).astype(jnp.bfloat16)
    return high, low


def exact_dot(onehot, value):
    high, low = split(value)
    both = jnp.concatenate([high, low], axis=0)
    return jnp.dot(jnp.concatenate([onehot, onehot], axis=1), both, preferred_element_type=jnp.float32)


def coupling(coef, warmth):
    flow = coef * warmth
    second = coolant_gain * coef * coef
    return jnp.concatenate([coef, flow, second, flow - second * warmth], axis=1)


def flip(z, layers, i):
    return jnp.where(z == 0, i, layers - 1 - i)


def pack_kernel(shape, u_ref, p_ref, c_ref, k_ref, f_ref, x_ref, *refs):
    own_ref, left_ref, right_ref, seg_ref = refs[3:7]
    sems = refs[-1]
    layers, rows = shape
    seg = f_ref.shape[0]
    z = lax.axis_index("gz")
    plane = layers * rows
    copies = []

    def fetch(src, dst):
        copies.append(pltpu.make_async_copy(src, dst, sems.at[len(copies)]))
        copies[-1].start()

    fetch(k_ref, own_ref.at[pl.ds(0, 2 * plane), :])
    for field, ref in enumerate((u_ref, p_ref, c_ref), 2):
        fetch(ref, own_ref.at[pl.ds(field * plane, plane), :])
    for j, ref in enumerate((x_ref, f_ref)):
        fetch(ref, own_ref.at[pl.ds(RAW * plane + j * seg, seg), :])
    for table, place in zip(refs[:3], refs[7:10]):
        fetch(table, place)
    chunk = rows // 4
    lane = lane_of(chunk)
    first = lane % GROUP < HALO
    columns = edge_columns(chunk, False), edge_columns(chunk, True)
    edges = RAW * plane + 2 * seg

    def gather(field, at, g):
        value = None
        for i in range(layers):
            start = pl.multiple_of((field * layers + flip(z, layers, i)) * rows + at, chunk)
            taken = take(own_ref[pl.ds(start, chunk), :], columns[g % 2])
            value = taken if value is None else jnp.where(lane // GROUP == (g // 2) * layers + i, taken, value)
        return value

    def place(g, part):
        return pl.ds(edges + ((g % 2) * RAW + part) * chunk, chunk)

    copies[0].wait()
    roots = pl.ds(0, 2 * plane)
    own_ref[roots, :] = jnp.sqrt(own_ref[roots, :])
    for field in range(4):
        if field >= 2:
            copies[field - 1].wait()
        for part in range(4):
            value = gather(field, part * chunk, field)
            if field >= 2:
                value = jnp.where(lane < LANES // 2, own_ref[place(field, part), :], value)
            own_ref[place(field, part), :] = value
    copies[3].wait()
    for g in range(4):
        value = gather(4, g * chunk, g)
        if g >= 2:
            value = jnp.where(lane < LANES // 2, own_ref[place(g, 4), :], value)
        own_ref[place(g, 4), :] = value
    for part in range(RAW):
        even, odd = own_ref[place(0, part), :], own_ref[place(1, part), :]
        left_ref[part * chunk : (part + 1) * chunk, :] = jnp.where(first, odd, even)
        right_ref[part * chunk : (part + 1) * chunk, :] = jnp.where(first, even, odd)
    for copy in copies[4:]:
        copy.wait()
    segments = own_ref[RAW * plane : RAW * plane + 2 * seg, :]
    seg_ref[...] = segments
    left_ref[RAW * chunk :, :] = segments
    right_ref[RAW * chunk :, :] = segments


class Strips:
    def __init__(self, refs, starts, cells_ref, start, rows, layers):
        self.refs, self.starts = refs, starts
        self.cells_ref, self.start = cells_ref, start
        self.rows, self.layers = rows, layers

    def both(self, field, start, n, x, gx, partner):
        chunk = self.rows // 4
        if field < 4:
            g, at = field, start
        else:
            g, at = start // chunk, 4 * chunk + start % chunk
        a, b = (ref[at + begin : at + begin + n, :] for ref, begin in zip(self.refs, self.starts))
        at = self.start + (g % 2) * RAW * chunk + at
        inside = self.cells_ref[at : at + n, :]
        from_left, from_right = jnp.where(x > 0, b, 0.0), jnp.where(x < gx - 1, a, 0.0)
        lane = lane_of(n)
        first = (lane % GROUP < HALO) if g % 2 == 0 else (lane % GROUP >= HALO)
        half = self.layers * GROUP
        src = lane % half
        if partner:
            src = (self.layers - 1 - src // GROUP) * GROUP + src % GROUP
        if g % 2 == 1:
            src = jnp.where(src % GROUP < HALO, src + HALO, src - HALO)
        src = src + half * (g // 2)
        return take(jnp.where(first, from_left, inside), src), take(jnp.where(first, inside, from_right), src)


def place_segments(x, gx, seg, coef_ref, warmth_ref, sources):
    for k, ref, at in sources:
        place = pl.ds(pl.multiple_of(lax.rem(x + k, gx) * seg, seg), seg)
        coef_ref[place, :] = ref[at : at + seg, :]
        warmth_ref[place, :] = ref[at + seg : at + 2 * seg, :]


def tables(z, group, layers, holder_ref, stratum_ref, transverse_ref):
    holder = holder_ref[pl.ds(group, 1), :]
    layer = stratum_ref[pl.ds(group, 1), :]
    layer = jnp.where(z == 0, layer, layers - 1 - layer)
    row = transverse_ref[pl.ds(group, 1), :]
    n = holder.shape[1]
    which = lax.broadcasted_iota(jnp.int32, (8, n), 0)
    stacked = jnp.where(which == 0, holder, jnp.where(which == 1, layer, row))
    eye = lax.broadcasted_iota(jnp.int32, (n, n), 0) == lax.broadcasted_iota(jnp.int32, (n, n), 1)
    columns = lax.dot_general(
        eye.astype(jnp.float32).astype(jnp.bfloat16),
        stacked.astype(jnp.float32).astype(jnp.bfloat16),
        (((1,), (1,)), ((), ())),
        preferred_element_type=jnp.float32,
    )
    return (holder, layer, row), columns


def as_onehot(mask):
    return jnp.where(mask, 1.0, 0.0).astype(jnp.bfloat16)


def combine(raw, added):
    s, t, u, power, storage = raw
    wall, flow, second, later = (added[:, i * LANES : (i + 1) * LANES] for i in range(4))
    return s, t, s * u, storage + wall, power + storage * u + flow, power + later, storage + second


def lengths_of(gx, chunk, seg):
    return [RAW * chunk + 2 * seg] * 2 + [2 * seg] * (gx - 3)


def edge_at(top, rows):
    return 0 if top is True else rows - HALO if top is False else pl.multiple_of(jnp.where(top, 0, rows - HALO), HALO)


def inner_at(top, rows):
    return HALO if top is True else rows - 2 * HALO if top is False else pl.multiple_of(jnp.where(top, HALO, rows - 2 * HALO), HALO)


def sides_of(gy, y):
    return [(y == 1, True)] if gy == 2 else [(True, y > 0), (False, y < gy - 1)]


def maps_kernel(gx, gy, shape, holder_ref, stratum_ref, transverse_ref, *refs):
    layers, rows = shape
    plane = layers * rows
    picks_ref, beside_ref, mine_ref = refs[6:]
    x, y, z = (lax.axis_index(a) for a in ("gx", "gy", "gz"))
    n = holder_ref.shape[1]
    for partner in range(2):
        cells_ref, rows_ref, masks_ref = refs[3 * partner : 3 * partner + 3]
        group = y * 2 + ((1 - z) if partner else z)
        (holder, layer, row), columns = tables(z, group, layers, holder_ref, stratum_ref, transverse_ref)
        cell = jnp.where(holder == x, layer * rows + row, -1)
        cells_ref[...] = as_onehot(lax.broadcasted_iota(jnp.int32, (plane, n), 0) == cell)
        rows_ref[...] = as_onehot(lax.broadcasted_iota(jnp.int32, (rows, n), 0) == row)
        holder, layer, row = (columns[:, j : j + 1].astype(jnp.int32) for j in range(3))
        lane = lane_of(n)
        first = lane % GROUP < HALO
        here = lane // GROUP == layer + partner * layers
        for side, begin in enumerate((x - 1, x)):
            mine = jnp.logical_and(here, holder == jnp.where(first, begin, begin + 1))
            masks_ref[side * n : (side + 1) * n, :] = jnp.where(mine, 1.0, 0.0)
        if partner:
            continue
        mine = holder == x
        mine_ref[...] = jnp.where(jnp.logical_and(mine, lane >= 0), 1.0, 0.0)
        spoilt = None
        for side, (above, live) in enumerate(sides_of(gy, y)):
            start = edge_at(above, rows)
            part = jnp.logical_and(row // HALO == start // HALO, live)
            spoilt = part if spoilt is None else jnp.logical_or(spoilt, part)
            cell = jnp.where(jnp.logical_and(mine, part), layer * HALO + row - start, -1)
            beside_ref[side * n : (side + 1) * n, :] = as_onehot(lane == cell)
        cell = jnp.where(jnp.logical_and(mine, jnp.logical_not(spoilt)), layer * rows + row, -1)
        picks_ref[...] = as_onehot(lax.broadcasted_iota(jnp.int32, (n, plane), 1) == cell)


def join_kernel(mine_ref, *refs):
    out_ref, at = refs[-1], 0
    for ref in refs[:-1]:
        n = ref.shape[0]
        out_ref[at : at + n, :] = ref[...]
        at += n


def partner_rows(layers):
    whole, at = [], 1
    for i in range(layers - 1, -1, -1):
        whole.append((i, HALO - layers + i, at))
        at += HALO - layers + i
    stride = -(-at // 8) * 8
    later, at = [], 0
    for f in range(2):
        for i in range(layers - 1, -1, -1):
            if ITERS - 1 - layers + i > 0:
                later.append((f, i, ITERS - 1 - layers + i, at))
                at += ITERS - 1 - layers + i
    return whole, stride, later, -(-at // 8) * 8


def fill_kernel(partner, gx, gy, shape, seg, *refs):
    layers, rows = shape
    cells_ref, where_ref, rows_ref, masks_ref = refs[:4]
    plane, chunk = layers * rows, rows // 4
    lengths = lengths_of(gx, chunk, seg)
    if partner:
        sources = [(refs[4], sum(lengths[:k])) for k in range(gx - 1)]
        refs = refs[5:]
    else:
        sources = [(ref, 0) for ref in refs[4 : 4 + gx - 1]]
        refs = refs[4 + gx - 1 :]
    sides = 1 if gy == 2 else 2
    out_ref = refs[0]
    if partner:
        coef_ref, warmth_ref = refs[1:3]
    else:
        strip_refs, partner_refs, segments_ref = refs[1 : 1 + sides], refs[1 + sides : 1 + 2 * sides], refs[1 + 2 * sides]
        n = segments_ref.shape[0] // 2
        coef_ref, warmth_ref = segments_ref.at[pl.ds(0, n), :], segments_ref.at[pl.ds(n, n), :]
    x, y, z = (lax.axis_index(a) for a in ("gx", "gy", "gz"))
    base = layers if partner else 0
    distances = [1, gx - 1] + list(range(2, gx - 1))
    held = [(k, ref, at + (RAW * chunk if j < 2 else 0)) for j, (k, (ref, at)) in enumerate(zip(distances, sources))]
    place_segments(x, gx, seg, coef_ref, warmth_ref, [(0, cells_ref, RAW * plane)] + held)
    coef, warmth = coef_ref[...], warmth_ref[...]
    n = coef.shape[0]
    added = exact_dot(where_ref[...], coupling(coef, warmth))
    near = edge_columns(n, False)
    beside = []
    for side in range(2):
        masked = take(coef, near) * masks_ref[side * n : (side + 1) * n, :]
        beside.append(exact_dot(rows_ref[...], coupling(masked, take(warmth, near))))
    planes = layers + 2
    for i in range(layers):
        src = flip(z, layers, i)
        raw = [cells_ref[pl.ds(pl.multiple_of((f * layers + src) * rows, rows), rows), :] for f in range(RAW)]
        for f, value in enumerate(combine(raw, added[i * rows : (i + 1) * rows])):
            out_ref[f * planes + i] = value
    strips = Strips(
        [ref for ref, _ in sources[:2]], [at for _, at in sources[:2]], cells_ref, RAW * plane + 2 * seg, rows, layers
    )
    half = lane_of(chunk) // (LANES // 2) == (1 if partner else 0)
    for part in range(4):
        here = slice(part * chunk, (part + 1) * chunk)
        raw = [strips.both(f, part * chunk, chunk, x, gx, partner) for f in range(RAW)]
        for side in range(2):
            cells = [jnp.where(half, value[side], 0.0) for value in raw]
            for f, value in enumerate(combine(cells, beside[side][here])):
                out_ref[f * planes + layers + side, here, :] = value
    if partner:
        return
    low = lane_of(HALO) < LANES // 2
    upper = lax.broadcasted_iota(jnp.int32, (HALO, LANES), 0) < HALO // 2
    sent = FIELDS - 1
    for strip_ref, partner_ref, (top, _) in zip(strip_refs, partner_refs, sides_of(gy, y)):
        edge = pl.ds(edge_at(top, rows), HALO)

        def give(strip_ref, j, values):
            *whole, e, g = values
            e = jnp.where(top, e, pltpu.roll(e, HALO // 2, 0))
            g = jnp.where(top, pltpu.roll(g, HALO // 2, 0), g)
            for f, value in enumerate(whole + [jnp.where(upper, e, g)]):
                at = j + f * HALO
                strip_ref[at : at + HALO, :] = value

        for i in range(layers):
            give(strip_ref, i * sent * HALO, [out_ref[f * planes + i, edge, :] for f in range(FIELDS)])
        values = []
        for f in range(FIELDS):
            left, right = (out_ref[f * planes + layers + side, edge, :] for side in range(2))
            values.append(jnp.where(low, left, pltpu.roll(right, LANES // 2, 1)))
        give(strip_ref, layers * sent * HALO, values)
        whole, stride, later, shared = partner_rows(layers)
        pieces = [(f, i, m, f * stride + at) for f in range(sent - 1) for i, m, at in whole]
        pieces += [(sent - 1 + f, i, m, (sent - 1) * stride + at) for f, i, m, at in later]
        for f, i, m, at in pieces:
            start = edge_at(top, rows) + jnp.where(top, 0, HALO - m)
            partner_ref[at : at + m, :] = out_ref[f * planes + i, pl.ds(start, m), :]
        give(partner_ref, (sent - 1) * stride + shared, values)


def planes_of(count, total):
    return list(range(count)) + [total - 2, total - 1]


def lateral(buf, at, n, which):
    sums = []
    for i in which:
        centre = buf[i, pl.ds(at, n), :]
        beside = pltpu.roll(centre, 1, 1) + pltpu.roll(centre, LANES - 1, 1)
        sums.append(beside + (buf[i, pl.ds(at - 1, n), :] + buf[i, pl.ds(at + 1, n), :]))
    return sums


def vertical(planes, edges, count):
    sums = []
    for i in range(count):
        near = [planes[j] for j in (i - 1, i + 1) if 0 <= j < len(planes)]
        sums.append(functools.reduce(jnp.add, near))
    for edge in edges:
        lane = lane_of(edge.shape[0])
        up = jnp.where(lane >= GROUP, pltpu.roll(edge, GROUP, 1), 0.0)
        down = jnp.where(lane < LANES - GROUP, pltpu.roll(edge, LANES - GROUP, 1), 0.0)
        sums.append(up + down)
    return sums


def coefficients(s_ref, at, n, raw, dests, to):
    a_ref, q_ref, r_ref, e_ref, g_ref = dests
    total = s_ref.shape[0]
    sums = lateral(s_ref, at, n, range(total))
    t = [raw(1, i) for i in range(total)]
    above = vertical(t[:-2], t[-2:], total - 2)
    here = pl.ds(to, n)
    for i in range(total):
        s = s_ref[i, pl.ds(at, n), :]
        diag = raw(3, i) + s * sums[i] + t[i] * above[i]
        inverse = 1.0 / jnp.where(diag > 0.0, diag, 1.0)
        scaled = s * inverse
        a_ref[i, here, :] = s * scaled
        r_ref[i, here, :] = raw(4, i) * scaled
        e_ref[i, here, :] = raw(5, i) * scaled
        g_ref[i, here, :] = raw(6, i) * inverse
        q_ref[i, here, :] = t[i] * jnp.where(s > 0.0, 1.0 / jnp.where(s > 0.0, s, 1.0), 0.0)


def sweep(src_ref, dst_ref, at, n, count, coefs, base):
    a_ref, q_ref, r_ref = coefs[:3]
    total = src_ref.shape[0]
    here, there = pl.ds(base, n), pl.ds(at, n)
    which = planes_of(count, total)
    sums = lateral(src_ref, at, n, which)
    scaled = [q_ref[i, here, :] * src_ref[i, there, :] for i in planes_of(min(count + 1, total - 2), total)]
    above = vertical(scaled[:-2], scaled[-2:], count)
    for j, i in enumerate(which):
        dst_ref[i, there, :] = r_ref[i, here, :] + a_ref[i, here, :] * (sums[j] + q_ref[i, here, :] * above[j])


def next_rhs(coefs, v_ref, at, n, base):
    r_ref, e_ref, g_ref = coefs[2:]
    here = pl.ds(base, n)
    for i in range(v_ref.shape[0]):
        r_ref[i, here, :] = e_ref[i, here, :] + g_ref[i, here, :] * v_ref[i, pl.ds(at, n), :]


def meet(v_ref, at, n, count, back):
    total = v_ref.shape[0]
    here = pl.ds(at, n)
    lane = lane_of(n)
    j, group = lane % GROUP, lane // GROUP
    outer = jnp.logical_or(lane < ITERS, lane >= LANES - ITERS)
    left, right = v_ref[total - 2, here, :], v_ref[total - 1, here, :]
    middle = jnp.where(j < HALO, right, left)
    for i in range(count):
        value = v_ref[i, here, :]
        if back:
            moved = pltpu.roll(value, (i * GROUP + HALO) % LANES, 1)
            left = jnp.where(jnp.logical_and(group == i, j >= GROUP - ITERS), moved, left)
            right = jnp.where(jnp.logical_and(group == i, j < ITERS), moved, right)
        v_ref[i, here, :] = jnp.where(outer, pltpu.roll(middle, LANES - (i * GROUP + HALO), 1), value)
    if back:
        v_ref[total - 2, here, :] = left
        v_ref[total - 1, here, :] = right


def needed(layers, n):
    return min(2 * layers, layers + STEPS * ITERS - 1 - n)


def two_steps(layers, sweep_all, between, after):
    for step in range(STEPS):
        whole = [n for n in range(step * ITERS, (step + 1) * ITERS) if needed(layers, n) == 2 * layers]
        pairs = len(whole) // 2

        def pair(k, carry):
            n = step * ITERS + 2 * k
            sweep_all(n, 0, 2 * layers)
            sweep_all(n + 1, 1, 2 * layers)
            return carry

        if pairs:
            lax.fori_loop(0, pairs, pair, 0)
        for n in range(step * ITERS + 2 * pairs, (step + 1) * ITERS):
            sweep_all(n, n % 2, needed(layers, n))
        after(step)
        if step < STEPS - 1:
            between()


PAD = 8


def tile_kernel(gx, gy, shape, *refs):
    layers, rows = shape
    own_ref, partner_ref, picks_ref, out_ref, below_ref, level_ref = refs[:6]
    s_ref, va_ref, vb_ref = refs[6:9]
    coefs = refs[9:]
    x, y, z = (lax.axis_index(a) for a in ("gx", "gy", "gz"))
    total = 2 * layers + 2
    zeros = jnp.zeros((PAD, LANES), jnp.float32)
    for ref in (s_ref, va_ref, vb_ref):
        for i in range(total):
            ref[i, 0:PAD, :] = zeros
            ref[i, PAD + rows : PAD + rows + PAD, :] = zeros

    def field(f, i, here):
        j = f * (layers + 2)
        if i >= 2 * layers:
            j = j + i - layers
            return own_ref[j, here, :] + partner_ref[j, here, :]
        return own_ref[j + i, here, :] if i < layers else partner_ref[j + i - layers, here, :]

    for i in range(total):
        s_ref[i, PAD : PAD + rows, :] = field(0, i, slice(None))
        va_ref[i, PAD : PAD + rows, :] = field(2, i, slice(None))
    n = 8
    for at in range(0, rows, n):
        coefficients(s_ref, PAD + at, n, lambda f, i: field(f, i, slice(at, at + n)), coefs, at)

    bufs = (va_ref, vb_ref)
    sides = sides_of(gy, y)

    def sweep_all(number, which, count):
        src_ref, dst_ref = bufs[which], bufs[1 - which]
        for side, (above, _) in enumerate(sides):
            inner = pl.ds(PAD + inner_at(above, rows), HALO)
            for i in range(total):
                level_ref[(side * STEPS * ITERS + number) * total + i] = src_ref[i, inner, :]
        for at in range(0, rows, n):
            sweep(src_ref, dst_ref, PAD + at, n, count, coefs, at)

    def after(step):
        last = step == STEPS - 1
        for at in range(0, rows, n):
            meet(va_ref, PAD + at, n, layers if last else 2 * layers, not last)
        heat = []
        for i in range(layers):
            here = pl.ds(PAD, rows)
            heat.append(va_ref[i, here, :] / s_ref[i, here, :])
            if step == STEPS - 1:
                out_ref[flip(z, layers, i)] = heat[-1]
        below_ref[step] = exact_dot(picks_ref[...], jnp.concatenate(heat, axis=0))

    def between():
        for at in range(0, rows, n):
            next_rhs(coefs, va_ref, PAD + at, n, at)

    two_steps(layers, sweep_all, between, after)


def edge_kernel(gx, gy, shape, seg, *refs):
    layers, rows = shape
    own_ref, partner_ref, picks_ref, mine_ref, segments_ref, below_ref, level_ref = refs[:7]
    sides_n = 1 if gy == 2 else 2
    along, across = refs[7 : 7 + sides_n], refs[7 + sides_n : 7 + 2 * sides_n]
    refs = refs[7 + 2 * sides_n :]
    heat_ref, returns = refs[0], refs[1 : 1 + gx]
    ret_ref, s_ref, va_ref, vb_ref = refs[1 + gx : 5 + gx]
    coefs = refs[5 + gx :]
    x, y, z = (lax.axis_index(a) for a in ("gx", "gy", "gz"))
    total = 2 * layers + 2
    count = mine_ref.shape[0]
    below = [below_ref[step] for step in range(STEPS)]
    lane = lane_of(HALO)
    low = lane < LANES // 2
    bufs = (va_ref, vb_ref)

    def tile(j):
        return pl.ds(j if isinstance(j, int) else pl.multiple_of(j, HALO), HALO)

    for side, (above, live) in enumerate(sides_of(gy, y)):
        def place(when_top, otherwise):
            if above is True or above is False:
                return when_top * HALO if above else otherwise * HALO
            return jnp.where(above, when_top * HALO, otherwise * HALO)

        outer, strip, edge, inner = place(0, 3), place(1, 2), place(2, 1), place(3, 0)
        edge_rows = tile(edge_at(above, rows))
        inner_rows = tile(inner_at(above, rows))

        def field(f, i, here):
            j = f * (layers + 2)
            if i >= 2 * layers:
                j = j + i - layers
                return own_ref[j, here, :] + partner_ref[j, here, :]
            return own_ref[j + i, here, :] if i < layers else partner_ref[j + i - layers, here, :]

        t_ref, d_ref, q_ref, e_ref, g_ref = coefs[1], coefs[0], coefs[2], coefs[3], coefs[4]
        keep = {0: s_ref, 1: t_ref, 2: va_ref, 3: d_ref, 4: q_ref, 5: e_ref, 6: g_ref}
        zeros = jnp.zeros((HALO, LANES), jnp.float32)
        src = lane % (LANES // 2)
        turned = (layers - 1 - src // GROUP) * GROUP + src % GROUP
        half_tile = lax.broadcasted_iota(jnp.int32, (HALO, LANES), 0) < HALO // 2

        def unpack(value, f):
            if f < FIELDS - 2:
                return value
            turned_value = pltpu.roll(value, HALO // 2, 0)
            if f == FIELDS - 2:
                at_top, at_bottom = jnp.where(half_tile, 0.0, turned_value), jnp.where(half_tile, value, 0.0)
            else:
                at_top, at_bottom = jnp.where(half_tile, 0.0, value), jnp.where(half_tile, turned_value, 0.0)
            return jnp.where(above, at_top, at_bottom)

        whole, stride, later, shared = partner_rows(layers)
        sublane = lax.broadcasted_iota(jnp.int32, (HALO, LANES), 0)

        def nearest(ref, m, at):
            at_top = jnp.where(sublane >= HALO - m, ref[at - HALO + m : at + m, :], 0.0)
            return jnp.where(above, at_top, jnp.where(sublane < m, ref[at : at + HALO, :], 0.0))

        for f in range(FIELDS):
            g = min(f, FIELDS - 2)
            if f < FIELDS - 2:
                rows_of = {i: (m, f * stride + at) for i, m, at in whole}
            else:
                rows_of = {i: (m, (FIELDS - 2) * stride + at) for which, i, m, at in later if which == f - FIELDS + 2}
            for i in range(total):
                if i < layers:
                    at = (i * (FIELDS - 1) + g) * HALO
                    value = unpack(along[side][at : at + HALO, :], f)
                elif i < 2 * layers:
                    j = 2 * layers - 1 - i
                    value = nearest(across[side], *rows_of[j]) if j in rows_of else zeros
                else:
                    at = (layers * (FIELDS - 1) + g) * HALO
                    half = (LANES // 2) * (i - 2 * layers)
                    a = take(along[side][at : at + HALO, :], src + half)
                    at = (FIELDS - 2) * stride + shared + g * HALO
                    b = take(across[side][at : at + HALO, :], turned + half)
                    value = unpack(jnp.where(low, a, b), f)
                ref, shift = keep[f], 0 if f in (0, 2) else HALO
                ref[i, tile(strip - shift), :] = value
                ref[i, tile(edge - shift), :] = field(f, i, edge_rows)
        for i in range(total):
            s_ref[i, tile(outer), :] = zeros
            va_ref[i, tile(outer), :] = zeros
            vb_ref[i, tile(outer), :] = zeros
            s_ref[i, tile(inner), :] = field(0, i, inner_rows)
        n = 2 * HALO
        held = [[keep[f][i, pl.ds(0, n), :] for i in range(total)] if f in (1, 3, 4, 5, 6) else None for f in range(FIELDS)]
        coefficients(s_ref, HALO, n, lambda f, i: held[f][i], coefs, 0)

        def sweep_all(number, which, needed_layers):
            src_ref, dst_ref = bufs[which], bufs[1 - which]
            for i in range(total):
                src_ref[i, tile(inner), :] = level_ref[(side * STEPS * ITERS + number) * total + i]
            sweep(src_ref, dst_ref, HALO, n, needed_layers, coefs, 0)

        picks = picks_ref[side * count : (side + 1) * count, :]

        def after(step):
            last = step == STEPS - 1
            meet(va_ref, HALO, n, layers if last else 2 * layers, not last)
            heat = []
            for i in range(layers):
                heat.append(va_ref[i, tile(edge), :] / s_ref[i, tile(edge), :])
                if step == STEPS - 1:
                    heat_ref[side * layers + flip(z, layers, i)] = heat[-1]
            heat.append(jnp.zeros((LANES - layers * HALO, LANES), jnp.float32))
            below[step] = below[step] + exact_dot(picks, jnp.concatenate(heat, axis=0))

        two_steps(layers, sweep_all, lambda: next_rhs(coefs, va_ref, HALO, n, 0), after)

    coef, warmth = segments_ref[:count, :], segments_ref[count:, :]
    for step in range(STEPS):
        warmth = warmth + coolant_gain * coef * (below[step] - warmth)
    ret_ref[...] = jnp.where(mine_ref[...] > 0.0, warmth, 0.0)
    for k, ref in enumerate(returns):
        ref[...] = ret_ref[pl.ds(pl.multiple_of(lax.rem(x + k, gx) * seg, seg), seg), :]


def merge_kernel(gy, whole_ref, heat_ref, out_ref):
    layers, rows, _ = whole_ref.shape
    out_ref[...] = whole_ref[...]
    for side, (above, live) in enumerate(sides_of(gy, lax.axis_index("gy"))):
        def put(side=side, above=above):
            out_ref[:, pl.ds(edge_at(above, rows), HALO), :] = heat_ref[side * layers : (side + 1) * layers]

        if live is True:
            put()
        else:
            pl.when(live)(put)


def local(gx, gy, gz, u, power, storage, conductance, warmth, coef, holder, stratum, transverse):
    layers, rows, columns = u.shape
    seg = warmth.shape[1]
    segments = stratum.shape[1]
    if gz != 2 or gx < 3 or columns != LANES or 2 * layers * GROUP != LANES or rows % 32:
        raise ValueError("unsupported shape")
    holder = holder[:, :, 0]
    shape = (layers, rows)
    f32 = jnp.float32
    chunk = rows // 4
    wide = RAW * chunk + 2 * seg

    def struct(*dims):
        return jax.ShapeDtypeStruct(dims, f32)

    def vmem(*dims):
        return pltpu.VMEM(dims, f32)

    indices = (holder, stratum, transverse)
    flat = [a.reshape(-1, LANES) for a in (u, power, storage, conductance, warmth, coef)]
    own, to_left, to_right, only, *indices = pl.pallas_call(
        functools.partial(pack_kernel, shape),
        out_shape=(
            struct(RAW * layers * rows + 2 * seg + 2 * RAW * chunk, LANES),
            struct(wide, LANES),
            struct(wide, LANES),
            struct(2 * seg, LANES),
            *(jax.ShapeDtypeStruct(a.shape, a.dtype) for a in indices),
        ),
        in_specs=[pl.BlockSpec(memory_space=pltpu.HBM)] * 9,
        out_specs=(VMEM,) * 7,
        scratch_shapes=[pltpu.SemaphoreType.DMA((9,))],
        compiler_params=PARAMS,
        name="pack",
    )(*(pltpu.with_memory_space_constraint(a, pltpu.HBM) for a in (*flat, *indices)))

    swap = [(0, 1), (1, 0)]
    partner = lax.ppermute(own, "gz", swap)
    def from_distance(value, k):
        return lax.ppermute(value, "gx", [(i, (i - k) % gx) for i in range(gx)])

    received = [from_distance(to_left, 1), from_distance(to_right, gx - 1)]
    received += [from_distance(only, k) for k in range(2, gx - 1)]

    sides = 1 if gy == 2 else 2
    fields = struct(FIELDS * (layers + 2), rows, LANES)
    strip_rows = (FIELDS - 1) * (layers + 1) * HALO
    _, stride, _, shared = partner_rows(layers)
    partner_strip = (FIELDS - 2) * stride + shared + (FIELDS - 1) * HALO
    sides = 1 if gy == 2 else 2
    bf16 = jnp.bfloat16
    one_group = (
        jax.ShapeDtypeStruct((layers * rows, segments), bf16),
        jax.ShapeDtypeStruct((rows, segments), bf16),
        struct(2 * segments, LANES),
    )
    maps = pl.pallas_call(
        functools.partial(maps_kernel, gx, gy, shape),
        out_shape=one_group
        + one_group
        + (
            jax.ShapeDtypeStruct((segments, layers * rows), bf16),
            jax.ShapeDtypeStruct((sides * segments, LANES), bf16),
            struct(segments, LANES),
        ),
        in_specs=[VMEM] * 3,
        out_specs=(VMEM,) * 9,
        compiler_params=PARAMS,
        cost_estimate=cost(1),
        name="maps",
    )(*indices)
    own_maps, partner_maps, (picks, picks_beside, mine) = maps[:3], maps[3:6], maps[6:]
    joined = pl.pallas_call(
        join_kernel,
        out_shape=struct(sum(a.shape[0] for a in received), LANES),
        in_specs=[pl.BlockSpec(memory_space=pl.ANY)] + [VMEM] * (gx - 1),
        out_specs=VMEM,
        compiler_params=PARAMS,
        name="join",
    )(mine, *received)
    late = lax.ppermute(joined, "gz", swap)
    filled = pl.pallas_call(
        functools.partial(fill_kernel, False, gx, gy, shape, seg),
        out_shape=(fields,) + (struct(strip_rows, LANES),) * sides
        + (struct(partner_strip, LANES),) * sides
        + (struct(2 * segments, LANES),),
        in_specs=[VMEM] * (4 + gx - 1),
        out_specs=(VMEM,) * (2 + 2 * sides),
        compiler_params=PARAMS,
        cost_estimate=cost(1.5),
        name="fill_own",
    )(own, *own_maps, *received)
    own_fields, held = filled[0], filled[-1]
    strips, partner_strips = filled[1 : 1 + sides], filled[1 + sides : 1 + 2 * sides]
    if gy == 2:
        routes = [(0, swap)]
    else:
        up = [(i, i + 1) for i in range(gy - 1)]
        routes = [(1, up), (0, [(j, i) for i, j in up])]
    along = [lax.ppermute(strips[side], "gy", pairs) for side, pairs in routes]
    across = []
    for side, pairs in routes:
        both = [(2 * i + z, 2 * j + 1 - z) for i, j in pairs for z in range(2)]
        across.append(lax.ppermute(partner_strips[side], ("gy", "gz"), both))

    partner_fields = pl.pallas_call(
        functools.partial(fill_kernel, True, gx, gy, shape, seg),
        out_shape=fields,
        in_specs=[VMEM] * 5,
        out_specs=VMEM,
        scratch_shapes=[vmem(segments, LANES)] * 2,
        compiler_params=PARAMS,
        cost_estimate=cost(1.5),
        name="fill_partner",
    )(partner, *partner_maps, late)

    total = 2 * layers + 2
    padded = vmem(total, rows + 2 * PAD, LANES)
    inside, below, levels = pl.pallas_call(
        functools.partial(tile_kernel, gx, gy, shape),
        out_shape=(
            struct(layers, rows, LANES),
            struct(STEPS, segments, LANES),
            struct(sides * STEPS * ITERS * total, HALO, LANES),
        ),
        in_specs=[VMEM] * 3,
        out_specs=(VMEM,) * 3,
        scratch_shapes=[padded] * 3 + [vmem(total, rows, LANES)] * 5,
        compiler_params=PARAMS,
        cost_estimate=cost(7),
        name="tile_sweeps",
    )(own_fields, partner_fields, picks)

    results = pl.pallas_call(
        functools.partial(edge_kernel, gx, gy, shape, seg),
        out_shape=(struct(sides * layers, HALO, LANES),) + (struct(seg, LANES),) * gx,
        in_specs=[VMEM] * (7 + 2 * sides),
        out_specs=(VMEM,) * (1 + gx),
        scratch_shapes=[vmem(segments, LANES)]
        + [vmem(total, 4 * HALO, LANES)] * 3
        + [vmem(total, 2 * HALO, LANES)] * 5,
        compiler_params=PARAMS,
        cost_estimate=cost(1.5),
        name="edge_sweeps",
    )(own_fields, partner_fields, picks_beside, mine, held, below, levels, *along, *across)
    heat, coolant = results[0], results[1]
    returned = [lax.ppermute(results[1 + k], "gx", [(i, (i + k) % gx) for i in range(gx)]) for k in range(1, gx)]
    temperature = pl.pallas_call(
        functools.partial(merge_kernel, gy),
        out_shape=struct(layers, rows, LANES),
        in_specs=[VMEM] * 2,
        out_specs=VMEM,
        compiler_params=PARAMS,
        cost_estimate=cost(1),
        name="merge",
    )(inside, heat)
    for value in returned:
        coolant = coolant + value
    return temperature, coolant[None]


def solution(mesh):
    gx, gy, gz = (mesh.shape[a] for a in ("gx", "gy", "gz"))
    cells = P(("stack", "gz"), "gy", "gx")
    segments = P(("stack", "gy", "gz"), "gx", None)
    return jax.shard_map(
        functools.partial(local, gx, gy, gz),
        mesh=mesh,
        in_specs=(cells, cells, cells, P(None, ("stack", "gz"), "gy", "gx"), segments, segments, P(), P(), P()),
        out_specs=(cells, segments),
        check_vma=False,
    )
```

```python
import functools

import jax
import jax.numpy as jnp
from jax import lax
from jax.experimental import pallas as pl
from jax.experimental.pallas import tpu as pltpu
from jax.sharding import PartitionSpec as P

STEPS = 2
ITERS = 4
HALO = STEPS * ITERS
GROUP = 2 * HALO
LANES = 128
RAW = 5
FIELDS = 7
coolant_gain = 0.5

VMEM = pl.BlockSpec(memory_space=pltpu.VMEM)
PARAMS = pltpu.CompilerParams(vmem_limit_bytes=40 * 1024 * 1024)


def cost(microseconds):
    return pl.CostEstimate(flops=0, bytes_accessed=int(microseconds * 3e6), transcendentals=0)


def lane_of(rows):
    return lax.broadcasted_iota(jnp.int32, (rows, LANES), 1)


def take(value, index):
    return jnp.take_along_axis(value, index, axis=1, mode="promise_in_bounds")


def edge_columns(rows, turned):
    j = lane_of(rows) % GROUP
    first = j < HALO
    return jnp.where(first, LANES - HALO + j, j - HALO) if not turned else jnp.where(first, j, LANES - GROUP + j)


def split(value):
    high = value.astype(jnp.bfloat16)
    low = (value - high.astype(jnp.float32)).astype(jnp.bfloat16)
    return high, low


def exact_dot(onehot, value):
    high, low = split(value)
    both = jnp.concatenate([high, low], axis=0)
    return jnp.dot(jnp.concatenate([onehot, onehot], axis=1), both, preferred_element_type=jnp.float32)


def coupling(coef, warmth):
    flow = coef * warmth
    second = coolant_gain * coef * coef
    return jnp.concatenate([coef, flow, second, flow - second * warmth], axis=1)


def flip(z, layers, i):
    return jnp.where(z == 0, i, layers - 1 - i)


def pack_kernel(shape, u_ref, p_ref, c_ref, k_ref, f_ref, x_ref, *refs):
    own_ref, left_ref, right_ref, seg_ref = refs[3:7]
    sems = refs[-1]
    layers, rows = shape
    seg = f_ref.shape[0]
    z = lax.axis_index("gz")
    plane = layers * rows
    copies = []

    def fetch(src, dst):
        copies.append(pltpu.make_async_copy(src, dst, sems.at[len(copies)]))
        copies[-1].start()

    fetch(k_ref, own_ref.at[pl.ds(0, 2 * plane), :])
    for field, ref in enumerate((u_ref, p_ref, c_ref), 2):
        fetch(ref, own_ref.at[pl.ds(field * plane, plane), :])
    for j, ref in enumerate((x_ref, f_ref)):
        fetch(ref, own_ref.at[pl.ds(RAW * plane + j * seg, seg), :])
    for table, place in zip(refs[:3], refs[7:10]):
        fetch(table, place)
    chunk = rows // 4
    lane = lane_of(chunk)
    first = lane % GROUP < HALO
    columns = edge_columns(chunk, False), edge_columns(chunk, True)
    edges = RAW * plane + 2 * seg

    def gather(field, at, g):
        value = None
        for i in range(layers):
            start = pl.multiple_of((field * layers + flip(z, layers, i)) * rows + at, chunk)
            taken = take(own_ref[pl.ds(start, chunk), :], columns[g % 2])
            value = taken if value is None else jnp.where(lane // GROUP == (g // 2) * layers + i, taken, value)
        return value

    def place(g, part):
        return pl.ds(edges + ((g % 2) * RAW + part) * chunk, chunk)

    copies[0].wait()
    roots = pl.ds(0, 2 * plane)
    own_ref[roots, :] = jnp.sqrt(own_ref[roots, :])
    for field in range(4):
        if field >= 2:
            copies[field - 1].wait()
        for part in range(4):
            value = gather(field, part * chunk, field)
            if field >= 2:
                value = jnp.where(lane < LANES // 2, own_ref[place(field, part), :], value)
            own_ref[place(field, part), :] = value
    copies[3].wait()
    for g in range(4):
        value = gather(4, g * chunk, g)
        if g >= 2:
            value = jnp.where(lane < LANES // 2, own_ref[place(g, 4), :], value)
        own_ref[place(g, 4), :] = value
    for part in range(RAW):
        even, odd = own_ref[place(0, part), :], own_ref[place(1, part), :]
        left_ref[part * chunk : (part + 1) * chunk, :] = jnp.where(first, odd, even)
        right_ref[part * chunk : (part + 1) * chunk, :] = jnp.where(first, even, odd)
    for copy in copies[4:]:
        copy.wait()
    segments = own_ref[RAW * plane : RAW * plane + 2 * seg, :]
    seg_ref[...] = segments
    left_ref[RAW * chunk :, :] = segments
    right_ref[RAW * chunk :, :] = segments


class Strips:
    def __init__(self, refs, starts, cells_ref, start, rows, layers):
        self.refs, self.starts = refs, starts
        self.cells_ref, self.start = cells_ref, start
        self.rows, self.layers = rows, layers

    def both(self, field, start, n, x, gx, partner):
        chunk = self.rows // 4
        if field < 4:
            g, at = field, start
        else:
            g, at = start // chunk, 4 * chunk + start % chunk
        a, b = (ref[at + begin : at + begin + n, :] for ref, begin in zip(self.refs, self.starts))
        at = self.start + (g % 2) * RAW * chunk + at
        inside = self.cells_ref[at : at + n, :]
        from_left, from_right = jnp.where(x > 0, b, 0.0), jnp.where(x < gx - 1, a, 0.0)
        lane = lane_of(n)
        first = (lane % GROUP < HALO) if g % 2 == 0 else (lane % GROUP >= HALO)
        half = self.layers * GROUP
        src = lane % half
        if partner:
            src = (self.layers - 1 - src // GROUP) * GROUP + src % GROUP
        if g % 2 == 1:
            src = jnp.where(src % GROUP < HALO, src + HALO, src - HALO)
        src = src + half * (g // 2)
        return take(jnp.where(first, from_left, inside), src), take(jnp.where(first, inside, from_right), src)


def place_segments(x, gx, seg, coef_ref, warmth_ref, sources):
    for k, ref, at in sources:
        place = pl.ds(pl.multiple_of(lax.rem(x + k, gx) * seg, seg), seg)
        coef_ref[place, :] = ref[at : at + seg, :]
        warmth_ref[place, :] = ref[at + seg : at + 2 * seg, :]


def tables(z, group, layers, holder_ref, stratum_ref, transverse_ref):
    holder = holder_ref[pl.ds(group, 1), :]
    layer = stratum_ref[pl.ds(group, 1), :]
    layer = jnp.where(z == 0, layer, layers - 1 - layer)
    row = transverse_ref[pl.ds(group, 1), :]
    n = holder.shape[1]
    which = lax.broadcasted_iota(jnp.int32, (8, n), 0)
    stacked = jnp.where(which == 0, holder, jnp.where(which == 1, layer, row))
    eye = lax.broadcasted_iota(jnp.int32, (n, n), 0) == lax.broadcasted_iota(jnp.int32, (n, n), 1)
    columns = lax.dot_general(
        eye.astype(jnp.float32).astype(jnp.bfloat16),
        stacked.astype(jnp.float32).astype(jnp.bfloat16),
        (((1,), (1,)), ((), ())),
        preferred_element_type=jnp.float32,
    )
    return (holder, layer, row), columns


def as_onehot(mask):
    return jnp.where(mask, 1.0, 0.0).astype(jnp.bfloat16)


def combine(raw, added):
    s, t, u, power, storage = raw
    wall, flow, second, later = (added[:, i * LANES : (i + 1) * LANES] for i in range(4))
    return s, t, s * u, storage + wall, power + storage * u + flow, power + later, storage + second


def lengths_of(gx, chunk, seg):
    return [RAW * chunk + 2 * seg] * 2 + [2 * seg] * (gx - 3)


def edge_at(top, rows):
    return 0 if top is True else rows - HALO if top is False else pl.multiple_of(jnp.where(top, 0, rows - HALO), HALO)


def inner_at(top, rows):
    return HALO if top is True else rows - 2 * HALO if top is False else pl.multiple_of(jnp.where(top, HALO, rows - 2 * HALO), HALO)


def sides_of(gy, y):
    return [(y == 1, True)] if gy == 2 else [(True, y > 0), (False, y < gy - 1)]


def maps_kernel(gx, gy, shape, holder_ref, stratum_ref, transverse_ref, *refs):
    layers, rows = shape
    plane = layers * rows
    picks_ref, beside_ref, mine_ref = refs[6:]
    x, y, z = (lax.axis_index(a) for a in ("gx", "gy", "gz"))
    n = holder_ref.shape[1]
    for partner in range(2):
        cells_ref, rows_ref, masks_ref = refs[3 * partner : 3 * partner + 3]
        group = y * 2 + ((1 - z) if partner else z)
        (holder, layer, row), columns = tables(z, group, layers, holder_ref, stratum_ref, transverse_ref)
        cell = jnp.where(holder == x, layer * rows + row, -1)
        cells_ref[...] = as_onehot(lax.broadcasted_iota(jnp.int32, (plane, n), 0) == cell)
        rows_ref[...] = as_onehot(lax.broadcasted_iota(jnp.int32, (rows, n), 0) == row)
        holder, layer, row = (columns[:, j : j + 1].astype(jnp.int32) for j in range(3))
        lane = lane_of(n)
        first = lane % GROUP < HALO
        here = lane // GROUP == layer + partner * layers
        for side, begin in enumerate((x - 1, x)):
            mine = jnp.logical_and(here, holder == jnp.where(first, begin, begin + 1))
            masks_ref[side * n : (side + 1) * n, :] = jnp.where(mine, 1.0, 0.0)
        if partner:
            continue
        mine = holder == x
        mine_ref[...] = jnp.where(jnp.logical_and(mine, lane >= 0), 1.0, 0.0)
        spoilt = None
        for side, (above, live) in enumerate(sides_of(gy, y)):
            start = edge_at(above, rows)
            part = jnp.logical_and(row // HALO == start // HALO, live)
            spoilt = part if spoilt is None else jnp.logical_or(spoilt, part)
            cell = jnp.where(jnp.logical_and(mine, part), layer * HALO + row - start, -1)
            beside_ref[side * n : (side + 1) * n, :] = as_onehot(lane == cell)
        cell = jnp.where(jnp.logical_and(mine, jnp.logical_not(spoilt)), layer * rows + row, -1)
        picks_ref[...] = as_onehot(lax.broadcasted_iota(jnp.int32, (n, plane), 1) == cell)


def join_kernel(mine_ref, *refs):
    out_ref, at = refs[-1], 0
    for ref in refs[:-1]:
        n = ref.shape[0]
        out_ref[at : at + n, :] = ref[...]
        at += n


def partner_rows(layers):
    whole, at = [], 1
    for i in range(layers - 1, -1, -1):
        whole.append((i, HALO - layers + i, at))
        at += HALO - layers + i
    stride = -(-at // 8) * 8
    later, at = [], 0
    for f in range(2):
        for i in range(layers - 1, -1, -1):
            if ITERS - 1 - layers + i > 0:
                later.append((f, i, ITERS - 1 - layers + i, at))
                at += ITERS - 1 - layers + i
    return whole, stride, later, -(-at // 8) * 8


def fill_kernel(partner, gx, gy, shape, seg, *refs):
    layers, rows = shape
    cells_ref, where_ref, rows_ref, masks_ref = refs[:4]
    plane, chunk = layers * rows, rows // 4
    lengths = lengths_of(gx, chunk, seg)
    if partner:
        sources = [(refs[4], sum(lengths[:k])) for k in range(gx - 1)]
        refs = refs[5:]
    else:
        sources = [(ref, 0) for ref in refs[4 : 4 + gx - 1]]
        refs = refs[4 + gx - 1 :]
    sides = 1 if gy == 2 else 2
    out_ref = refs[0]
    if partner:
        coef_ref, warmth_ref = refs[1:3]
    else:
        strip_refs, partner_refs, segments_ref = refs[1 : 1 + sides], refs[1 + sides : 1 + 2 * sides], refs[1 + 2 * sides]
        n = segments_ref.shape[0] // 2
        coef_ref, warmth_ref = segments_ref.at[pl.ds(0, n), :], segments_ref.at[pl.ds(n, n), :]
    x, y, z = (lax.axis_index(a) for a in ("gx", "gy", "gz"))
    base = layers if partner else 0
    distances = [1, gx - 1] + list(range(2, gx - 1))
    held = [(k, ref, at + (RAW * chunk if j < 2 else 0)) for j, (k, (ref, at)) in enumerate(zip(distances, sources))]
    place_segments(x, gx, seg, coef_ref, warmth_ref, [(0, cells_ref, RAW * plane)] + held)
    coef, warmth = coef_ref[...], warmth_ref[...]
    n = coef.shape[0]
    added = exact_dot(where_ref[...], coupling(coef, warmth))
    near = edge_columns(n, False)
    beside = []
    for side in range(2):
        masked = take(coef, near) * masks_ref[side * n : (side + 1) * n, :]
        beside.append(exact_dot(rows_ref[...], coupling(masked, take(warmth, near))))
    planes = layers + 2
    for i in range(layers):
        src = flip(z, layers, i)
        raw = [cells_ref[pl.ds(pl.multiple_of((f * layers + src) * rows, rows), rows), :] for f in range(RAW)]
        for f, value in enumerate(combine(raw, added[i * rows : (i + 1) * rows])):
            out_ref[f * planes + i] = value
    strips = Strips(
        [ref for ref, _ in sources[:2]], [at for _, at in sources[:2]], cells_ref, RAW * plane + 2 * seg, rows, layers
    )
    half = lane_of(chunk) // (LANES // 2) == (1 if partner else 0)
    for part in range(4):
        here = slice(part * chunk, (part + 1) * chunk)
        raw = [strips.both(f, part * chunk, chunk, x, gx, partner) for f in range(RAW)]
        for side in range(2):
            cells = [jnp.where(half, value[side], 0.0) for value in raw]
            for f, value in enumerate(combine(cells, beside[side][here])):
                out_ref[f * planes + layers + side, here, :] = value
    if partner:
        return
    low = lane_of(HALO) < LANES // 2
    upper = lax.broadcasted_iota(jnp.int32, (HALO, LANES), 0) < HALO // 2
    first = lane_of(HALO) % GROUP < HALO
    sent = FIELDS - 1
    for strip_ref, partner_ref, (top, _) in zip(strip_refs, partner_refs, sides_of(gy, y)):
        edge = pl.ds(edge_at(top, rows), HALO)

        def shrink(values):
            *whole, e, g = values
            e = jnp.where(top, e, pltpu.roll(e, HALO // 2, 0))
            g = jnp.where(top, pltpu.roll(g, HALO // 2, 0), g)
            return whole + [jnp.where(upper, e, g)]

        def give(ref, at, values):
            for f, value in enumerate(values):
                ref[at + f * HALO : at + (f + 1) * HALO, :] = value

        for i in range(layers):
            give(strip_ref, i * sent * HALO, shrink([out_ref[f * planes + i, edge, :] for f in range(FIELDS)]))
        outer = []
        for f in range(FIELDS):
            left, right = (out_ref[f * planes + layers + side, edge, :] for side in range(2))
            outer.append(jnp.where(first, left, right))
        outer = shrink(outer)
        values = [jnp.where(low, outer[j], pltpu.roll(outer[j + 1], LANES // 2, 1)) for j in range(0, sent, 2)]
        give(strip_ref, layers * sent * HALO, values)
        whole, stride, later, shared = partner_rows(layers)
        pieces = [(f, i, m, f * stride + at) for f in range(sent - 1) for i, m, at in whole]
        pieces += [(sent - 1 + f, i, m, (sent - 1) * stride + at) for f, i, m, at in later]
        for f, i, m, at in pieces:
            start = edge_at(top, rows) + jnp.where(top, 0, HALO - m)
            partner_ref[at : at + m, :] = out_ref[f * planes + i, pl.ds(start, m), :]
        give(partner_ref, (sent - 1) * stride + shared, values)


def planes_of(count, total):
    return list(range(count)) + [total - 2, total - 1]


def lateral(buf, at, n, which):
    sums = []
    for i in which:
        centre = buf[i, pl.ds(at, n), :]
        beside = pltpu.roll(centre, 1, 1) + pltpu.roll(centre, LANES - 1, 1)
        sums.append(beside + (buf[i, pl.ds(at - 1, n), :] + buf[i, pl.ds(at + 1, n), :]))
    return sums


def vertical(planes, edges, count):
    sums = []
    for i in range(count):
        near = [planes[j] for j in (i - 1, i + 1) if 0 <= j < len(planes)]
        sums.append(functools.reduce(jnp.add, near))
    for edge in edges:
        lane = lane_of(edge.shape[0])
        up = jnp.where(lane >= GROUP, pltpu.roll(edge, GROUP, 1), 0.0)
        down = jnp.where(lane < LANES - GROUP, pltpu.roll(edge, LANES - GROUP, 1), 0.0)
        sums.append(up + down)
    return sums


def coefficients(s_ref, at, n, raw, dests, to, outside):
    a_ref, q_ref, r_ref, e_ref, g_ref, root_ref = dests
    total = s_ref.shape[0]
    sums = lateral(s_ref, at, n, range(total))
    t = [raw(1, i) for i in range(total)]
    above = vertical(t[:-2], t[-2:], total - 2)
    here = pl.ds(to, n)
    for i in range(total):
        s = s_ref[i, pl.ds(at, n), :]
        diag = raw(3, i) + s * sums[i] + t[i] * above[i]
        if outside or i >= total - 2:
            inverse = 1.0 / jnp.where(diag > 0.0, diag, 1.0)
            root = jnp.where(s > 0.0, 1.0 / jnp.where(s > 0.0, s, 1.0), 0.0)
        else:
            inverse, root = 1.0 / diag, 1.0 / s
        if i < root_ref.shape[0]:
            root_ref[i, here, :] = root
        scaled = s * inverse
        a_ref[i, here, :] = s * scaled
        r_ref[i, here, :] = raw(4, i) * scaled
        e_ref[i, here, :] = raw(5, i) * scaled
        g_ref[i, here, :] = raw(6, i) * inverse
        q_ref[i, here, :] = t[i] * root


def sweep(src_ref, dst_ref, at, n, count, coefs, base):
    a_ref, q_ref, r_ref = coefs[:3]
    total = src_ref.shape[0]
    here, there = pl.ds(base, n), pl.ds(at, n)
    which = planes_of(count, total)
    sums = lateral(src_ref, at, n, which)
    scaled = [q_ref[i, here, :] * src_ref[i, there, :] for i in planes_of(min(count + 1, total - 2), total)]
    above = vertical(scaled[:-2], scaled[-2:], count)
    for j, i in enumerate(which):
        dst_ref[i, there, :] = r_ref[i, here, :] + a_ref[i, here, :] * (sums[j] + q_ref[i, here, :] * above[j])


def next_rhs(coefs, v_ref, at, n, base):
    r_ref, e_ref, g_ref = coefs[2:5]
    here = pl.ds(base, n)
    for i in range(v_ref.shape[0]):
        r_ref[i, here, :] = e_ref[i, here, :] + g_ref[i, here, :] * v_ref[i, pl.ds(at, n), :]


def meet(v_ref, at, n, count, back):
    total = v_ref.shape[0]
    here = pl.ds(at, n)
    lane = lane_of(n)
    j, group = lane % GROUP, lane // GROUP
    outer = jnp.logical_or(lane < ITERS, lane >= LANES - ITERS)
    left, right = v_ref[total - 2, here, :], v_ref[total - 1, here, :]
    middle = jnp.where(j < HALO, right, left)
    for i in range(count):
        value = v_ref[i, here, :]
        if back:
            moved = pltpu.roll(value, (i * GROUP + HALO) % LANES, 1)
            left = jnp.where(jnp.logical_and(group == i, j >= GROUP - ITERS), moved, left)
            right = jnp.where(jnp.logical_and(group == i, j < ITERS), moved, right)
        v_ref[i, here, :] = jnp.where(outer, pltpu.roll(middle, LANES - (i * GROUP + HALO), 1), value)
    if back:
        v_ref[total - 2, here, :] = left
        v_ref[total - 1, here, :] = right


def needed(layers, n):
    return min(2 * layers, layers + STEPS * ITERS - 1 - n)


def two_steps(layers, sweep_all, between, after):
    for step in range(STEPS):
        whole = [n for n in range(step * ITERS, (step + 1) * ITERS) if needed(layers, n) == 2 * layers]
        pairs = len(whole) // 2

        def pair(k, carry):
            n = step * ITERS + 2 * k
            sweep_all(n, 0, 2 * layers)
            sweep_all(n + 1, 1, 2 * layers)
            return carry

        if pairs:
            lax.fori_loop(0, pairs, pair, 0)
        for n in range(step * ITERS + 2 * pairs, (step + 1) * ITERS):
            sweep_all(n, n % 2, needed(layers, n))
        after(step)
        if step < STEPS - 1:
            between()


PAD = 8


def tile_kernel(gx, gy, shape, *refs):
    layers, rows = shape
    own_ref, partner_ref, picks_ref, out_ref, below_ref, level_ref = refs[:6]
    s_ref, va_ref, vb_ref = refs[6:9]
    coefs = refs[9:]
    x, y, z = (lax.axis_index(a) for a in ("gx", "gy", "gz"))
    total = 2 * layers + 2
    zeros = jnp.zeros((PAD, LANES), jnp.float32)
    for ref in (s_ref, va_ref, vb_ref):
        for i in range(total):
            ref[i, 0:PAD, :] = zeros
            ref[i, PAD + rows : PAD + rows + PAD, :] = zeros

    def field(f, i, here):
        j = f * (layers + 2)
        if i >= 2 * layers:
            j = j + i - layers
            return own_ref[j, here, :] + partner_ref[j, here, :]
        return own_ref[j + i, here, :] if i < layers else partner_ref[j + i - layers, here, :]

    for i in range(total):
        s_ref[i, PAD : PAD + rows, :] = field(0, i, slice(None))
        va_ref[i, PAD : PAD + rows, :] = field(2, i, slice(None))
    n = 8
    for at in range(0, rows, n):
        coefficients(s_ref, PAD + at, n, lambda f, i: field(f, i, slice(at, at + n)), coefs, at, False)

    bufs = (va_ref, vb_ref)
    sides = sides_of(gy, y)

    def sweep_all(number, which, count):
        src_ref, dst_ref = bufs[which], bufs[1 - which]
        for side, (above, _) in enumerate(sides):
            inner = pl.ds(PAD + inner_at(above, rows), HALO)
            for i in range(total):
                level_ref[(side * STEPS * ITERS + number) * total + i] = src_ref[i, inner, :]
        for at in range(0, rows, n):
            sweep(src_ref, dst_ref, PAD + at, n, count, coefs, at)

    def after(step):
        last = step == STEPS - 1
        for at in range(0, rows, n):
            meet(va_ref, PAD + at, n, layers if last else 2 * layers, not last)
        heat = []
        for i in range(layers):
            here = pl.ds(PAD, rows)
            heat.append(va_ref[i, here, :] * coefs[5][i])
            if step == STEPS - 1:
                out_ref[flip(z, layers, i)] = heat[-1]
        below_ref[step] = exact_dot(picks_ref[...], jnp.concatenate(heat, axis=0))

    def between():
        for at in range(0, rows, n):
            next_rhs(coefs, va_ref, PAD + at, n, at)

    two_steps(layers, sweep_all, between, after)


def edge_kernel(gx, gy, shape, seg, *refs):
    layers, rows = shape
    own_ref, partner_ref, picks_ref, mine_ref, segments_ref, below_ref, level_ref = refs[:7]
    sides_n = 1 if gy == 2 else 2
    along, across = refs[7 : 7 + sides_n], refs[7 + sides_n : 7 + 2 * sides_n]
    refs = refs[7 + 2 * sides_n :]
    heat_ref, returns = refs[0], refs[1 : 1 + gx]
    ret_ref, s_ref, va_ref, vb_ref = refs[1 + gx : 5 + gx]
    coefs = refs[5 + gx :]
    x, y, z = (lax.axis_index(a) for a in ("gx", "gy", "gz"))
    total = 2 * layers + 2
    count = mine_ref.shape[0]
    below = [below_ref[step] for step in range(STEPS)]
    lane = lane_of(HALO)
    low, first = lane < LANES // 2, lane % GROUP < HALO
    columns = edge_columns(HALO, False)
    bufs = (va_ref, vb_ref)

    def tile(j):
        return pl.ds(j if isinstance(j, int) else pl.multiple_of(j, HALO), HALO)

    for side, (above, live) in enumerate(sides_of(gy, y)):
        def place(when_top, otherwise):
            if above is True or above is False:
                return when_top * HALO if above else otherwise * HALO
            return jnp.where(above, when_top * HALO, otherwise * HALO)

        outer, strip, edge, inner = place(0, 3), place(1, 2), place(2, 1), place(3, 0)
        edge_rows = tile(edge_at(above, rows))
        inner_rows = tile(inner_at(above, rows))

        def field(f, i, here):
            j = f * (layers + 2)
            if i >= 2 * layers:
                j = j + i - layers
                return own_ref[j, here, :] + partner_ref[j, here, :]
            return own_ref[j + i, here, :] if i < layers else partner_ref[j + i - layers, here, :]

        t_ref, d_ref, q_ref, e_ref, g_ref = coefs[1], coefs[0], coefs[2], coefs[3], coefs[4]
        keep = {0: s_ref, 1: t_ref, 2: va_ref, 3: d_ref, 4: q_ref, 5: e_ref, 6: g_ref}
        zeros = jnp.zeros((HALO, LANES), jnp.float32)
        src = lane % (LANES // 2)
        turned = (layers - 1 - src // GROUP) * GROUP + src % GROUP
        half_tile = lax.broadcasted_iota(jnp.int32, (HALO, LANES), 0) < HALO // 2

        def unpack(value, f):
            if f < FIELDS - 2:
                return value
            turned_value = pltpu.roll(value, HALO // 2, 0)
            if f == FIELDS - 2:
                at_top, at_bottom = jnp.where(half_tile, 0.0, turned_value), jnp.where(half_tile, value, 0.0)
            else:
                at_top, at_bottom = jnp.where(half_tile, 0.0, value), jnp.where(half_tile, turned_value, 0.0)
            return jnp.where(above, at_top, at_bottom)

        whole, stride, later, shared = partner_rows(layers)
        sublane = lax.broadcasted_iota(jnp.int32, (HALO, LANES), 0)

        def nearest(ref, m, at):
            at_top = jnp.where(sublane >= HALO - m, ref[at - HALO + m : at + m, :], 0.0)
            return jnp.where(above, at_top, jnp.where(sublane < m, ref[at : at + HALO, :], 0.0))

        for f in range(FIELDS):
            g = min(f, FIELDS - 2)
            if f < FIELDS - 2:
                rows_of = {i: (m, f * stride + at) for i, m, at in whole}
            else:
                rows_of = {i: (m, (FIELDS - 2) * stride + at) for which, i, m, at in later if which == f - FIELDS + 2}
            values, inside = [], zeros
            for i in range(2 * layers):
                if i < layers:
                    at = (i * (FIELDS - 1) + g) * HALO
                    value = unpack(along[side][at : at + HALO, :], f)
                else:
                    j = 2 * layers - 1 - i
                    value = nearest(across[side], *rows_of[j]) if j in rows_of else zeros
                values.append(value)
                inside = jnp.where(lane // GROUP == i, take(value, columns), inside)
            half = (LANES // 2) * (g % 2)
            at = (layers * (FIELDS - 1) + g // 2) * HALO
            a = take(along[side][at : at + HALO, :], src + half)
            at = (FIELDS - 2) * stride + shared + (g // 2) * HALO
            b = take(across[side][at : at + HALO, :], turned + half)
            outside = unpack(jnp.where(low, a, b), f)
            values += [jnp.where(first, outside, inside), jnp.where(first, inside, outside)]
            for i, value in enumerate(values):
                ref, shift = keep[f], 0 if f in (0, 2) else HALO
                ref[i, tile(strip - shift), :] = value
                ref[i, tile(edge - shift), :] = field(f, i, edge_rows)
        for i in range(total):
            s_ref[i, tile(outer), :] = zeros
            va_ref[i, tile(outer), :] = zeros
            vb_ref[i, tile(outer), :] = zeros
            s_ref[i, tile(inner), :] = field(0, i, inner_rows)
        n = 2 * HALO
        held = [[keep[f][i, pl.ds(0, n), :] for i in range(total)] if f in (1, 3, 4, 5, 6) else None for f in range(FIELDS)]
        coefficients(s_ref, HALO, n, lambda f, i: held[f][i], coefs, 0, True)

        def sweep_all(number, which, needed_layers):
            src_ref, dst_ref = bufs[which], bufs[1 - which]
            for i in range(total):
                src_ref[i, tile(inner), :] = level_ref[(side * STEPS * ITERS + number) * total + i]
            sweep(src_ref, dst_ref, HALO, n, needed_layers, coefs, 0)

        picks = picks_ref[side * count : (side + 1) * count, :]

        def after(step):
            last = step == STEPS - 1
            meet(va_ref, HALO, n, layers if last else 2 * layers, not last)
            heat = []
            for i in range(layers):
                heat.append(va_ref[i, tile(edge), :] * coefs[5][i, tile(edge - HALO), :])
                if step == STEPS - 1:
                    heat_ref[side * layers + flip(z, layers, i)] = heat[-1]
            heat.append(jnp.zeros((LANES - layers * HALO, LANES), jnp.float32))
            below[step] = below[step] + exact_dot(picks, jnp.concatenate(heat, axis=0))

        two_steps(layers, sweep_all, lambda: next_rhs(coefs, va_ref, HALO, n, 0), after)

    coef, warmth = segments_ref[:count, :], segments_ref[count:, :]
    for step in range(STEPS):
        warmth = warmth + coolant_gain * coef * (below[step] - warmth)
    ret_ref[...] = jnp.where(mine_ref[...] > 0.0, warmth, 0.0)
    for k, ref in enumerate(returns):
        ref[...] = ret_ref[pl.ds(pl.multiple_of(lax.rem(x + k, gx) * seg, seg), seg), :]


def merge_kernel(gy, whole_ref, heat_ref, out_ref):
    layers, rows, _ = whole_ref.shape
    out_ref[...] = whole_ref[...]
    for side, (above, live) in enumerate(sides_of(gy, lax.axis_index("gy"))):
        def put(side=side, above=above):
            out_ref[:, pl.ds(edge_at(above, rows), HALO), :] = heat_ref[side * layers : (side + 1) * layers]

        if live is True:
            put()
        else:
            pl.when(live)(put)


def local(gx, gy, gz, u, power, storage, conductance, warmth, coef, holder, stratum, transverse):
    layers, rows, columns = u.shape
    seg = warmth.shape[1]
    segments = stratum.shape[1]
    if gz != 2 or gx < 3 or columns != LANES or 2 * layers * GROUP != LANES or rows % 32:
        raise ValueError("unsupported shape")
    holder = holder[:, :, 0]
    shape = (layers, rows)
    f32 = jnp.float32
    chunk = rows // 4
    wide = RAW * chunk + 2 * seg

    def struct(*dims):
        return jax.ShapeDtypeStruct(dims, f32)

    def vmem(*dims):
        return pltpu.VMEM(dims, f32)

    indices = (holder, stratum, transverse)
    flat = [a.reshape(-1, LANES) for a in (u, power, storage, conductance, warmth, coef)]
    own, to_left, to_right, only, *indices = pl.pallas_call(
        functools.partial(pack_kernel, shape),
        out_shape=(
            struct(RAW * layers * rows + 2 * seg + 2 * RAW * chunk, LANES),
            struct(wide, LANES),
            struct(wide, LANES),
            struct(2 * seg, LANES),
            *(jax.ShapeDtypeStruct(a.shape, a.dtype) for a in indices),
        ),
        in_specs=[pl.BlockSpec(memory_space=pltpu.HBM)] * 9,
        out_specs=(VMEM,) * 7,
        scratch_shapes=[pltpu.SemaphoreType.DMA((9,))],
        compiler_params=PARAMS,
        name="pack",
    )(*(pltpu.with_memory_space_constraint(a, pltpu.HBM) for a in (*flat, *indices)))

    swap = [(0, 1), (1, 0)]
    partner = lax.ppermute(own, "gz", swap)
    def from_distance(value, k):
        return lax.ppermute(value, "gx", [(i, (i - k) % gx) for i in range(gx)])

    received = [from_distance(to_left, 1), from_distance(to_right, gx - 1)]
    received += [from_distance(only, k) for k in range(2, gx - 1)]

    sides = 1 if gy == 2 else 2
    fields = struct(FIELDS * (layers + 2), rows, LANES)
    strip_rows = (FIELDS - 1) * layers * HALO + (FIELDS - 1) // 2 * HALO
    _, stride, _, shared = partner_rows(layers)
    partner_strip = (FIELDS - 2) * stride + shared + (FIELDS - 1) // 2 * HALO
    sides = 1 if gy == 2 else 2
    bf16 = jnp.bfloat16
    one_group = (
        jax.ShapeDtypeStruct((layers * rows, segments), bf16),
        jax.ShapeDtypeStruct((rows, segments), bf16),
        struct(2 * segments, LANES),
    )
    maps = pl.pallas_call(
        functools.partial(maps_kernel, gx, gy, shape),
        out_shape=one_group
        + one_group
        + (
            jax.ShapeDtypeStruct((segments, layers * rows), bf16),
            jax.ShapeDtypeStruct((sides * segments, LANES), bf16),
            struct(segments, LANES),
        ),
        in_specs=[VMEM] * 3,
        out_specs=(VMEM,) * 9,
        compiler_params=PARAMS,
        cost_estimate=cost(1),
        name="maps",
    )(*indices)
    own_maps, partner_maps, (picks, picks_beside, mine) = maps[:3], maps[3:6], maps[6:]
    joined = pl.pallas_call(
        join_kernel,
        out_shape=struct(sum(a.shape[0] for a in received), LANES),
        in_specs=[pl.BlockSpec(memory_space=pl.ANY)] + [VMEM] * (gx - 1),
        out_specs=VMEM,
        compiler_params=PARAMS,
        name="join",
    )(mine, *received)
    late = lax.ppermute(joined, "gz", swap)
    filled = pl.pallas_call(
        functools.partial(fill_kernel, False, gx, gy, shape, seg),
        out_shape=(fields,) + (struct(strip_rows, LANES),) * sides
        + (struct(partner_strip, LANES),) * sides
        + (struct(2 * segments, LANES),),
        in_specs=[VMEM] * (4 + gx - 1),
        out_specs=(VMEM,) * (2 + 2 * sides),
        compiler_params=PARAMS,
        cost_estimate=cost(1.5),
        name="fill_own",
    )(own, *own_maps, *received)
    own_fields, held = filled[0], filled[-1]
    strips, partner_strips = filled[1 : 1 + sides], filled[1 + sides : 1 + 2 * sides]
    if gy == 2:
        routes = [(0, swap)]
    else:
        up = [(i, i + 1) for i in range(gy - 1)]
        routes = [(1, up), (0, [(j, i) for i, j in up])]
    along = [lax.ppermute(strips[side], "gy", pairs) for side, pairs in routes]
    across = []
    for side, pairs in routes:
        both = [(2 * i + z, 2 * j + 1 - z) for i, j in pairs for z in range(2)]
        across.append(lax.ppermute(partner_strips[side], ("gy", "gz"), both))

    partner_fields = pl.pallas_call(
        functools.partial(fill_kernel, True, gx, gy, shape, seg),
        out_shape=fields,
        in_specs=[VMEM] * 5,
        out_specs=VMEM,
        scratch_shapes=[vmem(segments, LANES)] * 2,
        compiler_params=PARAMS,
        cost_estimate=cost(1.5),
        name="fill_partner",
    )(partner, *partner_maps, late)

    total = 2 * layers + 2
    padded = vmem(total, rows + 2 * PAD, LANES)
    inside, below, levels = pl.pallas_call(
        functools.partial(tile_kernel, gx, gy, shape),
        out_shape=(
            struct(layers, rows, LANES),
            struct(STEPS, segments, LANES),
            struct(sides * STEPS * ITERS * total, HALO, LANES),
        ),
        in_specs=[VMEM] * 3,
        out_specs=(VMEM,) * 3,
        scratch_shapes=[padded] * 3 + [vmem(total, rows, LANES)] * 5 + [vmem(layers, rows, LANES)],
        compiler_params=PARAMS,
        cost_estimate=cost(7),
        name="tile_sweeps",
    )(own_fields, partner_fields, picks)

    results = pl.pallas_call(
        functools.partial(edge_kernel, gx, gy, shape, seg),
        out_shape=(struct(sides * layers, HALO, LANES),) + (struct(seg, LANES),) * gx,
        in_specs=[VMEM] * (7 + 2 * sides),
        out_specs=(VMEM,) * (1 + gx),
        scratch_shapes=[vmem(segments, LANES)]
        + [vmem(total, 4 * HALO, LANES)] * 3
        + [vmem(total, 2 * HALO, LANES)] * 5
        + [vmem(layers, 2 * HALO, LANES)],
        compiler_params=PARAMS,
        cost_estimate=cost(1.5),
        name="edge_sweeps",
    )(own_fields, partner_fields, picks_beside, mine, held, below, levels, *along, *across)
    heat, coolant = results[0], results[1]
    returned = [lax.ppermute(results[1 + k], "gx", [(i, (i + k) % gx) for i in range(gx)]) for k in range(1, gx)]
    temperature = pl.pallas_call(
        functools.partial(merge_kernel, gy),
        out_shape=struct(layers, rows, LANES),
        in_specs=[VMEM] * 2,
        out_specs=VMEM,
        compiler_params=PARAMS,
        cost_estimate=cost(1),
        name="merge",
    )(inside, heat)
    for value in returned:
        coolant = coolant + value
    return temperature, coolant[None]


def solution(mesh):
    gx, gy, gz = (mesh.shape[a] for a in ("gx", "gy", "gz"))
    cells = P(("stack", "gz"), "gy", "gx")
    segments = P(("stack", "gy", "gz"), "gx", None)
    return jax.shard_map(
        functools.partial(local, gx, gy, gz),
        mesh=mesh,
        in_specs=(cells, cells, cells, P(None, ("stack", "gz"), "gy", "gx"), segments, segments, P(), P(), P()),
        out_specs=(cells, segments),
        check_vma=False,
    )
```

```python
import functools

import jax
import jax.numpy as jnp
from jax import lax
from jax.experimental import pallas as pl
from jax.experimental.pallas import tpu as pltpu
from jax.sharding import PartitionSpec as P

STEPS = 2
ITERS = 4
HALO = STEPS * ITERS
GROUP = 2 * HALO
LANES = 128
RAW = 5
FIELDS = 7
coolant_gain = 0.5

VMEM = pl.BlockSpec(memory_space=pltpu.VMEM)
PARAMS = pltpu.CompilerParams(vmem_limit_bytes=40 * 1024 * 1024)


def cost(microseconds):
    return pl.CostEstimate(flops=0, bytes_accessed=int(microseconds * 3e6), transcendentals=0)


def lane_of(rows):
    return lax.broadcasted_iota(jnp.int32, (rows, LANES), 1)


def take(value, index):
    return jnp.take_along_axis(value, index, axis=1, mode="promise_in_bounds")


def edge_columns(rows, turned):
    j = lane_of(rows) % GROUP
    first = j < HALO
    return jnp.where(first, LANES - HALO + j, j - HALO) if not turned else jnp.where(first, j, LANES - GROUP + j)


def split(value):
    high = value.astype(jnp.bfloat16)
    low = (value - high.astype(jnp.float32)).astype(jnp.bfloat16)
    return high, low


def exact_dot(onehot, value):
    high, low = split(value)
    both = jnp.concatenate([high, low], axis=0)
    return jnp.dot(jnp.concatenate([onehot, onehot], axis=1), both, preferred_element_type=jnp.float32)


def coupling(coef, warmth):
    flow = coef * warmth
    second = coolant_gain * coef * coef
    return jnp.concatenate([coef, flow, second, flow - second * warmth], axis=1)


def flip(z, layers, i):
    return jnp.where(z == 0, i, layers - 1 - i)


def pack_kernel(shape, u_ref, p_ref, c_ref, k_ref, f_ref, x_ref, *refs):
    own_ref, left_ref, right_ref, seg_ref = refs[3:7]
    sems = refs[-1]
    layers, rows = shape
    seg = f_ref.shape[0]
    z = lax.axis_index("gz")
    plane = layers * rows
    copies = []

    def fetch(src, dst):
        copies.append(pltpu.make_async_copy(src, dst, sems.at[len(copies)]))
        copies[-1].start()

    fetch(k_ref, own_ref.at[pl.ds(0, 2 * plane), :])
    for field, ref in enumerate((u_ref, p_ref, c_ref), 2):
        fetch(ref, own_ref.at[pl.ds(field * plane, plane), :])
    for j, ref in enumerate((x_ref, f_ref)):
        fetch(ref, own_ref.at[pl.ds(RAW * plane + j * seg, seg), :])
    for table, place in zip(refs[:3], refs[7:10]):
        fetch(table, place)
    chunk = rows // 4
    lane = lane_of(chunk)
    first = lane % GROUP < HALO
    columns = edge_columns(chunk, False), edge_columns(chunk, True)
    edges = RAW * plane + 2 * seg

    def gather(field, at, g):
        value = None
        for i in range(layers):
            start = pl.multiple_of((field * layers + flip(z, layers, i)) * rows + at, chunk)
            taken = take(own_ref[pl.ds(start, chunk), :], columns[g % 2])
            value = taken if value is None else jnp.where(lane // GROUP == (g // 2) * layers + i, taken, value)
        return value

    def place(g, part):
        return pl.ds(edges + ((g % 2) * RAW + part) * chunk, chunk)

    copies[0].wait()
    roots = pl.ds(0, 2 * plane)
    own_ref[roots, :] = jnp.sqrt(own_ref[roots, :])
    for field in range(4):
        if field >= 2:
            copies[field - 1].wait()
        for part in range(4):
            value = gather(field, part * chunk, field)
            if field >= 2:
                value = jnp.where(lane < LANES // 2, own_ref[place(field, part), :], value)
            own_ref[place(field, part), :] = value
    copies[3].wait()
    for g in range(4):
        value = gather(4, g * chunk, g)
        if g >= 2:
            value = jnp.where(lane < LANES // 2, own_ref[place(g, 4), :], value)
        own_ref[place(g, 4), :] = value
    for part in range(RAW):
        even, odd = own_ref[place(0, part), :], own_ref[place(1, part), :]
        left_ref[part * chunk : (part + 1) * chunk, :] = jnp.where(first, odd, even)
        right_ref[part * chunk : (part + 1) * chunk, :] = jnp.where(first, even, odd)
    for copy in copies[4:]:
        copy.wait()
    segments = own_ref[RAW * plane : RAW * plane + 2 * seg, :]
    seg_ref[...] = segments
    left_ref[RAW * chunk :, :] = segments
    right_ref[RAW * chunk :, :] = segments


class Strips:
    def __init__(self, refs, starts, cells_ref, start, rows, layers):
        self.refs, self.starts = refs, starts
        self.cells_ref, self.start = cells_ref, start
        self.rows, self.layers = rows, layers

    def both(self, field, start, n, x, gx, partner):
        chunk = self.rows // 4
        if field < 4:
            g, at = field, start
        else:
            g, at = start // chunk, 4 * chunk + start % chunk
        a, b = (ref[at + begin : at + begin + n, :] for ref, begin in zip(self.refs, self.starts))
        at = self.start + (g % 2) * RAW * chunk + at
        inside = self.cells_ref[at : at + n, :]
        from_left, from_right = jnp.where(x > 0, b, 0.0), jnp.where(x < gx - 1, a, 0.0)
        lane = lane_of(n)
        first = (lane % GROUP < HALO) if g % 2 == 0 else (lane % GROUP >= HALO)
        half = self.layers * GROUP
        src = lane % half
        if partner:
            src = (self.layers - 1 - src // GROUP) * GROUP + src % GROUP
        if g % 2 == 1:
            src = jnp.where(src % GROUP < HALO, src + HALO, src - HALO)
        src = src + half * (g // 2)
        return take(jnp.where(first, from_left, inside), src), take(jnp.where(first, inside, from_right), src)


def place_segments(x, gx, seg, coef_ref, warmth_ref, sources):
    for k, ref, at in sources:
        place = pl.ds(pl.multiple_of(lax.rem(x + k, gx) * seg, seg), seg)
        coef_ref[place, :] = ref[at : at + seg, :]
        warmth_ref[place, :] = ref[at + seg : at + 2 * seg, :]


def tables(z, group, layers, holder_ref, stratum_ref, transverse_ref):
    holder = holder_ref[pl.ds(group, 1), :]
    layer = stratum_ref[pl.ds(group, 1), :]
    layer = jnp.where(z == 0, layer, layers - 1 - layer)
    row = transverse_ref[pl.ds(group, 1), :]
    n = holder.shape[1]
    which = lax.broadcasted_iota(jnp.int32, (8, n), 0)
    stacked = jnp.where(which == 0, holder, jnp.where(which == 1, layer, row))
    eye = lax.broadcasted_iota(jnp.int32, (n, n), 0) == lax.broadcasted_iota(jnp.int32, (n, n), 1)
    columns = lax.dot_general(
        eye.astype(jnp.float32).astype(jnp.bfloat16),
        stacked.astype(jnp.float32).astype(jnp.bfloat16),
        (((1,), (1,)), ((), ())),
        preferred_element_type=jnp.float32,
    )
    return (holder, layer, row), columns


def as_onehot(mask):
    return jnp.where(mask, 1.0, 0.0).astype(jnp.bfloat16)


def combine(raw, added):
    s, t, u, power, storage = raw
    wall, flow, second, later = (added[:, i * LANES : (i + 1) * LANES] for i in range(4))
    return s, t, s * u, storage + wall, power + storage * u + flow, power + later, storage + second


def lengths_of(gx, chunk, seg):
    return [RAW * chunk + 2 * seg] * 2 + [2 * seg] * (gx - 3)


def edge_at(top, rows):
    return 0 if top is True else rows - HALO if top is False else pl.multiple_of(jnp.where(top, 0, rows - HALO), HALO)


def inner_at(top, rows):
    return HALO if top is True else rows - 2 * HALO if top is False else pl.multiple_of(jnp.where(top, HALO, rows - 2 * HALO), HALO)


def sides_of(gy, y):
    return [(y == 1, True)] if gy == 2 else [(True, y > 0), (False, y < gy - 1)]


def maps_kernel(gx, gy, shape, holder_ref, stratum_ref, transverse_ref, *refs):
    layers, rows = shape
    plane = layers * rows
    picks_ref, beside_ref, mine_ref = refs[6:]
    x, y, z = (lax.axis_index(a) for a in ("gx", "gy", "gz"))
    n = holder_ref.shape[1]
    for partner in range(2):
        cells_ref, rows_ref, masks_ref = refs[3 * partner : 3 * partner + 3]
        group = y * 2 + ((1 - z) if partner else z)
        (holder, layer, row), columns = tables(z, group, layers, holder_ref, stratum_ref, transverse_ref)
        cell = jnp.where(holder == x, layer * rows + row, -1)
        cells_ref[...] = as_onehot(lax.broadcasted_iota(jnp.int32, (plane, n), 0) == cell)
        rows_ref[...] = as_onehot(lax.broadcasted_iota(jnp.int32, (rows, n), 0) == row)
        holder, layer, row = (columns[:, j : j + 1].astype(jnp.int32) for j in range(3))
        lane = lane_of(n)
        first = lane % GROUP < HALO
        here = lane // GROUP == layer + partner * layers
        for side, begin in enumerate((x - 1, x)):
            mine = jnp.logical_and(here, holder == jnp.where(first, begin, begin + 1))
            masks_ref[side * n : (side + 1) * n, :] = jnp.where(mine, 1.0, 0.0)
        if partner:
            continue
        mine = holder == x
        mine_ref[...] = jnp.where(jnp.logical_and(mine, lane >= 0), 1.0, 0.0)
        spoilt = None
        for side, (above, live) in enumerate(sides_of(gy, y)):
            start = edge_at(above, rows)
            part = jnp.logical_and(row // HALO == start // HALO, live)
            spoilt = part if spoilt is None else jnp.logical_or(spoilt, part)
            cell = jnp.where(jnp.logical_and(mine, part), layer * HALO + row - start, -1)
            beside_ref[side * n : (side + 1) * n, :] = as_onehot(lane == cell)
        cell = jnp.where(jnp.logical_and(mine, jnp.logical_not(spoilt)), layer * rows + row, -1)
        picks_ref[...] = as_onehot(lax.broadcasted_iota(jnp.int32, (n, plane), 1) == cell)


def join_kernel(mine_ref, *refs):
    out_ref, at = refs[-1], 0
    for ref in refs[:-1]:
        n = ref.shape[0]
        out_ref[at : at + n, :] = ref[...]
        at += n


def partner_rows(layers):
    whole, at = [], 1
    for i in range(layers - 1, -1, -1):
        whole.append((i, HALO - layers + i, at))
        at += HALO - layers + i
    stride = -(-at // 8) * 8
    later, at = [], 0
    for f in range(2):
        for i in range(layers - 1, -1, -1):
            if ITERS - 1 - layers + i > 0:
                later.append((f, i, ITERS - 1 - layers + i, at))
                at += ITERS - 1 - layers + i
    return whole, stride, later, -(-at // 8) * 8


def fill_kernel(partner, gx, gy, shape, seg, *refs):
    layers, rows = shape
    cells_ref, where_ref, rows_ref, masks_ref = refs[:4]
    plane, chunk = layers * rows, rows // 4
    lengths = lengths_of(gx, chunk, seg)
    if partner:
        sources = [(refs[4], sum(lengths[:k])) for k in range(gx - 1)]
        refs = refs[5:]
    else:
        sources = [(ref, 0) for ref in refs[4 : 4 + gx - 1]]
        refs = refs[4 + gx - 1 :]
    sides = 1 if gy == 2 else 2
    out_ref = refs[0]
    if partner:
        coef_ref, warmth_ref = refs[1:3]
    else:
        strip_refs, partner_refs, segments_ref = refs[1 : 1 + sides], refs[1 + sides : 1 + 2 * sides], refs[1 + 2 * sides]
        n = segments_ref.shape[0] // 2
        coef_ref, warmth_ref = segments_ref.at[pl.ds(0, n), :], segments_ref.at[pl.ds(n, n), :]
    x, y, z = (lax.axis_index(a) for a in ("gx", "gy", "gz"))
    base = layers if partner else 0
    distances = [1, gx - 1] + list(range(2, gx - 1))
    held = [(k, ref, at + (RAW * chunk if j < 2 else 0)) for j, (k, (ref, at)) in enumerate(zip(distances, sources))]
    place_segments(x, gx, seg, coef_ref, warmth_ref, [(0, cells_ref, RAW * plane)] + held)
    coef, warmth = coef_ref[...], warmth_ref[...]
    n = coef.shape[0]
    added = exact_dot(where_ref[...], coupling(coef, warmth))
    near = edge_columns(n, False)
    beside = []
    for side in range(2):
        masked = take(coef, near) * masks_ref[side * n : (side + 1) * n, :]
        beside.append(exact_dot(rows_ref[...], coupling(masked, take(warmth, near))))
    planes = layers + 2
    for i in range(layers):
        src = flip(z, layers, i)
        raw = [cells_ref[pl.ds(pl.multiple_of((f * layers + src) * rows, rows), rows), :] for f in range(RAW)]
        for f, value in enumerate(combine(raw, added[i * rows : (i + 1) * rows])):
            out_ref[f * planes + i] = value
    strips = Strips(
        [ref for ref, _ in sources[:2]], [at for _, at in sources[:2]], cells_ref, RAW * plane + 2 * seg, rows, layers
    )
    half = lane_of(chunk) // (LANES // 2) == (1 if partner else 0)
    for part in range(4):
        here = slice(part * chunk, (part + 1) * chunk)
        raw = [strips.both(f, part * chunk, chunk, x, gx, partner) for f in range(RAW)]
        for side in range(2):
            cells = [jnp.where(half, value[side], 0.0) for value in raw]
            for f, value in enumerate(combine(cells, beside[side][here])):
                out_ref[f * planes + layers + side, here, :] = value
    if partner:
        return
    low = lane_of(HALO) < LANES // 2
    upper = lax.broadcasted_iota(jnp.int32, (HALO, LANES), 0) < HALO // 2
    first = lane_of(HALO) % GROUP < HALO
    sent = FIELDS - 1
    for strip_ref, partner_ref, (top, _) in zip(strip_refs, partner_refs, sides_of(gy, y)):
        edge = pl.ds(edge_at(top, rows), HALO)

        def shrink(values):
            *whole, e, g = values
            e = jnp.where(top, e, pltpu.roll(e, HALO // 2, 0))
            g = jnp.where(top, pltpu.roll(g, HALO // 2, 0), g)
            return whole + [jnp.where(upper, e, g)]

        def give(ref, at, values):
            for f, value in enumerate(values):
                ref[at + f * HALO : at + (f + 1) * HALO, :] = value

        for i in range(layers):
            give(strip_ref, i * sent * HALO, shrink([out_ref[f * planes + i, edge, :] for f in range(FIELDS)]))
        outer = []
        for f in range(FIELDS):
            left, right = (out_ref[f * planes + layers + side, edge, :] for side in range(2))
            outer.append(jnp.where(first, left, right))
        outer = shrink(outer)
        values = [jnp.where(low, outer[j], pltpu.roll(outer[j + 1], LANES // 2, 1)) for j in range(0, sent, 2)]
        give(strip_ref, layers * sent * HALO, values)
        whole, stride, later, shared = partner_rows(layers)
        pieces = [(f, i, m, f * stride + at) for f in range(sent - 1) for i, m, at in whole]
        pieces += [(sent - 1 + f, i, m, (sent - 1) * stride + at) for f, i, m, at in later]
        for f, i, m, at in pieces:
            start = edge_at(top, rows) + jnp.where(top, 0, HALO - m)
            partner_ref[at : at + m, :] = out_ref[f * planes + i, pl.ds(start, m), :]
        give(partner_ref, (sent - 1) * stride + shared, values)


def planes_of(count, total):
    return list(range(count)) + [total - 2, total - 1]


def lateral(buf, at, n, which):
    sums = []
    for i in which:
        centre = buf[i, pl.ds(at, n), :]
        beside = pltpu.roll(centre, 1, 1) + pltpu.roll(centre, LANES - 1, 1)
        sums.append(beside + (buf[i, pl.ds(at - 1, n), :] + buf[i, pl.ds(at + 1, n), :]))
    return sums


def vertical(planes, edges, count):
    sums = []
    for i in range(count):
        near = [planes[j] for j in (i - 1, i + 1) if 0 <= j < len(planes)]
        sums.append(functools.reduce(jnp.add, near))
    for edge in edges:
        lane = lane_of(edge.shape[0])
        up = jnp.where(lane >= GROUP, pltpu.roll(edge, GROUP, 1), 0.0)
        down = jnp.where(lane < LANES - GROUP, pltpu.roll(edge, LANES - GROUP, 1), 0.0)
        sums.append(up + down)
    return sums


def coefficients(s_ref, at, n, raw, dests, to, outside):
    a_ref, q_ref, r_ref, e_ref, g_ref, root_ref = dests
    total = s_ref.shape[0]
    sums = lateral(s_ref, at, n, range(total))
    t = [raw(1, i) for i in range(total)]
    above = vertical(t[:-2], t[-2:], total - 2)
    here = pl.ds(to, n)
    for i in range(total):
        s = s_ref[i, pl.ds(at, n), :]
        diag = raw(3, i) + s * sums[i] + t[i] * above[i]
        if outside or i >= total - 2:
            inverse = 1.0 / jnp.where(diag > 0.0, diag, 1.0)
            root = jnp.where(s > 0.0, 1.0 / jnp.where(s > 0.0, s, 1.0), 0.0)
        else:
            inverse, root = 1.0 / diag, 1.0 / s
        if i < root_ref.shape[0]:
            root_ref[i, here, :] = root
        scaled = s * inverse
        a_ref[i, here, :] = s * scaled
        r_ref[i, here, :] = raw(4, i) * scaled
        e_ref[i, here, :] = raw(5, i) * scaled
        g_ref[i, here, :] = raw(6, i) * inverse
        q_ref[i, here, :] = t[i] * root


def shifted_sums(distance):
    to = lax.broadcasted_iota(jnp.int32, (2 * LANES, LANES), 1)
    of = lax.broadcasted_iota(jnp.int32, (2 * LANES, LANES), 0) % LANES
    return as_onehot(jnp.abs(of - to) == distance)


def sweep_edges(src_ref, dst_ref, at, n, coefs, base, matrices):
    a_ref, q_ref, r_ref = coefs[:3]
    total = src_ref.shape[0]
    here, there = pl.ds(base, n), pl.ds(at, n)

    def product(value, matrix):
        return jnp.dot(jnp.concatenate(split(value), axis=1), matrix, preferred_element_type=jnp.float32)

    for i in (total - 2, total - 1):
        centre = src_ref[i, there, :]
        beside = product(centre, matrices[0])
        above = product(q_ref[i, here, :] * centre, matrices[1])
        beside = beside + (src_ref[i, pl.ds(at - 1, n), :] + src_ref[i, pl.ds(at + 1, n), :])
        dst_ref[i, there, :] = r_ref[i, here, :] + a_ref[i, here, :] * (beside + q_ref[i, here, :] * above)


def sweep(src_ref, dst_ref, at, n, count, coefs, base, edges=True):
    a_ref, q_ref, r_ref = coefs[:3]
    total = src_ref.shape[0]
    here, there = pl.ds(base, n), pl.ds(at, n)
    which = planes_of(count, total) if edges else list(range(count))
    sums = lateral(src_ref, at, n, which)
    scaled = [q_ref[i, here, :] * src_ref[i, there, :] for i in range(min(count + 1, total - 2))]
    outer = [q_ref[i, here, :] * src_ref[i, there, :] for i in which[count:]]
    above = vertical(scaled, outer, count)
    for j, i in enumerate(which):
        dst_ref[i, there, :] = r_ref[i, here, :] + a_ref[i, here, :] * (sums[j] + q_ref[i, here, :] * above[j])


def next_rhs(coefs, v_ref, at, n, base):
    r_ref, e_ref, g_ref = coefs[2:5]
    here = pl.ds(base, n)
    for i in range(v_ref.shape[0]):
        r_ref[i, here, :] = e_ref[i, here, :] + g_ref[i, here, :] * v_ref[i, pl.ds(at, n), :]


def meet(v_ref, at, n, count, back):
    total = v_ref.shape[0]
    here = pl.ds(at, n)
    lane = lane_of(n)
    j, group = lane % GROUP, lane // GROUP
    outer = jnp.logical_or(lane < ITERS, lane >= LANES - ITERS)
    left, right = v_ref[total - 2, here, :], v_ref[total - 1, here, :]
    middle = jnp.where(j < HALO, right, left)
    for i in range(count):
        value = v_ref[i, here, :]
        if back:
            moved = pltpu.roll(value, (i * GROUP + HALO) % LANES, 1)
            left = jnp.where(jnp.logical_and(group == i, j >= GROUP - ITERS), moved, left)
            right = jnp.where(jnp.logical_and(group == i, j < ITERS), moved, right)
        v_ref[i, here, :] = jnp.where(outer, pltpu.roll(middle, LANES - (i * GROUP + HALO), 1), value)
    if back:
        v_ref[total - 2, here, :] = left
        v_ref[total - 1, here, :] = right


def needed(layers, n):
    return min(2 * layers, layers + STEPS * ITERS - 1 - n)


def two_steps(layers, sweep_all, between, after):
    for step in range(STEPS):
        whole = [n for n in range(step * ITERS, (step + 1) * ITERS) if needed(layers, n) == 2 * layers]
        pairs = len(whole) // 2

        def pair(k, carry):
            n = step * ITERS + 2 * k
            sweep_all(n, 0, 2 * layers)
            sweep_all(n + 1, 1, 2 * layers)
            return carry

        if pairs:
            lax.fori_loop(0, pairs, pair, 0)
        for n in range(step * ITERS + 2 * pairs, (step + 1) * ITERS):
            sweep_all(n, n % 2, needed(layers, n))
        after(step)
        if step < STEPS - 1:
            between()


PAD = 8


def tile_kernel(gx, gy, shape, *refs):
    layers, rows = shape
    own_ref, partner_ref, picks_ref, out_ref, below_ref, level_ref = refs[:6]
    s_ref, va_ref, vb_ref = refs[6:9]
    coefs = refs[9:]
    x, y, z = (lax.axis_index(a) for a in ("gx", "gy", "gz"))
    total = 2 * layers + 2
    zeros = jnp.zeros((PAD, LANES), jnp.float32)
    for ref in (s_ref, va_ref, vb_ref):
        for i in range(total):
            ref[i, 0:PAD, :] = zeros
            ref[i, PAD + rows : PAD + rows + PAD, :] = zeros

    def field(f, i, here):
        j = f * (layers + 2)
        if i >= 2 * layers:
            j = j + i - layers
            return own_ref[j, here, :] + partner_ref[j, here, :]
        return own_ref[j + i, here, :] if i < layers else partner_ref[j + i - layers, here, :]

    for i in range(total):
        s_ref[i, PAD : PAD + rows, :] = field(0, i, slice(None))
        va_ref[i, PAD : PAD + rows, :] = field(2, i, slice(None))
    n = 8
    for at in range(0, rows, n):
        coefficients(s_ref, PAD + at, n, lambda f, i: field(f, i, slice(at, at + n)), coefs, at, False)

    bufs = (va_ref, vb_ref)
    sides = sides_of(gy, y)
    matrices = shifted_sums(1), shifted_sums(GROUP)

    def sweep_all(number, which, count):
        src_ref, dst_ref = bufs[which], bufs[1 - which]
        for side, (above, _) in enumerate(sides):
            inner = pl.ds(PAD + inner_at(above, rows), HALO)
            for i in range(total):
                level_ref[(side * STEPS * ITERS + number) * total + i] = src_ref[i, inner, :]
        sweep_edges(src_ref, dst_ref, PAD, rows, coefs, 0, matrices)
        for at in range(0, rows, n):
            sweep(src_ref, dst_ref, PAD + at, n, count, coefs, at, edges=False)

    def after(step):
        last = step == STEPS - 1
        for at in range(0, rows, n):
            meet(va_ref, PAD + at, n, layers if last else 2 * layers, not last)
        heat = []
        for i in range(layers):
            here = pl.ds(PAD, rows)
            heat.append(va_ref[i, here, :] * coefs[5][i])
            if step == STEPS - 1:
                out_ref[flip(z, layers, i)] = heat[-1]
        below_ref[step] = exact_dot(picks_ref[...], jnp.concatenate(heat, axis=0))

    def between():
        for at in range(0, rows, n):
            next_rhs(coefs, va_ref, PAD + at, n, at)

    two_steps(layers, sweep_all, between, after)


def edge_kernel(gx, gy, shape, seg, *refs):
    layers, rows = shape
    own_ref, partner_ref, picks_ref, mine_ref, segments_ref, below_ref, level_ref = refs[:7]
    sides_n = 1 if gy == 2 else 2
    along, across = refs[7 : 7 + sides_n], refs[7 + sides_n : 7 + 2 * sides_n]
    refs = refs[7 + 2 * sides_n :]
    heat_ref, returns = refs[0], refs[1 : 1 + gx]
    ret_ref, s_ref, va_ref, vb_ref = refs[1 + gx : 5 + gx]
    coefs = refs[5 + gx :]
    x, y, z = (lax.axis_index(a) for a in ("gx", "gy", "gz"))
    total = 2 * layers + 2
    count = mine_ref.shape[0]
    below = [below_ref[step] for step in range(STEPS)]
    lane = lane_of(HALO)
    low, first = lane < LANES // 2, lane % GROUP < HALO
    columns = edge_columns(HALO, False)
    bufs = (va_ref, vb_ref)

    def tile(j):
        return pl.ds(j if isinstance(j, int) else pl.multiple_of(j, HALO), HALO)

    for side, (above, live) in enumerate(sides_of(gy, y)):
        def place(when_top, otherwise):
            if above is True or above is False:
                return when_top * HALO if above else otherwise * HALO
            return jnp.where(above, when_top * HALO, otherwise * HALO)

        outer, strip, edge, inner = place(0, 3), place(1, 2), place(2, 1), place(3, 0)
        edge_rows = tile(edge_at(above, rows))
        inner_rows = tile(inner_at(above, rows))

        def field(f, i, here):
            j = f * (layers + 2)
            if i >= 2 * layers:
                j = j + i - layers
                return own_ref[j, here, :] + partner_ref[j, here, :]
            return own_ref[j + i, here, :] if i < layers else partner_ref[j + i - layers, here, :]

        t_ref, d_ref, q_ref, e_ref, g_ref = coefs[1], coefs[0], coefs[2], coefs[3], coefs[4]
        keep = {0: s_ref, 1: t_ref, 2: va_ref, 3: d_ref, 4: q_ref, 5: e_ref, 6: g_ref}
        zeros = jnp.zeros((HALO, LANES), jnp.float32)
        src = lane % (LANES // 2)
        turned = (layers - 1 - src // GROUP) * GROUP + src % GROUP
        half_tile = lax.broadcasted_iota(jnp.int32, (HALO, LANES), 0) < HALO // 2

        def unpack(value, f):
            if f < FIELDS - 2:
                return value
            turned_value = pltpu.roll(value, HALO // 2, 0)
            if f == FIELDS - 2:
                at_top, at_bottom = jnp.where(half_tile, 0.0, turned_value), jnp.where(half_tile, value, 0.0)
            else:
                at_top, at_bottom = jnp.where(half_tile, 0.0, value), jnp.where(half_tile, turned_value, 0.0)
            return jnp.where(above, at_top, at_bottom)

        whole, stride, later, shared = partner_rows(layers)
        sublane = lax.broadcasted_iota(jnp.int32, (HALO, LANES), 0)

        def nearest(ref, m, at):
            at_top = jnp.where(sublane >= HALO - m, ref[at - HALO + m : at + m, :], 0.0)
            return jnp.where(above, at_top, jnp.where(sublane < m, ref[at : at + HALO, :], 0.0))

        for f in range(FIELDS):
            g = min(f, FIELDS - 2)
            if f < FIELDS - 2:
                rows_of = {i: (m, f * stride + at) for i, m, at in whole}
            else:
                rows_of = {i: (m, (FIELDS - 2) * stride + at) for which, i, m, at in later if which == f - FIELDS + 2}
            values, inside = [], zeros
            for i in range(2 * layers):
                if i < layers:
                    at = (i * (FIELDS - 1) + g) * HALO
                    value = unpack(along[side][at : at + HALO, :], f)
                else:
                    j = 2 * layers - 1 - i
                    value = nearest(across[side], *rows_of[j]) if j in rows_of else zeros
                values.append(value)
                inside = jnp.where(lane // GROUP == i, take(value, columns), inside)
            half = (LANES // 2) * (g % 2)
            at = (layers * (FIELDS - 1) + g // 2) * HALO
            a = take(along[side][at : at + HALO, :], src + half)
            at = (FIELDS - 2) * stride + shared + (g // 2) * HALO
            b = take(across[side][at : at + HALO, :], turned + half)
            outside = unpack(jnp.where(low, a, b), f)
            values += [jnp.where(first, outside, inside), jnp.where(first, inside, outside)]
            for i, value in enumerate(values):
                ref, shift = keep[f], 0 if f in (0, 2) else HALO
                ref[i, tile(strip - shift), :] = value
                ref[i, tile(edge - shift), :] = field(f, i, edge_rows)
        for i in range(total):
            s_ref[i, tile(outer), :] = zeros
            va_ref[i, tile(outer), :] = zeros
            vb_ref[i, tile(outer), :] = zeros
            s_ref[i, tile(inner), :] = field(0, i, inner_rows)
        n = 2 * HALO
        held = [[keep[f][i, pl.ds(0, n), :] for i in range(total)] if f in (1, 3, 4, 5, 6) else None for f in range(FIELDS)]
        coefficients(s_ref, HALO, n, lambda f, i: held[f][i], coefs, 0, True)

        def sweep_all(number, which, needed_layers):
            src_ref, dst_ref = bufs[which], bufs[1 - which]
            for i in range(total):
                src_ref[i, tile(inner), :] = level_ref[(side * STEPS * ITERS + number) * total + i]
            sweep(src_ref, dst_ref, HALO, n, needed_layers, coefs, 0)

        picks = picks_ref[side * count : (side + 1) * count, :]

        def after(step):
            last = step == STEPS - 1
            meet(va_ref, HALO, n, layers if last else 2 * layers, not last)
            heat = []
            for i in range(layers):
                heat.append(va_ref[i, tile(edge), :] * coefs[5][i, tile(edge - HALO), :])
                if step == STEPS - 1:
                    heat_ref[side * layers + flip(z, layers, i)] = heat[-1]
            heat.append(jnp.zeros((LANES - layers * HALO, LANES), jnp.float32))
            below[step] = below[step] + exact_dot(picks, jnp.concatenate(heat, axis=0))

        two_steps(layers, sweep_all, lambda: next_rhs(coefs, va_ref, HALO, n, 0), after)

    coef, warmth = segments_ref[:count, :], segments_ref[count:, :]
    for step in range(STEPS):
        warmth = warmth + coolant_gain * coef * (below[step] - warmth)
    ret_ref[...] = jnp.where(mine_ref[...] > 0.0, warmth, 0.0)
    for k, ref in enumerate(returns):
        ref[...] = ret_ref[pl.ds(pl.multiple_of(lax.rem(x + k, gx) * seg, seg), seg), :]


def merge_kernel(gy, whole_ref, heat_ref, out_ref):
    layers, rows, _ = whole_ref.shape
    out_ref[...] = whole_ref[...]
    for side, (above, live) in enumerate(sides_of(gy, lax.axis_index("gy"))):
        def put(side=side, above=above):
            out_ref[:, pl.ds(edge_at(above, rows), HALO), :] = heat_ref[side * layers : (side + 1) * layers]

        if live is True:
            put()
        else:
            pl.when(live)(put)


def local(gx, gy, gz, u, power, storage, conductance, warmth, coef, holder, stratum, transverse):
    layers, rows, columns = u.shape
    seg = warmth.shape[1]
    segments = stratum.shape[1]
    if gz != 2 or gx < 3 or columns != LANES or 2 * layers * GROUP != LANES or rows % 32:
        raise ValueError("unsupported shape")
    holder = holder[:, :, 0]
    shape = (layers, rows)
    f32 = jnp.float32
    chunk = rows // 4
    wide = RAW * chunk + 2 * seg

    def struct(*dims):
        return jax.ShapeDtypeStruct(dims, f32)

    def vmem(*dims):
        return pltpu.VMEM(dims, f32)

    indices = (holder, stratum, transverse)
    flat = [a.reshape(-1, LANES) for a in (u, power, storage, conductance, warmth, coef)]
    own, to_left, to_right, only, *indices = pl.pallas_call(
        functools.partial(pack_kernel, shape),
        out_shape=(
            struct(RAW * layers * rows + 2 * seg + 2 * RAW * chunk, LANES),
            struct(wide, LANES),
            struct(wide, LANES),
            struct(2 * seg, LANES),
            *(jax.ShapeDtypeStruct(a.shape, a.dtype) for a in indices),
        ),
        in_specs=[pl.BlockSpec(memory_space=pltpu.HBM)] * 9,
        out_specs=(VMEM,) * 7,
        scratch_shapes=[pltpu.SemaphoreType.DMA((9,))],
        compiler_params=PARAMS,
        name="pack",
    )(*(pltpu.with_memory_space_constraint(a, pltpu.HBM) for a in (*flat, *indices)))

    swap = [(0, 1), (1, 0)]
    partner = lax.ppermute(own, "gz", swap)
    def from_distance(value, k):
        return lax.ppermute(value, "gx", [(i, (i - k) % gx) for i in range(gx)])

    received = [from_distance(to_left, 1), from_distance(to_right, gx - 1)]
    received += [from_distance(only, k) for k in range(2, gx - 1)]

    sides = 1 if gy == 2 else 2
    fields = struct(FIELDS * (layers + 2), rows, LANES)
    strip_rows = (FIELDS - 1) * layers * HALO + (FIELDS - 1) // 2 * HALO
    _, stride, _, shared = partner_rows(layers)
    partner_strip = (FIELDS - 2) * stride + shared + (FIELDS - 1) // 2 * HALO
    sides = 1 if gy == 2 else 2
    bf16 = jnp.bfloat16
    one_group = (
        jax.ShapeDtypeStruct((layers * rows, segments), bf16),
        jax.ShapeDtypeStruct((rows, segments), bf16),
        struct(2 * segments, LANES),
    )
    maps = pl.pallas_call(
        functools.partial(maps_kernel, gx, gy, shape),
        out_shape=one_group
        + one_group
        + (
            jax.ShapeDtypeStruct((segments, layers * rows), bf16),
            jax.ShapeDtypeStruct((sides * segments, LANES), bf16),
            struct(segments, LANES),
        ),
        in_specs=[VMEM] * 3,
        out_specs=(VMEM,) * 9,
        compiler_params=PARAMS,
        cost_estimate=cost(1),
        name="maps",
    )(*indices)
    own_maps, partner_maps, (picks, picks_beside, mine) = maps[:3], maps[3:6], maps[6:]
    joined = pl.pallas_call(
        join_kernel,
        out_shape=struct(sum(a.shape[0] for a in received), LANES),
        in_specs=[pl.BlockSpec(memory_space=pl.ANY)] + [VMEM] * (gx - 1),
        out_specs=VMEM,
        compiler_params=PARAMS,
        name="join",
    )(mine, *received)
    late = lax.ppermute(joined, "gz", swap)
    filled = pl.pallas_call(
        functools.partial(fill_kernel, False, gx, gy, shape, seg),
        out_shape=(fields,) + (struct(strip_rows, LANES),) * sides
        + (struct(partner_strip, LANES),) * sides
        + (struct(2 * segments, LANES),),
        in_specs=[VMEM] * (4 + gx - 1),
        out_specs=(VMEM,) * (2 + 2 * sides),
        compiler_params=PARAMS,
        cost_estimate=cost(1.5),
        name="fill_own",
    )(own, *own_maps, *received)
    own_fields, held = filled[0], filled[-1]
    strips, partner_strips = filled[1 : 1 + sides], filled[1 + sides : 1 + 2 * sides]
    if gy == 2:
        routes = [(0, swap)]
    else:
        up = [(i, i + 1) for i in range(gy - 1)]
        routes = [(1, up), (0, [(j, i) for i, j in up])]
    along = [lax.ppermute(strips[side], "gy", pairs) for side, pairs in routes]
    across = []
    for side, pairs in routes:
        both = [(2 * i + z, 2 * j + 1 - z) for i, j in pairs for z in range(2)]
        across.append(lax.ppermute(partner_strips[side], ("gy", "gz"), both))

    partner_fields = pl.pallas_call(
        functools.partial(fill_kernel, True, gx, gy, shape, seg),
        out_shape=fields,
        in_specs=[VMEM] * 5,
        out_specs=VMEM,
        scratch_shapes=[vmem(segments, LANES)] * 2,
        compiler_params=PARAMS,
        cost_estimate=cost(1.5),
        name="fill_partner",
    )(partner, *partner_maps, late)

    total = 2 * layers + 2
    padded = vmem(total, rows + 2 * PAD, LANES)
    inside, below, levels = pl.pallas_call(
        functools.partial(tile_kernel, gx, gy, shape),
        out_shape=(
            struct(layers, rows, LANES),
            struct(STEPS, segments, LANES),
            struct(sides * STEPS * ITERS * total, HALO, LANES),
        ),
        in_specs=[VMEM] * 3,
        out_specs=(VMEM,) * 3,
        scratch_shapes=[padded] * 3 + [vmem(total, rows, LANES)] * 5 + [vmem(layers, rows, LANES)],
        compiler_params=PARAMS,
        cost_estimate=cost(7),
        name="tile_sweeps",
    )(own_fields, partner_fields, picks)

    results = pl.pallas_call(
        functools.partial(edge_kernel, gx, gy, shape, seg),
        out_shape=(struct(sides * layers, HALO, LANES),) + (struct(seg, LANES),) * gx,
        in_specs=[VMEM] * (7 + 2 * sides),
        out_specs=(VMEM,) * (1 + gx),
        scratch_shapes=[vmem(segments, LANES)]
        + [vmem(total, 4 * HALO, LANES)] * 3
        + [vmem(total, 2 * HALO, LANES)] * 5
        + [vmem(layers, 2 * HALO, LANES)],
        compiler_params=PARAMS,
        cost_estimate=cost(1.5),
        name="edge_sweeps",
    )(own_fields, partner_fields, picks_beside, mine, held, below, levels, *along, *across)
    heat, coolant = results[0], results[1]
    returned = [lax.ppermute(results[1 + k], "gx", [(i, (i + k) % gx) for i in range(gx)]) for k in range(1, gx)]
    temperature = pl.pallas_call(
        functools.partial(merge_kernel, gy),
        out_shape=struct(layers, rows, LANES),
        in_specs=[VMEM] * 2,
        out_specs=VMEM,
        compiler_params=PARAMS,
        cost_estimate=cost(1),
        name="merge",
    )(inside, heat)
    for value in returned:
        coolant = coolant + value
    return temperature, coolant[None]


def solution(mesh):
    gx, gy, gz = (mesh.shape[a] for a in ("gx", "gy", "gz"))
    cells = P(("stack", "gz"), "gy", "gx")
    segments = P(("stack", "gy", "gz"), "gx", None)
    return jax.shard_map(
        functools.partial(local, gx, gy, gz),
        mesh=mesh,
        in_specs=(cells, cells, cells, P(None, ("stack", "gz"), "gy", "gx"), segments, segments, P(), P(), P()),
        out_specs=(cells, segments),
        check_vma=False,
    )
```

```python
import functools

import jax
import jax.numpy as jnp
from jax import lax
from jax.experimental import pallas as pl
from jax.experimental.pallas import tpu as pltpu
from jax.sharding import PartitionSpec as P

STEPS = 2
ITERS = 4
HALO = STEPS * ITERS
GROUP = 2 * HALO
LANES = 128
RAW = 5
FIELDS = 7
coolant_gain = 0.5

VMEM = pl.BlockSpec(memory_space=pltpu.VMEM)
PARAMS = pltpu.CompilerParams(vmem_limit_bytes=40 * 1024 * 1024)


def cost(microseconds):
    return pl.CostEstimate(flops=0, bytes_accessed=int(microseconds * 3e6), transcendentals=0)


def lane_of(rows):
    return lax.broadcasted_iota(jnp.int32, (rows, LANES), 1)


def take(value, index):
    return jnp.take_along_axis(value, index, axis=1, mode="promise_in_bounds")


def edge_columns(rows, turned):
    j = lane_of(rows) % GROUP
    first = j < HALO
    return jnp.where(first, LANES - HALO + j, j - HALO) if not turned else jnp.where(first, j, LANES - GROUP + j)


def split(value):
    high = value.astype(jnp.bfloat16)
    low = (value - high.astype(jnp.float32)).astype(jnp.bfloat16)
    return high, low


def exact_dot(onehot, value):
    high, low = split(value)
    both = jnp.concatenate([high, low], axis=0)
    return jnp.dot(jnp.concatenate([onehot, onehot], axis=1), both, preferred_element_type=jnp.float32)


def coupling(coef, warmth):
    flow = coef * warmth
    second = coolant_gain * coef * coef
    return jnp.concatenate([coef, flow, second, flow - second * warmth], axis=1)


def flip(z, layers, i):
    return jnp.where(z == 0, i, layers - 1 - i)


def pack_kernel(shape, u_ref, p_ref, c_ref, k_ref, f_ref, x_ref, *refs):
    own_ref, left_ref, right_ref, seg_ref = refs[3:7]
    sems = refs[-1]
    layers, rows = shape
    seg = f_ref.shape[0]
    z = lax.axis_index("gz")
    plane = layers * rows
    copies = []

    def fetch(src, dst):
        copies.append(pltpu.make_async_copy(src, dst, sems.at[len(copies)]))
        copies[-1].start()

    fetch(k_ref, own_ref.at[pl.ds(0, 2 * plane), :])
    for field, ref in enumerate((u_ref, p_ref, c_ref), 2):
        fetch(ref, own_ref.at[pl.ds(field * plane, plane), :])
    for j, ref in enumerate((x_ref, f_ref)):
        fetch(ref, own_ref.at[pl.ds(RAW * plane + j * seg, seg), :])
    for table, place in zip(refs[:3], refs[7:10]):
        fetch(table, place)
    chunk = rows // 4
    lane = lane_of(chunk)
    first = lane % GROUP < HALO
    columns = edge_columns(chunk, False), edge_columns(chunk, True)
    edges = RAW * plane + 2 * seg

    def gather(field, at, g):
        value = None
        for i in range(layers):
            start = pl.multiple_of((field * layers + flip(z, layers, i)) * rows + at, chunk)
            taken = take(own_ref[pl.ds(start, chunk), :], columns[g % 2])
            value = taken if value is None else jnp.where(lane // GROUP == (g // 2) * layers + i, taken, value)
        return value

    def place(g, part):
        return pl.ds(edges + ((g % 2) * RAW + part) * chunk, chunk)

    copies[0].wait()
    roots = pl.ds(0, 2 * plane)
    own_ref[roots, :] = jnp.sqrt(own_ref[roots, :])
    for field in range(4):
        if field >= 2:
            copies[field - 1].wait()
        for part in range(4):
            value = gather(field, part * chunk, field)
            if field >= 2:
                value = jnp.where(lane < LANES // 2, own_ref[place(field, part), :], value)
            own_ref[place(field, part), :] = value
    copies[3].wait()
    for g in range(4):
        value = gather(4, g * chunk, g)
        if g >= 2:
            value = jnp.where(lane < LANES // 2, own_ref[place(g, 4), :], value)
        own_ref[place(g, 4), :] = value
    for part in range(RAW):
        even, odd = own_ref[place(0, part), :], own_ref[place(1, part), :]
        left_ref[part * chunk : (part + 1) * chunk, :] = jnp.where(first, odd, even)
        right_ref[part * chunk : (part + 1) * chunk, :] = jnp.where(first, even, odd)
    for copy in copies[4:]:
        copy.wait()
    segments = own_ref[RAW * plane : RAW * plane + 2 * seg, :]
    seg_ref[...] = segments
    left_ref[RAW * chunk :, :] = segments
    right_ref[RAW * chunk :, :] = segments


class Strips:
    def __init__(self, refs, starts, cells_ref, start, rows, layers):
        self.refs, self.starts = refs, starts
        self.cells_ref, self.start = cells_ref, start
        self.rows, self.layers = rows, layers

    def both(self, field, start, n, x, gx, partner):
        chunk = self.rows // 4
        if field < 4:
            g, at = field, start
        else:
            g, at = start // chunk, 4 * chunk + start % chunk
        a, b = (ref[at + begin : at + begin + n, :] for ref, begin in zip(self.refs, self.starts))
        at = self.start + (g % 2) * RAW * chunk + at
        inside = self.cells_ref[at : at + n, :]
        from_left, from_right = jnp.where(x > 0, b, 0.0), jnp.where(x < gx - 1, a, 0.0)
        lane = lane_of(n)
        first = (lane % GROUP < HALO) if g % 2 == 0 else (lane % GROUP >= HALO)
        half = self.layers * GROUP
        src = lane % half
        if partner:
            src = (self.layers - 1 - src // GROUP) * GROUP + src % GROUP
        if g % 2 == 1:
            src = jnp.where(src % GROUP < HALO, src + HALO, src - HALO)
        src = src + half * (g // 2)
        return take(jnp.where(first, from_left, inside), src), take(jnp.where(first, inside, from_right), src)


def place_segments(x, gx, seg, coef_ref, warmth_ref, sources):
    for k, ref, at in sources:
        place = pl.ds(pl.multiple_of(lax.rem(x + k, gx) * seg, seg), seg)
        coef_ref[place, :] = ref[at : at + seg, :]
        warmth_ref[place, :] = ref[at + seg : at + 2 * seg, :]


def tables(z, group, layers, holder_ref, stratum_ref, transverse_ref):
    holder = holder_ref[pl.ds(group, 1), :]
    layer = stratum_ref[pl.ds(group, 1), :]
    layer = jnp.where(z == 0, layer, layers - 1 - layer)
    row = transverse_ref[pl.ds(group, 1), :]
    n = holder.shape[1]
    which = lax.broadcasted_iota(jnp.int32, (8, n), 0)
    stacked = jnp.where(which == 0, holder, jnp.where(which == 1, layer, row))
    eye = lax.broadcasted_iota(jnp.int32, (n, n), 0) == lax.broadcasted_iota(jnp.int32, (n, n), 1)
    columns = lax.dot_general(
        eye.astype(jnp.float32).astype(jnp.bfloat16),
        stacked.astype(jnp.float32).astype(jnp.bfloat16),
        (((1,), (1,)), ((), ())),
        preferred_element_type=jnp.float32,
    )
    return (holder, layer, row), columns


def as_onehot(mask):
    return jnp.where(mask, 1.0, 0.0).astype(jnp.bfloat16)


def combine(raw, added):
    s, t, u, power, storage = raw
    wall, flow, second, later = (added[:, i * LANES : (i + 1) * LANES] for i in range(4))
    return s, t, s * u, storage + wall, power + storage * u + flow, power + later, storage + second


def lengths_of(gx, chunk, seg):
    return [RAW * chunk + 2 * seg] * 2 + [2 * seg] * (gx - 3)


def return_rounds(gx):
    if gx == 4:
        return [
            [(0, 1), (1, 3), (3, 0)],
            [(1, 2), (2, 0), (3, 1)],
            [(0, 2), (1, 0), (2, 3)],
            [(2, 1), (3, 2), (0, 3)],
        ]
    return [[(i, (i + k) % gx) for i in range(gx)] for k in range(1, gx)]


def target_of(pairs, x):
    target = 0
    for i, j in pairs:
        target = jnp.where(x == i, j, target)
    return target


def edge_at(top, rows):
    return 0 if top is True else rows - HALO if top is False else pl.multiple_of(jnp.where(top, 0, rows - HALO), HALO)


def inner_at(top, rows):
    return HALO if top is True else rows - 2 * HALO if top is False else pl.multiple_of(jnp.where(top, HALO, rows - 2 * HALO), HALO)


def sides_of(gy, y):
    return [(y == 1, True)] if gy == 2 else [(True, y > 0), (False, y < gy - 1)]


def maps_kernel(gx, gy, shape, holder_ref, stratum_ref, transverse_ref, *refs):
    layers, rows = shape
    plane = layers * rows
    picks_ref, beside_ref, mine_ref = refs[6:]
    x, y, z = (lax.axis_index(a) for a in ("gx", "gy", "gz"))
    n = holder_ref.shape[1]
    for partner in range(2):
        cells_ref, rows_ref, masks_ref = refs[3 * partner : 3 * partner + 3]
        group = y * 2 + ((1 - z) if partner else z)
        (holder, layer, row), columns = tables(z, group, layers, holder_ref, stratum_ref, transverse_ref)
        cell = jnp.where(holder == x, layer * rows + row, -1)
        cells_ref[...] = as_onehot(lax.broadcasted_iota(jnp.int32, (plane, n), 0) == cell)
        rows_ref[...] = as_onehot(lax.broadcasted_iota(jnp.int32, (rows, n), 0) == row)
        holder, layer, row = (columns[:, j : j + 1].astype(jnp.int32) for j in range(3))
        lane = lane_of(n)
        first = lane % GROUP < HALO
        here = lane // GROUP == layer + partner * layers
        for side, begin in enumerate((x - 1, x)):
            mine = jnp.logical_and(here, holder == jnp.where(first, begin, begin + 1))
            masks_ref[side * n : (side + 1) * n, :] = jnp.where(mine, 1.0, 0.0)
        if partner:
            continue
        mine = holder == x
        mine_ref[...] = jnp.where(jnp.logical_and(mine, lane >= 0), 1.0, 0.0)
        spoilt = None
        for side, (above, live) in enumerate(sides_of(gy, y)):
            start = edge_at(above, rows)
            part = jnp.logical_and(row // HALO == start // HALO, live)
            spoilt = part if spoilt is None else jnp.logical_or(spoilt, part)
            cell = jnp.where(jnp.logical_and(mine, part), layer * HALO + row - start, -1)
            beside_ref[side * n : (side + 1) * n, :] = as_onehot(lane == cell)
        cell = jnp.where(jnp.logical_and(mine, jnp.logical_not(spoilt)), layer * rows + row, -1)
        picks_ref[...] = as_onehot(lax.broadcasted_iota(jnp.int32, (n, plane), 1) == cell)


def join_kernel(mine_ref, *refs):
    out_ref, at = refs[-1], 0
    for ref in refs[:-1]:
        n = ref.shape[0]
        out_ref[at : at + n, :] = ref[...]
        at += n


def partner_rows(layers):
    whole, at = [], 1
    for i in range(layers - 1, -1, -1):
        whole.append((i, HALO - layers + i, at))
        at += HALO - layers + i
    stride = -(-at // 8) * 8
    later, at = [], 0
    for f in range(2):
        for i in range(layers - 1, -1, -1):
            if ITERS - 1 - layers + i > 0:
                later.append((f, i, ITERS - 1 - layers + i, at))
                at += ITERS - 1 - layers + i
    return whole, stride, later, -(-at // 8) * 8


def fill_kernel(partner, gx, gy, shape, seg, *refs):
    layers, rows = shape
    cells_ref, where_ref, rows_ref, masks_ref = refs[:4]
    plane, chunk = layers * rows, rows // 4
    lengths = lengths_of(gx, chunk, seg)
    if partner:
        sources = [(refs[4], sum(lengths[:k])) for k in range(gx - 1)]
        refs = refs[5:]
    else:
        sources = [(ref, 0) for ref in refs[4 : 4 + gx - 1]]
        refs = refs[4 + gx - 1 :]
    sides = 1 if gy == 2 else 2
    out_ref = refs[0]
    if partner:
        coef_ref, warmth_ref = refs[1:3]
    else:
        strip_refs, partner_refs, segments_ref = refs[1 : 1 + sides], refs[1 + sides : 1 + 2 * sides], refs[1 + 2 * sides]
        n = segments_ref.shape[0] // 2
        coef_ref, warmth_ref = segments_ref.at[pl.ds(0, n), :], segments_ref.at[pl.ds(n, n), :]
    x, y, z = (lax.axis_index(a) for a in ("gx", "gy", "gz"))
    base = layers if partner else 0
    distances = [1, gx - 1] + list(range(2, gx - 1))
    held = [(k, ref, at + (RAW * chunk if j < 2 else 0)) for j, (k, (ref, at)) in enumerate(zip(distances, sources))]
    place_segments(x, gx, seg, coef_ref, warmth_ref, [(0, cells_ref, RAW * plane)] + held)
    coef, warmth = coef_ref[...], warmth_ref[...]
    n = coef.shape[0]
    added = exact_dot(where_ref[...], coupling(coef, warmth))
    near = edge_columns(n, False)
    beside = []
    for side in range(2):
        masked = take(coef, near) * masks_ref[side * n : (side + 1) * n, :]
        beside.append(exact_dot(rows_ref[...], coupling(masked, take(warmth, near))))
    planes = layers + 2
    for i in range(layers):
        src = flip(z, layers, i)
        raw = [cells_ref[pl.ds(pl.multiple_of((f * layers + src) * rows, rows), rows), :] for f in range(RAW)]
        for f, value in enumerate(combine(raw, added[i * rows : (i + 1) * rows])):
            out_ref[f * planes + i] = value
    strips = Strips(
        [ref for ref, _ in sources[:2]], [at for _, at in sources[:2]], cells_ref, RAW * plane + 2 * seg, rows, layers
    )
    half = lane_of(chunk) // (LANES // 2) == (1 if partner else 0)
    for part in range(4):
        here = slice(part * chunk, (part + 1) * chunk)
        raw = [strips.both(f, part * chunk, chunk, x, gx, partner) for f in range(RAW)]
        for side in range(2):
            cells = [jnp.where(half, value[side], 0.0) for value in raw]
            for f, value in enumerate(combine(cells, beside[side][here])):
                out_ref[f * planes + layers + side, here, :] = value
    if partner:
        return
    low = lane_of(HALO) < LANES // 2
    upper = lax.broadcasted_iota(jnp.int32, (HALO, LANES), 0) < HALO // 2
    first = lane_of(HALO) % GROUP < HALO
    sent = FIELDS - 1
    for strip_ref, partner_ref, (top, _) in zip(strip_refs, partner_refs, sides_of(gy, y)):
        edge = pl.ds(edge_at(top, rows), HALO)

        def shrink(values):
            *whole, e, g = values
            e = jnp.where(top, e, pltpu.roll(e, HALO // 2, 0))
            g = jnp.where(top, pltpu.roll(g, HALO // 2, 0), g)
            return whole + [jnp.where(upper, e, g)]

        def give(ref, at, values):
            for f, value in enumerate(values):
                ref[at + f * HALO : at + (f + 1) * HALO, :] = value

        for i in range(layers):
            give(strip_ref, i * sent * HALO, shrink([out_ref[f * planes + i, edge, :] for f in range(FIELDS)]))
        outer = []
        for f in range(FIELDS):
            left, right = (out_ref[f * planes + layers + side, edge, :] for side in range(2))
            outer.append(jnp.where(first, left, right))
        outer = shrink(outer)
        values = [jnp.where(low, outer[j], pltpu.roll(outer[j + 1], LANES // 2, 1)) for j in range(0, sent, 2)]
        give(strip_ref, layers * sent * HALO, values)
        whole, stride, later, shared = partner_rows(layers)
        pieces = [(f, i, m, f * stride + at) for f in range(sent - 1) for i, m, at in whole]
        pieces += [(sent - 1 + f, i, m, (sent - 1) * stride + at) for f, i, m, at in later]
        for f, i, m, at in pieces:
            start = edge_at(top, rows) + jnp.where(top, 0, HALO - m)
            partner_ref[at : at + m, :] = out_ref[f * planes + i, pl.ds(start, m), :]
        give(partner_ref, (sent - 1) * stride + shared, values)


def planes_of(count, total):
    return list(range(count)) + [total - 2, total - 1]


def lateral(buf, at, n, which):
    sums = []
    for i in which:
        centre = buf[i, pl.ds(at, n), :]
        beside = pltpu.roll(centre, 1, 1) + pltpu.roll(centre, LANES - 1, 1)
        sums.append(beside + (buf[i, pl.ds(at - 1, n), :] + buf[i, pl.ds(at + 1, n), :]))
    return sums


def vertical(planes, edges, count):
    sums = []
    for i in range(count):
        near = [planes[j] for j in (i - 1, i + 1) if 0 <= j < len(planes)]
        sums.append(functools.reduce(jnp.add, near))
    for edge in edges:
        lane = lane_of(edge.shape[0])
        up = jnp.where(lane >= GROUP, pltpu.roll(edge, GROUP, 1), 0.0)
        down = jnp.where(lane < LANES - GROUP, pltpu.roll(edge, LANES - GROUP, 1), 0.0)
        sums.append(up + down)
    return sums


def coefficients(s_ref, at, n, raw, dests, to, outside):
    a_ref, q_ref, r_ref, e_ref, g_ref, root_ref = dests
    total = s_ref.shape[0]
    sums = lateral(s_ref, at, n, range(total))
    t = [raw(1, i) for i in range(total)]
    above = vertical(t[:-2], t[-2:], total - 2)
    here = pl.ds(to, n)
    for i in range(total):
        s = s_ref[i, pl.ds(at, n), :]
        diag = raw(3, i) + s * sums[i] + t[i] * above[i]
        if outside or i >= total - 2:
            inverse = 1.0 / jnp.where(diag > 0.0, diag, 1.0)
            root = jnp.where(s > 0.0, 1.0 / jnp.where(s > 0.0, s, 1.0), 0.0)
        else:
            inverse, root = 1.0 / diag, 1.0 / s
        if i < root_ref.shape[0]:
            root_ref[i, here, :] = root
        scaled = s * inverse
        a_ref[i, here, :] = s * scaled
        r_ref[i, here, :] = raw(4, i) * scaled
        e_ref[i, here, :] = raw(5, i) * scaled
        g_ref[i, here, :] = raw(6, i) * inverse
        q_ref[i, here, :] = t[i] * root


def shifted_sums(distance):
    to = lax.broadcasted_iota(jnp.int32, (2 * LANES, LANES), 1)
    of = lax.broadcasted_iota(jnp.int32, (2 * LANES, LANES), 0) % LANES
    return as_onehot(jnp.abs(of - to) == distance)


def sweep_edges(src_ref, dst_ref, at, n, coefs, base, matrices):
    a_ref, q_ref, r_ref = coefs[:3]
    total = src_ref.shape[0]
    here, there = pl.ds(base, n), pl.ds(at, n)

    def product(value, matrix):
        return jnp.dot(jnp.concatenate(split(value), axis=1), matrix, preferred_element_type=jnp.float32)

    for i in (total - 2, total - 1):
        centre = src_ref[i, there, :]
        beside = product(centre, matrices[0])
        above = product(q_ref[i, here, :] * centre, matrices[1])
        beside = beside + (src_ref[i, pl.ds(at - 1, n), :] + src_ref[i, pl.ds(at + 1, n), :])
        dst_ref[i, there, :] = r_ref[i, here, :] + a_ref[i, here, :] * (beside + q_ref[i, here, :] * above)


def sweep(src_ref, dst_ref, at, n, count, coefs, base, edges=True):
    a_ref, q_ref, r_ref = coefs[:3]
    total = src_ref.shape[0]
    here, there = pl.ds(base, n), pl.ds(at, n)
    which = planes_of(count, total) if edges else list(range(count))
    sums = lateral(src_ref, at, n, which)
    scaled = [q_ref[i, here, :] * src_ref[i, there, :] for i in range(min(count + 1, total - 2))]
    outer = [q_ref[i, here, :] * src_ref[i, there, :] for i in which[count:]]
    above = vertical(scaled, outer, count)
    for j, i in enumerate(which):
        dst_ref[i, there, :] = r_ref[i, here, :] + a_ref[i, here, :] * (sums[j] + q_ref[i, here, :] * above[j])


def next_rhs(coefs, v_ref, at, n, base):
    r_ref, e_ref, g_ref = coefs[2:5]
    here = pl.ds(base, n)
    for i in range(v_ref.shape[0]):
        r_ref[i, here, :] = e_ref[i, here, :] + g_ref[i, here, :] * v_ref[i, pl.ds(at, n), :]


def meet(v_ref, at, n, count, back):
    total = v_ref.shape[0]
    here = pl.ds(at, n)
    lane = lane_of(n)
    j, group = lane % GROUP, lane // GROUP
    outer = jnp.logical_or(lane < ITERS, lane >= LANES - ITERS)
    left, right = v_ref[total - 2, here, :], v_ref[total - 1, here, :]
    middle = jnp.where(j < HALO, right, left)
    for i in range(count):
        value = v_ref[i, here, :]
        if back:
            moved = pltpu.roll(value, (i * GROUP + HALO) % LANES, 1)
            left = jnp.where(jnp.logical_and(group == i, j >= GROUP - ITERS), moved, left)
            right = jnp.where(jnp.logical_and(group == i, j < ITERS), moved, right)
        v_ref[i, here, :] = jnp.where(outer, pltpu.roll(middle, LANES - (i * GROUP + HALO), 1), value)
    if back:
        v_ref[total - 2, here, :] = left
        v_ref[total - 1, here, :] = right


def needed(layers, n):
    return min(2 * layers, layers + STEPS * ITERS - 1 - n)


def two_steps(layers, sweep_all, between, after):
    for step in range(STEPS):
        whole = [n for n in range(step * ITERS, (step + 1) * ITERS) if needed(layers, n) == 2 * layers]
        pairs = len(whole) // 2

        def pair(k, carry):
            n = step * ITERS + 2 * k
            sweep_all(n, 0, 2 * layers)
            sweep_all(n + 1, 1, 2 * layers)
            return carry

        if pairs:
            lax.fori_loop(0, pairs, pair, 0)
        for n in range(step * ITERS + 2 * pairs, (step + 1) * ITERS):
            sweep_all(n, n % 2, needed(layers, n))
        after(step)
        if step < STEPS - 1:
            between()


PAD = 8


def tile_kernel(gx, gy, shape, *refs):
    layers, rows = shape
    own_ref, partner_ref, picks_ref, out_ref, below_ref, level_ref = refs[:6]
    s_ref, va_ref, vb_ref = refs[6:9]
    coefs = refs[9:]
    x, y, z = (lax.axis_index(a) for a in ("gx", "gy", "gz"))
    total = 2 * layers + 2
    zeros = jnp.zeros((PAD, LANES), jnp.float32)
    for ref in (s_ref, va_ref, vb_ref):
        for i in range(total):
            ref[i, 0:PAD, :] = zeros
            ref[i, PAD + rows : PAD + rows + PAD, :] = zeros

    def field(f, i, here):
        j = f * (layers + 2)
        if i >= 2 * layers:
            j = j + i - layers
            return own_ref[j, here, :] + partner_ref[j, here, :]
        return own_ref[j + i, here, :] if i < layers else partner_ref[j + i - layers, here, :]

    for i in range(total):
        s_ref[i, PAD : PAD + rows, :] = field(0, i, slice(None))
        va_ref[i, PAD : PAD + rows, :] = field(2, i, slice(None))
    n = 8
    for at in range(0, rows, n):
        coefficients(s_ref, PAD + at, n, lambda f, i: field(f, i, slice(at, at + n)), coefs, at, False)

    bufs = (va_ref, vb_ref)
    sides = sides_of(gy, y)
    matrices = shifted_sums(1), shifted_sums(GROUP)

    def sweep_all(number, which, count):
        src_ref, dst_ref = bufs[which], bufs[1 - which]
        for side, (above, _) in enumerate(sides):
            inner = pl.ds(PAD + inner_at(above, rows), HALO)
            for i in range(total):
                level_ref[(side * STEPS * ITERS + number) * total + i] = src_ref[i, inner, :]
        sweep_edges(src_ref, dst_ref, PAD, rows, coefs, 0, matrices)
        for at in range(0, rows, n):
            sweep(src_ref, dst_ref, PAD + at, n, count, coefs, at, edges=False)

    def after(step):
        last = step == STEPS - 1
        for at in range(0, rows, n):
            meet(va_ref, PAD + at, n, layers if last else 2 * layers, not last)
        heat = []
        for i in range(layers):
            here = pl.ds(PAD, rows)
            heat.append(va_ref[i, here, :] * coefs[5][i])
            if step == STEPS - 1:
                out_ref[flip(z, layers, i)] = heat[-1]
        below_ref[step] = exact_dot(picks_ref[...], jnp.concatenate(heat, axis=0))

    def between():
        for at in range(0, rows, n):
            next_rhs(coefs, va_ref, PAD + at, n, at)

    two_steps(layers, sweep_all, between, after)


def edge_kernel(gx, gy, shape, seg, *refs):
    layers, rows = shape
    own_ref, partner_ref, picks_ref, mine_ref, segments_ref, below_ref, level_ref = refs[:7]
    sides_n = 1 if gy == 2 else 2
    along, across = refs[7 : 7 + sides_n], refs[7 + sides_n : 7 + 2 * sides_n]
    refs = refs[7 + 2 * sides_n :]
    rounds = return_rounds(gx)
    heat_ref, keep_ref, returns = refs[0], refs[1], refs[2 : 2 + len(rounds)]
    ret_ref, s_ref, va_ref, vb_ref, *coefs = refs[2 + len(rounds) :]
    x, y, z = (lax.axis_index(a) for a in ("gx", "gy", "gz"))
    total = 2 * layers + 2
    count = mine_ref.shape[0]
    below = [below_ref[step] for step in range(STEPS)]
    lane = lane_of(HALO)
    low, first = lane < LANES // 2, lane % GROUP < HALO
    columns = edge_columns(HALO, False)
    bufs = (va_ref, vb_ref)

    def tile(j):
        return pl.ds(j if isinstance(j, int) else pl.multiple_of(j, HALO), HALO)

    for side, (above, live) in enumerate(sides_of(gy, y)):
        def place(when_top, otherwise):
            if above is True or above is False:
                return when_top * HALO if above else otherwise * HALO
            return jnp.where(above, when_top * HALO, otherwise * HALO)

        outer, strip, edge, inner = place(0, 3), place(1, 2), place(2, 1), place(3, 0)
        edge_rows = tile(edge_at(above, rows))
        inner_rows = tile(inner_at(above, rows))

        def field(f, i, here):
            j = f * (layers + 2)
            if i >= 2 * layers:
                j = j + i - layers
                return own_ref[j, here, :] + partner_ref[j, here, :]
            return own_ref[j + i, here, :] if i < layers else partner_ref[j + i - layers, here, :]

        t_ref, d_ref, q_ref, e_ref, g_ref = coefs[1], coefs[0], coefs[2], coefs[3], coefs[4]
        keep = {0: s_ref, 1: t_ref, 2: va_ref, 3: d_ref, 4: q_ref, 5: e_ref, 6: g_ref}
        zeros = jnp.zeros((HALO, LANES), jnp.float32)
        src = lane % (LANES // 2)
        turned = (layers - 1 - src // GROUP) * GROUP + src % GROUP
        half_tile = lax.broadcasted_iota(jnp.int32, (HALO, LANES), 0) < HALO // 2

        def unpack(value, f):
            if f < FIELDS - 2:
                return value
            turned_value = pltpu.roll(value, HALO // 2, 0)
            if f == FIELDS - 2:
                at_top, at_bottom = jnp.where(half_tile, 0.0, turned_value), jnp.where(half_tile, value, 0.0)
            else:
                at_top, at_bottom = jnp.where(half_tile, 0.0, value), jnp.where(half_tile, turned_value, 0.0)
            return jnp.where(above, at_top, at_bottom)

        whole, stride, later, shared = partner_rows(layers)
        sublane = lax.broadcasted_iota(jnp.int32, (HALO, LANES), 0)

        def nearest(ref, m, at):
            at_top = jnp.where(sublane >= HALO - m, ref[at - HALO + m : at + m, :], 0.0)
            return jnp.where(above, at_top, jnp.where(sublane < m, ref[at : at + HALO, :], 0.0))

        for f in range(FIELDS):
            g = min(f, FIELDS - 2)
            if f < FIELDS - 2:
                rows_of = {i: (m, f * stride + at) for i, m, at in whole}
            else:
                rows_of = {i: (m, (FIELDS - 2) * stride + at) for which, i, m, at in later if which == f - FIELDS + 2}
            values, inside = [], zeros
            for i in range(2 * layers):
                if i < layers:
                    at = (i * (FIELDS - 1) + g) * HALO
                    value = unpack(along[side][at : at + HALO, :], f)
                else:
                    j = 2 * layers - 1 - i
                    value = nearest(across[side], *rows_of[j]) if j in rows_of else zeros
                values.append(value)
                inside = jnp.where(lane // GROUP == i, take(value, columns), inside)
            half = (LANES // 2) * (g % 2)
            at = (layers * (FIELDS - 1) + g // 2) * HALO
            a = take(along[side][at : at + HALO, :], src + half)
            at = (FIELDS - 2) * stride + shared + (g // 2) * HALO
            b = take(across[side][at : at + HALO, :], turned + half)
            outside = unpack(jnp.where(low, a, b), f)
            values += [jnp.where(first, outside, inside), jnp.where(first, inside, outside)]
            for i, value in enumerate(values):
                ref, shift = keep[f], 0 if f in (0, 2) else HALO
                ref[i, tile(strip - shift), :] = value
                ref[i, tile(edge - shift), :] = field(f, i, edge_rows)
        for i in range(total):
            s_ref[i, tile(outer), :] = zeros
            va_ref[i, tile(outer), :] = zeros
            vb_ref[i, tile(outer), :] = zeros
            s_ref[i, tile(inner), :] = field(0, i, inner_rows)
        n = 2 * HALO
        held = [[keep[f][i, pl.ds(0, n), :] for i in range(total)] if f in (1, 3, 4, 5, 6) else None for f in range(FIELDS)]
        coefficients(s_ref, HALO, n, lambda f, i: held[f][i], coefs, 0, True)

        def sweep_all(number, which, needed_layers):
            src_ref, dst_ref = bufs[which], bufs[1 - which]
            for i in range(total):
                src_ref[i, tile(inner), :] = level_ref[(side * STEPS * ITERS + number) * total + i]
            sweep(src_ref, dst_ref, HALO, n, needed_layers, coefs, 0)

        picks = picks_ref[side * count : (side + 1) * count, :]

        def after(step):
            last = step == STEPS - 1
            meet(va_ref, HALO, n, layers if last else 2 * layers, not last)
            heat = []
            for i in range(layers):
                heat.append(va_ref[i, tile(edge), :] * coefs[5][i, tile(edge - HALO), :])
                if step == STEPS - 1:
                    heat_ref[side * layers + flip(z, layers, i)] = heat[-1]
            heat.append(jnp.zeros((LANES - layers * HALO, LANES), jnp.float32))
            below[step] = below[step] + exact_dot(picks, jnp.concatenate(heat, axis=0))

        two_steps(layers, sweep_all, lambda: next_rhs(coefs, va_ref, HALO, n, 0), after)

    coef, warmth = segments_ref[:count, :], segments_ref[count:, :]
    for step in range(STEPS):
        warmth = warmth + coolant_gain * coef * (below[step] - warmth)
    ret_ref[...] = jnp.where(mine_ref[...] > 0.0, warmth, 0.0)
    keep_ref[...] = ret_ref[pl.ds(pl.multiple_of(x * seg, seg), seg), :]
    for pairs, ref in zip(rounds, returns):
        ref[...] = ret_ref[pl.ds(pl.multiple_of(target_of(pairs, x) * seg, seg), seg), :]


def merge_kernel(gy, whole_ref, heat_ref, out_ref):
    layers, rows, _ = whole_ref.shape
    out_ref[...] = whole_ref[...]
    for side, (above, live) in enumerate(sides_of(gy, lax.axis_index("gy"))):
        def put(side=side, above=above):
            out_ref[:, pl.ds(edge_at(above, rows), HALO), :] = heat_ref[side * layers : (side + 1) * layers]

        if live is True:
            put()
        else:
            pl.when(live)(put)


def local(gx, gy, gz, u, power, storage, conductance, warmth, coef, holder, stratum, transverse):
    layers, rows, columns = u.shape
    seg = warmth.shape[1]
    segments = stratum.shape[1]
    if gz != 2 or gx < 3 or columns != LANES or 2 * layers * GROUP != LANES or rows % 32:
        raise ValueError("unsupported shape")
    holder = holder[:, :, 0]
    shape = (layers, rows)
    f32 = jnp.float32
    chunk = rows // 4
    wide = RAW * chunk + 2 * seg

    def struct(*dims):
        return jax.ShapeDtypeStruct(dims, f32)

    def vmem(*dims):
        return pltpu.VMEM(dims, f32)

    indices = (holder, stratum, transverse)
    flat = [a.reshape(-1, LANES) for a in (u, power, storage, conductance, warmth, coef)]
    own, to_left, to_right, only, *indices = pl.pallas_call(
        functools.partial(pack_kernel, shape),
        out_shape=(
            struct(RAW * layers * rows + 2 * seg + 2 * RAW * chunk, LANES),
            struct(wide, LANES),
            struct(wide, LANES),
            struct(2 * seg, LANES),
            *(jax.ShapeDtypeStruct(a.shape, a.dtype) for a in indices),
        ),
        in_specs=[pl.BlockSpec(memory_space=pltpu.HBM)] * 9,
        out_specs=(VMEM,) * 7,
        scratch_shapes=[pltpu.SemaphoreType.DMA((9,))],
        compiler_params=PARAMS,
        name="pack",
    )(*(pltpu.with_memory_space_constraint(a, pltpu.HBM) for a in (*flat, *indices)))

    swap = [(0, 1), (1, 0)]
    partner = lax.ppermute(own, "gz", swap)
    def from_distance(value, k):
        return lax.ppermute(value, "gx", [(i, (i - k) % gx) for i in range(gx)])

    received = [from_distance(to_left, 1), from_distance(to_right, gx - 1)]
    received += [from_distance(only, k) for k in range(2, gx - 1)]

    sides = 1 if gy == 2 else 2
    fields = struct(FIELDS * (layers + 2), rows, LANES)
    strip_rows = (FIELDS - 1) * layers * HALO + (FIELDS - 1) // 2 * HALO
    _, stride, _, shared = partner_rows(layers)
    partner_strip = (FIELDS - 2) * stride + shared + (FIELDS - 1) // 2 * HALO
    sides = 1 if gy == 2 else 2
    bf16 = jnp.bfloat16
    one_group = (
        jax.ShapeDtypeStruct((layers * rows, segments), bf16),
        jax.ShapeDtypeStruct((rows, segments), bf16),
        struct(2 * segments, LANES),
    )
    maps = pl.pallas_call(
        functools.partial(maps_kernel, gx, gy, shape),
        out_shape=one_group
        + one_group
        + (
            jax.ShapeDtypeStruct((segments, layers * rows), bf16),
            jax.ShapeDtypeStruct((sides * segments, LANES), bf16),
            struct(segments, LANES),
        ),
        in_specs=[VMEM] * 3,
        out_specs=(VMEM,) * 9,
        compiler_params=PARAMS,
        cost_estimate=cost(1),
        name="maps",
    )(*indices)
    own_maps, partner_maps, (picks, picks_beside, mine) = maps[:3], maps[3:6], maps[6:]
    joined = pl.pallas_call(
        join_kernel,
        out_shape=struct(sum(a.shape[0] for a in received), LANES),
        in_specs=[pl.BlockSpec(memory_space=pl.ANY)] + [VMEM] * (gx - 1),
        out_specs=VMEM,
        compiler_params=PARAMS,
        name="join",
    )(mine, *received)
    late = lax.ppermute(joined, "gz", swap)
    filled = pl.pallas_call(
        functools.partial(fill_kernel, False, gx, gy, shape, seg),
        out_shape=(fields,) + (struct(strip_rows, LANES),) * sides
        + (struct(partner_strip, LANES),) * sides
        + (struct(2 * segments, LANES),),
        in_specs=[VMEM] * (4 + gx - 1),
        out_specs=(VMEM,) * (2 + 2 * sides),
        compiler_params=PARAMS,
        cost_estimate=cost(1.5),
        name="fill_own",
    )(own, *own_maps, *received)
    own_fields, held = filled[0], filled[-1]
    strips, partner_strips = filled[1 : 1 + sides], filled[1 + sides : 1 + 2 * sides]
    if gy == 2:
        routes = [(0, swap)]
    else:
        up = [(i, i + 1) for i in range(gy - 1)]
        routes = [(1, up), (0, [(j, i) for i, j in up])]
    along = [lax.ppermute(strips[side], "gy", pairs) for side, pairs in routes]
    across = []
    for side, pairs in routes:
        both = [(2 * i + z, 2 * j + 1 - z) for i, j in pairs for z in range(2)]
        across.append(lax.ppermute(partner_strips[side], ("gy", "gz"), both))

    partner_fields = pl.pallas_call(
        functools.partial(fill_kernel, True, gx, gy, shape, seg),
        out_shape=fields,
        in_specs=[VMEM] * 5,
        out_specs=VMEM,
        scratch_shapes=[vmem(segments, LANES)] * 2,
        compiler_params=PARAMS,
        cost_estimate=cost(1.5),
        name="fill_partner",
    )(partner, *partner_maps, late)

    total = 2 * layers + 2
    padded = vmem(total, rows + 2 * PAD, LANES)
    inside, below, levels = pl.pallas_call(
        functools.partial(tile_kernel, gx, gy, shape),
        out_shape=(
            struct(layers, rows, LANES),
            struct(STEPS, segments, LANES),
            struct(sides * STEPS * ITERS * total, HALO, LANES),
        ),
        in_specs=[VMEM] * 3,
        out_specs=(VMEM,) * 3,
        scratch_shapes=[padded] * 3 + [vmem(total, rows, LANES)] * 5 + [vmem(layers, rows, LANES)],
        compiler_params=PARAMS,
        cost_estimate=cost(7),
        name="tile_sweeps",
    )(own_fields, partner_fields, picks)

    rounds = return_rounds(gx)
    results = pl.pallas_call(
        functools.partial(edge_kernel, gx, gy, shape, seg),
        out_shape=(struct(sides * layers, HALO, LANES),) + (struct(seg, LANES),) * (1 + len(rounds)),
        in_specs=[VMEM] * (7 + 2 * sides),
        out_specs=(VMEM,) * (2 + len(rounds)),
        scratch_shapes=[vmem(segments, LANES)]
        + [vmem(total, 4 * HALO, LANES)] * 3
        + [vmem(total, 2 * HALO, LANES)] * 5
        + [vmem(layers, 2 * HALO, LANES)],
        compiler_params=PARAMS,
        cost_estimate=cost(1.5),
        name="edge_sweeps",
    )(own_fields, partner_fields, picks_beside, mine, held, below, levels, *along, *across)
    heat, coolant = results[0], results[1]
    returned = [lax.ppermute(value, "gx", pairs) for value, pairs in zip(results[2:], rounds)]
    temperature = pl.pallas_call(
        functools.partial(merge_kernel, gy),
        out_shape=struct(layers, rows, LANES),
        in_specs=[VMEM] * 2,
        out_specs=VMEM,
        compiler_params=PARAMS,
        cost_estimate=cost(1),
        name="merge",
    )(inside, heat)
    for value in returned:
        coolant = coolant + value
    return temperature, coolant[None]


def solution(mesh):
    gx, gy, gz = (mesh.shape[a] for a in ("gx", "gy", "gz"))
    cells = P(("stack", "gz"), "gy", "gx")
    segments = P(("stack", "gy", "gz"), "gx", None)
    return jax.shard_map(
        functools.partial(local, gx, gy, gz),
        mesh=mesh,
        in_specs=(cells, cells, cells, P(None, ("stack", "gz"), "gy", "gx"), segments, segments, P(), P(), P()),
        out_specs=(cells, segments),
        check_vma=False,
    )
```

```python
import functools

import jax
import jax.numpy as jnp
from jax import lax
from jax.experimental import pallas as pl
from jax.experimental.pallas import tpu as pltpu
from jax.sharding import PartitionSpec as P

STEPS = 2
ITERS = 4
HALO = STEPS * ITERS
GROUP = 2 * HALO
LANES = 128
RAW = 5
FIELDS = 7
coolant_gain = 0.5

VMEM = pl.BlockSpec(memory_space=pltpu.VMEM)
PARAMS = pltpu.CompilerParams(vmem_limit_bytes=40 * 1024 * 1024)


def cost(microseconds):
    return pl.CostEstimate(flops=0, bytes_accessed=int(microseconds * 3e6), transcendentals=0)


def lane_of(rows):
    return lax.broadcasted_iota(jnp.int32, (rows, LANES), 1)


def take(value, index):
    return jnp.take_along_axis(value, index, axis=1, mode="promise_in_bounds")


def edge_columns(rows, turned):
    j = lane_of(rows) % GROUP
    first = j < HALO
    return jnp.where(first, LANES - HALO + j, j - HALO) if not turned else jnp.where(first, j, LANES - GROUP + j)


def split(value):
    high = value.astype(jnp.bfloat16)
    low = (value - high.astype(jnp.float32)).astype(jnp.bfloat16)
    return high, low


def exact_dot(onehot, value):
    high, low = split(value)
    both = jnp.concatenate([high, low], axis=0)
    return jnp.dot(jnp.concatenate([onehot, onehot], axis=1), both, preferred_element_type=jnp.float32)


def coupling(coef, warmth):
    flow = coef * warmth
    second = coolant_gain * coef * coef
    return jnp.concatenate([coef, flow, second, flow - second * warmth], axis=1)


def flip(z, layers, i):
    return jnp.where(z == 0, i, layers - 1 - i)


def pack_kernel(shape, u_ref, p_ref, c_ref, k_ref, f_ref, x_ref, *refs):
    own_ref, left_ref, right_ref, seg_ref = refs[3:7]
    sems = refs[-1]
    layers, rows = shape
    seg = f_ref.shape[0]
    z = lax.axis_index("gz")
    plane = layers * rows
    copies = []

    def fetch(src, dst):
        copies.append(pltpu.make_async_copy(src, dst, sems.at[len(copies)]))
        copies[-1].start()

    fetch(k_ref, own_ref.at[pl.ds(0, 2 * plane), :])
    for field, ref in enumerate((u_ref, p_ref, c_ref), 2):
        fetch(ref, own_ref.at[pl.ds(field * plane, plane), :])
    for j, ref in enumerate((x_ref, f_ref)):
        fetch(ref, own_ref.at[pl.ds(RAW * plane + j * seg, seg), :])
    for table, place in zip(refs[:3], refs[7:10]):
        fetch(table, place)
    chunk = rows // 4
    lane = lane_of(chunk)
    first = lane % GROUP < HALO
    columns = edge_columns(chunk, False), edge_columns(chunk, True)
    edges = RAW * plane + 2 * seg

    def gather(field, at, g):
        value = None
        for i in range(layers):
            start = pl.multiple_of((field * layers + flip(z, layers, i)) * rows + at, chunk)
            taken = take(own_ref[pl.ds(start, chunk), :], columns[g % 2])
            value = taken if value is None else jnp.where(lane // GROUP == (g // 2) * layers + i, taken, value)
        return value

    def place(g, part):
        return pl.ds(edges + ((g % 2) * RAW + part) * chunk, chunk)

    copies[0].wait()
    roots = pl.ds(0, 2 * plane)
    own_ref[roots, :] = jnp.sqrt(own_ref[roots, :])
    for field in range(4):
        if field >= 2:
            copies[field - 1].wait()
        for part in range(4):
            value = gather(field, part * chunk, field)
            if field >= 2:
                value = jnp.where(lane < LANES // 2, own_ref[place(field, part), :], value)
            own_ref[place(field, part), :] = value
    copies[3].wait()
    for g in range(4):
        value = gather(4, g * chunk, g)
        if g >= 2:
            value = jnp.where(lane < LANES // 2, own_ref[place(g, 4), :], value)
        own_ref[place(g, 4), :] = value
    for part in range(RAW):
        even, odd = own_ref[place(0, part), :], own_ref[place(1, part), :]
        left_ref[part * chunk : (part + 1) * chunk, :] = jnp.where(first, odd, even)
        right_ref[part * chunk : (part + 1) * chunk, :] = jnp.where(first, even, odd)
    for copy in copies[4:]:
        copy.wait()
    segments = own_ref[RAW * plane : RAW * plane + 2 * seg, :]
    seg_ref[...] = segments
    left_ref[RAW * chunk :, :] = segments
    right_ref[RAW * chunk :, :] = segments


class Strips:
    def __init__(self, refs, starts, cells_ref, start, rows, layers):
        self.refs, self.starts = refs, starts
        self.cells_ref, self.start = cells_ref, start
        self.rows, self.layers = rows, layers

    def both(self, field, start, n, x, gx, partner):
        chunk = self.rows // 4
        if field < 4:
            g, at = field, start
        else:
            g, at = start // chunk, 4 * chunk + start % chunk
        a, b = (ref[at + begin : at + begin + n, :] for ref, begin in zip(self.refs, self.starts))
        at = self.start + (g % 2) * RAW * chunk + at
        inside = self.cells_ref[at : at + n, :]
        from_left, from_right = jnp.where(x > 0, b, 0.0), jnp.where(x < gx - 1, a, 0.0)
        lane = lane_of(n)
        first = (lane % GROUP < HALO) if g % 2 == 0 else (lane % GROUP >= HALO)
        half = self.layers * GROUP
        src = lane % half
        if partner:
            src = (self.layers - 1 - src // GROUP) * GROUP + src % GROUP
        if g % 2 == 1:
            src = jnp.where(src % GROUP < HALO, src + HALO, src - HALO)
        src = src + half * (g // 2)
        return take(jnp.where(first, from_left, inside), src), take(jnp.where(first, inside, from_right), src)


def place_segments(x, gx, seg, coef_ref, warmth_ref, sources):
    for k, ref, at in sources:
        place = pl.ds(pl.multiple_of(lax.rem(x + k, gx) * seg, seg), seg)
        coef_ref[place, :] = ref[at : at + seg, :]
        warmth_ref[place, :] = ref[at + seg : at + 2 * seg, :]


def tables(z, group, layers, holder_ref, stratum_ref, transverse_ref):
    holder = holder_ref[pl.ds(group, 1), :]
    layer = stratum_ref[pl.ds(group, 1), :]
    layer = jnp.where(z == 0, layer, layers - 1 - layer)
    row = transverse_ref[pl.ds(group, 1), :]
    n = holder.shape[1]
    which = lax.broadcasted_iota(jnp.int32, (8, n), 0)
    stacked = jnp.where(which == 0, holder, jnp.where(which == 1, layer, row))
    eye = lax.broadcasted_iota(jnp.int32, (n, n), 0) == lax.broadcasted_iota(jnp.int32, (n, n), 1)
    columns = lax.dot_general(
        eye.astype(jnp.float32).astype(jnp.bfloat16),
        stacked.astype(jnp.float32).astype(jnp.bfloat16),
        (((1,), (1,)), ((), ())),
        preferred_element_type=jnp.float32,
    )
    return (holder, layer, row), columns


def as_onehot(mask):
    return jnp.where(mask, 1.0, 0.0).astype(jnp.bfloat16)


def combine(raw, added):
    s, t, u, power, storage = raw
    wall, flow, second, later = (added[:, i * LANES : (i + 1) * LANES] for i in range(4))
    return s, t, s * u, storage + wall, power + storage * u + flow, power + later, storage + second


def lengths_of(gx, chunk, seg):
    return [RAW * chunk + 2 * seg] * 2 + [2 * seg] * (gx - 3)


def edge_at(top, rows):
    return 0 if top is True else rows - HALO if top is False else pl.multiple_of(jnp.where(top, 0, rows - HALO), HALO)


def inner_at(top, rows):
    return HALO if top is True else rows - 2 * HALO if top is False else pl.multiple_of(jnp.where(top, HALO, rows - 2 * HALO), HALO)


def sides_of(gy, y):
    return [(y == 1, True)] if gy == 2 else [(True, y > 0), (False, y < gy - 1)]


def maps_kernel(gx, gy, shape, holder_ref, stratum_ref, transverse_ref, *refs):
    layers, rows = shape
    plane = layers * rows
    picks_ref, beside_ref, mine_ref, near_ref, line_ref = refs[6:]
    x, y, z = (lax.axis_index(a) for a in ("gx", "gy", "gz"))
    n = holder_ref.shape[1]
    for partner in range(2):
        cells_ref, rows_ref, masks_ref = refs[3 * partner : 3 * partner + 3]
        group = y * 2 + ((1 - z) if partner else z)
        (holder, layer, row), columns = tables(z, group, layers, holder_ref, stratum_ref, transverse_ref)
        cell = jnp.where(holder == x, layer * rows + row, -1)
        cells_ref[...] = as_onehot(lax.broadcasted_iota(jnp.int32, (plane, n), 0) == cell)
        rows_ref[...] = as_onehot(lax.broadcasted_iota(jnp.int32, (rows, n), 0) == row)
        if not partner:
            near, m = layers * HALO, 2 * HALO
            for side, (above, _) in enumerate(sides_of(gy, y)):
                start = edge_at(above, rows)
                at_edge = row // HALO == start // HALO
                cell = jnp.where(jnp.logical_and(holder == x, at_edge), layer * HALO + row - start, -1)
                near_ref[side * near : (side + 1) * near, :] = as_onehot(
                    lax.broadcasted_iota(jnp.int32, (near, n), 0) == cell
                )
                cell = jnp.where(at_edge, row - start, -1)
                line_ref[side * m : (side + 1) * m, :] = as_onehot(lax.broadcasted_iota(jnp.int32, (m, n), 0) == cell)
        holder, layer, row = (columns[:, j : j + 1].astype(jnp.int32) for j in range(3))
        lane = lane_of(n)
        first = lane % GROUP < HALO
        here = lane // GROUP == layer + partner * layers
        for side, begin in enumerate((x - 1, x)):
            mine = jnp.logical_and(here, holder == jnp.where(first, begin, begin + 1))
            masks_ref[side * n : (side + 1) * n, :] = jnp.where(mine, 1.0, 0.0)
        if partner:
            continue
        mine = holder == x
        mine_ref[...] = jnp.where(jnp.logical_and(mine, lane >= 0), 1.0, 0.0)
        spoilt = None
        for side, (above, live) in enumerate(sides_of(gy, y)):
            start = edge_at(above, rows)
            part = jnp.logical_and(row // HALO == start // HALO, live)
            spoilt = part if spoilt is None else jnp.logical_or(spoilt, part)
            cell = jnp.where(jnp.logical_and(mine, part), layer * HALO + row - start, -1)
            beside_ref[side * n : (side + 1) * n, :] = as_onehot(lane == cell)
        cell = jnp.where(jnp.logical_and(mine, jnp.logical_not(spoilt)), layer * rows + row, -1)
        picks_ref[...] = as_onehot(lax.broadcasted_iota(jnp.int32, (n, plane), 1) == cell)


def join_kernel(mine_ref, *refs):
    out_ref, at = refs[-1], 0
    for ref in refs[:-1]:
        n = ref.shape[0]
        out_ref[at : at + n, :] = ref[...]
        at += n


def partner_rows(layers):
    whole, at = [], 1
    for i in range(layers - 1, -1, -1):
        whole.append((i, HALO - layers + i, at))
        at += HALO - layers + i
    stride = -(-at // 8) * 8
    later, at = [], 0
    for f in range(2):
        for i in range(layers - 1, -1, -1):
            if ITERS - 1 - layers + i > 0:
                later.append((f, i, ITERS - 1 - layers + i, at))
                at += ITERS - 1 - layers + i
    return whole, stride, later, -(-at // 8) * 8


def fill_kernel(partner, gx, gy, shape, seg, *refs):
    layers, rows = shape
    cells_ref, where_ref, rows_ref, masks_ref = refs[:4]
    plane, chunk = layers * rows, rows // 4
    lengths = lengths_of(gx, chunk, seg)
    x, z = lax.axis_index("gx"), lax.axis_index("gz")
    if partner:
        late_ref, out_ref, coef_ref, warmth_ref = refs[4:]
        sources = [(late_ref, sum(lengths[:k])) for k in range(gx - 1)]
        lay_segments(x, gx, seg, chunk, cells_ref, RAW * plane, sources, coef_ref, warmth_ref)
        coef, warmth = coef_ref[...], warmth_ref[...]
    else:
        right_ref, left_ref, segments_ref, out_ref = refs[4:]
        sources = [(right_ref, 0), (left_ref, 0)]
        n = segments_ref.shape[0] // 2
        coef, warmth = segments_ref[:n, :], segments_ref[n:, :]
    n = coef.shape[0]
    added = exact_dot(where_ref[...], coupling(coef, warmth))
    near = edge_columns(n, False)
    beside = []
    for side in range(2):
        masked = take(coef, near) * masks_ref[side * n : (side + 1) * n, :]
        beside.append(exact_dot(rows_ref[...], coupling(masked, take(warmth, near))))
    planes = layers + 2
    for i in range(layers):
        src = flip(z, layers, i)
        raw = [cells_ref[pl.ds(pl.multiple_of((f * layers + src) * rows, rows), rows), :] for f in range(RAW)]
        for f, value in enumerate(combine(raw, added[i * rows : (i + 1) * rows])):
            out_ref[f * planes + i] = value
    strips = Strips(
        [ref for ref, _ in sources[:2]], [at for _, at in sources[:2]], cells_ref, RAW * plane + 2 * seg, rows, layers
    )
    half = lane_of(chunk) // (LANES // 2) == (1 if partner else 0)
    for part in range(4):
        here = slice(part * chunk, (part + 1) * chunk)
        raw = [strips.both(f, part * chunk, chunk, x, gx, partner) for f in range(RAW)]
        for side in range(2):
            cells = [jnp.where(half, value[side], 0.0) for value in raw]
            for f, value in enumerate(combine(cells, beside[side][here])):
                out_ref[f * planes + layers + side, here, :] = value


def lay_segments(x, gx, seg, chunk, own_ref, at, sources, coef_ref, warmth_ref):
    distances = [1, gx - 1] + list(range(2, gx - 1))
    held = [(k, ref, at + (RAW * chunk if j < 2 else 0)) for j, (k, (ref, at)) in enumerate(zip(distances, sources))]
    place_segments(x, gx, seg, coef_ref, warmth_ref, [(0, own_ref, at)] + held)


def strip_kernel(gx, gy, shape, seg, *refs):
    layers, rows = shape
    cells_ref, near_ref, line_ref, masks_ref = refs[:4]
    received, refs = refs[4 : 4 + gx - 1], refs[4 + gx - 1 :]
    sides = 1 if gy == 2 else 2
    strip_refs, partner_refs, segments_ref = refs[:sides], refs[sides : 2 * sides], refs[2 * sides]
    plane, chunk = layers * rows, rows // 4
    x, y, z = (lax.axis_index(a) for a in ("gx", "gy", "gz"))
    n = segments_ref.shape[0] // 2
    coef_ref, warmth_ref = segments_ref.at[pl.ds(0, n), :], segments_ref.at[pl.ds(n, n), :]
    lay_segments(x, gx, seg, chunk, cells_ref, RAW * plane, [(ref, 0) for ref in received], coef_ref, warmth_ref)
    coef, warmth = coef_ref[...], warmth_ref[...]
    coupled = coupling(coef, warmth)
    columns = edge_columns(n, False)
    coef, warmth = take(coef, columns), take(warmth, columns)
    outer = [coupling(coef * masks_ref[side * n : (side + 1) * n, :], warmth) for side in range(2)]
    strips = Strips(received[:2], [0, 0], cells_ref, RAW * plane + 2 * seg, rows, layers)
    low = lane_of(HALO) < LANES // 2
    first = lane_of(HALO) % GROUP < HALO
    upper = lax.broadcasted_iota(jnp.int32, (HALO, LANES), 0) < HALO // 2
    sent = FIELDS - 1

    def give(ref, at, values):
        for f, value in enumerate(values):
            ref[at + f * HALO : at + (f + 1) * HALO, :] = value

    def make(side, top):
        start = 0 if top else rows - HALO
        strip_ref, partner_ref = strip_refs[side], partner_refs[side]

        def shrink(values):
            *whole, e, g = values
            if top:
                g = pltpu.roll(g, HALO // 2, 0)
            else:
                e = pltpu.roll(e, HALO // 2, 0)
            return whole + [jnp.where(upper, e, g)]

        near = layers * HALO
        added = exact_dot(near_ref[side * near : (side + 1) * near, :], coupled)
        line = line_ref[side * 2 * HALO : (side + 1) * 2 * HALO, :]
        beside = [exact_dot(line, part)[:HALO] for part in outer]
        whole, stride, later, shared = partner_rows(layers)
        for i in range(layers):
            src = flip(z, layers, i)
            raw = [
                cells_ref[pl.ds(pl.multiple_of((f * layers + src) * rows + start, HALO), HALO), :] for f in range(RAW)
            ]
            values = combine(raw, added[i * HALO : (i + 1) * HALO])
            give(strip_ref, i * sent * HALO, shrink(values))
            pieces = [(f, m, f * stride + at) for f in range(sent - 1) for j, m, at in whole if j == i]
            pieces += [(sent - 1 + f, m, (sent - 1) * stride + at) for f, j, m, at in later if j == i]
            for f, m, at in pieces:
                skip = 0 if top else HALO - m
                partner_ref[at : at + m, :] = values[f][skip : skip + m]
        raw = [strips.both(f, start, HALO, x, gx, False) for f in range(RAW)]
        left, right = (combine([value[j] for value in raw], beside[j]) for j in range(2))
        values = shrink([jnp.where(first, a, b) for a, b in zip(left, right)])
        values = [jnp.where(low, values[j], pltpu.roll(values[j + 1], LANES // 2, 1)) for j in range(0, sent, 2)]
        give(strip_ref, layers * sent * HALO, values)
        give(partner_ref, (sent - 1) * stride + shared, values)

    for side, (top, _) in enumerate(sides_of(gy, y)):
        if top is True or top is False:
            make(side, top)
        else:
            pl.when(top)(functools.partial(make, side, True))
            pl.when(jnp.logical_not(top))(functools.partial(make, side, False))


def planes_of(count, total):
    return list(range(count)) + [total - 2, total - 1]


def lateral(buf, at, n, which):
    sums = []
    for i in which:
        centre = buf[i, pl.ds(at, n), :]
        beside = pltpu.roll(centre, 1, 1) + pltpu.roll(centre, LANES - 1, 1)
        sums.append(beside + (buf[i, pl.ds(at - 1, n), :] + buf[i, pl.ds(at + 1, n), :]))
    return sums


def vertical(planes, edges, count):
    sums = []
    for i in range(count):
        near = [planes[j] for j in (i - 1, i + 1) if 0 <= j < len(planes)]
        sums.append(functools.reduce(jnp.add, near))
    for edge in edges:
        lane = lane_of(edge.shape[0])
        up = jnp.where(lane >= GROUP, pltpu.roll(edge, GROUP, 1), 0.0)
        down = jnp.where(lane < LANES - GROUP, pltpu.roll(edge, LANES - GROUP, 1), 0.0)
        sums.append(up + down)
    return sums


def coefficients(s_ref, at, n, raw, dests, to, outside):
    a_ref, q_ref, r_ref, e_ref, g_ref, root_ref = dests
    total = s_ref.shape[0]
    sums = lateral(s_ref, at, n, range(total))
    t = [raw(1, i) for i in range(total)]
    above = vertical(t[:-2], t[-2:], total - 2)
    here = pl.ds(to, n)
    for i in range(total):
        s = s_ref[i, pl.ds(at, n), :]
        diag = raw(3, i) + s * sums[i] + t[i] * above[i]
        if outside or i >= total - 2:
            inverse = 1.0 / jnp.where(diag > 0.0, diag, 1.0)
            root = jnp.where(s > 0.0, 1.0 / jnp.where(s > 0.0, s, 1.0), 0.0)
        else:
            inverse, root = 1.0 / diag, 1.0 / s
        if i < root_ref.shape[0]:
            root_ref[i, here, :] = root
        scaled = s * inverse
        a_ref[i, here, :] = s * scaled
        r_ref[i, here, :] = raw(4, i) * scaled
        e_ref[i, here, :] = raw(5, i) * scaled
        g_ref[i, here, :] = raw(6, i) * inverse
        q_ref[i, here, :] = t[i] * root


def shifted_sums(distance):
    to = lax.broadcasted_iota(jnp.int32, (2 * LANES, LANES), 1)
    of = lax.broadcasted_iota(jnp.int32, (2 * LANES, LANES), 0) % LANES
    return as_onehot(jnp.abs(of - to) == distance)


def sweep_edges(src_ref, dst_ref, at, n, coefs, base, matrices):
    a_ref, q_ref, r_ref = coefs[:3]
    total = src_ref.shape[0]
    here, there = pl.ds(base, n), pl.ds(at, n)

    def product(value, matrix):
        return jnp.dot(jnp.concatenate(split(value), axis=1), matrix, preferred_element_type=jnp.float32)

    for i in (total - 2, total - 1):
        centre = src_ref[i, there, :]
        beside = product(centre, matrices[0])
        above = product(q_ref[i, here, :] * centre, matrices[1])
        beside = beside + (src_ref[i, pl.ds(at - 1, n), :] + src_ref[i, pl.ds(at + 1, n), :])
        dst_ref[i, there, :] = r_ref[i, here, :] + a_ref[i, here, :] * (beside + q_ref[i, here, :] * above)


def sweep(src_ref, dst_ref, at, n, count, coefs, base, edges=True):
    a_ref, q_ref, r_ref = coefs[:3]
    total = src_ref.shape[0]
    here, there = pl.ds(base, n), pl.ds(at, n)
    which = planes_of(count, total) if edges else list(range(count))
    sums = lateral(src_ref, at, n, which)
    scaled = [q_ref[i, here, :] * src_ref[i, there, :] for i in range(min(count + 1, total - 2))]
    outer = [q_ref[i, here, :] * src_ref[i, there, :] for i in which[count:]]
    above = vertical(scaled, outer, count)
    for j, i in enumerate(which):
        dst_ref[i, there, :] = r_ref[i, here, :] + a_ref[i, here, :] * (sums[j] + q_ref[i, here, :] * above[j])


def next_rhs(coefs, v_ref, at, n, base):
    r_ref, e_ref, g_ref = coefs[2:5]
    here = pl.ds(base, n)
    for i in range(v_ref.shape[0]):
        r_ref[i, here, :] = e_ref[i, here, :] + g_ref[i, here, :] * v_ref[i, pl.ds(at, n), :]


def meet(v_ref, at, n, count, back):
    total = v_ref.shape[0]
    here = pl.ds(at, n)
    lane = lane_of(n)
    j, group = lane % GROUP, lane // GROUP
    outer = jnp.logical_or(lane < ITERS, lane >= LANES - ITERS)
    left, right = v_ref[total - 2, here, :], v_ref[total - 1, here, :]
    middle = jnp.where(j < HALO, right, left)
    for i in range(count):
        value = v_ref[i, here, :]
        if back:
            moved = pltpu.roll(value, (i * GROUP + HALO) % LANES, 1)
            left = jnp.where(jnp.logical_and(group == i, j >= GROUP - ITERS), moved, left)
            right = jnp.where(jnp.logical_and(group == i, j < ITERS), moved, right)
        v_ref[i, here, :] = jnp.where(outer, pltpu.roll(middle, LANES - (i * GROUP + HALO), 1), value)
    if back:
        v_ref[total - 2, here, :] = left
        v_ref[total - 1, here, :] = right


def needed(layers, n):
    return min(2 * layers, layers + STEPS * ITERS - 1 - n)


def two_steps(layers, sweep_all, between, after):
    for step in range(STEPS):
        whole = [n for n in range(step * ITERS, (step + 1) * ITERS) if needed(layers, n) == 2 * layers]
        pairs = len(whole) // 2

        def pair(k, carry):
            n = step * ITERS + 2 * k
            sweep_all(n, 0, 2 * layers)
            sweep_all(n + 1, 1, 2 * layers)
            return carry

        if pairs:
            lax.fori_loop(0, pairs, pair, 0)
        for n in range(step * ITERS + 2 * pairs, (step + 1) * ITERS):
            sweep_all(n, n % 2, needed(layers, n))
        after(step)
        if step < STEPS - 1:
            between()


PAD = 8


def tile_kernel(gx, gy, shape, *refs):
    layers, rows = shape
    own_ref, partner_ref, picks_ref, out_ref, below_ref, level_ref = refs[:6]
    s_ref, va_ref, vb_ref = refs[6:9]
    coefs = refs[9:]
    x, y, z = (lax.axis_index(a) for a in ("gx", "gy", "gz"))
    total = 2 * layers + 2
    zeros = jnp.zeros((PAD, LANES), jnp.float32)
    for ref in (s_ref, va_ref, vb_ref):
        for i in range(total):
            ref[i, 0:PAD, :] = zeros
            ref[i, PAD + rows : PAD + rows + PAD, :] = zeros

    def field(f, i, here):
        j = f * (layers + 2)
        if i >= 2 * layers:
            j = j + i - layers
            return own_ref[j, here, :] + partner_ref[j, here, :]
        return own_ref[j + i, here, :] if i < layers else partner_ref[j + i - layers, here, :]

    for i in range(total):
        s_ref[i, PAD : PAD + rows, :] = field(0, i, slice(None))
        va_ref[i, PAD : PAD + rows, :] = field(2, i, slice(None))
    n = 8
    for at in range(0, rows, n):
        coefficients(s_ref, PAD + at, n, lambda f, i: field(f, i, slice(at, at + n)), coefs, at, False)

    bufs = (va_ref, vb_ref)
    sides = sides_of(gy, y)
    matrices = shifted_sums(1), shifted_sums(GROUP)

    def sweep_all(number, which, count):
        src_ref, dst_ref = bufs[which], bufs[1 - which]
        for side, (above, _) in enumerate(sides):
            inner = pl.ds(PAD + inner_at(above, rows), HALO)
            for i in range(total):
                level_ref[(side * STEPS * ITERS + number) * total + i] = src_ref[i, inner, :]
        sweep_edges(src_ref, dst_ref, PAD, rows, coefs, 0, matrices)
        for at in range(0, rows, n):
            sweep(src_ref, dst_ref, PAD + at, n, count, coefs, at, edges=False)

    def after(step):
        last = step == STEPS - 1
        for at in range(0, rows, n):
            meet(va_ref, PAD + at, n, layers if last else 2 * layers, not last)
        heat = []
        for i in range(layers):
            here = pl.ds(PAD, rows)
            heat.append(va_ref[i, here, :] * coefs[5][i])
            if step == STEPS - 1:
                out_ref[flip(z, layers, i)] = heat[-1]
        below_ref[step] = exact_dot(picks_ref[...], jnp.concatenate(heat, axis=0))

    def between():
        for at in range(0, rows, n):
            next_rhs(coefs, va_ref, PAD + at, n, at)

    two_steps(layers, sweep_all, between, after)


def edge_kernel(gx, gy, shape, seg, *refs):
    layers, rows = shape
    own_ref, partner_ref, picks_ref, mine_ref, segments_ref, below_ref, level_ref = refs[:7]
    sides_n = 1 if gy == 2 else 2
    along, across = refs[7 : 7 + sides_n], refs[7 + sides_n : 7 + 2 * sides_n]
    refs = refs[7 + 2 * sides_n :]
    heat_ref, returns = refs[0], refs[1 : 1 + gx]
    ret_ref, s_ref, va_ref, vb_ref = refs[1 + gx : 5 + gx]
    coefs = refs[5 + gx :]
    x, y, z = (lax.axis_index(a) for a in ("gx", "gy", "gz"))
    total = 2 * layers + 2
    count = mine_ref.shape[0]
    below = [below_ref[step] for step in range(STEPS)]
    lane = lane_of(HALO)
    low, first = lane < LANES // 2, lane % GROUP < HALO
    columns = edge_columns(HALO, False)
    bufs = (va_ref, vb_ref)

    def tile(j):
        return pl.ds(j if isinstance(j, int) else pl.multiple_of(j, HALO), HALO)

    for side, (above, live) in enumerate(sides_of(gy, y)):
        def place(when_top, otherwise):
            if above is True or above is False:
                return when_top * HALO if above else otherwise * HALO
            return jnp.where(above, when_top * HALO, otherwise * HALO)

        outer, strip, edge, inner = place(0, 3), place(1, 2), place(2, 1), place(3, 0)
        edge_rows = tile(edge_at(above, rows))
        inner_rows = tile(inner_at(above, rows))

        def field(f, i, here):
            j = f * (layers + 2)
            if i >= 2 * layers:
                j = j + i - layers
                return own_ref[j, here, :] + partner_ref[j, here, :]
            return own_ref[j + i, here, :] if i < layers else partner_ref[j + i - layers, here, :]

        t_ref, d_ref, q_ref, e_ref, g_ref = coefs[1], coefs[0], coefs[2], coefs[3], coefs[4]
        keep = {0: s_ref, 1: t_ref, 2: va_ref, 3: d_ref, 4: q_ref, 5: e_ref, 6: g_ref}
        zeros = jnp.zeros((HALO, LANES), jnp.float32)
        src = lane % (LANES // 2)
        turned = (layers - 1 - src // GROUP) * GROUP + src % GROUP
        half_tile = lax.broadcasted_iota(jnp.int32, (HALO, LANES), 0) < HALO // 2

        def unpack(value, f):
            if f < FIELDS - 2:
                return value
            turned_value = pltpu.roll(value, HALO // 2, 0)
            if f == FIELDS - 2:
                at_top, at_bottom = jnp.where(half_tile, 0.0, turned_value), jnp.where(half_tile, value, 0.0)
            else:
                at_top, at_bottom = jnp.where(half_tile, 0.0, value), jnp.where(half_tile, turned_value, 0.0)
            return jnp.where(above, at_top, at_bottom)

        whole, stride, later, shared = partner_rows(layers)
        sublane = lax.broadcasted_iota(jnp.int32, (HALO, LANES), 0)

        def nearest(ref, m, at):
            at_top = jnp.where(sublane >= HALO - m, ref[at - HALO + m : at + m, :], 0.0)
            return jnp.where(above, at_top, jnp.where(sublane < m, ref[at : at + HALO, :], 0.0))

        for f in range(FIELDS):
            g = min(f, FIELDS - 2)
            if f < FIELDS - 2:
                rows_of = {i: (m, f * stride + at) for i, m, at in whole}
            else:
                rows_of = {i: (m, (FIELDS - 2) * stride + at) for which, i, m, at in later if which == f - FIELDS + 2}
            values, inside = [], zeros
            for i in range(2 * layers):
                if i < layers:
                    at = (i * (FIELDS - 1) + g) * HALO
                    value = unpack(along[side][at : at + HALO, :], f)
                else:
                    j = 2 * layers - 1 - i
                    value = nearest(across[side], *rows_of[j]) if j in rows_of else zeros
                values.append(value)
                inside = jnp.where(lane // GROUP == i, take(value, columns), inside)
            half = (LANES // 2) * (g % 2)
            at = (layers * (FIELDS - 1) + g // 2) * HALO
            a = take(along[side][at : at + HALO, :], src + half)
            at = (FIELDS - 2) * stride + shared + (g // 2) * HALO
            b = take(across[side][at : at + HALO, :], turned + half)
            outside = unpack(jnp.where(low, a, b), f)
            values += [jnp.where(first, outside, inside), jnp.where(first, inside, outside)]
            for i, value in enumerate(values):
                ref, shift = keep[f], 0 if f in (0, 2) else HALO
                ref[i, tile(strip - shift), :] = value
                ref[i, tile(edge - shift), :] = field(f, i, edge_rows)
        for i in range(total):
            s_ref[i, tile(outer), :] = zeros
            va_ref[i, tile(outer), :] = zeros
            vb_ref[i, tile(outer), :] = zeros
            s_ref[i, tile(inner), :] = field(0, i, inner_rows)
        n = 2 * HALO
        held = [[keep[f][i, pl.ds(0, n), :] for i in range(total)] if f in (1, 3, 4, 5, 6) else None for f in range(FIELDS)]
        coefficients(s_ref, HALO, n, lambda f, i: held[f][i], coefs, 0, True)

        def sweep_all(number, which, needed_layers):
            src_ref, dst_ref = bufs[which], bufs[1 - which]
            for i in range(total):
                src_ref[i, tile(inner), :] = level_ref[(side * STEPS * ITERS + number) * total + i]
            sweep(src_ref, dst_ref, HALO, n, needed_layers, coefs, 0)

        picks = picks_ref[side * count : (side + 1) * count, :]

        def after(step):
            last = step == STEPS - 1
            meet(va_ref, HALO, n, layers if last else 2 * layers, not last)
            heat = []
            for i in range(layers):
                heat.append(va_ref[i, tile(edge), :] * coefs[5][i, tile(edge - HALO), :])
                if step == STEPS - 1:
                    heat_ref[side * layers + flip(z, layers, i)] = heat[-1]
            heat.append(jnp.zeros((LANES - layers * HALO, LANES), jnp.float32))
            below[step] = below[step] + exact_dot(picks, jnp.concatenate(heat, axis=0))

        two_steps(layers, sweep_all, lambda: next_rhs(coefs, va_ref, HALO, n, 0), after)

    coef, warmth = segments_ref[:count, :], segments_ref[count:, :]
    for step in range(STEPS):
        warmth = warmth + coolant_gain * coef * (below[step] - warmth)
    ret_ref[...] = jnp.where(mine_ref[...] > 0.0, warmth, 0.0)
    for k, ref in enumerate(returns):
        ref[...] = ret_ref[pl.ds(pl.multiple_of(lax.rem(x + k, gx) * seg, seg), seg), :]


def merge_kernel(gy, whole_ref, heat_ref, out_ref):
    layers, rows, _ = whole_ref.shape
    out_ref[...] = whole_ref[...]
    for side, (above, live) in enumerate(sides_of(gy, lax.axis_index("gy"))):
        def put(side=side, above=above):
            out_ref[:, pl.ds(edge_at(above, rows), HALO), :] = heat_ref[side * layers : (side + 1) * layers]

        if live is True:
            put()
        else:
            pl.when(live)(put)


def local(gx, gy, gz, u, power, storage, conductance, warmth, coef, holder, stratum, transverse):
    layers, rows, columns = u.shape
    seg = warmth.shape[1]
    segments = stratum.shape[1]
    if gz != 2 or gx < 3 or columns != LANES or 2 * layers * GROUP != LANES or rows % 32:
        raise ValueError("unsupported shape")
    holder = holder[:, :, 0]
    shape = (layers, rows)
    f32 = jnp.float32
    chunk = rows // 4
    wide = RAW * chunk + 2 * seg

    def struct(*dims):
        return jax.ShapeDtypeStruct(dims, f32)

    def vmem(*dims):
        return pltpu.VMEM(dims, f32)

    indices = (holder, stratum, transverse)
    flat = [a.reshape(-1, LANES) for a in (u, power, storage, conductance, warmth, coef)]
    own, to_left, to_right, only, *indices = pl.pallas_call(
        functools.partial(pack_kernel, shape),
        out_shape=(
            struct(RAW * layers * rows + 2 * seg + 2 * RAW * chunk, LANES),
            struct(wide, LANES),
            struct(wide, LANES),
            struct(2 * seg, LANES),
            *(jax.ShapeDtypeStruct(a.shape, a.dtype) for a in indices),
        ),
        in_specs=[pl.BlockSpec(memory_space=pltpu.HBM)] * 9,
        out_specs=(VMEM,) * 7,
        scratch_shapes=[pltpu.SemaphoreType.DMA((9,))],
        compiler_params=PARAMS,
        name="pack",
    )(*(pltpu.with_memory_space_constraint(a, pltpu.HBM) for a in (*flat, *indices)))

    swap = [(0, 1), (1, 0)]
    partner = lax.ppermute(own, "gz", swap)
    def from_distance(value, k):
        return lax.ppermute(value, "gx", [(i, (i - k) % gx) for i in range(gx)])

    received = [from_distance(to_left, 1), from_distance(to_right, gx - 1)]
    received += [from_distance(only, k) for k in range(2, gx - 1)]

    sides = 1 if gy == 2 else 2
    fields = struct(FIELDS * (layers + 2), rows, LANES)
    strip_rows = (FIELDS - 1) * layers * HALO + (FIELDS - 1) // 2 * HALO
    _, stride, _, shared = partner_rows(layers)
    partner_strip = (FIELDS - 2) * stride + shared + (FIELDS - 1) // 2 * HALO
    sides = 1 if gy == 2 else 2
    bf16 = jnp.bfloat16
    one_group = (
        jax.ShapeDtypeStruct((layers * rows, segments), bf16),
        jax.ShapeDtypeStruct((rows, segments), bf16),
        struct(2 * segments, LANES),
    )
    maps = pl.pallas_call(
        functools.partial(maps_kernel, gx, gy, shape),
        out_shape=one_group
        + one_group
        + (
            jax.ShapeDtypeStruct((segments, layers * rows), bf16),
            jax.ShapeDtypeStruct((sides * segments, LANES), bf16),
            struct(segments, LANES),
            jax.ShapeDtypeStruct((sides * layers * HALO, segments), bf16),
            jax.ShapeDtypeStruct((sides * 2 * HALO, segments), bf16),
        ),
        in_specs=[VMEM] * 3,
        out_specs=(VMEM,) * 11,
        compiler_params=PARAMS,
        cost_estimate=cost(1),
        name="maps",
    )(*indices)
    own_maps, partner_maps, (picks, picks_beside, mine, near, line) = maps[:3], maps[3:6], maps[6:]
    joined = pl.pallas_call(
        join_kernel,
        out_shape=struct(sum(a.shape[0] for a in received), LANES),
        in_specs=[pl.BlockSpec(memory_space=pl.ANY)] + [VMEM] * (gx - 1),
        out_specs=VMEM,
        compiler_params=PARAMS,
        name="join",
    )(mine, *received)
    late = lax.ppermute(joined, "gz", swap)
    made = pl.pallas_call(
        functools.partial(strip_kernel, gx, gy, shape, seg),
        out_shape=(struct(strip_rows, LANES),) * sides
        + (struct(partner_strip, LANES),) * sides
        + (struct(2 * segments, LANES),),
        in_specs=[VMEM] * (4 + gx - 1),
        out_specs=(VMEM,) * (1 + 2 * sides),
        compiler_params=PARAMS,
        cost_estimate=cost(0.5),
        name="strips",
    )(own, near, line, own_maps[2], *received)
    strips, partner_strips, held = made[:sides], made[sides : 2 * sides], made[2 * sides]
    own_fields = pl.pallas_call(
        functools.partial(fill_kernel, False, gx, gy, shape, seg),
        out_shape=fields,
        in_specs=[VMEM] * 7,
        out_specs=VMEM,
        compiler_params=PARAMS,
        cost_estimate=cost(1.5),
        name="fill_own",
    )(own, *own_maps, *received[:2], held)
    if gy == 2:
        routes = [(0, swap)]
    else:
        up = [(i, i + 1) for i in range(gy - 1)]
        routes = [(1, up), (0, [(j, i) for i, j in up])]
    along = [lax.ppermute(strips[side], "gy", pairs) for side, pairs in routes]
    across = []
    for side, pairs in routes:
        both = [(2 * i + z, 2 * j + 1 - z) for i, j in pairs for z in range(2)]
        across.append(lax.ppermute(partner_strips[side], ("gy", "gz"), both))

    partner_fields = pl.pallas_call(
        functools.partial(fill_kernel, True, gx, gy, shape, seg),
        out_shape=fields,
        in_specs=[VMEM] * 5,
        out_specs=VMEM,
        scratch_shapes=[vmem(segments, LANES)] * 2,
        compiler_params=PARAMS,
        cost_estimate=cost(1.5),
        name="fill_partner",
    )(partner, *partner_maps, late)

    total = 2 * layers + 2
    padded = vmem(total, rows + 2 * PAD, LANES)
    inside, below, levels = pl.pallas_call(
        functools.partial(tile_kernel, gx, gy, shape),
        out_shape=(
            struct(layers, rows, LANES),
            struct(STEPS, segments, LANES),
            struct(sides * STEPS * ITERS * total, HALO, LANES),
        ),
        in_specs=[VMEM] * 3,
        out_specs=(VMEM,) * 3,
        scratch_shapes=[padded] * 3 + [vmem(total, rows, LANES)] * 5 + [vmem(layers, rows, LANES)],
        compiler_params=PARAMS,
        cost_estimate=cost(7),
        name="tile_sweeps",
    )(own_fields, partner_fields, picks)

    results = pl.pallas_call(
        functools.partial(edge_kernel, gx, gy, shape, seg),
        out_shape=(struct(sides * layers, HALO, LANES),) + (struct(seg, LANES),) * gx,
        in_specs=[VMEM] * (7 + 2 * sides),
        out_specs=(VMEM,) * (1 + gx),
        scratch_shapes=[vmem(segments, LANES)]
        + [vmem(total, 4 * HALO, LANES)] * 3
        + [vmem(total, 2 * HALO, LANES)] * 5
        + [vmem(layers, 2 * HALO, LANES)],
        compiler_params=PARAMS,
        cost_estimate=cost(1.5),
        name="edge_sweeps",
    )(own_fields, partner_fields, picks_beside, mine, held, below, levels, *along, *across)
    heat, coolant = results[0], results[1]
    returned = [lax.ppermute(results[1 + k], "gx", [(i, (i + k) % gx) for i in range(gx)]) for k in range(1, gx)]
    temperature = pl.pallas_call(
        functools.partial(merge_kernel, gy),
        out_shape=struct(layers, rows, LANES),
        in_specs=[VMEM] * 2,
        out_specs=VMEM,
        compiler_params=PARAMS,
        cost_estimate=cost(1),
        name="merge",
    )(inside, heat)
    for value in returned:
        coolant = coolant + value
    return temperature, coolant[None]


def solution(mesh):
    gx, gy, gz = (mesh.shape[a] for a in ("gx", "gy", "gz"))
    cells = P(("stack", "gz"), "gy", "gx")
    segments = P(("stack", "gy", "gz"), "gx", None)
    return jax.shard_map(
        functools.partial(local, gx, gy, gz),
        mesh=mesh,
        in_specs=(cells, cells, cells, P(None, ("stack", "gz"), "gy", "gx"), segments, segments, P(), P(), P()),
        out_specs=(cells, segments),
        check_vma=False,
    )
```

```python
import functools

import jax
import jax.numpy as jnp
from jax import lax
from jax.experimental import pallas as pl
from jax.experimental.pallas import tpu as pltpu
from jax.sharding import PartitionSpec as P

STEPS = 2
ITERS = 4
HALO = STEPS * ITERS
GROUP = 2 * HALO
LANES = 128
RAW = 5
FIELDS = 7
coolant_gain = 0.5

VMEM = pl.BlockSpec(memory_space=pltpu.VMEM)
PARAMS = pltpu.CompilerParams(vmem_limit_bytes=40 * 1024 * 1024)


def cost(microseconds):
    return pl.CostEstimate(flops=0, bytes_accessed=int(microseconds * 3e6), transcendentals=0)


def lane_of(rows):
    return lax.broadcasted_iota(jnp.int32, (rows, LANES), 1)


def take(value, index):
    return jnp.take_along_axis(value, index, axis=1, mode="promise_in_bounds")


def edge_columns(rows, turned):
    j = lane_of(rows) % GROUP
    first = j < HALO
    return jnp.where(first, LANES - HALO + j, j - HALO) if not turned else jnp.where(first, j, LANES - GROUP + j)


def split(value):
    high = value.astype(jnp.bfloat16)
    low = (value - high.astype(jnp.float32)).astype(jnp.bfloat16)
    return high, low


def exact_dot(onehot, value):
    high, low = split(value)
    both = jnp.concatenate([high, low], axis=0)
    return jnp.dot(jnp.concatenate([onehot, onehot], axis=1), both, preferred_element_type=jnp.float32)


def coupling(coef, warmth):
    flow = coef * warmth
    second = coolant_gain * coef * coef
    return jnp.concatenate([coef, flow, second, flow - second * warmth], axis=1)


def flip(z, layers, i):
    return jnp.where(z == 0, i, layers - 1 - i)


def pack_kernel(shape, u_ref, p_ref, c_ref, k_ref, f_ref, x_ref, *refs):
    own_ref, left_ref, right_ref, seg_ref = refs[3:7]
    sems = refs[-1]
    layers, rows = shape
    seg = f_ref.shape[0]
    z = lax.axis_index("gz")
    plane = layers * rows
    copies = []

    def fetch(src, dst):
        copies.append(pltpu.make_async_copy(src, dst, sems.at[len(copies)]))
        copies[-1].start()

    fetch(k_ref, own_ref.at[pl.ds(0, 2 * plane), :])
    for field, ref in enumerate((u_ref, p_ref, c_ref), 2):
        fetch(ref, own_ref.at[pl.ds(field * plane, plane), :])
    for j, ref in enumerate((x_ref, f_ref)):
        fetch(ref, own_ref.at[pl.ds(RAW * plane + j * seg, seg), :])
    for table, place in zip(refs[:3], refs[7:10]):
        fetch(table, place)
    chunk = rows // 4
    lane = lane_of(chunk)
    first = lane % GROUP < HALO
    columns = edge_columns(chunk, False), edge_columns(chunk, True)
    edges = RAW * plane + 2 * seg

    def gather(field, at, g):
        value = None
        for i in range(layers):
            start = pl.multiple_of((field * layers + flip(z, layers, i)) * rows + at, chunk)
            taken = take(own_ref[pl.ds(start, chunk), :], columns[g % 2])
            value = taken if value is None else jnp.where(lane // GROUP == (g // 2) * layers + i, taken, value)
        return value

    def place(g, part):
        return pl.ds(edges + ((g % 2) * RAW + part) * chunk, chunk)

    copies[0].wait()
    roots = pl.ds(0, 2 * plane)
    own_ref[roots, :] = jnp.sqrt(own_ref[roots, :])
    for field in range(4):
        if field >= 2:
            copies[field - 1].wait()
        for part in range(4):
            value = gather(field, part * chunk, field)
            if field >= 2:
                value = jnp.where(lane < LANES // 2, own_ref[place(field, part), :], value)
            own_ref[place(field, part), :] = value
    copies[3].wait()
    for g in range(4):
        value = gather(4, g * chunk, g)
        if g >= 2:
            value = jnp.where(lane < LANES // 2, own_ref[place(g, 4), :], value)
        own_ref[place(g, 4), :] = value
    for part in range(RAW):
        even, odd = own_ref[place(0, part), :], own_ref[place(1, part), :]
        left_ref[part * chunk : (part + 1) * chunk, :] = jnp.where(first, odd, even)
        right_ref[part * chunk : (part + 1) * chunk, :] = jnp.where(first, even, odd)
    for copy in copies[4:]:
        copy.wait()
    segments = own_ref[RAW * plane : RAW * plane + 2 * seg, :]
    seg_ref[...] = segments
    left_ref[RAW * chunk :, :] = segments
    right_ref[RAW * chunk :, :] = segments


class Strips:
    def __init__(self, refs, starts, cells_ref, start, rows, layers):
        self.refs, self.starts = refs, starts
        self.cells_ref, self.start = cells_ref, start
        self.rows, self.layers = rows, layers

    def both(self, field, start, n, x, gx, partner):
        chunk = self.rows // 4
        if field < 4:
            g, at = field, start
        else:
            g, at = start // chunk, 4 * chunk + start % chunk
        a, b = (ref[at + begin : at + begin + n, :] for ref, begin in zip(self.refs, self.starts))
        at = self.start + (g % 2) * RAW * chunk + at
        inside = self.cells_ref[at : at + n, :]
        from_left, from_right = jnp.where(x > 0, b, 0.0), jnp.where(x < gx - 1, a, 0.0)
        lane = lane_of(n)
        first = (lane % GROUP < HALO) if g % 2 == 0 else (lane % GROUP >= HALO)
        half = self.layers * GROUP
        src = lane % half
        if partner:
            src = (self.layers - 1 - src // GROUP) * GROUP + src % GROUP
        if g % 2 == 1:
            src = jnp.where(src % GROUP < HALO, src + HALO, src - HALO)
        src = src + half * (g // 2)
        return take(jnp.where(first, from_left, inside), src), take(jnp.where(first, inside, from_right), src)


def place_segments(x, gx, seg, coef_ref, warmth_ref, sources):
    for k, ref, at in sources:
        place = pl.ds(pl.multiple_of(lax.rem(x + k, gx) * seg, seg), seg)
        coef_ref[place, :] = ref[at : at + seg, :]
        warmth_ref[place, :] = ref[at + seg : at + 2 * seg, :]


def tables(z, group, layers, holder_ref, stratum_ref, transverse_ref):
    holder = holder_ref[pl.ds(group, 1), :]
    layer = stratum_ref[pl.ds(group, 1), :]
    layer = jnp.where(z == 0, layer, layers - 1 - layer)
    row = transverse_ref[pl.ds(group, 1), :]
    n = holder.shape[1]
    which = lax.broadcasted_iota(jnp.int32, (8, n), 0)
    stacked = jnp.where(which == 0, holder, jnp.where(which == 1, layer, row))
    eye = lax.broadcasted_iota(jnp.int32, (n, n), 0) == lax.broadcasted_iota(jnp.int32, (n, n), 1)
    columns = lax.dot_general(
        eye.astype(jnp.float32).astype(jnp.bfloat16),
        stacked.astype(jnp.float32).astype(jnp.bfloat16),
        (((1,), (1,)), ((), ())),
        preferred_element_type=jnp.float32,
    )
    return (holder, layer, row), columns


def as_onehot(mask):
    return jnp.where(mask, 1.0, 0.0).astype(jnp.bfloat16)


def combine(raw, added):
    s, t, u, power, storage = raw
    wall, flow, second, later = (added[:, i * LANES : (i + 1) * LANES] for i in range(4))
    return s, t, s * u, storage + wall, power + storage * u + flow, power + later, storage + second


def lengths_of(gx, chunk, seg):
    return [RAW * chunk + 2 * seg] * 2 + [2 * seg] * (gx - 3)


def edge_at(top, rows):
    return 0 if top is True else rows - HALO if top is False else pl.multiple_of(jnp.where(top, 0, rows - HALO), HALO)


def inner_at(top, rows):
    return HALO if top is True else rows - 2 * HALO if top is False else pl.multiple_of(jnp.where(top, HALO, rows - 2 * HALO), HALO)


def sides_of(gy, y):
    return [(y == 1, True)] if gy == 2 else [(True, y > 0), (False, y < gy - 1)]


def maps_kernel(gx, gy, shape, holder_ref, stratum_ref, transverse_ref, *refs):
    layers, rows = shape
    plane = layers * rows
    picks_ref, beside_ref, mine_ref, near_ref, line_ref = refs[6:]
    x, y, z = (lax.axis_index(a) for a in ("gx", "gy", "gz"))
    n = holder_ref.shape[1]
    for partner in range(2):
        cells_ref, rows_ref, masks_ref = refs[3 * partner : 3 * partner + 3]
        group = y * 2 + ((1 - z) if partner else z)
        (holder, layer, row), columns = tables(z, group, layers, holder_ref, stratum_ref, transverse_ref)
        cell = jnp.where(holder == x, layer * rows + row, -1)
        cells_ref[...] = as_onehot(lax.broadcasted_iota(jnp.int32, (plane, n), 0) == cell)
        rows_ref[...] = as_onehot(lax.broadcasted_iota(jnp.int32, (rows, n), 0) == row)
        if not partner:
            near, m = layers * HALO, 2 * HALO
            for side, (above, _) in enumerate(sides_of(gy, y)):
                start = edge_at(above, rows)
                at_edge = row // HALO == start // HALO
                cell = jnp.where(jnp.logical_and(holder == x, at_edge), layer * HALO + row - start, -1)
                near_ref[side * near : (side + 1) * near, :] = as_onehot(
                    lax.broadcasted_iota(jnp.int32, (near, n), 0) == cell
                )
                cell = jnp.where(at_edge, row - start, -1)
                line_ref[side * m : (side + 1) * m, :] = as_onehot(lax.broadcasted_iota(jnp.int32, (m, n), 0) == cell)
        holder, layer, row = (columns[:, j : j + 1].astype(jnp.int32) for j in range(3))
        lane = lane_of(n)
        first = lane % GROUP < HALO
        here = lane // GROUP == layer + partner * layers
        for side, begin in enumerate((x - 1, x)):
            mine = jnp.logical_and(here, holder == jnp.where(first, begin, begin + 1))
            masks_ref[side * n : (side + 1) * n, :] = jnp.where(mine, 1.0, 0.0)
        if partner:
            continue
        mine = holder == x
        mine_ref[...] = jnp.where(jnp.logical_and(mine, lane >= 0), 1.0, 0.0)
        spoilt = None
        for side, (above, live) in enumerate(sides_of(gy, y)):
            start = edge_at(above, rows)
            part = jnp.logical_and(row // HALO == start // HALO, live)
            spoilt = part if spoilt is None else jnp.logical_or(spoilt, part)
            cell = jnp.where(jnp.logical_and(mine, part), layer * HALO + row - start, -1)
            beside_ref[side * n : (side + 1) * n, :] = as_onehot(lane == cell)
        cell = jnp.where(jnp.logical_and(mine, jnp.logical_not(spoilt)), layer * rows + row, -1)
        picks_ref[...] = as_onehot(lax.broadcasted_iota(jnp.int32, (n, plane), 1) == cell)


def join_kernel(mine_ref, *refs):
    out_ref, at = refs[-1], 0
    for ref in refs[:-1]:
        n = ref.shape[0]
        out_ref[at : at + n, :] = ref[...]
        at += n


def partner_rows(layers):
    whole, at = [], 1
    for i in range(layers - 1, -1, -1):
        whole.append((i, HALO - layers + i, at))
        at += HALO - layers + i
    stride = -(-at // 8) * 8
    later, at = [], 0
    for f in range(2):
        for i in range(layers - 1, -1, -1):
            if ITERS - 1 - layers + i > 0:
                later.append((f, i, ITERS - 1 - layers + i, at))
                at += ITERS - 1 - layers + i
    return whole, stride, later, -(-at // 8) * 8


def fill_kernel(partner, gx, gy, shape, seg, *refs):
    layers, rows = shape
    cells_ref, where_ref, rows_ref, masks_ref = refs[:4]
    plane, chunk = layers * rows, rows // 4
    lengths = lengths_of(gx, chunk, seg)
    x, z = lax.axis_index("gx"), lax.axis_index("gz")
    if partner:
        late_ref, out_ref, coef_ref, warmth_ref = refs[4:]
        sources = [(late_ref, sum(lengths[:k])) for k in range(gx - 1)]
        lay_segments(x, gx, seg, chunk, cells_ref, RAW * plane, sources, coef_ref, warmth_ref)
        coef, warmth = coef_ref[...], warmth_ref[...]
    else:
        right_ref, left_ref, segments_ref, out_ref = refs[4:]
        sources = [(right_ref, 0), (left_ref, 0)]
        n = segments_ref.shape[0] // 2
        coef, warmth = segments_ref[:n, :], segments_ref[n:, :]
    n = coef.shape[0]
    added = exact_dot(where_ref[...], coupling(coef, warmth))
    near = edge_columns(n, False)
    beside = []
    for side in range(2):
        masked = take(coef, near) * masks_ref[side * n : (side + 1) * n, :]
        beside.append(exact_dot(rows_ref[...], coupling(masked, take(warmth, near))))
    planes = layers + 2
    for i in range(layers):
        src = flip(z, layers, i)
        raw = [cells_ref[pl.ds(pl.multiple_of((f * layers + src) * rows, rows), rows), :] for f in range(RAW)]
        for f, value in enumerate(combine(raw, added[i * rows : (i + 1) * rows])):
            out_ref[f * planes + i] = value
    strips = Strips(
        [ref for ref, _ in sources[:2]], [at for _, at in sources[:2]], cells_ref, RAW * plane + 2 * seg, rows, layers
    )
    half = lane_of(chunk) // (LANES // 2) == (1 if partner else 0)
    for part in range(4):
        here = slice(part * chunk, (part + 1) * chunk)
        raw = [strips.both(f, part * chunk, chunk, x, gx, partner) for f in range(RAW)]
        for side in range(2):
            cells = [jnp.where(half, value[side], 0.0) for value in raw]
            for f, value in enumerate(combine(cells, beside[side][here])):
                out_ref[f * planes + layers + side, here, :] = value


def lay_segments(x, gx, seg, chunk, own_ref, at, sources, coef_ref, warmth_ref):
    distances = [1, gx - 1] + list(range(2, gx - 1))
    held = [(k, ref, at + (RAW * chunk if j < 2 else 0)) for j, (k, (ref, at)) in enumerate(zip(distances, sources))]
    place_segments(x, gx, seg, coef_ref, warmth_ref, [(0, own_ref, at)] + held)


def strip_kernel(gx, gy, shape, seg, *refs):
    layers, rows = shape
    cells_ref, near_ref, line_ref, masks_ref = refs[:4]
    received, refs = refs[4 : 4 + gx - 1], refs[4 + gx - 1 :]
    sides = 1 if gy == 2 else 2
    strip_refs, partner_refs, segments_ref = refs[:sides], refs[sides : 2 * sides], refs[2 * sides]
    plane, chunk = layers * rows, rows // 4
    x, y, z = (lax.axis_index(a) for a in ("gx", "gy", "gz"))
    n = segments_ref.shape[0] // 2
    coef_ref, warmth_ref = segments_ref.at[pl.ds(0, n), :], segments_ref.at[pl.ds(n, n), :]
    lay_segments(x, gx, seg, chunk, cells_ref, RAW * plane, [(ref, 0) for ref in received], coef_ref, warmth_ref)
    coef, warmth = coef_ref[...], warmth_ref[...]
    coupled = coupling(coef, warmth)
    columns = edge_columns(n, False)
    coef, warmth = take(coef, columns), take(warmth, columns)
    outer = [coupling(coef * masks_ref[side * n : (side + 1) * n, :], warmth) for side in range(2)]
    strips = Strips(received[:2], [0, 0], cells_ref, RAW * plane + 2 * seg, rows, layers)
    low = lane_of(HALO) < LANES // 2
    first = lane_of(HALO) % GROUP < HALO
    upper = lax.broadcasted_iota(jnp.int32, (HALO, LANES), 0) < HALO // 2
    sent = FIELDS - 1

    def give(ref, at, values):
        for f, value in enumerate(values):
            ref[at + f * HALO : at + (f + 1) * HALO, :] = value

    def make(side, top):
        start = 0 if top else rows - HALO
        strip_ref, partner_ref = strip_refs[side], partner_refs[side]

        def shrink(values):
            *whole, e, g = values
            if top:
                g = pltpu.roll(g, HALO // 2, 0)
            else:
                e = pltpu.roll(e, HALO // 2, 0)
            return whole + [jnp.where(upper, e, g)]

        near = layers * HALO
        added = exact_dot(near_ref[side * near : (side + 1) * near, :], coupled)
        line = line_ref[side * 2 * HALO : (side + 1) * 2 * HALO, :]
        beside = [exact_dot(line, part)[:HALO] for part in outer]
        whole, stride, later, shared = partner_rows(layers)
        for i in range(layers):
            src = flip(z, layers, i)
            raw = [
                cells_ref[pl.ds(pl.multiple_of((f * layers + src) * rows + start, HALO), HALO), :] for f in range(RAW)
            ]
            values = combine(raw, added[i * HALO : (i + 1) * HALO])
            give(strip_ref, i * sent * HALO, shrink(values))
            pieces = [(f, m, f * stride + at) for f in range(sent - 1) for j, m, at in whole if j == i]
            pieces += [(sent - 1 + f, m, (sent - 1) * stride + at) for f, j, m, at in later if j == i]
            for f, m, at in pieces:
                skip = 0 if top else HALO - m
                partner_ref[at : at + m, :] = values[f][skip : skip + m]
        raw = [strips.both(f, start, HALO, x, gx, False) for f in range(RAW)]
        left, right = (combine([value[j] for value in raw], beside[j]) for j in range(2))
        values = shrink([jnp.where(first, a, b) for a, b in zip(left, right)])
        values = [jnp.where(low, values[j], pltpu.roll(values[j + 1], LANES // 2, 1)) for j in range(0, sent, 2)]
        give(strip_ref, layers * sent * HALO, values)
        give(partner_ref, (sent - 1) * stride + shared, values)

    for side, (top, _) in enumerate(sides_of(gy, y)):
        if top is True or top is False:
            make(side, top)
        else:
            pl.when(top)(functools.partial(make, side, True))
            pl.when(jnp.logical_not(top))(functools.partial(make, side, False))


def planes_of(count, total):
    return list(range(count)) + [total - 2, total - 1]


def lateral(buf, at, n, which):
    sums = []
    for i in which:
        centre = buf[i, pl.ds(at, n), :]
        beside = pltpu.roll(centre, 1, 1) + pltpu.roll(centre, LANES - 1, 1)
        sums.append(beside + (buf[i, pl.ds(at - 1, n), :] + buf[i, pl.ds(at + 1, n), :]))
    return sums


def vertical(planes, edges, count):
    sums = []
    for i in range(count):
        near = [planes[j] for j in (i - 1, i + 1) if 0 <= j < len(planes)]
        sums.append(functools.reduce(jnp.add, near))
    for edge in edges:
        lane = lane_of(edge.shape[0])
        up = jnp.where(lane >= GROUP, pltpu.roll(edge, GROUP, 1), 0.0)
        down = jnp.where(lane < LANES - GROUP, pltpu.roll(edge, LANES - GROUP, 1), 0.0)
        sums.append(up + down)
    return sums


def coefficients(s_ref, at, n, raw, dests, to, outside):
    a_ref, q_ref, r_ref, e_ref, g_ref, root_ref = dests
    total = s_ref.shape[0]
    sums = lateral(s_ref, at, n, range(total))
    t = [raw(1, i) for i in range(total)]
    above = vertical(t[:-2], t[-2:], total - 2)
    here = pl.ds(to, n)
    for i in range(total):
        s = s_ref[i, pl.ds(at, n), :]
        diag = raw(3, i) + s * sums[i] + t[i] * above[i]
        if outside or i >= total - 2:
            inverse = 1.0 / jnp.where(diag > 0.0, diag, 1.0)
            root = jnp.where(s > 0.0, 1.0 / jnp.where(s > 0.0, s, 1.0), 0.0)
        else:
            inverse, root = 1.0 / diag, 1.0 / s
        if i < root_ref.shape[0]:
            root_ref[i, here, :] = root
        scaled = s * inverse
        a_ref[i, here, :] = s * scaled
        r_ref[i, here, :] = raw(4, i) * scaled
        e_ref[i, here, :] = raw(5, i) * scaled
        g_ref[i, here, :] = raw(6, i) * inverse
        q_ref[i, here, :] = t[i] * root


def shifted_sums(distance):
    to = lax.broadcasted_iota(jnp.int32, (2 * LANES, LANES), 1)
    of = lax.broadcasted_iota(jnp.int32, (2 * LANES, LANES), 0) % LANES
    return as_onehot(jnp.abs(of - to) == distance)


def sweep_edges(src_ref, dst_ref, at, n, coefs, base, matrices):
    a_ref, q_ref, r_ref = coefs[:3]
    total = src_ref.shape[0]
    here, there = pl.ds(base, n), pl.ds(at, n)

    def product(value, matrix):
        return jnp.dot(jnp.concatenate(split(value), axis=1), matrix, preferred_element_type=jnp.float32)

    for i in (total - 2, total - 1):
        centre = src_ref[i, there, :]
        beside = product(centre, matrices[0])
        above = product(q_ref[i, here, :] * centre, matrices[1])
        beside = beside + (src_ref[i, pl.ds(at - 1, n), :] + src_ref[i, pl.ds(at + 1, n), :])
        dst_ref[i, there, :] = r_ref[i, here, :] + a_ref[i, here, :] * (beside + q_ref[i, here, :] * above)


def sweep(src_ref, dst_ref, at, n, count, coefs, base, edges=True):
    a_ref, q_ref, r_ref = coefs[:3]
    total = src_ref.shape[0]
    here, there = pl.ds(base, n), pl.ds(at, n)
    which = planes_of(count, total) if edges else list(range(count))
    sums = lateral(src_ref, at, n, which)
    scaled = [q_ref[i, here, :] * src_ref[i, there, :] for i in range(min(count + 1, total - 2))]
    outer = [q_ref[i, here, :] * src_ref[i, there, :] for i in which[count:]]
    above = vertical(scaled, outer, count)
    for j, i in enumerate(which):
        dst_ref[i, there, :] = r_ref[i, here, :] + a_ref[i, here, :] * (sums[j] + q_ref[i, here, :] * above[j])


def next_rhs(coefs, v_ref, at, n, base):
    r_ref, e_ref, g_ref = coefs[2:5]
    here = pl.ds(base, n)
    for i in range(v_ref.shape[0]):
        r_ref[i, here, :] = e_ref[i, here, :] + g_ref[i, here, :] * v_ref[i, pl.ds(at, n), :]


def meet(v_ref, at, n, count, back):
    total = v_ref.shape[0]
    here = pl.ds(at, n)
    lane = lane_of(n)
    j, group = lane % GROUP, lane // GROUP
    outer = jnp.logical_or(lane < ITERS, lane >= LANES - ITERS)
    left, right = v_ref[total - 2, here, :], v_ref[total - 1, here, :]
    middle = jnp.where(j < HALO, right, left)
    for i in range(count):
        value = v_ref[i, here, :]
        if back:
            moved = pltpu.roll(value, (i * GROUP + HALO) % LANES, 1)
            left = jnp.where(jnp.logical_and(group == i, j >= GROUP - ITERS), moved, left)
            right = jnp.where(jnp.logical_and(group == i, j < ITERS), moved, right)
        v_ref[i, here, :] = jnp.where(outer, pltpu.roll(middle, LANES - (i * GROUP + HALO), 1), value)
    if back:
        v_ref[total - 2, here, :] = left
        v_ref[total - 1, here, :] = right


def needed(layers, n):
    return min(2 * layers, layers + STEPS * ITERS - 1 - n)


def two_steps(layers, sweep_all, between, after):
    for step in range(STEPS):
        for n in range(step * ITERS, (step + 1) * ITERS):
            sweep_all(n, n % 2, needed(layers, n))
        after(step)
        if step < STEPS - 1:
            between()


PAD = 8


def tile_kernel(gx, gy, shape, *refs):
    layers, rows = shape
    own_ref, partner_ref, picks_ref, out_ref, below_ref, level_ref = refs[:6]
    s_ref, va_ref, vb_ref = refs[6:9]
    coefs = refs[9:]
    x, y, z = (lax.axis_index(a) for a in ("gx", "gy", "gz"))
    total = 2 * layers + 2
    zeros = jnp.zeros((PAD, LANES), jnp.float32)
    for ref in (s_ref, va_ref, vb_ref):
        for i in range(total):
            ref[i, 0:PAD, :] = zeros
            ref[i, PAD + rows : PAD + rows + PAD, :] = zeros

    def field(f, i, here):
        j = f * (layers + 2)
        if i >= 2 * layers:
            j = j + i - layers
            return own_ref[j, here, :] + partner_ref[j, here, :]
        return own_ref[j + i, here, :] if i < layers else partner_ref[j + i - layers, here, :]

    for i in range(total):
        s_ref[i, PAD : PAD + rows, :] = field(0, i, slice(None))
        va_ref[i, PAD : PAD + rows, :] = field(2, i, slice(None))
    n = 8
    for at in range(0, rows, n):
        coefficients(s_ref, PAD + at, n, lambda f, i: field(f, i, slice(at, at + n)), coefs, at, False)

    bufs = (va_ref, vb_ref)
    sides = sides_of(gy, y)
    matrices = shifted_sums(1), shifted_sums(GROUP)

    def sweep_all(number, which, count):
        src_ref, dst_ref = bufs[which], bufs[1 - which]
        for side, (above, _) in enumerate(sides):
            inner = pl.ds(PAD + inner_at(above, rows), HALO)
            for i in range(total):
                level_ref[(side * STEPS * ITERS + number) * total + i] = src_ref[i, inner, :]
        sweep_edges(src_ref, dst_ref, PAD, rows, coefs, 0, matrices)
        for at in range(0, rows, n):
            sweep(src_ref, dst_ref, PAD + at, n, count, coefs, at, edges=False)

    def after(step):
        last = step == STEPS - 1
        for at in range(0, rows, n):
            meet(va_ref, PAD + at, n, layers if last else 2 * layers, not last)
        heat = []
        for i in range(layers):
            here = pl.ds(PAD, rows)
            heat.append(va_ref[i, here, :] * coefs[5][i])
            if step == STEPS - 1:
                out_ref[flip(z, layers, i)] = heat[-1]
        below_ref[step] = exact_dot(picks_ref[...], jnp.concatenate(heat, axis=0))

    def between():
        for at in range(0, rows, n):
            next_rhs(coefs, va_ref, PAD + at, n, at)

    two_steps(layers, sweep_all, between, after)


def edge_kernel(gx, gy, shape, seg, *refs):
    layers, rows = shape
    own_ref, partner_ref, picks_ref, mine_ref, segments_ref, below_ref, level_ref = refs[:7]
    sides_n = 1 if gy == 2 else 2
    along, across = refs[7 : 7 + sides_n], refs[7 + sides_n : 7 + 2 * sides_n]
    refs = refs[7 + 2 * sides_n :]
    heat_ref, returns = refs[0], refs[1 : 1 + gx]
    ret_ref, s_ref, va_ref, vb_ref = refs[1 + gx : 5 + gx]
    coefs = refs[5 + gx :]
    x, y, z = (lax.axis_index(a) for a in ("gx", "gy", "gz"))
    total = 2 * layers + 2
    count = mine_ref.shape[0]
    below = [below_ref[step] for step in range(STEPS)]
    lane = lane_of(HALO)
    low, first = lane < LANES // 2, lane % GROUP < HALO
    columns = edge_columns(HALO, False)
    bufs = (va_ref, vb_ref)

    def tile(j):
        return pl.ds(j if isinstance(j, int) else pl.multiple_of(j, HALO), HALO)

    for side, (above, live) in enumerate(sides_of(gy, y)):
        def place(when_top, otherwise):
            if above is True or above is False:
                return when_top * HALO if above else otherwise * HALO
            return jnp.where(above, when_top * HALO, otherwise * HALO)

        outer, strip, edge, inner = place(0, 3), place(1, 2), place(2, 1), place(3, 0)
        edge_rows = tile(edge_at(above, rows))
        inner_rows = tile(inner_at(above, rows))

        def field(f, i, here):
            j = f * (layers + 2)
            if i >= 2 * layers:
                j = j + i - layers
                return own_ref[j, here, :] + partner_ref[j, here, :]
            return own_ref[j + i, here, :] if i < layers else partner_ref[j + i - layers, here, :]

        t_ref, d_ref, q_ref, e_ref, g_ref = coefs[1], coefs[0], coefs[2], coefs[3], coefs[4]
        keep = {0: s_ref, 1: t_ref, 2: va_ref, 3: d_ref, 4: q_ref, 5: e_ref, 6: g_ref}
        zeros = jnp.zeros((HALO, LANES), jnp.float32)
        src = lane % (LANES // 2)
        turned = (layers - 1 - src // GROUP) * GROUP + src % GROUP
        half_tile = lax.broadcasted_iota(jnp.int32, (HALO, LANES), 0) < HALO // 2

        def unpack(value, f):
            if f < FIELDS - 2:
                return value
            turned_value = pltpu.roll(value, HALO // 2, 0)
            if f == FIELDS - 2:
                at_top, at_bottom = jnp.where(half_tile, 0.0, turned_value), jnp.where(half_tile, value, 0.0)
            else:
                at_top, at_bottom = jnp.where(half_tile, 0.0, value), jnp.where(half_tile, turned_value, 0.0)
            return jnp.where(above, at_top, at_bottom)

        whole, stride, later, shared = partner_rows(layers)
        sublane = lax.broadcasted_iota(jnp.int32, (HALO, LANES), 0)

        def nearest(ref, m, at):
            at_top = jnp.where(sublane >= HALO - m, ref[at - HALO + m : at + m, :], 0.0)
            return jnp.where(above, at_top, jnp.where(sublane < m, ref[at : at + HALO, :], 0.0))

        for f in range(FIELDS):
            g = min(f, FIELDS - 2)
            if f < FIELDS - 2:
                rows_of = {i: (m, f * stride + at) for i, m, at in whole}
            else:
                rows_of = {i: (m, (FIELDS - 2) * stride + at) for which, i, m, at in later if which == f - FIELDS + 2}
            values, inside = [], zeros
            for i in range(2 * layers):
                if i < layers:
                    at = (i * (FIELDS - 1) + g) * HALO
                    value = unpack(along[side][at : at + HALO, :], f)
                else:
                    j = 2 * layers - 1 - i
                    value = nearest(across[side], *rows_of[j]) if j in rows_of else zeros
                values.append(value)
                inside = jnp.where(lane // GROUP == i, take(value, columns), inside)
            half = (LANES // 2) * (g % 2)
            at = (layers * (FIELDS - 1) + g // 2) * HALO
            a = take(along[side][at : at + HALO, :], src + half)
            at = (FIELDS - 2) * stride + shared + (g // 2) * HALO
            b = take(across[side][at : at + HALO, :], turned + half)
            outside = unpack(jnp.where(low, a, b), f)
            values += [jnp.where(first, outside, inside), jnp.where(first, inside, outside)]
            for i, value in enumerate(values):
                ref, shift = keep[f], 0 if f in (0, 2) else HALO
                ref[i, tile(strip - shift), :] = value
                ref[i, tile(edge - shift), :] = field(f, i, edge_rows)
        for i in range(total):
            s_ref[i, tile(outer), :] = zeros
            va_ref[i, tile(outer), :] = zeros
            vb_ref[i, tile(outer), :] = zeros
            s_ref[i, tile(inner), :] = field(0, i, inner_rows)
        n = 2 * HALO
        held = [[keep[f][i, pl.ds(0, n), :] for i in range(total)] if f in (1, 3, 4, 5, 6) else None for f in range(FIELDS)]
        coefficients(s_ref, HALO, n, lambda f, i: held[f][i], coefs, 0, True)

        def sweep_all(number, which, needed_layers):
            src_ref, dst_ref = bufs[which], bufs[1 - which]
            for i in range(total):
                src_ref[i, tile(inner), :] = level_ref[(side * STEPS * ITERS + number) * total + i]
            sweep(src_ref, dst_ref, HALO, n, needed_layers, coefs, 0)

        picks = picks_ref[side * count : (side + 1) * count, :]

        def after(step):
            last = step == STEPS - 1
            meet(va_ref, HALO, n, layers if last else 2 * layers, not last)
            heat = []
            for i in range(layers):
                heat.append(va_ref[i, tile(edge), :] * coefs[5][i, tile(edge - HALO), :])
                if step == STEPS - 1:
                    heat_ref[side * layers + flip(z, layers, i)] = heat[-1]
            heat.append(jnp.zeros((LANES - layers * HALO, LANES), jnp.float32))
            below[step] = below[step] + exact_dot(picks, jnp.concatenate(heat, axis=0))

        two_steps(layers, sweep_all, lambda: next_rhs(coefs, va_ref, HALO, n, 0), after)

    coef, warmth = segments_ref[:count, :], segments_ref[count:, :]
    for step in range(STEPS):
        warmth = warmth + coolant_gain * coef * (below[step] - warmth)
    ret_ref[...] = jnp.where(mine_ref[...] > 0.0, warmth, 0.0)
    for k, ref in enumerate(returns):
        ref[...] = ret_ref[pl.ds(pl.multiple_of(lax.rem(x + k, gx) * seg, seg), seg), :]


def merge_kernel(gy, whole_ref, heat_ref, out_ref):
    layers, rows, _ = whole_ref.shape
    out_ref[...] = whole_ref[...]
    for side, (above, live) in enumerate(sides_of(gy, lax.axis_index("gy"))):
        def put(side=side, above=above):
            out_ref[:, pl.ds(edge_at(above, rows), HALO), :] = heat_ref[side * layers : (side + 1) * layers]

        if live is True:
            put()
        else:
            pl.when(live)(put)


def local(gx, gy, gz, u, power, storage, conductance, warmth, coef, holder, stratum, transverse):
    layers, rows, columns = u.shape
    seg = warmth.shape[1]
    segments = stratum.shape[1]
    if gz != 2 or gx < 3 or columns != LANES or 2 * layers * GROUP != LANES or rows % 32:
        raise ValueError("unsupported shape")
    holder = holder[:, :, 0]
    shape = (layers, rows)
    f32 = jnp.float32
    chunk = rows // 4
    wide = RAW * chunk + 2 * seg

    def struct(*dims):
        return jax.ShapeDtypeStruct(dims, f32)

    def vmem(*dims):
        return pltpu.VMEM(dims, f32)

    indices = (holder, stratum, transverse)
    flat = [a.reshape(-1, LANES) for a in (u, power, storage, conductance, warmth, coef)]
    own, to_left, to_right, only, *indices = pl.pallas_call(
        functools.partial(pack_kernel, shape),
        out_shape=(
            struct(RAW * layers * rows + 2 * seg + 2 * RAW * chunk, LANES),
            struct(wide, LANES),
            struct(wide, LANES),
            struct(2 * seg, LANES),
            *(jax.ShapeDtypeStruct(a.shape, a.dtype) for a in indices),
        ),
        in_specs=[pl.BlockSpec(memory_space=pltpu.HBM)] * 9,
        out_specs=(VMEM,) * 7,
        scratch_shapes=[pltpu.SemaphoreType.DMA((9,))],
        compiler_params=PARAMS,
        name="pack",
    )(*(pltpu.with_memory_space_constraint(a, pltpu.HBM) for a in (*flat, *indices)))

    swap = [(0, 1), (1, 0)]
    partner = lax.ppermute(own, "gz", swap)
    def from_distance(value, k):
        return lax.ppermute(value, "gx", [(i, (i - k) % gx) for i in range(gx)])

    received = [from_distance(to_left, 1), from_distance(to_right, gx - 1)]
    received += [from_distance(only, k) for k in range(2, gx - 1)]

    sides = 1 if gy == 2 else 2
    fields = struct(FIELDS * (layers + 2), rows, LANES)
    strip_rows = (FIELDS - 1) * layers * HALO + (FIELDS - 1) // 2 * HALO
    _, stride, _, shared = partner_rows(layers)
    partner_strip = (FIELDS - 2) * stride + shared + (FIELDS - 1) // 2 * HALO
    sides = 1 if gy == 2 else 2
    bf16 = jnp.bfloat16
    one_group = (
        jax.ShapeDtypeStruct((layers * rows, segments), bf16),
        jax.ShapeDtypeStruct((rows, segments), bf16),
        struct(2 * segments, LANES),
    )
    maps = pl.pallas_call(
        functools.partial(maps_kernel, gx, gy, shape),
        out_shape=one_group
        + one_group
        + (
            jax.ShapeDtypeStruct((segments, layers * rows), bf16),
            jax.ShapeDtypeStruct((sides * segments, LANES), bf16),
            struct(segments, LANES),
            jax.ShapeDtypeStruct((sides * layers * HALO, segments), bf16),
            jax.ShapeDtypeStruct((sides * 2 * HALO, segments), bf16),
        ),
        in_specs=[VMEM] * 3,
        out_specs=(VMEM,) * 11,
        compiler_params=PARAMS,
        cost_estimate=cost(1),
        name="maps",
    )(*indices)
    own_maps, partner_maps, (picks, picks_beside, mine, near, line) = maps[:3], maps[3:6], maps[6:]
    joined = pl.pallas_call(
        join_kernel,
        out_shape=struct(sum(a.shape[0] for a in received), LANES),
        in_specs=[pl.BlockSpec(memory_space=pl.ANY)] + [VMEM] * (gx - 1),
        out_specs=VMEM,
        compiler_params=PARAMS,
        name="join",
    )(mine, *received)
    late = lax.ppermute(joined, "gz", swap)
    made = pl.pallas_call(
        functools.partial(strip_kernel, gx, gy, shape, seg),
        out_shape=(struct(strip_rows, LANES),) * sides
        + (struct(partner_strip, LANES),) * sides
        + (struct(2 * segments, LANES),),
        in_specs=[VMEM] * (4 + gx - 1),
        out_specs=(VMEM,) * (1 + 2 * sides),
        compiler_params=PARAMS,
        cost_estimate=cost(0.5),
        name="strips",
    )(own, near, line, own_maps[2], *received)
    strips, partner_strips, held = made[:sides], made[sides : 2 * sides], made[2 * sides]
    own_fields = pl.pallas_call(
        functools.partial(fill_kernel, False, gx, gy, shape, seg),
        out_shape=fields,
        in_specs=[VMEM] * 7,
        out_specs=VMEM,
        compiler_params=PARAMS,
        cost_estimate=cost(1.5),
        name="fill_own",
    )(own, *own_maps, *received[:2], held)
    if gy == 2:
        routes = [(0, swap)]
    else:
        up = [(i, i + 1) for i in range(gy - 1)]
        routes = [(1, up), (0, [(j, i) for i, j in up])]
    along = [lax.ppermute(strips[side], "gy", pairs) for side, pairs in routes]
    across = []
    for side, pairs in routes:
        both = [(2 * i + z, 2 * j + 1 - z) for i, j in pairs for z in range(2)]
        across.append(lax.ppermute(partner_strips[side], ("gy", "gz"), both))

    partner_fields = pl.pallas_call(
        functools.partial(fill_kernel, True, gx, gy, shape, seg),
        out_shape=fields,
        in_specs=[VMEM] * 5,
        out_specs=VMEM,
        scratch_shapes=[vmem(segments, LANES)] * 2,
        compiler_params=PARAMS,
        cost_estimate=cost(1.5),
        name="fill_partner",
    )(partner, *partner_maps, late)

    total = 2 * layers + 2
    padded = vmem(total, rows + 2 * PAD, LANES)
    inside, below, levels = pl.pallas_call(
        functools.partial(tile_kernel, gx, gy, shape),
        out_shape=(
            struct(layers, rows, LANES),
            struct(STEPS, segments, LANES),
            struct(sides * STEPS * ITERS * total, HALO, LANES),
        ),
        in_specs=[VMEM] * 3,
        out_specs=(VMEM,) * 3,
        scratch_shapes=[padded] * 3 + [vmem(total, rows, LANES)] * 5 + [vmem(layers, rows, LANES)],
        compiler_params=PARAMS,
        cost_estimate=cost(7),
        name="tile_sweeps",
    )(own_fields, partner_fields, picks)

    results = pl.pallas_call(
        functools.partial(edge_kernel, gx, gy, shape, seg),
        out_shape=(struct(sides * layers, HALO, LANES),) + (struct(seg, LANES),) * gx,
        in_specs=[VMEM] * (7 + 2 * sides),
        out_specs=(VMEM,) * (1 + gx),
        scratch_shapes=[vmem(segments, LANES)]
        + [vmem(total, 4 * HALO, LANES)] * 3
        + [vmem(total, 2 * HALO, LANES)] * 5
        + [vmem(layers, 2 * HALO, LANES)],
        compiler_params=PARAMS,
        cost_estimate=cost(1.5),
        name="edge_sweeps",
    )(own_fields, partner_fields, picks_beside, mine, held, below, levels, *along, *across)
    heat, coolant = results[0], results[1]
    returned = [lax.ppermute(results[1 + k], "gx", [(i, (i + k) % gx) for i in range(gx)]) for k in range(1, gx)]
    temperature = pl.pallas_call(
        functools.partial(merge_kernel, gy),
        out_shape=struct(layers, rows, LANES),
        in_specs=[VMEM] * 2,
        out_specs=VMEM,
        compiler_params=PARAMS,
        cost_estimate=cost(1),
        name="merge",
    )(inside, heat)
    for value in returned:
        coolant = coolant + value
    return temperature, coolant[None]


def solution(mesh):
    gx, gy, gz = (mesh.shape[a] for a in ("gx", "gy", "gz"))
    cells = P(("stack", "gz"), "gy", "gx")
    segments = P(("stack", "gy", "gz"), "gx", None)
    return jax.shard_map(
        functools.partial(local, gx, gy, gz),
        mesh=mesh,
        in_specs=(cells, cells, cells, P(None, ("stack", "gz"), "gy", "gx"), segments, segments, P(), P(), P()),
        out_specs=(cells, segments),
        check_vma=False,
    )
```

```python
import functools

import jax
import jax.numpy as jnp
from jax import lax
from jax.experimental import pallas as pl
from jax.experimental.pallas import tpu as pltpu
from jax.sharding import PartitionSpec as P

STEPS = 2
ITERS = 4
HALO = STEPS * ITERS
GROUP = 2 * HALO
LANES = 128
RAW = 5
FIELDS = 7
coolant_gain = 0.5

VMEM = pl.BlockSpec(memory_space=pltpu.VMEM)
PARAMS = pltpu.CompilerParams(vmem_limit_bytes=40 * 1024 * 1024)


def cost(microseconds):
    return pl.CostEstimate(flops=0, bytes_accessed=int(microseconds * 3e6), transcendentals=0)


def lane_of(rows):
    return lax.broadcasted_iota(jnp.int32, (rows, LANES), 1)


def take(value, index):
    return jnp.take_along_axis(value, index, axis=1, mode="promise_in_bounds")


def edge_columns(rows, turned):
    j = lane_of(rows) % GROUP
    first = j < HALO
    return jnp.where(first, LANES - HALO + j, j - HALO) if not turned else jnp.where(first, j, LANES - GROUP + j)


def split(value):
    high = value.astype(jnp.bfloat16)
    low = (value - high.astype(jnp.float32)).astype(jnp.bfloat16)
    return high, low


def exact_dot(onehot, value):
    high, low = split(value)
    both = jnp.concatenate([high, low], axis=0)
    return jnp.dot(jnp.concatenate([onehot, onehot], axis=1), both, preferred_element_type=jnp.float32)


def coupling(coef, warmth):
    flow = coef * warmth
    second = coolant_gain * coef * coef
    return jnp.concatenate([coef, flow, second, flow - second * warmth], axis=1)


def flip(z, layers, i):
    return jnp.where(z == 0, i, layers - 1 - i)


def pack_kernel(shape, u_ref, p_ref, c_ref, k_ref, f_ref, x_ref, *refs):
    own_ref, left_ref, right_ref, seg_ref = refs[3:7]
    sems = refs[-1]
    layers, rows = shape
    seg = f_ref.shape[0]
    z = lax.axis_index("gz")
    plane = layers * rows
    copies = []

    def fetch(src, dst):
        copies.append(pltpu.make_async_copy(src, dst, sems.at[len(copies)]))
        copies[-1].start()

    fetch(k_ref, own_ref.at[pl.ds(0, 2 * plane), :])
    for field, ref in enumerate((u_ref, p_ref, c_ref), 2):
        fetch(ref, own_ref.at[pl.ds(field * plane, plane), :])
    for j, ref in enumerate((x_ref, f_ref)):
        fetch(ref, own_ref.at[pl.ds(RAW * plane + j * seg, seg), :])
    for table, place in zip(refs[:3], refs[7:10]):
        fetch(table, place)
    chunk = rows // 4
    lane = lane_of(chunk)
    first = lane % GROUP < HALO
    columns = edge_columns(chunk, False), edge_columns(chunk, True)
    edges = RAW * plane + 2 * seg

    def gather(field, at, g):
        value = None
        for i in range(layers):
            start = pl.multiple_of((field * layers + flip(z, layers, i)) * rows + at, chunk)
            taken = take(own_ref[pl.ds(start, chunk), :], columns[g % 2])
            value = taken if value is None else jnp.where(lane // GROUP == (g // 2) * layers + i, taken, value)
        return value

    def place(g, part):
        return pl.ds(edges + ((g % 2) * RAW + part) * chunk, chunk)

    copies[0].wait()
    roots = pl.ds(0, 2 * plane)
    own_ref[roots, :] = jnp.sqrt(own_ref[roots, :])
    for field in range(4):
        if field >= 2:
            copies[field - 1].wait()
        for part in range(4):
            value = gather(field, part * chunk, field)
            if field >= 2:
                value = jnp.where(lane < LANES // 2, own_ref[place(field, part), :], value)
            own_ref[place(field, part), :] = value
    copies[3].wait()
    for g in range(4):
        value = gather(4, g * chunk, g)
        if g >= 2:
            value = jnp.where(lane < LANES // 2, own_ref[place(g, 4), :], value)
        own_ref[place(g, 4), :] = value
    for part in range(RAW):
        even, odd = own_ref[place(0, part), :], own_ref[place(1, part), :]
        left_ref[part * chunk : (part + 1) * chunk, :] = jnp.where(first, odd, even)
        right_ref[part * chunk : (part + 1) * chunk, :] = jnp.where(first, even, odd)
    for copy in copies[4:]:
        copy.wait()
    segments = own_ref[RAW * plane : RAW * plane + 2 * seg, :]
    seg_ref[...] = segments
    left_ref[RAW * chunk :, :] = segments
    right_ref[RAW * chunk :, :] = segments


class Strips:
    def __init__(self, refs, starts, cells_ref, start, rows, layers):
        self.refs, self.starts = refs, starts
        self.cells_ref, self.start = cells_ref, start
        self.rows, self.layers = rows, layers

    def both(self, field, start, n, x, gx, partner):
        chunk = self.rows // 4
        if field < 4:
            g, at = field, start
        else:
            g, at = start // chunk, 4 * chunk + start % chunk
        a, b = (ref[at + begin : at + begin + n, :] for ref, begin in zip(self.refs, self.starts))
        at = self.start + (g % 2) * RAW * chunk + at
        inside = self.cells_ref[at : at + n, :]
        from_left, from_right = jnp.where(x > 0, b, 0.0), jnp.where(x < gx - 1, a, 0.0)
        lane = lane_of(n)
        first = (lane % GROUP < HALO) if g % 2 == 0 else (lane % GROUP >= HALO)
        half = self.layers * GROUP
        src = lane % half
        if partner:
            src = (self.layers - 1 - src // GROUP) * GROUP + src % GROUP
        if g % 2 == 1:
            src = jnp.where(src % GROUP < HALO, src + HALO, src - HALO)
        src = src + half * (g // 2)
        return take(jnp.where(first, from_left, inside), src), take(jnp.where(first, inside, from_right), src)


def place_segments(x, gx, seg, coef_ref, warmth_ref, sources):
    for k, ref, at in sources:
        place = pl.ds(pl.multiple_of(lax.rem(x + k, gx) * seg, seg), seg)
        coef_ref[place, :] = ref[at : at + seg, :]
        warmth_ref[place, :] = ref[at + seg : at + 2 * seg, :]


def tables(z, group, layers, holder_ref, stratum_ref, transverse_ref):
    holder = holder_ref[pl.ds(group, 1), :]
    layer = stratum_ref[pl.ds(group, 1), :]
    layer = jnp.where(z == 0, layer, layers - 1 - layer)
    row = transverse_ref[pl.ds(group, 1), :]
    n = holder.shape[1]
    which = lax.broadcasted_iota(jnp.int32, (8, n), 0)
    stacked = jnp.where(which == 0, holder, jnp.where(which == 1, layer, row))
    eye = lax.broadcasted_iota(jnp.int32, (n, n), 0) == lax.broadcasted_iota(jnp.int32, (n, n), 1)
    columns = lax.dot_general(
        eye.astype(jnp.float32).astype(jnp.bfloat16),
        stacked.astype(jnp.float32).astype(jnp.bfloat16),
        (((1,), (1,)), ((), ())),
        preferred_element_type=jnp.float32,
    )
    return (holder, layer, row), columns


def as_onehot(mask):
    return jnp.where(mask, 1.0, 0.0).astype(jnp.bfloat16)


def combine(raw, added):
    s, t, u, power, storage = raw
    wall, flow, second, later = (added[:, i * LANES : (i + 1) * LANES] for i in range(4))
    return s, t, s * u, storage + wall, power + storage * u + flow, power + later, storage + second


def lengths_of(gx, chunk, seg):
    return [RAW * chunk + 2 * seg] * 2 + [2 * seg] * (gx - 3)


def edge_at(top, rows):
    return 0 if top is True else rows - HALO if top is False else pl.multiple_of(jnp.where(top, 0, rows - HALO), HALO)


def inner_at(top, rows):
    return HALO if top is True else rows - 2 * HALO if top is False else pl.multiple_of(jnp.where(top, HALO, rows - 2 * HALO), HALO)


def sides_of(gy, y):
    return [(y == 1, True)] if gy == 2 else [(True, y > 0), (False, y < gy - 1)]


def maps_kernel(gx, gy, shape, holder_ref, stratum_ref, transverse_ref, *refs):
    layers, rows = shape
    plane = layers * rows
    picks_ref, beside_ref, mine_ref, near_ref, line_ref = refs[6:]
    x, y, z = (lax.axis_index(a) for a in ("gx", "gy", "gz"))
    n = holder_ref.shape[1]
    for partner in range(2):
        cells_ref, rows_ref, masks_ref = refs[3 * partner : 3 * partner + 3]
        group = y * 2 + ((1 - z) if partner else z)
        (holder, layer, row), columns = tables(z, group, layers, holder_ref, stratum_ref, transverse_ref)
        cell = jnp.where(holder == x, layer * rows + row, -1)
        cells_ref[...] = as_onehot(lax.broadcasted_iota(jnp.int32, (plane, n), 0) == cell)
        rows_ref[...] = as_onehot(lax.broadcasted_iota(jnp.int32, (rows, n), 0) == row)
        if not partner:
            near, m = layers * HALO, 2 * HALO
            for side, (above, _) in enumerate(sides_of(gy, y)):
                start = edge_at(above, rows)
                at_edge = row // HALO == start // HALO
                cell = jnp.where(jnp.logical_and(holder == x, at_edge), layer * HALO + row - start, -1)
                near_ref[side * near : (side + 1) * near, :] = as_onehot(
                    lax.broadcasted_iota(jnp.int32, (near, n), 0) == cell
                )
                cell = jnp.where(at_edge, row - start, -1)
                line_ref[side * m : (side + 1) * m, :] = as_onehot(lax.broadcasted_iota(jnp.int32, (m, n), 0) == cell)
        holder, layer, row = (columns[:, j : j + 1].astype(jnp.int32) for j in range(3))
        lane = lane_of(n)
        first = lane % GROUP < HALO
        here = lane // GROUP == layer + partner * layers
        for side, begin in enumerate((x - 1, x)):
            mine = jnp.logical_and(here, holder == jnp.where(first, begin, begin + 1))
            masks_ref[side * n : (side + 1) * n, :] = jnp.where(mine, 1.0, 0.0)
        if partner:
            continue
        mine = holder == x
        mine_ref[...] = jnp.where(jnp.logical_and(mine, lane >= 0), 1.0, 0.0)
        spoilt = None
        for side, (above, live) in enumerate(sides_of(gy, y)):
            start = edge_at(above, rows)
            part = jnp.logical_and(row // HALO == start // HALO, live)
            spoilt = part if spoilt is None else jnp.logical_or(spoilt, part)
            cell = jnp.where(jnp.logical_and(mine, part), layer * HALO + row - start, -1)
            beside_ref[side * n : (side + 1) * n, :] = as_onehot(lane == cell)
        cell = jnp.where(jnp.logical_and(mine, jnp.logical_not(spoilt)), layer * rows + row, -1)
        picks_ref[...] = as_onehot(lax.broadcasted_iota(jnp.int32, (n, plane), 1) == cell)


def join_kernel(mine_ref, *refs):
    out_ref, at = refs[-1], 0
    for ref in refs[:-1]:
        n = ref.shape[0]
        out_ref[at : at + n, :] = ref[...]
        at += n


def partner_rows(layers):
    whole, at = [], 1
    for i in range(layers - 1, -1, -1):
        whole.append((i, HALO - layers + i, at))
        at += HALO - layers + i
    stride = -(-at // 8) * 8
    later, at = [], 0
    for f in range(2):
        for i in range(layers - 1, -1, -1):
            if ITERS - 1 - layers + i > 0:
                later.append((f, i, ITERS - 1 - layers + i, at))
                at += ITERS - 1 - layers + i
    return whole, stride, later, -(-at // 8) * 8


def fill_kernel(partner, gx, gy, shape, seg, *refs):
    layers, rows = shape
    cells_ref, where_ref, rows_ref, masks_ref = refs[:4]
    plane, chunk = layers * rows, rows // 4
    lengths = lengths_of(gx, chunk, seg)
    x, z = lax.axis_index("gx"), lax.axis_index("gz")
    if partner:
        late_ref, out_ref, coef_ref, warmth_ref = refs[4:]
        sources = [(late_ref, sum(lengths[:k])) for k in range(gx - 1)]
        lay_segments(x, gx, seg, chunk, cells_ref, RAW * plane, sources, coef_ref, warmth_ref)
        coef, warmth = coef_ref[...], warmth_ref[...]
    else:
        right_ref, left_ref, segments_ref, out_ref = refs[4:]
        sources = [(right_ref, 0), (left_ref, 0)]
        n = segments_ref.shape[0] // 2
        coef, warmth = segments_ref[:n, :], segments_ref[n:, :]
    n = coef.shape[0]
    added = exact_dot(where_ref[...], coupling(coef, warmth))
    near = edge_columns(n, False)
    beside = []
    for side in range(2):
        masked = take(coef, near) * masks_ref[side * n : (side + 1) * n, :]
        beside.append(exact_dot(rows_ref[...], coupling(masked, take(warmth, near))))
    planes = layers + 2
    for i in range(layers):
        src = flip(z, layers, i)
        raw = [cells_ref[pl.ds(pl.multiple_of((f * layers + src) * rows, rows), rows), :] for f in range(RAW)]
        for f, value in enumerate(combine(raw, added[i * rows : (i + 1) * rows])):
            out_ref[f * planes + i] = value
    strips = Strips(
        [ref for ref, _ in sources[:2]], [at for _, at in sources[:2]], cells_ref, RAW * plane + 2 * seg, rows, layers
    )
    half = lane_of(chunk) // (LANES // 2) == (1 if partner else 0)
    for part in range(4):
        here = slice(part * chunk, (part + 1) * chunk)
        raw = [strips.both(f, part * chunk, chunk, x, gx, partner) for f in range(RAW)]
        for side in range(2):
            cells = [jnp.where(half, value[side], 0.0) for value in raw]
            for f, value in enumerate(combine(cells, beside[side][here])):
                out_ref[f * planes + layers + side, here, :] = value


def lay_segments(x, gx, seg, chunk, own_ref, at, sources, coef_ref, warmth_ref):
    distances = [1, gx - 1] + list(range(2, gx - 1))
    held = [(k, ref, at + (RAW * chunk if j < 2 else 0)) for j, (k, (ref, at)) in enumerate(zip(distances, sources))]
    place_segments(x, gx, seg, coef_ref, warmth_ref, [(0, own_ref, at)] + held)


def strip_kernel(gx, gy, shape, seg, *refs):
    layers, rows = shape
    cells_ref, near_ref, line_ref, masks_ref = refs[:4]
    received, refs = refs[4 : 4 + gx - 1], refs[4 + gx - 1 :]
    sides = 1 if gy == 2 else 2
    strip_refs, partner_refs, segments_ref = refs[:sides], refs[sides : 2 * sides], refs[2 * sides]
    plane, chunk = layers * rows, rows // 4
    x, y, z = (lax.axis_index(a) for a in ("gx", "gy", "gz"))
    n = segments_ref.shape[0] // 2
    coef_ref, warmth_ref = segments_ref.at[pl.ds(0, n), :], segments_ref.at[pl.ds(n, n), :]
    lay_segments(x, gx, seg, chunk, cells_ref, RAW * plane, [(ref, 0) for ref in received], coef_ref, warmth_ref)
    coef, warmth = coef_ref[...], warmth_ref[...]
    coupled = coupling(coef, warmth)
    columns = edge_columns(n, False)
    coef, warmth = take(coef, columns), take(warmth, columns)
    mask = jnp.where(lane_of(n) % GROUP < HALO, masks_ref[:n, :], masks_ref[n:, :])
    outer = coupling(coef * mask, warmth)
    strips = Strips(received[:2], [0, 0], cells_ref, RAW * plane + 2 * seg, rows, layers)
    low = lane_of(HALO) < LANES // 2
    first = lane_of(HALO) % GROUP < HALO
    upper = lax.broadcasted_iota(jnp.int32, (HALO, LANES), 0) < HALO // 2
    sent = FIELDS - 1

    def give(ref, at, values):
        for f, value in enumerate(values):
            ref[at + f * HALO : at + (f + 1) * HALO, :] = value

    def make(side, top):
        start = 0 if top else rows - HALO
        strip_ref, partner_ref = strip_refs[side], partner_refs[side]

        def shrink(values):
            *whole, e, g = values
            if top:
                g = pltpu.roll(g, HALO // 2, 0)
            else:
                e = pltpu.roll(e, HALO // 2, 0)
            return whole + [jnp.where(upper, e, g)]

        near = layers * HALO
        added = exact_dot(near_ref[side * near : (side + 1) * near, :], coupled)
        line = line_ref[side * 2 * HALO : (side + 1) * 2 * HALO, :]
        beside = exact_dot(line, outer)[:HALO]
        whole, stride, later, shared = partner_rows(layers)
        for i in range(layers):
            src = flip(z, layers, i)
            raw = [
                cells_ref[pl.ds(pl.multiple_of((f * layers + src) * rows + start, HALO), HALO), :] for f in range(RAW)
            ]
            values = combine(raw, added[i * HALO : (i + 1) * HALO])
            give(strip_ref, i * sent * HALO, shrink(values))
            pieces = [(f, m, f * stride + at) for f in range(sent - 1) for j, m, at in whole if j == i]
            pieces += [(sent - 1 + f, m, (sent - 1) * stride + at) for f, j, m, at in later if j == i]
            for f, m, at in pieces:
                skip = 0 if top else HALO - m
                partner_ref[at : at + m, :] = values[f][skip : skip + m]
        raw = [jnp.where(first, *strips.both(f, start, HALO, x, gx, False)) for f in range(RAW)]
        values = shrink(combine(raw, beside))
        values = [jnp.where(low, values[j], pltpu.roll(values[j + 1], LANES // 2, 1)) for j in range(0, sent, 2)]
        give(strip_ref, layers * sent * HALO, values)
        give(partner_ref, (sent - 1) * stride + shared, values)

    for side, (top, _) in enumerate(sides_of(gy, y)):
        if top is True or top is False:
            make(side, top)
        else:
            pl.when(top)(functools.partial(make, side, True))
            pl.when(jnp.logical_not(top))(functools.partial(make, side, False))


def planes_of(count, total):
    return list(range(count)) + [total - 2, total - 1]


def lateral(buf, at, n, which):
    sums = []
    for i in which:
        centre = buf[i, pl.ds(at, n), :]
        beside = pltpu.roll(centre, 1, 1) + pltpu.roll(centre, LANES - 1, 1)
        sums.append(beside + (buf[i, pl.ds(at - 1, n), :] + buf[i, pl.ds(at + 1, n), :]))
    return sums


def vertical(planes, edges, count):
    sums = []
    for i in range(count):
        near = [planes[j] for j in (i - 1, i + 1) if 0 <= j < len(planes)]
        sums.append(functools.reduce(jnp.add, near))
    for edge in edges:
        lane = lane_of(edge.shape[0])
        up = jnp.where(lane >= GROUP, pltpu.roll(edge, GROUP, 1), 0.0)
        down = jnp.where(lane < LANES - GROUP, pltpu.roll(edge, LANES - GROUP, 1), 0.0)
        sums.append(up + down)
    return sums


def coefficients(s_ref, at, n, raw, dests, to, outside):
    a_ref, q_ref, r_ref, e_ref, g_ref, root_ref = dests
    total = s_ref.shape[0]
    sums = lateral(s_ref, at, n, range(total))
    t = [raw(1, i) for i in range(total)]
    above = vertical(t[:-2], t[-2:], total - 2)
    here = pl.ds(to, n)
    for i in range(total):
        s = s_ref[i, pl.ds(at, n), :]
        diag = raw(3, i) + s * sums[i] + t[i] * above[i]
        if outside or i >= total - 2:
            inverse = 1.0 / jnp.where(diag > 0.0, diag, 1.0)
            root = jnp.where(s > 0.0, 1.0 / jnp.where(s > 0.0, s, 1.0), 0.0)
        else:
            inverse, root = 1.0 / diag, 1.0 / s
        if i < root_ref.shape[0]:
            root_ref[i, here, :] = root
        scaled = s * inverse
        a_ref[i, here, :] = s * scaled
        r_ref[i, here, :] = raw(4, i) * scaled
        e_ref[i, here, :] = raw(5, i) * scaled
        g_ref[i, here, :] = raw(6, i) * inverse
        q_ref[i, here, :] = t[i] * root


def shifted_sums(distance):
    to = lax.broadcasted_iota(jnp.int32, (2 * LANES, LANES), 1)
    of = lax.broadcasted_iota(jnp.int32, (2 * LANES, LANES), 0) % LANES
    return as_onehot(jnp.abs(of - to) == distance)


def sweep_edges(src_ref, dst_ref, at, n, coefs, base, matrices):
    a_ref, q_ref, r_ref = coefs[:3]
    total = src_ref.shape[0]
    here, there = pl.ds(base, n), pl.ds(at, n)

    def product(value, matrix):
        return jnp.dot(jnp.concatenate(split(value), axis=1), matrix, preferred_element_type=jnp.float32)

    for i in (total - 2, total - 1):
        centre = src_ref[i, there, :]
        beside = product(centre, matrices[0])
        above = product(q_ref[i, here, :] * centre, matrices[1])
        beside = beside + (src_ref[i, pl.ds(at - 1, n), :] + src_ref[i, pl.ds(at + 1, n), :])
        dst_ref[i, there, :] = r_ref[i, here, :] + a_ref[i, here, :] * (beside + q_ref[i, here, :] * above)


def sweep(src_ref, dst_ref, at, n, count, coefs, base, edges=True):
    a_ref, q_ref, r_ref = coefs[:3]
    total = src_ref.shape[0]
    here, there = pl.ds(base, n), pl.ds(at, n)
    which = planes_of(count, total) if edges else list(range(count))
    sums = lateral(src_ref, at, n, which)
    scaled = [q_ref[i, here, :] * src_ref[i, there, :] for i in range(min(count + 1, total - 2))]
    outer = [q_ref[i, here, :] * src_ref[i, there, :] for i in which[count:]]
    above = vertical(scaled, outer, count)
    for j, i in enumerate(which):
        dst_ref[i, there, :] = r_ref[i, here, :] + a_ref[i, here, :] * (sums[j] + q_ref[i, here, :] * above[j])


def next_rhs(coefs, v_ref, at, n, base):
    r_ref, e_ref, g_ref = coefs[2:5]
    here = pl.ds(base, n)
    for i in range(v_ref.shape[0]):
        r_ref[i, here, :] = e_ref[i, here, :] + g_ref[i, here, :] * v_ref[i, pl.ds(at, n), :]


def meet(v_ref, at, n, count, back):
    total = v_ref.shape[0]
    here = pl.ds(at, n)
    lane = lane_of(n)
    j, group = lane % GROUP, lane // GROUP
    outer = jnp.logical_or(lane < ITERS, lane >= LANES - ITERS)
    left, right = v_ref[total - 2, here, :], v_ref[total - 1, here, :]
    middle = jnp.where(j < HALO, right, left)
    for i in range(count):
        value = v_ref[i, here, :]
        if back:
            moved = pltpu.roll(value, (i * GROUP + HALO) % LANES, 1)
            left = jnp.where(jnp.logical_and(group == i, j >= GROUP - ITERS), moved, left)
            right = jnp.where(jnp.logical_and(group == i, j < ITERS), moved, right)
        v_ref[i, here, :] = jnp.where(outer, pltpu.roll(middle, LANES - (i * GROUP + HALO), 1), value)
    if back:
        v_ref[total - 2, here, :] = left
        v_ref[total - 1, here, :] = right


def needed(layers, n):
    return min(2 * layers, layers + STEPS * ITERS - 1 - n)


def two_steps(layers, sweep_all, between, after):
    for step in range(STEPS):
        for n in range(step * ITERS, (step + 1) * ITERS):
            sweep_all(n, n % 2, needed(layers, n))
        after(step)
        if step < STEPS - 1:
            between()


PAD = 8


def tile_kernel(gx, gy, shape, *refs):
    layers, rows = shape
    own_ref, partner_ref, picks_ref, out_ref, below_ref, level_ref = refs[:6]
    s_ref, va_ref, vb_ref = refs[6:9]
    coefs = refs[9:]
    x, y, z = (lax.axis_index(a) for a in ("gx", "gy", "gz"))
    total = 2 * layers + 2
    zeros = jnp.zeros((PAD, LANES), jnp.float32)
    for ref in (s_ref, va_ref, vb_ref):
        for i in range(total):
            ref[i, 0:PAD, :] = zeros
            ref[i, PAD + rows : PAD + rows + PAD, :] = zeros

    def field(f, i, here):
        j = f * (layers + 2)
        if i >= 2 * layers:
            j = j + i - layers
            return own_ref[j, here, :] + partner_ref[j, here, :]
        return own_ref[j + i, here, :] if i < layers else partner_ref[j + i - layers, here, :]

    for i in range(total):
        s_ref[i, PAD : PAD + rows, :] = field(0, i, slice(None))
        va_ref[i, PAD : PAD + rows, :] = field(2, i, slice(None))
    n = 8
    for at in range(0, rows, n):
        coefficients(s_ref, PAD + at, n, lambda f, i: field(f, i, slice(at, at + n)), coefs, at, False)

    bufs = (va_ref, vb_ref)
    sides = sides_of(gy, y)
    matrices = shifted_sums(1), shifted_sums(GROUP)

    def sweep_all(number, which, count):
        src_ref, dst_ref = bufs[which], bufs[1 - which]
        for side, (above, _) in enumerate(sides):
            inner = pl.ds(PAD + inner_at(above, rows), HALO)
            for i in range(total):
                level_ref[(side * STEPS * ITERS + number) * total + i] = src_ref[i, inner, :]
        sweep_edges(src_ref, dst_ref, PAD, rows, coefs, 0, matrices)
        for at in range(0, rows, n):
            sweep(src_ref, dst_ref, PAD + at, n, count, coefs, at, edges=False)

    def after(step):
        last = step == STEPS - 1
        for at in range(0, rows, n):
            meet(va_ref, PAD + at, n, layers if last else 2 * layers, not last)
        heat = []
        for i in range(layers):
            here = pl.ds(PAD, rows)
            heat.append(va_ref[i, here, :] * coefs[5][i])
            if step == STEPS - 1:
                out_ref[flip(z, layers, i)] = heat[-1]
        below_ref[step] = exact_dot(picks_ref[...], jnp.concatenate(heat, axis=0))

    def between():
        for at in range(0, rows, n):
            next_rhs(coefs, va_ref, PAD + at, n, at)

    two_steps(layers, sweep_all, between, after)


def edge_kernel(gx, gy, shape, seg, *refs):
    layers, rows = shape
    own_ref, partner_ref, picks_ref, mine_ref, segments_ref, below_ref, level_ref = refs[:7]
    sides_n = 1 if gy == 2 else 2
    along, across = refs[7 : 7 + sides_n], refs[7 + sides_n : 7 + 2 * sides_n]
    refs = refs[7 + 2 * sides_n :]
    heat_ref, returns = refs[0], refs[1 : 1 + gx]
    ret_ref, s_ref, va_ref, vb_ref = refs[1 + gx : 5 + gx]
    coefs = refs[5 + gx :]
    x, y, z = (lax.axis_index(a) for a in ("gx", "gy", "gz"))
    total = 2 * layers + 2
    count = mine_ref.shape[0]
    below = [below_ref[step] for step in range(STEPS)]
    lane = lane_of(HALO)
    low, first = lane < LANES // 2, lane % GROUP < HALO
    columns = edge_columns(HALO, False)
    bufs = (va_ref, vb_ref)

    def tile(j):
        return pl.ds(j if isinstance(j, int) else pl.multiple_of(j, HALO), HALO)

    for side, (above, live) in enumerate(sides_of(gy, y)):
        def place(when_top, otherwise):
            if above is True or above is False:
                return when_top * HALO if above else otherwise * HALO
            return jnp.where(above, when_top * HALO, otherwise * HALO)

        outer, strip, edge, inner = place(0, 3), place(1, 2), place(2, 1), place(3, 0)
        edge_rows = tile(edge_at(above, rows))
        inner_rows = tile(inner_at(above, rows))

        def field(f, i, here):
            j = f * (layers + 2)
            if i >= 2 * layers:
                j = j + i - layers
                return own_ref[j, here, :] + partner_ref[j, here, :]
            return own_ref[j + i, here, :] if i < layers else partner_ref[j + i - layers, here, :]

        t_ref, d_ref, q_ref, e_ref, g_ref = coefs[1], coefs[0], coefs[2], coefs[3], coefs[4]
        keep = {0: s_ref, 1: t_ref, 2: va_ref, 3: d_ref, 4: q_ref, 5: e_ref, 6: g_ref}
        zeros = jnp.zeros((HALO, LANES), jnp.float32)
        src = lane % (LANES // 2)
        turned = (layers - 1 - src // GROUP) * GROUP + src % GROUP
        half_tile = lax.broadcasted_iota(jnp.int32, (HALO, LANES), 0) < HALO // 2

        def unpack(value, f):
            if f < FIELDS - 2:
                return value
            turned_value = pltpu.roll(value, HALO // 2, 0)
            if f == FIELDS - 2:
                at_top, at_bottom = jnp.where(half_tile, 0.0, turned_value), jnp.where(half_tile, value, 0.0)
            else:
                at_top, at_bottom = jnp.where(half_tile, 0.0, value), jnp.where(half_tile, turned_value, 0.0)
            return jnp.where(above, at_top, at_bottom)

        whole, stride, later, shared = partner_rows(layers)
        sublane = lax.broadcasted_iota(jnp.int32, (HALO, LANES), 0)

        def nearest(ref, m, at):
            at_top = jnp.where(sublane >= HALO - m, ref[at - HALO + m : at + m, :], 0.0)
            return jnp.where(above, at_top, jnp.where(sublane < m, ref[at : at + HALO, :], 0.0))

        for f in range(FIELDS):
            g = min(f, FIELDS - 2)
            if f < FIELDS - 2:
                rows_of = {i: (m, f * stride + at) for i, m, at in whole}
            else:
                rows_of = {i: (m, (FIELDS - 2) * stride + at) for which, i, m, at in later if which == f - FIELDS + 2}
            values, inside = [], zeros
            for i in range(2 * layers):
                if i < layers:
                    at = (i * (FIELDS - 1) + g) * HALO
                    value = unpack(along[side][at : at + HALO, :], f)
                else:
                    j = 2 * layers - 1 - i
                    value = nearest(across[side], *rows_of[j]) if j in rows_of else zeros
                values.append(value)
                inside = jnp.where(lane // GROUP == i, take(value, columns), inside)
            half = (LANES // 2) * (g % 2)
            at = (layers * (FIELDS - 1) + g // 2) * HALO
            a = take(along[side][at : at + HALO, :], src + half)
            at = (FIELDS - 2) * stride + shared + (g // 2) * HALO
            b = take(across[side][at : at + HALO, :], turned + half)
            outside = unpack(jnp.where(low, a, b), f)
            values += [jnp.where(first, outside, inside), jnp.where(first, inside, outside)]
            for i, value in enumerate(values):
                ref, shift = keep[f], 0 if f in (0, 2) else HALO
                ref[i, tile(strip - shift), :] = value
                ref[i, tile(edge - shift), :] = field(f, i, edge_rows)
        for i in range(total):
            s_ref[i, tile(outer), :] = zeros
            va_ref[i, tile(outer), :] = zeros
            vb_ref[i, tile(outer), :] = zeros
            s_ref[i, tile(inner), :] = field(0, i, inner_rows)
        n = 2 * HALO
        held = [[keep[f][i, pl.ds(0, n), :] for i in range(total)] if f in (1, 3, 4, 5, 6) else None for f in range(FIELDS)]
        coefficients(s_ref, HALO, n, lambda f, i: held[f][i], coefs, 0, True)

        def sweep_all(number, which, needed_layers):
            src_ref, dst_ref = bufs[which], bufs[1 - which]
            for i in range(total):
                src_ref[i, tile(inner), :] = level_ref[(side * STEPS * ITERS + number) * total + i]
            sweep(src_ref, dst_ref, HALO, n, needed_layers, coefs, 0)

        picks = picks_ref[side * count : (side + 1) * count, :]

        def after(step):
            last = step == STEPS - 1
            meet(va_ref, HALO, n, layers if last else 2 * layers, not last)
            heat = []
            for i in range(layers):
                heat.append(va_ref[i, tile(edge), :] * coefs[5][i, tile(edge - HALO), :])
                if step == STEPS - 1:
                    heat_ref[side * layers + flip(z, layers, i)] = heat[-1]
            heat.append(jnp.zeros((LANES - layers * HALO, LANES), jnp.float32))
            below[step] = below[step] + exact_dot(picks, jnp.concatenate(heat, axis=0))

        two_steps(layers, sweep_all, lambda: next_rhs(coefs, va_ref, HALO, n, 0), after)

    coef, warmth = segments_ref[:count, :], segments_ref[count:, :]
    for step in range(STEPS):
        warmth = warmth + coolant_gain * coef * (below[step] - warmth)
    ret_ref[...] = jnp.where(mine_ref[...] > 0.0, warmth, 0.0)
    for k, ref in enumerate(returns):
        ref[...] = ret_ref[pl.ds(pl.multiple_of(lax.rem(x + k, gx) * seg, seg), seg), :]


def merge_kernel(gy, whole_ref, heat_ref, out_ref):
    layers, rows, _ = whole_ref.shape
    out_ref[...] = whole_ref[...]
    for side, (above, live) in enumerate(sides_of(gy, lax.axis_index("gy"))):
        def put(side=side, above=above):
            out_ref[:, pl.ds(edge_at(above, rows), HALO), :] = heat_ref[side * layers : (side + 1) * layers]

        if live is True:
            put()
        else:
            pl.when(live)(put)


def local(gx, gy, gz, u, power, storage, conductance, warmth, coef, holder, stratum, transverse):
    layers, rows, columns = u.shape
    seg = warmth.shape[1]
    segments = stratum.shape[1]
    if gz != 2 or gx < 3 or columns != LANES or 2 * layers * GROUP != LANES or rows % 32:
        raise ValueError("unsupported shape")
    holder = holder[:, :, 0]
    shape = (layers, rows)
    f32 = jnp.float32
    chunk = rows // 4
    wide = RAW * chunk + 2 * seg

    def struct(*dims):
        return jax.ShapeDtypeStruct(dims, f32)

    def vmem(*dims):
        return pltpu.VMEM(dims, f32)

    indices = (holder, stratum, transverse)
    flat = [a.reshape(-1, LANES) for a in (u, power, storage, conductance, warmth, coef)]
    own, to_left, to_right, only, *indices = pl.pallas_call(
        functools.partial(pack_kernel, shape),
        out_shape=(
            struct(RAW * layers * rows + 2 * seg + 2 * RAW * chunk, LANES),
            struct(wide, LANES),
            struct(wide, LANES),
            struct(2 * seg, LANES),
            *(jax.ShapeDtypeStruct(a.shape, a.dtype) for a in indices),
        ),
        in_specs=[pl.BlockSpec(memory_space=pltpu.HBM)] * 9,
        out_specs=(VMEM,) * 7,
        scratch_shapes=[pltpu.SemaphoreType.DMA((9,))],
        compiler_params=PARAMS,
        name="pack",
    )(*(pltpu.with_memory_space_constraint(a, pltpu.HBM) for a in (*flat, *indices)))

    swap = [(0, 1), (1, 0)]
    partner = lax.ppermute(own, "gz", swap)
    def from_distance(value, k):
        return lax.ppermute(value, "gx", [(i, (i - k) % gx) for i in range(gx)])

    received = [from_distance(to_left, 1), from_distance(to_right, gx - 1)]
    received += [from_distance(only, k) for k in range(2, gx - 1)]

    sides = 1 if gy == 2 else 2
    fields = struct(FIELDS * (layers + 2), rows, LANES)
    strip_rows = (FIELDS - 1) * layers * HALO + (FIELDS - 1) // 2 * HALO
    _, stride, _, shared = partner_rows(layers)
    partner_strip = (FIELDS - 2) * stride + shared + (FIELDS - 1) // 2 * HALO
    sides = 1 if gy == 2 else 2
    bf16 = jnp.bfloat16
    one_group = (
        jax.ShapeDtypeStruct((layers * rows, segments), bf16),
        jax.ShapeDtypeStruct((rows, segments), bf16),
        struct(2 * segments, LANES),
    )
    maps = pl.pallas_call(
        functools.partial(maps_kernel, gx, gy, shape),
        out_shape=one_group
        + one_group
        + (
            jax.ShapeDtypeStruct((segments, layers * rows), bf16),
            jax.ShapeDtypeStruct((sides * segments, LANES), bf16),
            struct(segments, LANES),
            jax.ShapeDtypeStruct((sides * layers * HALO, segments), bf16),
            jax.ShapeDtypeStruct((sides * 2 * HALO, segments), bf16),
        ),
        in_specs=[VMEM] * 3,
        out_specs=(VMEM,) * 11,
        compiler_params=PARAMS,
        cost_estimate=cost(1),
        name="maps",
    )(*indices)
    own_maps, partner_maps, (picks, picks_beside, mine, near, line) = maps[:3], maps[3:6], maps[6:]
    joined = pl.pallas_call(
        join_kernel,
        out_shape=struct(sum(a.shape[0] for a in received), LANES),
        in_specs=[pl.BlockSpec(memory_space=pl.ANY)] + [VMEM] * (gx - 1),
        out_specs=VMEM,
        compiler_params=PARAMS,
        name="join",
    )(mine, *received)
    late = lax.ppermute(joined, "gz", swap)
    made = pl.pallas_call(
        functools.partial(strip_kernel, gx, gy, shape, seg),
        out_shape=(struct(strip_rows, LANES),) * sides
        + (struct(partner_strip, LANES),) * sides
        + (struct(2 * segments, LANES),),
        in_specs=[VMEM] * (4 + gx - 1),
        out_specs=(VMEM,) * (1 + 2 * sides),
        compiler_params=PARAMS,
        cost_estimate=cost(0.5),
        name="strips",
    )(own, near, line, own_maps[2], *received)
    strips, partner_strips, held = made[:sides], made[sides : 2 * sides], made[2 * sides]
    own_fields = pl.pallas_call(
        functools.partial(fill_kernel, False, gx, gy, shape, seg),
        out_shape=fields,
        in_specs=[VMEM] * 7,
        out_specs=VMEM,
        compiler_params=PARAMS,
        cost_estimate=cost(1.5),
        name="fill_own",
    )(own, *own_maps, *received[:2], held)
    if gy == 2:
        routes = [(0, swap)]
    else:
        up = [(i, i + 1) for i in range(gy - 1)]
        routes = [(1, up), (0, [(j, i) for i, j in up])]
    along = [lax.ppermute(strips[side], "gy", pairs) for side, pairs in routes]
    across = []
    for side, pairs in routes:
        both = [(2 * i + z, 2 * j + 1 - z) for i, j in pairs for z in range(2)]
        across.append(lax.ppermute(partner_strips[side], ("gy", "gz"), both))

    partner_fields = pl.pallas_call(
        functools.partial(fill_kernel, True, gx, gy, shape, seg),
        out_shape=fields,
        in_specs=[VMEM] * 5,
        out_specs=VMEM,
        scratch_shapes=[vmem(segments, LANES)] * 2,
        compiler_params=PARAMS,
        cost_estimate=cost(1.5),
        name="fill_partner",
    )(partner, *partner_maps, late)

    total = 2 * layers + 2
    padded = vmem(total, rows + 2 * PAD, LANES)
    inside, below, levels = pl.pallas_call(
        functools.partial(tile_kernel, gx, gy, shape),
        out_shape=(
            struct(layers, rows, LANES),
            struct(STEPS, segments, LANES),
            struct(sides * STEPS * ITERS * total, HALO, LANES),
        ),
        in_specs=[VMEM] * 3,
        out_specs=(VMEM,) * 3,
        scratch_shapes=[padded] * 3 + [vmem(total, rows, LANES)] * 5 + [vmem(layers, rows, LANES)],
        compiler_params=PARAMS,
        cost_estimate=cost(7),
        name="tile_sweeps",
    )(own_fields, partner_fields, picks)

    results = pl.pallas_call(
        functools.partial(edge_kernel, gx, gy, shape, seg),
        out_shape=(struct(sides * layers, HALO, LANES),) + (struct(seg, LANES),) * gx,
        in_specs=[VMEM] * (7 + 2 * sides),
        out_specs=(VMEM,) * (1 + gx),
        scratch_shapes=[vmem(segments, LANES)]
        + [vmem(total, 4 * HALO, LANES)] * 3
        + [vmem(total, 2 * HALO, LANES)] * 5
        + [vmem(layers, 2 * HALO, LANES)],
        compiler_params=PARAMS,
        cost_estimate=cost(1.5),
        name="edge_sweeps",
    )(own_fields, partner_fields, picks_beside, mine, held, below, levels, *along, *across)
    heat, coolant = results[0], results[1]
    returned = [lax.ppermute(results[1 + k], "gx", [(i, (i + k) % gx) for i in range(gx)]) for k in range(1, gx)]
    temperature = pl.pallas_call(
        functools.partial(merge_kernel, gy),
        out_shape=struct(layers, rows, LANES),
        in_specs=[VMEM] * 2,
        out_specs=VMEM,
        compiler_params=PARAMS,
        cost_estimate=cost(1),
        name="merge",
    )(inside, heat)
    for value in returned:
        coolant = coolant + value
    return temperature, coolant[None]


def solution(mesh):
    gx, gy, gz = (mesh.shape[a] for a in ("gx", "gy", "gz"))
    cells = P(("stack", "gz"), "gy", "gx")
    segments = P(("stack", "gy", "gz"), "gx", None)
    return jax.shard_map(
        functools.partial(local, gx, gy, gz),
        mesh=mesh,
        in_specs=(cells, cells, cells, P(None, ("stack", "gz"), "gy", "gx"), segments, segments, P(), P(), P()),
        out_specs=(cells, segments),
        check_vma=False,
    )
```

```python
import functools

import jax
import jax.numpy as jnp
from jax import lax
from jax.experimental import pallas as pl
from jax.experimental.pallas import tpu as pltpu
from jax.sharding import PartitionSpec as P

STEPS = 2
ITERS = 4
HALO = STEPS * ITERS
GROUP = 2 * HALO
LANES = 128
RAW = 5
FIELDS = 7
coolant_gain = 0.5

VMEM = pl.BlockSpec(memory_space=pltpu.VMEM)
PARAMS = pltpu.CompilerParams(vmem_limit_bytes=40 * 1024 * 1024)


def cost(microseconds):
    return pl.CostEstimate(flops=0, bytes_accessed=int(microseconds * 3e6), transcendentals=0)


def lane_of(rows):
    return lax.broadcasted_iota(jnp.int32, (rows, LANES), 1)


def take(value, index):
    return jnp.take_along_axis(value, index, axis=1, mode="promise_in_bounds")


def edge_columns(rows, turned):
    j = lane_of(rows) % GROUP
    first = j < HALO
    return jnp.where(first, LANES - HALO + j, j - HALO) if not turned else jnp.where(first, j, LANES - GROUP + j)


def split(value):
    high = value.astype(jnp.bfloat16)
    low = (value - high.astype(jnp.float32)).astype(jnp.bfloat16)
    return high, low


def exact_dot(onehot, value):
    high, low = split(value)
    both = jnp.concatenate([high, low], axis=0)
    return jnp.dot(jnp.concatenate([onehot, onehot], axis=1), both, preferred_element_type=jnp.float32)


def coupling(coef, warmth):
    flow = coef * warmth
    second = coolant_gain * coef * coef
    return jnp.concatenate([coef, flow, second, flow - second * warmth], axis=1)


def flip(z, layers, i):
    return jnp.where(z == 0, i, layers - 1 - i)


def pack_kernel(shape, u_ref, p_ref, c_ref, k_ref, f_ref, x_ref, *refs):
    own_ref, left_ref, right_ref, seg_ref = refs[3:7]
    sems = refs[-1]
    layers, rows = shape
    seg = f_ref.shape[0]
    z = lax.axis_index("gz")
    plane = layers * rows
    copies = []

    def fetch(src, dst):
        copies.append(pltpu.make_async_copy(src, dst, sems.at[len(copies)]))
        copies[-1].start()

    fetch(k_ref, own_ref.at[pl.ds(0, 2 * plane), :])
    for field, ref in enumerate((u_ref, p_ref, c_ref), 2):
        fetch(ref, own_ref.at[pl.ds(field * plane, plane), :])
    for j, ref in enumerate((x_ref, f_ref)):
        fetch(ref, own_ref.at[pl.ds(RAW * plane + j * seg, seg), :])
    for table, place in zip(refs[:3], refs[7:10]):
        fetch(table, place)
    chunk = rows // 4
    lane = lane_of(chunk)
    first = lane % GROUP < HALO
    columns = edge_columns(chunk, False), edge_columns(chunk, True)
    edges = RAW * plane + 2 * seg

    def gather(field, at, g):
        value = None
        for i in range(layers):
            start = pl.multiple_of((field * layers + flip(z, layers, i)) * rows + at, chunk)
            taken = take(own_ref[pl.ds(start, chunk), :], columns[g % 2])
            value = taken if value is None else jnp.where(lane // GROUP == (g // 2) * layers + i, taken, value)
        return value

    def place(g, part):
        return pl.ds(edges + ((g % 2) * RAW + part) * chunk, chunk)

    copies[0].wait()
    roots = pl.ds(0, 2 * plane)
    own_ref[roots, :] = jnp.sqrt(own_ref[roots, :])
    for field in range(4):
        if field >= 2:
            copies[field - 1].wait()
        for part in range(4):
            value = gather(field, part * chunk, field)
            if field >= 2:
                value = jnp.where(lane < LANES // 2, own_ref[place(field, part), :], value)
            own_ref[place(field, part), :] = value
    copies[3].wait()
    for g in range(4):
        value = gather(4, g * chunk, g)
        if g >= 2:
            value = jnp.where(lane < LANES // 2, own_ref[place(g, 4), :], value)
        own_ref[place(g, 4), :] = value
    for part in range(RAW):
        even, odd = own_ref[place(0, part), :], own_ref[place(1, part), :]
        left_ref[part * chunk : (part + 1) * chunk, :] = jnp.where(first, odd, even)
        right_ref[part * chunk : (part + 1) * chunk, :] = jnp.where(first, even, odd)
    for copy in copies[4:]:
        copy.wait()
    segments = own_ref[RAW * plane : RAW * plane + 2 * seg, :]
    seg_ref[...] = segments
    left_ref[RAW * chunk :, :] = segments
    right_ref[RAW * chunk :, :] = segments


class Strips:
    def __init__(self, refs, starts, cells_ref, start, rows, layers):
        self.refs, self.starts = refs, starts
        self.cells_ref, self.start = cells_ref, start
        self.rows, self.layers = rows, layers

    def both(self, field, start, n, x, gx, partner):
        chunk = self.rows // 4
        if field < 4:
            g, at = field, start
        else:
            g, at = start // chunk, 4 * chunk + start % chunk
        a, b = (ref[at + begin : at + begin + n, :] for ref, begin in zip(self.refs, self.starts))
        at = self.start + (g % 2) * RAW * chunk + at
        inside = self.cells_ref[at : at + n, :]
        from_left, from_right = jnp.where(x > 0, b, 0.0), jnp.where(x < gx - 1, a, 0.0)
        lane = lane_of(n)
        first = (lane % GROUP < HALO) if g % 2 == 0 else (lane % GROUP >= HALO)
        half = self.layers * GROUP
        src = lane % half
        if partner:
            src = (self.layers - 1 - src // GROUP) * GROUP + src % GROUP
        if g % 2 == 1:
            src = jnp.where(src % GROUP < HALO, src + HALO, src - HALO)
        src = src + half * (g // 2)
        return take(jnp.where(first, from_left, inside), src), take(jnp.where(first, inside, from_right), src)


def place_segments(x, gx, seg, coef_ref, warmth_ref, sources):
    for k, ref, at in sources:
        place = pl.ds(pl.multiple_of(lax.rem(x + k, gx) * seg, seg), seg)
        coef_ref[place, :] = ref[at : at + seg, :]
        warmth_ref[place, :] = ref[at + seg : at + 2 * seg, :]


def tables(z, group, layers, holder_ref, stratum_ref, transverse_ref):
    holder = holder_ref[pl.ds(group, 1), :]
    layer = stratum_ref[pl.ds(group, 1), :]
    layer = jnp.where(z == 0, layer, layers - 1 - layer)
    row = transverse_ref[pl.ds(group, 1), :]
    n = holder.shape[1]
    which = lax.broadcasted_iota(jnp.int32, (8, n), 0)
    stacked = jnp.where(which == 0, holder, jnp.where(which == 1, layer, row))
    eye = lax.broadcasted_iota(jnp.int32, (n, n), 0) == lax.broadcasted_iota(jnp.int32, (n, n), 1)
    columns = lax.dot_general(
        eye.astype(jnp.float32).astype(jnp.bfloat16),
        stacked.astype(jnp.float32).astype(jnp.bfloat16),
        (((1,), (1,)), ((), ())),
        preferred_element_type=jnp.float32,
    )
    return (holder, layer, row), columns


def as_onehot(mask):
    return jnp.where(mask, 1.0, 0.0).astype(jnp.bfloat16)


def combine(raw, added):
    s, t, u, power, storage = raw
    wall, flow, second, later = (added[:, i * LANES : (i + 1) * LANES] for i in range(4))
    return s, t, s * u, storage + wall, power + storage * u + flow, power + later, storage + second


def lengths_of(gx, chunk, seg):
    return [RAW * chunk + 2 * seg] * 2 + [2 * seg] * (gx - 3)


def edge_at(top, rows):
    return 0 if top is True else rows - HALO if top is False else pl.multiple_of(jnp.where(top, 0, rows - HALO), HALO)


def inner_at(top, rows):
    return HALO if top is True else rows - 2 * HALO if top is False else pl.multiple_of(jnp.where(top, HALO, rows - 2 * HALO), HALO)


def sides_of(gy, y):
    return [(y == 1, True)] if gy == 2 else [(True, y > 0), (False, y < gy - 1)]


def maps_kernel(gx, gy, shape, holder_ref, stratum_ref, transverse_ref, *refs):
    layers, rows = shape
    plane = layers * rows
    picks_ref, beside_ref, mine_ref, near_ref, line_ref = refs[6:]
    x, y, z = (lax.axis_index(a) for a in ("gx", "gy", "gz"))
    n = holder_ref.shape[1]
    for partner in range(2):
        cells_ref, rows_ref, masks_ref = refs[3 * partner : 3 * partner + 3]
        group = y * 2 + ((1 - z) if partner else z)
        (holder, layer, row), columns = tables(z, group, layers, holder_ref, stratum_ref, transverse_ref)
        cell = jnp.where(holder == x, layer * rows + row, -1)
        cells_ref[...] = as_onehot(lax.broadcasted_iota(jnp.int32, (plane, n), 0) == cell)
        rows_ref[...] = as_onehot(lax.broadcasted_iota(jnp.int32, (rows, n), 0) == row)
        if not partner:
            near, m = layers * HALO, 2 * HALO
            for side, (above, _) in enumerate(sides_of(gy, y)):
                start = edge_at(above, rows)
                at_edge = row // HALO == start // HALO
                cell = jnp.where(jnp.logical_and(holder == x, at_edge), layer * HALO + row - start, -1)
                near_ref[side * near : (side + 1) * near, :] = as_onehot(
                    lax.broadcasted_iota(jnp.int32, (near, n), 0) == cell
                )
                cell = jnp.where(at_edge, row - start, -1)
                line_ref[side * m : (side + 1) * m, :] = as_onehot(lax.broadcasted_iota(jnp.int32, (m, n), 0) == cell)
        holder, layer, row = (columns[:, j : j + 1].astype(jnp.int32) for j in range(3))
        lane = lane_of(n)
        first = lane % GROUP < HALO
        here = lane // GROUP == layer + partner * layers
        for side, begin in enumerate((x - 1, x)):
            mine = jnp.logical_and(here, holder == jnp.where(first, begin, begin + 1))
            masks_ref[side * n : (side + 1) * n, :] = jnp.where(mine, 1.0, 0.0)
        if partner:
            continue
        mine = holder == x
        mine_ref[...] = jnp.where(jnp.logical_and(mine, lane >= 0), 1.0, 0.0)
        spoilt = None
        for side, (above, live) in enumerate(sides_of(gy, y)):
            start = edge_at(above, rows)
            part = jnp.logical_and(row // HALO == start // HALO, live)
            spoilt = part if spoilt is None else jnp.logical_or(spoilt, part)
            cell = jnp.where(jnp.logical_and(mine, part), layer * HALO + row - start, -1)
            beside_ref[side * n : (side + 1) * n, :] = as_onehot(lane == cell)
        cell = jnp.where(jnp.logical_and(mine, jnp.logical_not(spoilt)), layer * rows + row, -1)
        picks_ref[...] = as_onehot(lax.broadcasted_iota(jnp.int32, (n, plane), 1) == cell)


def join_kernel(mine_ref, *refs):
    out_ref, at = refs[-1], 0
    for ref in refs[:-1]:
        n = ref.shape[0]
        out_ref[at : at + n, :] = ref[...]
        at += n


def partner_rows(layers):
    whole, at = [], 1
    for i in range(layers - 1, -1, -1):
        whole.append((i, HALO - layers + i, at))
        at += HALO - layers + i
    stride = -(-at // 8) * 8
    later, at = [], 0
    for f in range(2):
        for i in range(layers - 1, -1, -1):
            if ITERS - 1 - layers + i > 0:
                later.append((f, i, ITERS - 1 - layers + i, at))
                at += ITERS - 1 - layers + i
    return whole, stride, later, -(-at // 8) * 8


def fill_kernel(partner, gx, gy, shape, seg, *refs):
    layers, rows = shape
    cells_ref, where_ref, rows_ref, masks_ref = refs[:4]
    plane, chunk = layers * rows, rows // 4
    lengths = lengths_of(gx, chunk, seg)
    x, z = lax.axis_index("gx"), lax.axis_index("gz")
    if partner:
        late_ref, out_ref, coef_ref, warmth_ref = refs[4:]
        sources = [(late_ref, sum(lengths[:k])) for k in range(gx - 1)]
        lay_segments(x, gx, seg, chunk, cells_ref, RAW * plane, sources, coef_ref, warmth_ref)
        coef, warmth = coef_ref[...], warmth_ref[...]
    else:
        right_ref, left_ref, segments_ref, out_ref = refs[4:]
        sources = [(right_ref, 0), (left_ref, 0)]
        n = segments_ref.shape[0] // 2
        coef, warmth = segments_ref[:n, :], segments_ref[n:, :]
    n = coef.shape[0]
    added = exact_dot(where_ref[...], coupling(coef, warmth))
    near = edge_columns(n, False)
    beside = []
    for side in range(2):
        masked = take(coef, near) * masks_ref[side * n : (side + 1) * n, :]
        beside.append(exact_dot(rows_ref[...], coupling(masked, take(warmth, near))))
    planes = layers + 2
    for i in range(layers):
        src = flip(z, layers, i)
        raw = [cells_ref[pl.ds(pl.multiple_of((f * layers + src) * rows, rows), rows), :] for f in range(RAW)]
        for f, value in enumerate(combine(raw, added[i * rows : (i + 1) * rows])):
            out_ref[f * planes + i] = value
    strips = Strips(
        [ref for ref, _ in sources[:2]], [at for _, at in sources[:2]], cells_ref, RAW * plane + 2 * seg, rows, layers
    )
    half = lane_of(chunk) // (LANES // 2) == (1 if partner else 0)
    for part in range(4):
        here = slice(part * chunk, (part + 1) * chunk)
        raw = [strips.both(f, part * chunk, chunk, x, gx, partner) for f in range(RAW)]
        for side in range(2):
            cells = [jnp.where(half, value[side], 0.0) for value in raw]
            for f, value in enumerate(combine(cells, beside[side][here])):
                out_ref[f * planes + layers + side, here, :] = value


def lay_segments(x, gx, seg, chunk, own_ref, at, sources, coef_ref, warmth_ref):
    distances = [1, gx - 1] + list(range(2, gx - 1))
    held = [(k, ref, at + (RAW * chunk if j < 2 else 0)) for j, (k, (ref, at)) in enumerate(zip(distances, sources))]
    place_segments(x, gx, seg, coef_ref, warmth_ref, [(0, own_ref, at)] + held)


def strip_kernel(gx, gy, shape, seg, *refs):
    layers, rows = shape
    cells_ref, near_ref, line_ref, masks_ref = refs[:4]
    received, refs = refs[4 : 4 + gx - 1], refs[4 + gx - 1 :]
    sides = 1 if gy == 2 else 2
    strip_refs, partner_refs, segments_ref = refs[:sides], refs[sides : 2 * sides], refs[2 * sides]
    plane, chunk = layers * rows, rows // 4
    x, y, z = (lax.axis_index(a) for a in ("gx", "gy", "gz"))
    n = segments_ref.shape[0] // 2
    coef_ref, warmth_ref = segments_ref.at[pl.ds(0, n), :], segments_ref.at[pl.ds(n, n), :]
    lay_segments(x, gx, seg, chunk, cells_ref, RAW * plane, [(ref, 0) for ref in received], coef_ref, warmth_ref)
    coef, warmth = coef_ref[...], warmth_ref[...]
    coupled = coupling(coef, warmth)
    columns = edge_columns(n, False)
    coef, warmth = take(coef, columns), take(warmth, columns)
    mask = jnp.where(lane_of(n) % GROUP < HALO, masks_ref[:n, :], masks_ref[n:, :])
    outer = coupling(coef * mask, warmth)
    strips = Strips(received[:2], [0, 0], cells_ref, RAW * plane + 2 * seg, rows, layers)
    low = lane_of(HALO) < LANES // 2
    first = lane_of(HALO) % GROUP < HALO
    upper = lax.broadcasted_iota(jnp.int32, (HALO, LANES), 0) < HALO // 2
    sent = FIELDS - 1

    def give(ref, at, values):
        for f, value in enumerate(values):
            ref[at + f * HALO : at + (f + 1) * HALO, :] = value

    def make(side, top):
        start = 0 if top else rows - HALO
        strip_ref, partner_ref = strip_refs[side], partner_refs[side]

        def shrink(values):
            *whole, e, g = values
            if top:
                g = pltpu.roll(g, HALO // 2, 0)
            else:
                e = pltpu.roll(e, HALO // 2, 0)
            return whole + [jnp.where(upper, e, g)]

        near = layers * HALO
        added = exact_dot(near_ref[side * near : (side + 1) * near, :], coupled)
        line = line_ref[side * 2 * HALO : (side + 1) * 2 * HALO, :]
        beside = exact_dot(line, outer)[:HALO]
        whole, stride, later, shared = partner_rows(layers)
        for i in range(layers):
            src = flip(z, layers, i)
            raw = [
                cells_ref[pl.ds(pl.multiple_of((f * layers + src) * rows + start, HALO), HALO), :] for f in range(RAW)
            ]
            values = combine(raw, added[i * HALO : (i + 1) * HALO])
            give(strip_ref, i * sent * HALO, shrink(values))
            pieces = [(f, m, f * stride + at) for f in range(sent - 1) for j, m, at in whole if j == i]
            pieces += [(sent - 1 + f, m, (sent - 1) * stride + at) for f, j, m, at in later if j == i]
            for f, m, at in pieces:
                skip = 0 if top else HALO - m
                partner_ref[at : at + m, :] = values[f][skip : skip + m]
        raw = [jnp.where(first, *strips.both(f, start, HALO, x, gx, False)) for f in range(RAW)]
        values = shrink(combine(raw, beside))
        values = [jnp.where(low, values[j], pltpu.roll(values[j + 1], LANES // 2, 1)) for j in range(0, sent, 2)]
        give(strip_ref, layers * sent * HALO, values)
        give(partner_ref, (sent - 1) * stride + shared, values)

    for side, (top, _) in enumerate(sides_of(gy, y)):
        if top is True or top is False:
            make(side, top)
        else:
            pl.when(top)(functools.partial(make, side, True))
            pl.when(jnp.logical_not(top))(functools.partial(make, side, False))


def planes_of(count, total):
    return list(range(count)) + [total - 2, total - 1]


def lateral(buf, at, n, which):
    sums = []
    for i in which:
        centre = buf[i, pl.ds(at, n), :]
        beside = pltpu.roll(centre, 1, 1) + pltpu.roll(centre, LANES - 1, 1)
        sums.append(beside + (buf[i, pl.ds(at - 1, n), :] + buf[i, pl.ds(at + 1, n), :]))
    return sums


def vertical(planes, edges, count):
    sums = []
    for i in range(count):
        near = [planes[j] for j in (i - 1, i + 1) if 0 <= j < len(planes)]
        sums.append(functools.reduce(jnp.add, near))
    for edge in edges:
        lane = lane_of(edge.shape[0])
        up = jnp.where(lane >= GROUP, pltpu.roll(edge, GROUP, 1), 0.0)
        down = jnp.where(lane < LANES - GROUP, pltpu.roll(edge, LANES - GROUP, 1), 0.0)
        sums.append(up + down)
    return sums


def coefficients(s_ref, at, n, raw, dests, to, outside):
    a_ref, q_ref, r_ref, e_ref, g_ref, root_ref = dests
    total = s_ref.shape[0]
    sums = lateral(s_ref, at, n, range(total))
    t = [raw(1, i) for i in range(total)]
    above = vertical(t[:-2], t[-2:], total - 2)
    here = pl.ds(to, n)
    for i in range(total):
        s = s_ref[i, pl.ds(at, n), :]
        diag = raw(3, i) + s * sums[i] + t[i] * above[i]
        if outside or i >= total - 2:
            inverse = 1.0 / jnp.where(diag > 0.0, diag, 1.0)
            root = jnp.where(s > 0.0, 1.0 / jnp.where(s > 0.0, s, 1.0), 0.0)
        else:
            inverse, root = 1.0 / diag, 1.0 / s
        if i < root_ref.shape[0]:
            root_ref[i, here, :] = root
        scaled = s * inverse
        a_ref[i, here, :] = s * scaled
        r_ref[i, here, :] = raw(4, i) * scaled
        e_ref[i, here, :] = raw(5, i) * scaled
        g_ref[i, here, :] = raw(6, i) * inverse
        q_ref[i, here, :] = t[i] * root


def shifted_sums(distance):
    to = lax.broadcasted_iota(jnp.int32, (2 * LANES, LANES), 1)
    of = lax.broadcasted_iota(jnp.int32, (2 * LANES, LANES), 0) % LANES
    return as_onehot(jnp.abs(of - to) == distance)


def sweep_edges(src_ref, dst_ref, at, n, coefs, base, matrices):
    a_ref, q_ref, r_ref = coefs[:3]
    total = src_ref.shape[0]
    here, there = pl.ds(base, n), pl.ds(at, n)

    def product(value, matrix):
        return jnp.dot(jnp.concatenate(split(value), axis=1), matrix, preferred_element_type=jnp.float32)

    for i in (total - 2, total - 1):
        centre = src_ref[i, there, :]
        beside = product(centre, matrices[0])
        above = product(q_ref[i, here, :] * centre, matrices[1])
        beside = beside + (src_ref[i, pl.ds(at - 1, n), :] + src_ref[i, pl.ds(at + 1, n), :])
        dst_ref[i, there, :] = r_ref[i, here, :] + a_ref[i, here, :] * (beside + q_ref[i, here, :] * above)


def sweep(src_ref, dst_ref, at, n, count, coefs, base, edges=True):
    a_ref, q_ref, r_ref = coefs[:3]
    total = src_ref.shape[0]
    here, there = pl.ds(base, n), pl.ds(at, n)
    which = planes_of(count, total) if edges else list(range(count))
    sums = lateral(src_ref, at, n, which)
    scaled = [q_ref[i, here, :] * src_ref[i, there, :] for i in range(min(count + 1, total - 2))]
    outer = [q_ref[i, here, :] * src_ref[i, there, :] for i in which[count:]]
    above = vertical(scaled, outer, count)
    for j, i in enumerate(which):
        dst_ref[i, there, :] = r_ref[i, here, :] + a_ref[i, here, :] * (sums[j] + q_ref[i, here, :] * above[j])


def next_rhs(coefs, v_ref, at, n, base):
    r_ref, e_ref, g_ref = coefs[2:5]
    here = pl.ds(base, n)
    for i in range(v_ref.shape[0]):
        r_ref[i, here, :] = e_ref[i, here, :] + g_ref[i, here, :] * v_ref[i, pl.ds(at, n), :]


def meet(v_ref, at, n, count, back):
    total = v_ref.shape[0]
    here = pl.ds(at, n)
    lane = lane_of(n)
    j, group = lane % GROUP, lane // GROUP
    outer = jnp.logical_or(lane < ITERS, lane >= LANES - ITERS)
    left, right = v_ref[total - 2, here, :], v_ref[total - 1, here, :]
    middle = jnp.where(j < HALO, right, left)
    for i in range(count):
        value = v_ref[i, here, :]
        if back:
            moved = pltpu.roll(value, (i * GROUP + HALO) % LANES, 1)
            left = jnp.where(jnp.logical_and(group == i, j >= GROUP - ITERS), moved, left)
            right = jnp.where(jnp.logical_and(group == i, j < ITERS), moved, right)
        v_ref[i, here, :] = jnp.where(outer, pltpu.roll(middle, LANES - (i * GROUP + HALO), 1), value)
    if back:
        v_ref[total - 2, here, :] = left
        v_ref[total - 1, here, :] = right


def needed(layers, n):
    return min(2 * layers, layers + STEPS * ITERS - 1 - n)


def two_steps(layers, sweep_all, between, after):
    for step in range(STEPS):
        for n in range(step * ITERS, (step + 1) * ITERS):
            sweep_all(n, n % 2, needed(layers, n))
        after(step)
        if step < STEPS - 1:
            between()


PAD = 8


def tile_kernel(gx, gy, shape, *refs):
    layers, rows = shape
    own_ref, partner_ref, picks_ref, out_ref, below_ref, level_ref = refs[:6]
    s_ref, va_ref, vb_ref = refs[6:9]
    coefs = refs[9:]
    x, y, z = (lax.axis_index(a) for a in ("gx", "gy", "gz"))
    total = 2 * layers + 2
    zeros = jnp.zeros((PAD, LANES), jnp.float32)
    for ref in (s_ref, va_ref, vb_ref):
        for i in range(total):
            ref[i, 0:PAD, :] = zeros
            ref[i, PAD + rows : PAD + rows + PAD, :] = zeros

    def field(f, i, here):
        j = f * (layers + 2)
        if i >= 2 * layers:
            j = j + i - layers
            return own_ref[j, here, :] + partner_ref[j, here, :]
        return own_ref[j + i, here, :] if i < layers else partner_ref[j + i - layers, here, :]

    for i in range(total):
        s_ref[i, PAD : PAD + rows, :] = field(0, i, slice(None))
        va_ref[i, PAD : PAD + rows, :] = field(2, i, slice(None))
    n = 8
    for at in range(0, rows, n):
        coefficients(s_ref, PAD + at, n, lambda f, i: field(f, i, slice(at, at + n)), coefs, at, False)

    bufs = (va_ref, vb_ref)
    sides = sides_of(gy, y)
    matrices = shifted_sums(1), shifted_sums(GROUP)

    def sweep_all(number, which, count):
        src_ref, dst_ref = bufs[which], bufs[1 - which]
        for side, (above, _) in enumerate(sides):
            inner = pl.ds(PAD + inner_at(above, rows), HALO)
            for i in range(total):
                level_ref[(side * STEPS * ITERS + number) * total + i] = src_ref[i, inner, :]
        sweep_edges(src_ref, dst_ref, PAD, rows, coefs, 0, matrices)
        for at in range(0, rows, n):
            sweep(src_ref, dst_ref, PAD + at, n, count, coefs, at, edges=False)

    def after(step):
        last = step == STEPS - 1
        for at in range(0, rows, n):
            meet(va_ref, PAD + at, n, layers if last else 2 * layers, not last)
        heat = []
        for i in range(layers):
            here = pl.ds(PAD, rows)
            heat.append(va_ref[i, here, :] * coefs[5][i])
            if step == STEPS - 1:
                out_ref[flip(z, layers, i)] = heat[-1]
        below_ref[step] = exact_dot(picks_ref[...], jnp.concatenate(heat, axis=0))

    def between():
        for at in range(0, rows, n):
            next_rhs(coefs, va_ref, PAD + at, n, at)

    two_steps(layers, sweep_all, between, after)


def edge_kernel(gx, gy, shape, seg, *refs):
    layers, rows = shape
    own_ref, partner_ref, picks_ref, mine_ref, segments_ref, below_ref, level_ref = refs[:7]
    sides_n = 1 if gy == 2 else 2
    along, across = refs[7 : 7 + sides_n], refs[7 + sides_n : 7 + 2 * sides_n]
    refs = refs[7 + 2 * sides_n :]
    heat_ref, returns = refs[0], refs[1 : 1 + gx]
    ret_ref, s_ref, va_ref, vb_ref = refs[1 + gx : 5 + gx]
    coefs = refs[5 + gx :]
    x, y, z = (lax.axis_index(a) for a in ("gx", "gy", "gz"))
    total = 2 * layers + 2
    count = mine_ref.shape[0]
    below = [below_ref[step] for step in range(STEPS)]
    lane = lane_of(HALO)
    low, first = lane < LANES // 2, lane % GROUP < HALO
    columns = edge_columns(HALO, False)
    bufs = (va_ref, vb_ref)

    def tile(j):
        return pl.ds(j if isinstance(j, int) else pl.multiple_of(j, HALO), HALO)

    for side, (above, live) in enumerate(sides_of(gy, y)):
        def place(when_top, otherwise):
            if above is True or above is False:
                return when_top * HALO if above else otherwise * HALO
            return jnp.where(above, when_top * HALO, otherwise * HALO)

        outer, strip, edge, inner = place(0, 3), place(1, 2), place(2, 1), place(3, 0)
        edge_rows = tile(edge_at(above, rows))
        inner_rows = tile(inner_at(above, rows))

        def field(f, i, here):
            j = f * (layers + 2)
            if i >= 2 * layers:
                j = j + i - layers
                return own_ref[j, here, :] + partner_ref[j, here, :]
            return own_ref[j + i, here, :] if i < layers else partner_ref[j + i - layers, here, :]

        t_ref, d_ref, q_ref, e_ref, g_ref = coefs[1], coefs[0], coefs[2], coefs[3], coefs[4]
        keep = {0: s_ref, 1: t_ref, 2: va_ref, 3: d_ref, 4: q_ref, 5: e_ref, 6: g_ref}
        zeros = jnp.zeros((HALO, LANES), jnp.float32)
        src = lane % (LANES // 2)
        turned = (layers - 1 - src // GROUP) * GROUP + src % GROUP
        half_tile = lax.broadcasted_iota(jnp.int32, (HALO, LANES), 0) < HALO // 2

        def unpack(value, f):
            if f < FIELDS - 2:
                return value
            turned_value = pltpu.roll(value, HALO // 2, 0)
            if f == FIELDS - 2:
                at_top, at_bottom = jnp.where(half_tile, 0.0, turned_value), jnp.where(half_tile, value, 0.0)
            else:
                at_top, at_bottom = jnp.where(half_tile, 0.0, value), jnp.where(half_tile, turned_value, 0.0)
            return jnp.where(above, at_top, at_bottom)

        whole, stride, later, shared = partner_rows(layers)
        sublane = lax.broadcasted_iota(jnp.int32, (HALO, LANES), 0)

        def nearest(ref, m, at):
            at_top = jnp.where(sublane >= HALO - m, ref[at - HALO + m : at + m, :], 0.0)
            return jnp.where(above, at_top, jnp.where(sublane < m, ref[at : at + HALO, :], 0.0))

        for f in range(FIELDS):
            g = min(f, FIELDS - 2)
            if f < FIELDS - 2:
                rows_of = {i: (m, f * stride + at) for i, m, at in whole}
            else:
                rows_of = {i: (m, (FIELDS - 2) * stride + at) for which, i, m, at in later if which == f - FIELDS + 2}
            values, inside = [], zeros
            for i in range(2 * layers):
                if i < layers:
                    at = (i * (FIELDS - 1) + g) * HALO
                    value = unpack(along[side][at : at + HALO, :], f)
                else:
                    j = 2 * layers - 1 - i
                    value = nearest(across[side], *rows_of[j]) if j in rows_of else zeros
                values.append(value)
                inside = jnp.where(lane // GROUP == i, take(value, columns), inside)
            half = (LANES // 2) * (g % 2)
            at = (layers * (FIELDS - 1) + g // 2) * HALO
            a = take(along[side][at : at + HALO, :], src + half)
            at = (FIELDS - 2) * stride + shared + (g // 2) * HALO
            b = take(across[side][at : at + HALO, :], turned + half)
            outside = unpack(jnp.where(low, a, b), f)
            values += [jnp.where(first, outside, inside), jnp.where(first, inside, outside)]
            for i, value in enumerate(values):
                ref, shift = keep[f], 0 if f in (0, 2) else HALO
                ref[i, tile(strip - shift), :] = value
                ref[i, tile(edge - shift), :] = field(f, i, edge_rows)
        for i in range(total):
            s_ref[i, tile(outer), :] = zeros
            va_ref[i, tile(outer), :] = zeros
            vb_ref[i, tile(outer), :] = zeros
            s_ref[i, tile(inner), :] = field(0, i, inner_rows)
        n = 2 * HALO
        held = [[keep[f][i, pl.ds(0, n), :] for i in range(total)] if f in (1, 3, 4, 5, 6) else None for f in range(FIELDS)]
        coefficients(s_ref, HALO, n, lambda f, i: held[f][i], coefs, 0, True)

        def sweep_all(number, which, needed_layers):
            src_ref, dst_ref = bufs[which], bufs[1 - which]
            for i in range(total):
                src_ref[i, tile(inner), :] = level_ref[(side * STEPS * ITERS + number) * total + i]
            sweep(src_ref, dst_ref, HALO, n, needed_layers, coefs, 0)

        picks = picks_ref[side * count : (side + 1) * count, :]

        def after(step):
            last = step == STEPS - 1
            meet(va_ref, HALO, n, layers if last else 2 * layers, not last)
            heat = []
            for i in range(layers):
                heat.append(va_ref[i, tile(edge), :] * coefs[5][i, tile(edge - HALO), :])
                if step == STEPS - 1:
                    heat_ref[side * layers + flip(z, layers, i)] = heat[-1]
            heat.append(jnp.zeros((LANES - layers * HALO, LANES), jnp.float32))
            below[step] = below[step] + exact_dot(picks, jnp.concatenate(heat, axis=0))

        two_steps(layers, sweep_all, lambda: next_rhs(coefs, va_ref, HALO, n, 0), after)

    coef, warmth = segments_ref[:count, :], segments_ref[count:, :]
    for step in range(STEPS):
        warmth = warmth + coolant_gain * coef * (below[step] - warmth)
    ret_ref[...] = jnp.where(mine_ref[...] > 0.0, warmth, 0.0)
    for k, ref in enumerate(returns):
        ref[...] = ret_ref[pl.ds(pl.multiple_of(lax.rem(x + k, gx) * seg, seg), seg), :]


def merge_kernel(gy, whole_ref, heat_ref, out_ref):
    layers, rows, _ = whole_ref.shape
    out_ref[...] = whole_ref[...]
    for side, (above, live) in enumerate(sides_of(gy, lax.axis_index("gy"))):
        def put(side=side, above=above):
            out_ref[:, pl.ds(edge_at(above, rows), HALO), :] = heat_ref[side * layers : (side + 1) * layers]

        if live is True:
            put()
        else:
            pl.when(live)(put)


def local(gx, gy, gz, u, power, storage, conductance, warmth, coef, holder, stratum, transverse):
    layers, rows, columns = u.shape
    seg = warmth.shape[1]
    segments = stratum.shape[1]
    if gz != 2 or gx < 3 or columns != LANES or 2 * layers * GROUP != LANES or rows % 32:
        raise ValueError("unsupported shape")
    holder = holder[:, :, 0]
    shape = (layers, rows)
    f32 = jnp.float32
    chunk = rows // 4
    wide = RAW * chunk + 2 * seg

    def struct(*dims):
        return jax.ShapeDtypeStruct(dims, f32)

    def vmem(*dims):
        return pltpu.VMEM(dims, f32)

    indices = (holder, stratum, transverse)
    flat = [a.reshape(-1, LANES) for a in (u, power, storage, conductance, warmth, coef)]
    own, to_left, to_right, only, *indices = pl.pallas_call(
        functools.partial(pack_kernel, shape),
        out_shape=(
            struct(RAW * layers * rows + 2 * seg + 2 * RAW * chunk, LANES),
            struct(wide, LANES),
            struct(wide, LANES),
            struct(2 * seg, LANES),
            *(jax.ShapeDtypeStruct(a.shape, a.dtype) for a in indices),
        ),
        in_specs=[pl.BlockSpec(memory_space=pltpu.HBM)] * 9,
        out_specs=(VMEM,) * 7,
        scratch_shapes=[pltpu.SemaphoreType.DMA((9,))],
        compiler_params=PARAMS,
        name="pack",
    )(*(pltpu.with_memory_space_constraint(a, pltpu.HBM) for a in (*flat, *indices)))

    swap = [(0, 1), (1, 0)]
    partner = lax.ppermute(own, "gz", swap)
    def from_distance(value, k):
        return lax.ppermute(value, "gx", [(i, (i - k) % gx) for i in range(gx)])

    from_left = from_distance(to_right, gx - 1)
    received = [from_distance(to_left, 1), from_left]
    received += [from_distance(only, k) for k in range(2, gx - 1)]

    sides = 1 if gy == 2 else 2
    fields = struct(FIELDS * (layers + 2), rows, LANES)
    strip_rows = (FIELDS - 1) * layers * HALO + (FIELDS - 1) // 2 * HALO
    _, stride, _, shared = partner_rows(layers)
    partner_strip = (FIELDS - 2) * stride + shared + (FIELDS - 1) // 2 * HALO
    sides = 1 if gy == 2 else 2
    bf16 = jnp.bfloat16
    one_group = (
        jax.ShapeDtypeStruct((layers * rows, segments), bf16),
        jax.ShapeDtypeStruct((rows, segments), bf16),
        struct(2 * segments, LANES),
    )
    maps = pl.pallas_call(
        functools.partial(maps_kernel, gx, gy, shape),
        out_shape=one_group
        + one_group
        + (
            jax.ShapeDtypeStruct((segments, layers * rows), bf16),
            jax.ShapeDtypeStruct((sides * segments, LANES), bf16),
            struct(segments, LANES),
            jax.ShapeDtypeStruct((sides * layers * HALO, segments), bf16),
            jax.ShapeDtypeStruct((sides * 2 * HALO, segments), bf16),
        ),
        in_specs=[VMEM] * 3,
        out_specs=(VMEM,) * 11,
        compiler_params=PARAMS,
        cost_estimate=cost(1),
        name="maps",
    )(*indices)
    own_maps, partner_maps, (picks, picks_beside, mine, near, line) = maps[:3], maps[3:6], maps[6:]
    joined = pl.pallas_call(
        join_kernel,
        out_shape=struct(sum(a.shape[0] for a in received), LANES),
        in_specs=[pl.BlockSpec(memory_space=pl.ANY)] + [VMEM] * (gx - 1),
        out_specs=VMEM,
        compiler_params=PARAMS,
        name="join",
    )(mine, *received)
    late = lax.ppermute(joined, "gz", swap)
    made = pl.pallas_call(
        functools.partial(strip_kernel, gx, gy, shape, seg),
        out_shape=(struct(strip_rows, LANES),) * sides
        + (struct(partner_strip, LANES),) * sides
        + (struct(2 * segments, LANES),),
        in_specs=[VMEM] * (4 + gx - 1),
        out_specs=(VMEM,) * (1 + 2 * sides),
        compiler_params=PARAMS,
        cost_estimate=cost(0.5),
        name="strips",
    )(own, near, line, own_maps[2], *received)
    strips, partner_strips, held = made[:sides], made[sides : 2 * sides], made[2 * sides]
    own_fields = pl.pallas_call(
        functools.partial(fill_kernel, False, gx, gy, shape, seg),
        out_shape=fields,
        in_specs=[VMEM] * 7,
        out_specs=VMEM,
        compiler_params=PARAMS,
        cost_estimate=cost(1.5),
        name="fill_own",
    )(own, *own_maps, *received[:2], held)
    if gy == 2:
        routes = [(0, swap)]
    else:
        up = [(i, i + 1) for i in range(gy - 1)]
        routes = [(1, up), (0, [(j, i) for i, j in up])]
    along = [lax.ppermute(strips[side], "gy", pairs) for side, pairs in routes]
    across = []
    for side, pairs in routes:
        both = [(2 * i + z, 2 * j + 1 - z) for i, j in pairs for z in range(2)]
        across.append(lax.ppermute(partner_strips[side], ("gy", "gz"), both))

    partner_fields = pl.pallas_call(
        functools.partial(fill_kernel, True, gx, gy, shape, seg),
        out_shape=fields,
        in_specs=[VMEM] * 5,
        out_specs=VMEM,
        scratch_shapes=[vmem(segments, LANES)] * 2,
        compiler_params=PARAMS,
        cost_estimate=cost(1.5),
        name="fill_partner",
    )(partner, *partner_maps, late)

    total = 2 * layers + 2
    padded = vmem(total, rows + 2 * PAD, LANES)
    inside, below, levels = pl.pallas_call(
        functools.partial(tile_kernel, gx, gy, shape),
        out_shape=(
            struct(layers, rows, LANES),
            struct(STEPS, segments, LANES),
            struct(sides * STEPS * ITERS * total, HALO, LANES),
        ),
        in_specs=[VMEM] * 3,
        out_specs=(VMEM,) * 3,
        scratch_shapes=[padded] * 3 + [vmem(total, rows, LANES)] * 5 + [vmem(layers, rows, LANES)],
        compiler_params=PARAMS,
        cost_estimate=cost(7),
        name="tile_sweeps",
    )(own_fields, partner_fields, picks)

    results = pl.pallas_call(
        functools.partial(edge_kernel, gx, gy, shape, seg),
        out_shape=(struct(sides * layers, HALO, LANES),) + (struct(seg, LANES),) * gx,
        in_specs=[VMEM] * (7 + 2 * sides),
        out_specs=(VMEM,) * (1 + gx),
        scratch_shapes=[vmem(segments, LANES)]
        + [vmem(total, 4 * HALO, LANES)] * 3
        + [vmem(total, 2 * HALO, LANES)] * 5
        + [vmem(layers, 2 * HALO, LANES)],
        compiler_params=PARAMS,
        cost_estimate=cost(1.5),
        name="edge_sweeps",
    )(own_fields, partner_fields, picks_beside, mine, held, below, levels, *along, *across)
    heat, coolant = results[0], results[1]
    returned = [lax.ppermute(results[1 + k], "gx", [(i, (i + k) % gx) for i in range(gx)]) for k in range(1, gx)]
    temperature = pl.pallas_call(
        functools.partial(merge_kernel, gy),
        out_shape=struct(layers, rows, LANES),
        in_specs=[VMEM] * 2,
        out_specs=VMEM,
        compiler_params=PARAMS,
        cost_estimate=cost(1),
        name="merge",
    )(inside, heat)
    for value in returned:
        coolant = coolant + value
    return temperature, coolant[None]


def solution(mesh):
    gx, gy, gz = (mesh.shape[a] for a in ("gx", "gy", "gz"))
    cells = P(("stack", "gz"), "gy", "gx")
    segments = P(("stack", "gy", "gz"), "gx", None)
    return jax.shard_map(
        functools.partial(local, gx, gy, gz),
        mesh=mesh,
        in_specs=(cells, cells, cells, P(None, ("stack", "gz"), "gy", "gx"), segments, segments, P(), P(), P()),
        out_specs=(cells, segments),
        check_vma=False,
    )
```

```python
import functools

import jax
import jax.numpy as jnp
from jax import lax
from jax.experimental import pallas as pl
from jax.experimental.pallas import tpu as pltpu
from jax.sharding import PartitionSpec as P

STEPS = 2
ITERS = 4
HALO = STEPS * ITERS
GROUP = 2 * HALO
LANES = 128
RAW = 5
FIELDS = 7
coolant_gain = 0.5

VMEM = pl.BlockSpec(memory_space=pltpu.VMEM)
PARAMS = pltpu.CompilerParams(vmem_limit_bytes=40 * 1024 * 1024)


def cost(microseconds):
    return pl.CostEstimate(flops=0, bytes_accessed=int(microseconds * 3e6), transcendentals=0)


def lane_of(rows):
    return lax.broadcasted_iota(jnp.int32, (rows, LANES), 1)


def take(value, index):
    return jnp.take_along_axis(value, index, axis=1, mode="promise_in_bounds")


def edge_columns(rows, turned):
    j = lane_of(rows) % GROUP
    first = j < HALO
    return jnp.where(first, LANES - HALO + j, j - HALO) if not turned else jnp.where(first, j, LANES - GROUP + j)


def split(value):
    high = value.astype(jnp.bfloat16)
    low = (value - high.astype(jnp.float32)).astype(jnp.bfloat16)
    return high, low


def exact_dot(onehot, value):
    high, low = split(value)
    both = jnp.concatenate([high, low], axis=0)
    return jnp.dot(jnp.concatenate([onehot, onehot], axis=1), both, preferred_element_type=jnp.float32)


def coupling(coef, warmth):
    flow = coef * warmth
    second = coolant_gain * coef * coef
    return jnp.concatenate([coef, flow, second, flow - second * warmth], axis=1)


def flip(z, layers, i):
    return jnp.where(z == 0, i, layers - 1 - i)


def pack_kernel(shape, u_ref, p_ref, c_ref, k_ref, f_ref, x_ref, *refs):
    own_ref, left_ref, right_ref, seg_ref = refs[3:7]
    sems = refs[-1]
    layers, rows = shape
    seg = f_ref.shape[0]
    z = lax.axis_index("gz")
    plane = layers * rows
    copies = []

    def fetch(src, dst):
        copies.append(pltpu.make_async_copy(src, dst, sems.at[len(copies)]))
        copies[-1].start()

    fetch(k_ref, own_ref.at[pl.ds(0, 2 * plane), :])
    for field, ref in enumerate((u_ref, p_ref, c_ref), 2):
        fetch(ref, own_ref.at[pl.ds(field * plane, plane), :])
    for j, ref in enumerate((x_ref, f_ref)):
        fetch(ref, own_ref.at[pl.ds(RAW * plane + j * seg, seg), :])
    for table, place in zip(refs[:3], refs[7:10]):
        fetch(table, place)
    chunk = rows // 4
    lane = lane_of(chunk)
    first = lane % GROUP < HALO
    columns = edge_columns(chunk, False), edge_columns(chunk, True)
    edges = RAW * plane + 2 * seg

    def gather(field, at, g):
        value = None
        for i in range(layers):
            start = pl.multiple_of((field * layers + flip(z, layers, i)) * rows + at, chunk)
            taken = take(own_ref[pl.ds(start, chunk), :], columns[g % 2])
            value = taken if value is None else jnp.where(lane // GROUP == (g // 2) * layers + i, taken, value)
        return value

    def place(g, part):
        return pl.ds(edges + ((g % 2) * RAW + part) * chunk, chunk)

    copies[0].wait()
    roots = pl.ds(0, 2 * plane)
    own_ref[roots, :] = jnp.sqrt(own_ref[roots, :])
    for field in range(4):
        if field >= 2:
            copies[field - 1].wait()
        for part in range(4):
            value = gather(field, part * chunk, field)
            if field >= 2:
                value = jnp.where(lane < LANES // 2, own_ref[place(field, part), :], value)
            own_ref[place(field, part), :] = value
    copies[3].wait()
    for g in range(4):
        value = gather(4, g * chunk, g)
        if g >= 2:
            value = jnp.where(lane < LANES // 2, own_ref[place(g, 4), :], value)
        own_ref[place(g, 4), :] = value
    for part in range(RAW):
        even, odd = own_ref[place(0, part), :], own_ref[place(1, part), :]
        left_ref[part * chunk : (part + 1) * chunk, :] = jnp.where(first, odd, even)
        right_ref[part * chunk : (part + 1) * chunk, :] = jnp.where(first, even, odd)
    for copy in copies[4:]:
        copy.wait()
    segments = own_ref[RAW * plane : RAW * plane + 2 * seg, :]
    seg_ref[...] = segments
    left_ref[RAW * chunk :, :] = segments
    right_ref[RAW * chunk :, :] = segments


class Strips:
    def __init__(self, refs, starts, cells_ref, start, rows, layers):
        self.refs, self.starts = refs, starts
        self.cells_ref, self.start = cells_ref, start
        self.rows, self.layers = rows, layers

    def both(self, field, start, n, x, gx, partner):
        chunk = self.rows // 4
        if field < 4:
            g, at = field, start
        else:
            g, at = start // chunk, 4 * chunk + start % chunk
        a, b = (ref[at + begin : at + begin + n, :] for ref, begin in zip(self.refs, self.starts))
        at = self.start + (g % 2) * RAW * chunk + at
        inside = self.cells_ref[at : at + n, :]
        from_left, from_right = jnp.where(x > 0, b, 0.0), jnp.where(x < gx - 1, a, 0.0)
        lane = lane_of(n)
        first = (lane % GROUP < HALO) if g % 2 == 0 else (lane % GROUP >= HALO)
        half = self.layers * GROUP
        src = lane % half
        if partner:
            src = (self.layers - 1 - src // GROUP) * GROUP + src % GROUP
        if g % 2 == 1:
            src = jnp.where(src % GROUP < HALO, src + HALO, src - HALO)
        src = src + half * (g // 2)
        return take(jnp.where(first, from_left, inside), src), take(jnp.where(first, inside, from_right), src)


def place_segments(x, gx, seg, coef_ref, warmth_ref, sources):
    for k, ref, at in sources:
        place = pl.ds(pl.multiple_of(lax.rem(x + k, gx) * seg, seg), seg)
        coef_ref[place, :] = ref[at : at + seg, :]
        warmth_ref[place, :] = ref[at + seg : at + 2 * seg, :]


def tables(z, group, layers, holder_ref, stratum_ref, transverse_ref):
    holder = holder_ref[pl.ds(group, 1), :]
    layer = stratum_ref[pl.ds(group, 1), :]
    layer = jnp.where(z == 0, layer, layers - 1 - layer)
    row = transverse_ref[pl.ds(group, 1), :]
    n = holder.shape[1]
    which = lax.broadcasted_iota(jnp.int32, (8, n), 0)
    stacked = jnp.where(which == 0, holder, jnp.where(which == 1, layer, row))
    eye = lax.broadcasted_iota(jnp.int32, (n, n), 0) == lax.broadcasted_iota(jnp.int32, (n, n), 1)
    columns = lax.dot_general(
        eye.astype(jnp.float32).astype(jnp.bfloat16),
        stacked.astype(jnp.float32).astype(jnp.bfloat16),
        (((1,), (1,)), ((), ())),
        preferred_element_type=jnp.float32,
    )
    return (holder, layer, row), columns


def as_onehot(mask):
    return jnp.where(mask, 1.0, 0.0).astype(jnp.bfloat16)


def combine(raw, added):
    s, t, u, power, storage = raw
    wall, flow, second, later = (added[:, i * LANES : (i + 1) * LANES] for i in range(4))
    return s, t, s * u, storage + wall, power + storage * u + flow, power + later, storage + second


def lengths_of(gx, chunk, seg):
    return [RAW * chunk + 2 * seg] * 2 + [2 * seg] * (gx - 3)


def edge_at(top, rows):
    return 0 if top is True else rows - HALO if top is False else pl.multiple_of(jnp.where(top, 0, rows - HALO), HALO)


def inner_at(top, rows):
    return HALO if top is True else rows - 2 * HALO if top is False else pl.multiple_of(jnp.where(top, HALO, rows - 2 * HALO), HALO)


def sides_of(gy, y):
    return [(y == 1, True)] if gy == 2 else [(True, y > 0), (False, y < gy - 1)]


def maps_kernel(gx, gy, shape, holder_ref, stratum_ref, transverse_ref, *refs):
    layers, rows = shape
    plane = layers * rows
    picks_ref, beside_ref, mine_ref, near_ref, line_ref = refs[6:]
    x, y, z = (lax.axis_index(a) for a in ("gx", "gy", "gz"))
    n = holder_ref.shape[1]
    for partner in range(2):
        cells_ref, rows_ref, masks_ref = refs[3 * partner : 3 * partner + 3]
        group = y * 2 + ((1 - z) if partner else z)
        (holder, layer, row), columns = tables(z, group, layers, holder_ref, stratum_ref, transverse_ref)
        cell = jnp.where(holder == x, layer * rows + row, -1)
        cells_ref[...] = as_onehot(lax.broadcasted_iota(jnp.int32, (plane, n), 0) == cell)
        rows_ref[...] = as_onehot(lax.broadcasted_iota(jnp.int32, (rows, n), 0) == row)
        if not partner:
            near, m = layers * HALO, 2 * HALO
            for side, (above, _) in enumerate(sides_of(gy, y)):
                start = edge_at(above, rows)
                at_edge = row // HALO == start // HALO
                cell = jnp.where(jnp.logical_and(holder == x, at_edge), layer * HALO + row - start, -1)
                near_ref[side * near : (side + 1) * near, :] = as_onehot(
                    lax.broadcasted_iota(jnp.int32, (near, n), 0) == cell
                )
                cell = jnp.where(at_edge, row - start, -1)
                line_ref[side * m : (side + 1) * m, :] = as_onehot(lax.broadcasted_iota(jnp.int32, (m, n), 0) == cell)
        holder, layer, row = (columns[:, j : j + 1].astype(jnp.int32) for j in range(3))
        lane = lane_of(n)
        first = lane % GROUP < HALO
        here = lane // GROUP == layer + partner * layers
        for side, begin in enumerate((x - 1, x)):
            mine = jnp.logical_and(here, holder == jnp.where(first, begin, begin + 1))
            masks_ref[side * n : (side + 1) * n, :] = jnp.where(mine, 1.0, 0.0)
        if partner:
            continue
        mine = holder == x
        mine_ref[...] = jnp.where(jnp.logical_and(mine, lane >= 0), 1.0, 0.0)
        spoilt = None
        for side, (above, live) in enumerate(sides_of(gy, y)):
            start = edge_at(above, rows)
            part = jnp.logical_and(row // HALO == start // HALO, live)
            spoilt = part if spoilt is None else jnp.logical_or(spoilt, part)
            cell = jnp.where(jnp.logical_and(mine, part), layer * HALO + row - start, -1)
            beside_ref[side * n : (side + 1) * n, :] = as_onehot(lane == cell)
        cell = jnp.where(jnp.logical_and(mine, jnp.logical_not(spoilt)), layer * rows + row, -1)
        picks_ref[...] = as_onehot(lax.broadcasted_iota(jnp.int32, (n, plane), 1) == cell)


def join_kernel(mine_ref, *refs):
    out_ref, at = refs[-1], 0
    for ref in refs[:-1]:
        n = ref.shape[0]
        out_ref[at : at + n, :] = ref[...]
        at += n


def partner_rows(layers):
    whole, at = [], 1
    for i in range(layers - 1, -1, -1):
        whole.append((i, HALO - layers + i, at))
        at += HALO - layers + i
    stride = -(-at // 8) * 8
    later, at = [], 0
    for f in range(2):
        for i in range(layers - 1, -1, -1):
            if ITERS - 1 - layers + i > 0:
                later.append((f, i, ITERS - 1 - layers + i, at))
                at += ITERS - 1 - layers + i
    return whole, stride, later, -(-at // 8) * 8


def fill_kernel(partner, gx, gy, shape, seg, *refs):
    layers, rows = shape
    cells_ref, where_ref, rows_ref, masks_ref = refs[:4]
    plane, chunk = layers * rows, rows // 4
    lengths = lengths_of(gx, chunk, seg)
    x, z = lax.axis_index("gx"), lax.axis_index("gz")
    if partner:
        late_ref, out_ref, coef_ref, warmth_ref = refs[4:]
        sources = [(late_ref, sum(lengths[:k])) for k in range(gx - 1)]
        lay_segments(x, gx, seg, chunk, cells_ref, RAW * plane, sources, coef_ref, warmth_ref)
        coef, warmth = coef_ref[...], warmth_ref[...]
    else:
        right_ref, left_ref, segments_ref, out_ref = refs[4:]
        sources = [(right_ref, 0), (left_ref, 0)]
        n = segments_ref.shape[0] // 2
        coef, warmth = segments_ref[:n, :], segments_ref[n:, :]
    n = coef.shape[0]
    added = exact_dot(where_ref[...], coupling(coef, warmth))
    near = edge_columns(n, False)
    beside = []
    for side in range(2):
        masked = take(coef, near) * masks_ref[side * n : (side + 1) * n, :]
        beside.append(exact_dot(rows_ref[...], coupling(masked, take(warmth, near))))
    planes = layers + 2
    for i in range(layers):
        src = flip(z, layers, i)
        raw = [cells_ref[pl.ds(pl.multiple_of((f * layers + src) * rows, rows), rows), :] for f in range(RAW)]
        for f, value in enumerate(combine(raw, added[i * rows : (i + 1) * rows])):
            out_ref[f * planes + i] = value
    strips = Strips(
        [ref for ref, _ in sources[:2]], [at for _, at in sources[:2]], cells_ref, RAW * plane + 2 * seg, rows, layers
    )
    half = lane_of(chunk) // (LANES // 2) == (1 if partner else 0)
    for part in range(4):
        here = slice(part * chunk, (part + 1) * chunk)
        raw = [strips.both(f, part * chunk, chunk, x, gx, partner) for f in range(RAW)]
        for side in range(2):
            cells = [jnp.where(half, value[side], 0.0) for value in raw]
            for f, value in enumerate(combine(cells, beside[side][here])):
                out_ref[f * planes + layers + side, here, :] = value


def lay_segments(x, gx, seg, chunk, own_ref, at, sources, coef_ref, warmth_ref):
    distances = [1, gx - 1] + list(range(2, gx - 1))
    held = [(k, ref, at + (RAW * chunk if j < 2 else 0)) for j, (k, (ref, at)) in enumerate(zip(distances, sources))]
    place_segments(x, gx, seg, coef_ref, warmth_ref, [(0, own_ref, at)] + held)


def strip_kernel(gx, gy, shape, seg, *refs):
    layers, rows = shape
    cells_ref, near_ref, line_ref, masks_ref = refs[:4]
    received, refs = refs[4 : 4 + gx - 1], refs[4 + gx - 1 :]
    sides = 1 if gy == 2 else 2
    strip_refs, partner_refs, segments_ref = refs[:sides], refs[sides : 2 * sides], refs[2 * sides]
    plane, chunk = layers * rows, rows // 4
    x, y, z = (lax.axis_index(a) for a in ("gx", "gy", "gz"))
    n = segments_ref.shape[0] // 2
    coef_ref, warmth_ref = segments_ref.at[pl.ds(0, n), :], segments_ref.at[pl.ds(n, n), :]
    lay_segments(x, gx, seg, chunk, cells_ref, RAW * plane, [(ref, 0) for ref in received], coef_ref, warmth_ref)
    coef, warmth = coef_ref[...], warmth_ref[...]
    coupled = coupling(coef, warmth)
    columns = edge_columns(n, False)
    coef, warmth = take(coef, columns), take(warmth, columns)
    mask = jnp.where(lane_of(n) % GROUP < HALO, masks_ref[:n, :], masks_ref[n:, :])
    outer = coupling(coef * mask, warmth)
    strips = Strips(received[:2], [0, 0], cells_ref, RAW * plane + 2 * seg, rows, layers)
    low = lane_of(HALO) < LANES // 2
    first = lane_of(HALO) % GROUP < HALO
    upper = lax.broadcasted_iota(jnp.int32, (HALO, LANES), 0) < HALO // 2
    sent = FIELDS - 1

    def give(ref, at, values):
        for f, value in enumerate(values):
            ref[at + f * HALO : at + (f + 1) * HALO, :] = value

    def make(side, top):
        start = 0 if top else rows - HALO
        strip_ref, partner_ref = strip_refs[side], partner_refs[side]

        def shrink(values):
            *whole, e, g = values
            if top:
                g = pltpu.roll(g, HALO // 2, 0)
            else:
                e = pltpu.roll(e, HALO // 2, 0)
            return whole + [jnp.where(upper, e, g)]

        near = layers * HALO
        added = exact_dot(near_ref[side * near : (side + 1) * near, :], coupled)
        line = line_ref[side * 2 * HALO : (side + 1) * 2 * HALO, :]
        beside = exact_dot(line, outer)[:HALO]
        whole, stride, later, shared = partner_rows(layers)
        for i in range(layers):
            src = flip(z, layers, i)
            raw = [
                cells_ref[pl.ds(pl.multiple_of((f * layers + src) * rows + start, HALO), HALO), :] for f in range(RAW)
            ]
            values = combine(raw, added[i * HALO : (i + 1) * HALO])
            give(strip_ref, i * sent * HALO, shrink(values))
            pieces = [(f, m, f * stride + at) for f in range(sent - 1) for j, m, at in whole if j == i]
            pieces += [(sent - 1 + f, m, (sent - 1) * stride + at) for f, j, m, at in later if j == i]
            for f, m, at in pieces:
                skip = 0 if top else HALO - m
                partner_ref[at : at + m, :] = values[f][skip : skip + m]
        raw = [jnp.where(first, *strips.both(f, start, HALO, x, gx, False)) for f in range(RAW)]
        values = shrink(combine(raw, beside))
        values = [jnp.where(low, values[j], pltpu.roll(values[j + 1], LANES // 2, 1)) for j in range(0, sent, 2)]
        give(strip_ref, layers * sent * HALO, values)
        give(partner_ref, (sent - 1) * stride + shared, values)

    for side, (top, _) in enumerate(sides_of(gy, y)):
        if top is True or top is False:
            make(side, top)
        else:
            pl.when(top)(functools.partial(make, side, True))
            pl.when(jnp.logical_not(top))(functools.partial(make, side, False))


def planes_of(count, total):
    return list(range(count)) + [total - 2, total - 1]


def lateral(buf, at, n, which):
    sums = []
    for i in which:
        centre = buf[i, pl.ds(at, n), :]
        beside = pltpu.roll(centre, 1, 1) + pltpu.roll(centre, LANES - 1, 1)
        sums.append(beside + (buf[i, pl.ds(at - 1, n), :] + buf[i, pl.ds(at + 1, n), :]))
    return sums


def vertical(planes, edges, count):
    sums = []
    for i in range(count):
        near = [planes[j] for j in (i - 1, i + 1) if 0 <= j < len(planes)]
        sums.append(functools.reduce(jnp.add, near))
    for edge in edges:
        lane = lane_of(edge.shape[0])
        up = jnp.where(lane >= GROUP, pltpu.roll(edge, GROUP, 1), 0.0)
        down = jnp.where(lane < LANES - GROUP, pltpu.roll(edge, LANES - GROUP, 1), 0.0)
        sums.append(up + down)
    return sums


def coefficients(s_ref, at, n, raw, dests, to, outside):
    a_ref, q_ref, r_ref, e_ref, g_ref, root_ref = dests
    total = s_ref.shape[0]
    sums = lateral(s_ref, at, n, range(total))
    t = [raw(1, i) for i in range(total)]
    above = vertical(t[:-2], t[-2:], total - 2)
    here = pl.ds(to, n)
    for i in range(total):
        s = s_ref[i, pl.ds(at, n), :]
        diag = raw(3, i) + s * sums[i] + t[i] * above[i]
        if outside or i >= total - 2:
            inverse = 1.0 / jnp.where(diag > 0.0, diag, 1.0)
            root = jnp.where(s > 0.0, 1.0 / jnp.where(s > 0.0, s, 1.0), 0.0)
        else:
            inverse, root = 1.0 / diag, 1.0 / s
        if i < root_ref.shape[0]:
            root_ref[i, here, :] = root
        scaled = s * inverse
        a_ref[i, here, :] = s * scaled
        r_ref[i, here, :] = raw(4, i) * scaled
        e_ref[i, here, :] = raw(5, i) * scaled
        g_ref[i, here, :] = raw(6, i) * inverse
        q_ref[i, here, :] = t[i] * root


def shifted_sums(distance):
    to = lax.broadcasted_iota(jnp.int32, (2 * LANES, LANES), 1)
    of = lax.broadcasted_iota(jnp.int32, (2 * LANES, LANES), 0) % LANES
    return as_onehot(jnp.abs(of - to) == distance)


def sweep_edges(src_ref, dst_ref, at, n, coefs, base, matrices):
    a_ref, q_ref, r_ref = coefs[:3]
    total = src_ref.shape[0]
    here, there = pl.ds(base, n), pl.ds(at, n)

    def product(value, matrix):
        return jnp.dot(jnp.concatenate(split(value), axis=1), matrix, preferred_element_type=jnp.float32)

    for i in (total - 2, total - 1):
        centre = src_ref[i, there, :]
        beside = product(centre, matrices[0])
        above = product(q_ref[i, here, :] * centre, matrices[1])
        beside = beside + (src_ref[i, pl.ds(at - 1, n), :] + src_ref[i, pl.ds(at + 1, n), :])
        dst_ref[i, there, :] = r_ref[i, here, :] + a_ref[i, here, :] * (beside + q_ref[i, here, :] * above)


def sweep(src_ref, dst_ref, at, n, count, coefs, base, edges=True):
    a_ref, q_ref, r_ref = coefs[:3]
    total = src_ref.shape[0]
    here, there = pl.ds(base, n), pl.ds(at, n)
    which = planes_of(count, total) if edges else list(range(count))
    sums = lateral(src_ref, at, n, which)
    scaled = [q_ref[i, here, :] * src_ref[i, there, :] for i in range(min(count + 1, total - 2))]
    outer = [q_ref[i, here, :] * src_ref[i, there, :] for i in which[count:]]
    above = vertical(scaled, outer, count)
    for j, i in enumerate(which):
        dst_ref[i, there, :] = r_ref[i, here, :] + a_ref[i, here, :] * (sums[j] + q_ref[i, here, :] * above[j])


def next_rhs(coefs, v_ref, at, n, base):
    r_ref, e_ref, g_ref = coefs[2:5]
    here = pl.ds(base, n)
    for i in range(v_ref.shape[0]):
        r_ref[i, here, :] = e_ref[i, here, :] + g_ref[i, here, :] * v_ref[i, pl.ds(at, n), :]


def meet(v_ref, at, n, count, back):
    total = v_ref.shape[0]
    here = pl.ds(at, n)
    lane = lane_of(n)
    j, group = lane % GROUP, lane // GROUP
    outer = jnp.logical_or(lane < ITERS, lane >= LANES - ITERS)
    left, right = v_ref[total - 2, here, :], v_ref[total - 1, here, :]
    middle = jnp.where(j < HALO, right, left)
    for i in range(count):
        value = v_ref[i, here, :]
        if back:
            moved = pltpu.roll(value, (i * GROUP + HALO) % LANES, 1)
            left = jnp.where(jnp.logical_and(group == i, j >= GROUP - ITERS), moved, left)
            right = jnp.where(jnp.logical_and(group == i, j < ITERS), moved, right)
        v_ref[i, here, :] = jnp.where(outer, pltpu.roll(middle, LANES - (i * GROUP + HALO), 1), value)
    if back:
        v_ref[total - 2, here, :] = left
        v_ref[total - 1, here, :] = right


def needed(layers, n):
    return min(2 * layers, layers + STEPS * ITERS - 1 - n)


def two_steps(layers, sweep_all, between, after):
    for step in range(STEPS):
        for n in range(step * ITERS, (step + 1) * ITERS):
            sweep_all(n, n % 2, needed(layers, n))
        after(step)
        if step < STEPS - 1:
            between()


PAD = 8


def tile_kernel(gx, gy, shape, *refs):
    layers, rows = shape
    own_ref, partner_ref, picks_ref, out_ref, below_ref, level_ref = refs[:6]
    s_ref, va_ref, vb_ref = refs[6:9]
    coefs = refs[9:]
    x, y, z = (lax.axis_index(a) for a in ("gx", "gy", "gz"))
    total = 2 * layers + 2
    zeros = jnp.zeros((PAD, LANES), jnp.float32)
    for ref in (s_ref, va_ref, vb_ref):
        for i in range(total):
            ref[i, 0:PAD, :] = zeros
            ref[i, PAD + rows : PAD + rows + PAD, :] = zeros

    def field(f, i, here):
        j = f * (layers + 2)
        if i >= 2 * layers:
            j = j + i - layers
            return own_ref[j, here, :] + partner_ref[j, here, :]
        return own_ref[j + i, here, :] if i < layers else partner_ref[j + i - layers, here, :]

    for i in range(total):
        s_ref[i, PAD : PAD + rows, :] = field(0, i, slice(None))
        va_ref[i, PAD : PAD + rows, :] = field(2, i, slice(None))
    n = 8
    for at in range(0, rows, n):
        coefficients(s_ref, PAD + at, n, lambda f, i: field(f, i, slice(at, at + n)), coefs, at, False)

    bufs = (va_ref, vb_ref)
    sides = sides_of(gy, y)
    matrices = shifted_sums(1), shifted_sums(GROUP)

    def sweep_all(number, which, count):
        src_ref, dst_ref = bufs[which], bufs[1 - which]
        for side, (above, _) in enumerate(sides):
            inner = pl.ds(PAD + inner_at(above, rows), HALO)
            for i in range(total):
                level_ref[(side * STEPS * ITERS + number) * total + i] = src_ref[i, inner, :]
        sweep_edges(src_ref, dst_ref, PAD, rows, coefs, 0, matrices)
        for at in range(0, rows, n):
            sweep(src_ref, dst_ref, PAD + at, n, count, coefs, at, edges=False)

    def after(step):
        last = step == STEPS - 1
        for at in range(0, rows, n):
            meet(va_ref, PAD + at, n, layers if last else 2 * layers, not last)
        heat = []
        for i in range(layers):
            here = pl.ds(PAD, rows)
            heat.append(va_ref[i, here, :] * coefs[5][i])
            if step == STEPS - 1:
                out_ref[flip(z, layers, i)] = heat[-1]
        below_ref[step] = exact_dot(picks_ref[...], jnp.concatenate(heat, axis=0))

    def between():
        for at in range(0, rows, n):
            next_rhs(coefs, va_ref, PAD + at, n, at)

    two_steps(layers, sweep_all, between, after)


def edge_kernel(gx, gy, shape, seg, *refs):
    layers, rows = shape
    own_ref, partner_ref, picks_ref, mine_ref, segments_ref, below_ref, level_ref = refs[:7]
    sides_n = 1 if gy == 2 else 2
    along, across = refs[7 : 7 + sides_n], refs[7 + sides_n : 7 + 2 * sides_n]
    refs = refs[7 + 2 * sides_n :]
    heat_ref, returns = refs[0], refs[1 : 1 + gx]
    ret_ref, s_ref, va_ref, vb_ref = refs[1 + gx : 5 + gx]
    coefs = refs[5 + gx :]
    x, y, z = (lax.axis_index(a) for a in ("gx", "gy", "gz"))
    total = 2 * layers + 2
    count = mine_ref.shape[0]
    below = [below_ref[step] for step in range(STEPS)]
    lane = lane_of(HALO)
    low, first = lane < LANES // 2, lane % GROUP < HALO
    columns = edge_columns(HALO, False)
    bufs = (va_ref, vb_ref)

    def tile(j):
        return pl.ds(j if isinstance(j, int) else pl.multiple_of(j, HALO), HALO)

    for side, (above, live) in enumerate(sides_of(gy, y)):
        def place(when_top, otherwise):
            if above is True or above is False:
                return when_top * HALO if above else otherwise * HALO
            return jnp.where(above, when_top * HALO, otherwise * HALO)

        outer, strip, edge, inner = place(0, 3), place(1, 2), place(2, 1), place(3, 0)
        edge_rows = tile(edge_at(above, rows))
        inner_rows = tile(inner_at(above, rows))

        def field(f, i, here):
            j = f * (layers + 2)
            if i >= 2 * layers:
                j = j + i - layers
                return own_ref[j, here, :] + partner_ref[j, here, :]
            return own_ref[j + i, here, :] if i < layers else partner_ref[j + i - layers, here, :]

        t_ref, d_ref, q_ref, e_ref, g_ref = coefs[1], coefs[0], coefs[2], coefs[3], coefs[4]
        keep = {0: s_ref, 1: t_ref, 2: va_ref, 3: d_ref, 4: q_ref, 5: e_ref, 6: g_ref}
        zeros = jnp.zeros((HALO, LANES), jnp.float32)
        src = lane % (LANES // 2)
        turned = (layers - 1 - src // GROUP) * GROUP + src % GROUP
        half_tile = lax.broadcasted_iota(jnp.int32, (HALO, LANES), 0) < HALO // 2

        def unpack(value, f):
            if f < FIELDS - 2:
                return value
            turned_value = pltpu.roll(value, HALO // 2, 0)
            if f == FIELDS - 2:
                at_top, at_bottom = jnp.where(half_tile, 0.0, turned_value), jnp.where(half_tile, value, 0.0)
            else:
                at_top, at_bottom = jnp.where(half_tile, 0.0, value), jnp.where(half_tile, turned_value, 0.0)
            return jnp.where(above, at_top, at_bottom)

        whole, stride, later, shared = partner_rows(layers)
        sublane = lax.broadcasted_iota(jnp.int32, (HALO, LANES), 0)

        def nearest(ref, m, at):
            at_top = jnp.where(sublane >= HALO - m, ref[at - HALO + m : at + m, :], 0.0)
            return jnp.where(above, at_top, jnp.where(sublane < m, ref[at : at + HALO, :], 0.0))

        for f in range(FIELDS):
            g = min(f, FIELDS - 2)
            if f < FIELDS - 2:
                rows_of = {i: (m, f * stride + at) for i, m, at in whole}
            else:
                rows_of = {i: (m, (FIELDS - 2) * stride + at) for which, i, m, at in later if which == f - FIELDS + 2}
            values, inside = [], zeros
            for i in range(2 * layers):
                if i < layers:
                    at = (i * (FIELDS - 1) + g) * HALO
                    value = unpack(along[side][at : at + HALO, :], f)
                else:
                    j = 2 * layers - 1 - i
                    value = nearest(across[side], *rows_of[j]) if j in rows_of else zeros
                values.append(value)
                inside = jnp.where(lane // GROUP == i, take(value, columns), inside)
            half = (LANES // 2) * (g % 2)
            at = (layers * (FIELDS - 1) + g // 2) * HALO
            a = take(along[side][at : at + HALO, :], src + half)
            at = (FIELDS - 2) * stride + shared + (g // 2) * HALO
            b = take(across[side][at : at + HALO, :], turned + half)
            outside = unpack(jnp.where(low, a, b), f)
            values += [jnp.where(first, outside, inside), jnp.where(first, inside, outside)]
            for i, value in enumerate(values):
                ref, shift = keep[f], 0 if f in (0, 2) else HALO
                ref[i, tile(strip - shift), :] = value
                ref[i, tile(edge - shift), :] = field(f, i, edge_rows)
        for i in range(total):
            s_ref[i, tile(outer), :] = zeros
            va_ref[i, tile(outer), :] = zeros
            vb_ref[i, tile(outer), :] = zeros
            s_ref[i, tile(inner), :] = field(0, i, inner_rows)
        n = 2 * HALO
        held = [[keep[f][i, pl.ds(0, n), :] for i in range(total)] if f in (1, 3, 4, 5, 6) else None for f in range(FIELDS)]
        coefficients(s_ref, HALO, n, lambda f, i: held[f][i], coefs, 0, True)

        def sweep_all(number, which, needed_layers):
            src_ref, dst_ref = bufs[which], bufs[1 - which]
            for i in range(total):
                src_ref[i, tile(inner), :] = level_ref[(side * STEPS * ITERS + number) * total + i]
            for at in range(0, n, HALO):
                sweep(src_ref, dst_ref, HALO + at, HALO, needed_layers, coefs, at)

        picks = picks_ref[side * count : (side + 1) * count, :]

        def after(step):
            last = step == STEPS - 1
            meet(va_ref, HALO, n, layers if last else 2 * layers, not last)
            heat = []
            for i in range(layers):
                heat.append(va_ref[i, tile(edge), :] * coefs[5][i, tile(edge - HALO), :])
                if step == STEPS - 1:
                    heat_ref[side * layers + flip(z, layers, i)] = heat[-1]
            heat.append(jnp.zeros((LANES - layers * HALO, LANES), jnp.float32))
            below[step] = below[step] + exact_dot(picks, jnp.concatenate(heat, axis=0))

        two_steps(layers, sweep_all, lambda: next_rhs(coefs, va_ref, HALO, n, 0), after)

    coef, warmth = segments_ref[:count, :], segments_ref[count:, :]
    for step in range(STEPS):
        warmth = warmth + coolant_gain * coef * (below[step] - warmth)
    ret_ref[...] = jnp.where(mine_ref[...] > 0.0, warmth, 0.0)
    for k, ref in enumerate(returns):
        ref[...] = ret_ref[pl.ds(pl.multiple_of(lax.rem(x + k, gx) * seg, seg), seg), :]


def merge_kernel(gy, whole_ref, heat_ref, out_ref):
    layers, rows, _ = whole_ref.shape
    out_ref[...] = whole_ref[...]
    for side, (above, live) in enumerate(sides_of(gy, lax.axis_index("gy"))):
        def put(side=side, above=above):
            out_ref[:, pl.ds(edge_at(above, rows), HALO), :] = heat_ref[side * layers : (side + 1) * layers]

        if live is True:
            put()
        else:
            pl.when(live)(put)


def local(gx, gy, gz, u, power, storage, conductance, warmth, coef, holder, stratum, transverse):
    layers, rows, columns = u.shape
    seg = warmth.shape[1]
    segments = stratum.shape[1]
    if gz != 2 or gx < 3 or columns != LANES or 2 * layers * GROUP != LANES or rows % 32:
        raise ValueError("unsupported shape")
    holder = holder[:, :, 0]
    shape = (layers, rows)
    f32 = jnp.float32
    chunk = rows // 4
    wide = RAW * chunk + 2 * seg

    def struct(*dims):
        return jax.ShapeDtypeStruct(dims, f32)

    def vmem(*dims):
        return pltpu.VMEM(dims, f32)

    indices = (holder, stratum, transverse)
    flat = [a.reshape(-1, LANES) for a in (u, power, storage, conductance, warmth, coef)]
    own, to_left, to_right, only, *indices = pl.pallas_call(
        functools.partial(pack_kernel, shape),
        out_shape=(
            struct(RAW * layers * rows + 2 * seg + 2 * RAW * chunk, LANES),
            struct(wide, LANES),
            struct(wide, LANES),
            struct(2 * seg, LANES),
            *(jax.ShapeDtypeStruct(a.shape, a.dtype) for a in indices),
        ),
        in_specs=[pl.BlockSpec(memory_space=pltpu.HBM)] * 9,
        out_specs=(VMEM,) * 7,
        scratch_shapes=[pltpu.SemaphoreType.DMA((9,))],
        compiler_params=PARAMS,
        name="pack",
    )(*(pltpu.with_memory_space_constraint(a, pltpu.HBM) for a in (*flat, *indices)))

    swap = [(0, 1), (1, 0)]
    partner = lax.ppermute(own, "gz", swap)
    def from_distance(value, k):
        return lax.ppermute(value, "gx", [(i, (i - k) % gx) for i in range(gx)])

    received = [from_distance(to_left, 1), from_distance(to_right, gx - 1)]
    received += [from_distance(only, k) for k in range(2, gx - 1)]

    sides = 1 if gy == 2 else 2
    fields = struct(FIELDS * (layers + 2), rows, LANES)
    strip_rows = (FIELDS - 1) * layers * HALO + (FIELDS - 1) // 2 * HALO
    _, stride, _, shared = partner_rows(layers)
    partner_strip = (FIELDS - 2) * stride + shared + (FIELDS - 1) // 2 * HALO
    sides = 1 if gy == 2 else 2
    bf16 = jnp.bfloat16
    one_group = (
        jax.ShapeDtypeStruct((layers * rows, segments), bf16),
        jax.ShapeDtypeStruct((rows, segments), bf16),
        struct(2 * segments, LANES),
    )
    maps = pl.pallas_call(
        functools.partial(maps_kernel, gx, gy, shape),
        out_shape=one_group
        + one_group
        + (
            jax.ShapeDtypeStruct((segments, layers * rows), bf16),
            jax.ShapeDtypeStruct((sides * segments, LANES), bf16),
            struct(segments, LANES),
            jax.ShapeDtypeStruct((sides * layers * HALO, segments), bf16),
            jax.ShapeDtypeStruct((sides * 2 * HALO, segments), bf16),
        ),
        in_specs=[VMEM] * 3,
        out_specs=(VMEM,) * 11,
        compiler_params=PARAMS,
        cost_estimate=cost(1),
        name="maps",
    )(*indices)
    own_maps, partner_maps, (picks, picks_beside, mine, near, line) = maps[:3], maps[3:6], maps[6:]
    joined = pl.pallas_call(
        join_kernel,
        out_shape=struct(sum(a.shape[0] for a in received), LANES),
        in_specs=[pl.BlockSpec(memory_space=pl.ANY)] + [VMEM] * (gx - 1),
        out_specs=VMEM,
        compiler_params=PARAMS,
        name="join",
    )(mine, *received)
    late = lax.ppermute(joined, "gz", swap)
    made = pl.pallas_call(
        functools.partial(strip_kernel, gx, gy, shape, seg),
        out_shape=(struct(strip_rows, LANES),) * sides
        + (struct(partner_strip, LANES),) * sides
        + (struct(2 * segments, LANES),),
        in_specs=[VMEM] * (4 + gx - 1),
        out_specs=(VMEM,) * (1 + 2 * sides),
        compiler_params=PARAMS,
        cost_estimate=cost(0.5),
        name="strips",
    )(own, near, line, own_maps[2], *received)
    strips, partner_strips, held = made[:sides], made[sides : 2 * sides], made[2 * sides]
    own_fields = pl.pallas_call(
        functools.partial(fill_kernel, False, gx, gy, shape, seg),
        out_shape=fields,
        in_specs=[VMEM] * 7,
        out_specs=VMEM,
        compiler_params=PARAMS,
        cost_estimate=cost(1.5),
        name="fill_own",
    )(own, *own_maps, *received[:2], held)
    if gy == 2:
        routes = [(0, swap)]
    else:
        up = [(i, i + 1) for i in range(gy - 1)]
        routes = [(1, up), (0, [(j, i) for i, j in up])]
    along = [lax.ppermute(strips[side], "gy", pairs) for side, pairs in routes]
    across = []
    for side, pairs in routes:
        both = [(2 * i + z, 2 * j + 1 - z) for i, j in pairs for z in range(2)]
        across.append(lax.ppermute(partner_strips[side], ("gy", "gz"), both))

    partner_fields = pl.pallas_call(
        functools.partial(fill_kernel, True, gx, gy, shape, seg),
        out_shape=fields,
        in_specs=[VMEM] * 5,
        out_specs=VMEM,
        scratch_shapes=[vmem(segments, LANES)] * 2,
        compiler_params=PARAMS,
        cost_estimate=cost(1.5),
        name="fill_partner",
    )(partner, *partner_maps, late)

    total = 2 * layers + 2
    padded = vmem(total, rows + 2 * PAD, LANES)
    inside, below, levels = pl.pallas_call(
        functools.partial(tile_kernel, gx, gy, shape),
        out_shape=(
            struct(layers, rows, LANES),
            struct(STEPS, segments, LANES),
            struct(sides * STEPS * ITERS * total, HALO, LANES),
        ),
        in_specs=[VMEM] * 3,
        out_specs=(VMEM,) * 3,
        scratch_shapes=[padded] * 3 + [vmem(total, rows, LANES)] * 5 + [vmem(layers, rows, LANES)],
        compiler_params=PARAMS,
        cost_estimate=cost(7),
        name="tile_sweeps",
    )(own_fields, partner_fields, picks)

    results = pl.pallas_call(
        functools.partial(edge_kernel, gx, gy, shape, seg),
        out_shape=(struct(sides * layers, HALO, LANES),) + (struct(seg, LANES),) * gx,
        in_specs=[VMEM] * (7 + 2 * sides),
        out_specs=(VMEM,) * (1 + gx),
        scratch_shapes=[vmem(segments, LANES)]
        + [vmem(total, 4 * HALO, LANES)] * 3
        + [vmem(total, 2 * HALO, LANES)] * 5
        + [vmem(layers, 2 * HALO, LANES)],
        compiler_params=PARAMS,
        cost_estimate=cost(1.5),
        name="edge_sweeps",
    )(own_fields, partner_fields, picks_beside, mine, held, below, levels, *along, *across)
    heat, coolant = results[0], results[1]
    returned = [lax.ppermute(results[1 + k], "gx", [(i, (i + k) % gx) for i in range(gx)]) for k in range(1, gx)]
    temperature = pl.pallas_call(
        functools.partial(merge_kernel, gy),
        out_shape=struct(layers, rows, LANES),
        in_specs=[VMEM] * 2,
        out_specs=VMEM,
        compiler_params=PARAMS,
        cost_estimate=cost(1),
        name="merge",
    )(inside, heat)
    for value in returned:
        coolant = coolant + value
    return temperature, coolant[None]


def solution(mesh):
    gx, gy, gz = (mesh.shape[a] for a in ("gx", "gy", "gz"))
    cells = P(("stack", "gz"), "gy", "gx")
    segments = P(("stack", "gy", "gz"), "gx", None)
    return jax.shard_map(
        functools.partial(local, gx, gy, gz),
        mesh=mesh,
        in_specs=(cells, cells, cells, P(None, ("stack", "gz"), "gy", "gx"), segments, segments, P(), P(), P()),
        out_specs=(cells, segments),
        check_vma=False,
    )
```
